32 devices in a mesh: dp: 8 (over z, y), tensor: 4 (over x, core).
Axes of the slice: x: 2, y: 2, z: 4, core: 2. Of those that a mesh axis runs over, the one named last changes fastest.
Arguments:
- inputs: float32 [16384, 768], P('dp'), may hold values from -6 to 6
- segment_ids: int32 [32, 512], P('dp'), may hold values from 0 to 7, never falling along the last dimension, each value on 1 to 128 neighbouring positions
- w_qkv: float32 [3, 768, 768], P(None, None, 'tensor')
- b_qv: float32 [2, 768], P(None, 'tensor'), may hold values from -3 to 3
- w_out: float32 [768, 768], P('tensor')
- w_ff1: float32 [768, 3072], P(None, 'tensor')
- b_ff1: float32 [3072], P('tensor'), may hold values from -3 to 3
- w_ff2: float32 [3072, 768], P('tensor')
- norm_gains: float32 [2, 768], replicated, may hold values from 0.25 to 1.75
- shift_biases: float32 [4, 768], replicated, may hold values from -2 to 2
- act_ranges: float32 [4], replicated, may hold values from 1 to 24
- cotangent: float32 [16384, 768], P('dp'), may hold values from -6 to 6
Outputs:
- layer_out: float32 [16384, 768], P('dp')
- input_grad: float32 [16384, 768], P('dp')
- grad_qkv: float32 [3, 768, 768], P(None, None, 'tensor')
- grad_bqv: float32 [2, 768], P(None, 'tensor')
- grad_out: float32 [768, 768], P('tensor')
- grad_ff1: float32 [768, 3072], P(None, 'tensor')
- grad_bff1: float32 [3072], P('tensor')
- grad_ff2: float32 [3072, 768], P('tensor')
- grad_gains: float32 [2, 768], P(None, 'tensor')
- grad_shifts: float32 [4, 768], P(None, 'tensor')
- weight_max: float32 [6], replicated
The draws below stay inside these ranges and needn't reach their ends.
Inputs may be any that keep to these rules, and one draw needn't show every extreme that they name: `segment_ids`: equal ids within a packed row mark one example; ids never fall along a row.
All inputs are finite; a program needn't handle non-finite values.
Results may differ from the reference program's by a relative error of at most 0.019.
Values may be sent and summed in bfloat16 or wider, within the bound.
A program may use at most 192 MiB of HBM per device.

```python
import math
import jax
import jax.numpy as jnp
import numpy as np
from jax import lax

D = 768
HEADS = 12
HD = 64
FF = 3072
SEQ = 512
ROWS = 32
TOKENS = 16384
N_TENSOR = 4


def heavy_matrix(key, shape, fan):
    first, second = jax.random.split(key)
    base = jnp.clip(jax.random.normal(first, shape, jnp.float32), -6.0, 6.0)
    spread = jnp.clip(jax.random.normal(second, shape, jnp.float32), -4.0, 4.0)
    return base * jnp.exp(0.5 * spread) * (0.7788 / math.sqrt(fan))


def draw_w_qkv(key, part):
    key = jax.random.fold_in(key, 11)
    return heavy_matrix(key, (3, D, D), D)


def draw_w_out(key, part):
    key = jax.random.fold_in(key, 12)
    return heavy_matrix(key, (D, D), D // 16)


def draw_w_ff1(key, part):
    key = jax.random.fold_in(key, 13)
    return heavy_matrix(key, (D, FF), D)


def draw_w_ff2(key, part):
    key = jax.random.fold_in(key, 14)
    return heavy_matrix(key, (FF, D), FF)


def draw_act_ranges(key, part):
    key = jax.random.fold_in(key, 15)
    base = jnp.array([6.0, 1.0, 6.0, 4.0], jnp.float32)
    factor = jnp.exp(jax.random.uniform(key, (4,), jnp.float32, 0.0, math.log(4.0)))
    return base * factor


def steps_of(key, extent, cuts, least, high):
    gain = 1.0
    for dim, blocks in cuts:
        heights = jax.random.uniform(jax.random.fold_in(jax.random.fold_in(key, 6), dim), (blocks,), jnp.float32, least / len(cuts), high / len(cuts))
        gain = gain * jnp.repeat(jnp.exp(heights), extent[dim] // blocks).reshape((-1,) + (1,) * (len(extent) - 1 - dim))
    return gain


def profile(number_of, total, limit, slope):
    loads = [(1 << 20) // math.isqrt(grade ** slope) + 1 for grade in range(2, number_of + 1)]
    spare, given = total - limit - (number_of - 1), [1] * (number_of - 1)
    while spare > 0:
        free = [i for i in range(number_of - 1) if given[i] < limit]
        mass, left = sum([loads[i] for i in free]), spare
        for i in free:
            extra = min(limit - given[i], max(1, left * loads[i] // mass), spare)
            given[i] = given[i] + extra
            spare = spare - extra
    return np.array([limit] + given)


def uneven_parts(stream_key, number_of, total, limit, skew):
    if number_of == 2:
        one = jax.random.randint(stream_key, (), max(1, total - limit), min(limit, total - 1) + 1)
        return jnp.stack([one, total - one])
    lengths = jnp.asarray(profile(number_of, total, limit, skew), jnp.int32)
    couples = (number_of - 1) // 2
    giver, taker = lengths[1:1 + 2 * couples:2], lengths[2:2 + 2 * couples:2]
    slack = jnp.minimum(giver - 1, limit - taker)
    passed = jax.random.randint(jax.random.fold_in(stream_key, 1), (couples,), 0, 1 << 20) % (slack + 1)
    lengths = lengths.at[1:1 + 2 * couples:2].set(giver - passed).at[2:2 + 2 * couples:2].set(taker + passed)
    return lengths[jax.random.permutation(jax.random.fold_in(stream_key, 2), number_of)]


def normal_values(own_key, dims, width, most, cuts=(), kind=jnp.bfloat16):
    drawn = jax.random.normal(own_key, dims, jnp.float32) * width
    if len(cuts) > 0:
        drawn = steps_of(own_key, dims, cuts, -0.22, 0.18) * drawn
    return jnp.clip(drawn, min=-most, max=most).astype(kind)


def setup_inputs(seed: int = 0) -> dict:
    streams_of = jax.random.split(jax.random.key(seed), 13)
    inputs = normal_values(streams_of[0], (TOKENS, D), 1.0, 6.0, ((0, 8),), jnp.float32)
    segment_ids = jax.vmap(lambda own: jnp.searchsorted(jnp.cumsum(uneven_parts(own, 8, SEQ, SEQ // 4, 2)), jnp.arange(SEQ), side="right"))(jax.random.split(streams_of[1], ROWS)).reshape((ROWS, SEQ)).astype(jnp.int32)
    w_qkv = draw_w_qkv(jax.random.fold_in(streams_of[12], 71), 0)
    b_qv = normal_values(streams_of[3], (2, D), 0.5, 3.0, ((1, 4),), jnp.float32)
    w_out = draw_w_out(jax.random.fold_in(streams_of[12], 71), 0)
    w_ff1 = draw_w_ff1(jax.random.fold_in(streams_of[12], 71), 0)
    b_ff1 = normal_values(streams_of[6], (FF,), 0.5, 3.0, ((0, 4),), jnp.float32)
    w_ff2 = draw_w_ff2(jax.random.fold_in(streams_of[12], 71), 0)
    norm_gains = jnp.clip(1.0 + 0.15 * jax.random.normal(streams_of[8], (2, D), jnp.float32), 0.25, 1.75)
    shift_biases = normal_values(streams_of[9], (4, D), 0.3, 2.0, (), jnp.float32)
    act_ranges = draw_act_ranges(jax.random.fold_in(streams_of[12], 71), 0)
    cotangent = normal_values(streams_of[11], (TOKENS, D), 1.0, 6.0, ((0, 8),), jnp.float32)
    return dict(inputs=inputs, segment_ids=segment_ids, w_qkv=w_qkv, b_qv=b_qv, w_out=w_out, w_ff1=w_ff1, b_ff1=b_ff1, w_ff2=w_ff2, norm_gains=norm_gains, shift_biases=shift_biases, act_ranges=act_ranges, cotangent=cotangent)


TWO_PI = 2.0 * math.pi
MASKED = -1e+30
EPSILON = 1e-06
ROOT_HALF = 0.7071067811865476
HIGHEST = lax.Precision.HIGHEST

@jax.custom_vjp
def low(v):
    return lax.optimization_barrier(v.astype(jnp.bfloat16)).astype(jnp.float32)

@jax.custom_vjp
def low_back(v):
    return v

def low_keep(v):
    return (low(v), None)

def low_pass(kept, grad):
    return (grad,)

def back_keep(v):
    return (v, None)

def back_low(kept, grad):
    return (low(grad),)
low.defvjp(low_keep, low_pass)
low_back.defvjp(back_keep, back_low)

def staircase(levels):
    return levels - jnp.sin(TWO_PI * levels) / TWO_PI

def stair_weight(matrix, largest):
    return largest / 127.0 * staircase(127.0 * matrix / largest)

def stair_act(values, bound, offset):
    squash = jnp.tanh(values / bound)
    if offset is None:
        offset = -(bound / 127.0) * jnp.sin(TWO_PI * 127.0 * squash) / TWO_PI
    return (bound * squash + offset, offset)

def layer_norm(hidden, gain_row, shift_row):
    average = lax.optimization_barrier(jnp.mean(hidden, -1, keepdims=True))
    centred = hidden - average
    normed = centred * lax.rsqrt(lax.optimization_barrier(jnp.mean(centred * centred, -1, keepdims=True)) + EPSILON)
    return normed * gain_row + shift_row

def gelu_exact(values):
    return 0.5 * values * (1.0 + lax.erf(values * ROOT_HALF))

def attend(pieces):
    queries, keys_in, values_in, segment = pieces
    scores = low_back(jnp.einsum('qhd,khd->hqk', queries, keys_in, precision=HIGHEST) * 0.125)
    same_doc = segment[:, None] == segment[None, :]
    scores = jnp.where(same_doc[None], scores, MASKED)
    largest = lax.optimization_barrier(jnp.max(scores, -1, keepdims=True))
    weights_exp = jnp.exp(scores - largest)
    probs = weights_exp / lax.optimization_barrier(jnp.sum(weights_exp, -1, keepdims=True))
    return jnp.einsum('hqk,khd->qhd', low(probs), values_in, precision=HIGHEST)

def group_sum(left, right, groups):
    tokens_here = left.shape[0]
    inner = left.shape[1] // groups
    parts = jnp.einsum('tgc,gcd->gtd', left.reshape(tokens_here, groups, inner), right.reshape(groups, inner, right.shape[1]), precision=HIGHEST)
    return lax.optimization_barrier(jnp.sum(low(parts), 0))

def block_forward(params, noise, inputs, seg_block, act_ranges, offsets):
    w_qkv, b_qv, w_out, w_ff1, b_ff1, w_ff2, norm_gains, shift_biases = params
    noise_qkv, noise_out, noise_ff1, noise_ff2 = noise
    if offsets is None:
        offsets = (None, None, None, None)
    tokens_here = inputs.shape[0]
    seq_count = seg_block.shape[0]
    x_act, off_x = stair_act(inputs, act_ranges[0], offsets[0])
    x_low = low(x_act)
    proj = jnp.einsum('td,jde->jte', x_low, low(w_qkv + noise_qkv), precision=HIGHEST)
    queries = low(low_back(proj[0] + b_qv[0]))
    keys_all = low(low_back(proj[1]))
    values_all = low(low_back(proj[2] + b_qv[1]))
    shape_heads = (seq_count, SEQ, HEADS, HD)
    context = lax.map(jax.checkpoint(attend), (queries.reshape(shape_heads), keys_all.reshape(shape_heads), values_all.reshape(shape_heads), seg_block))
    context = context.reshape(tokens_here, D)
    c_act, off_c = stair_act(low_back(context), act_ranges[1], offsets[1])
    c_low = low(c_act)
    attn = low_back(group_sum(c_low, low(w_out + noise_out), N_TENSOR)) + shift_biases[0]
    first = layer_norm(inputs + attn, norm_gains[0], shift_biases[1])
    n_act, off_n = stair_act(first, act_ranges[2], offsets[2])
    n_low = low(n_act)
    pre = low_back(jnp.dot(n_low, low(w_ff1 + noise_ff1), precision=HIGHEST)) + b_ff1
    g_act, off_g = stair_act(gelu_exact(pre), act_ranges[3], offsets[3])
    g_low = low(g_act)
    ffn = low_back(group_sum(g_low, low(w_ff2 + noise_ff2), N_TENSOR)) + shift_biases[2]
    result = layer_norm(first + ffn, norm_gains[1], shift_biases[3])
    return (result, (off_x, off_c, off_n, off_g))

def reference(inputs, segment_ids, w_qkv, b_qv, w_out, w_ff1, b_ff1, w_ff2, norm_gains, shift_biases, act_ranges, cotangent):
    weight_max = jnp.stack([jnp.max(jnp.abs(w_qkv[0])), jnp.max(jnp.abs(w_qkv[1])), jnp.max(jnp.abs(w_qkv[2])), jnp.max(jnp.abs(w_out)), jnp.max(jnp.abs(w_ff1)), jnp.max(jnp.abs(w_ff2))])
    noise_qkv = jnp.stack([stair_weight(w_qkv[member], weight_max[member]) for member in range(3)]) - w_qkv
    noise_out = stair_weight(w_out, weight_max[3]) - w_out
    noise_ff1 = stair_weight(w_ff1, weight_max[4]) - w_ff1
    noise_ff2 = stair_weight(w_ff2, weight_max[5]) - w_ff2
    noise = (noise_qkv, noise_out, noise_ff1, noise_ff2)
    params = (w_qkv, b_qv, w_out, w_ff1, b_ff1, w_ff2, norm_gains, shift_biases)
    total_seqs = segment_ids.shape[0]
    group = math.gcd(total_seqs, max(1, 4096 // SEQ))
    blocks = total_seqs // group
    x_blocks = inputs.reshape(blocks, group * SEQ, D)
    seg_blocks = segment_ids.reshape(blocks, group, SEQ)
    dy_blocks = cotangent.reshape(blocks, group * SEQ, D)

    def block_step(totals, pieces):
        x_block, seg_block, dy_block = pieces
        offsets = block_forward(params, noise, x_block, seg_block, act_ranges, None)[1]
        outputs, pullback = jax.vjp(lambda par, xx: block_forward(par, noise, xx, seg_block, act_ranges, offsets)[0], params, x_block)
        grads, d_input = pullback(dy_block)
        return (jax.tree.map(jnp.add, totals, grads), (outputs, d_input))
    start = jax.tree.map(jnp.zeros_like, params)
    grads, (outputs, d_inputs) = lax.scan(block_step, start, (x_blocks, seg_blocks, dy_blocks))
    layer_out = outputs.reshape(TOKENS, D)
    input_grad = d_inputs.reshape(TOKENS, D)
    grad_qkv, grad_bqv, grad_out, grad_ff1, grad_bff1, grad_ff2, grad_gains, grad_shifts = grads
    return (layer_out, input_grad, grad_qkv, grad_bqv, grad_out, grad_ff1, grad_bff1, grad_ff2, grad_gains, grad_shifts, weight_max)
```

```python
import functools
import math

import jax
import jax.numpy as jnp
from jax import lax
from jax.experimental import pallas as pl
from jax.experimental.pallas import tpu as pltpu
from jax.sharding import PartitionSpec as P

HD = 64
SPAN = 128
QB = 256
MASKED = -1e30
EPSILON = 1e-06
ROOT_HALF = 0.7071067811865476
INV_ROOT_TWO_PI = 0.3989422804014327
STAIR = (
    6.579734980213376,
    -12.987641368031495,
    12.20087719668052,
    -6.61489684889321,
    2.04264519055443,
)
MIB = 1 << 20
MESH = pl.DeviceIdType.MESH
F32 = jnp.float32
BF16 = jnp.bfloat16
ANY = pl.BlockSpec(memory_space=pl.ANY)
VMEM = pl.BlockSpec(memory_space=pltpu.VMEM)
SMEM = pl.BlockSpec(memory_space=pltpu.SMEM)
S = jax.ShapeDtypeStruct


def flip(value, bit):
    return value + bit - 2 * bit * ((value // bit) % 2)


def dot_nn(left, right):
    return lax.dot_general(left, right, (((1,), (0,)), ((), ())), preferred_element_type=F32)


def dot_nt(left, right):
    return lax.dot_general(left, right, (((1,), (1,)), ((), ())), preferred_element_type=F32)


def dot_tn(left, right):
    return lax.dot_general(left, right, (((0,), (0,)), ((), ())), preferred_element_type=F32)


def stairs(levels):
    whole = jnp.round(levels)
    rest = levels - whole
    square = rest * rest
    curve = STAIR[4]
    for factor in STAIR[3::-1]:
        curve = curve * square + factor
    return whole + rest * square * curve


def quantize(values, bound):
    squash = jnp.tanh(values * (1.0 / bound))
    return stairs(127.0 * squash) * (bound / 127.0), squash


def norm(hidden):
    centred = hidden - jnp.mean(hidden, -1, keepdims=True)
    inverse = lax.rsqrt(jnp.mean(centred * centred, -1, keepdims=True) + EPSILON)
    return centred * inverse, inverse


def norm_back(scaled, normed, inverse):
    return inverse * (
        scaled
        - jnp.mean(scaled, -1, keepdims=True)
        - normed * jnp.mean(scaled * normed, -1, keepdims=True)
    )


def windows(length):
    found = []
    for first in range(0, length, QB):
        low = max(0, first - SPAN)
        found.append((first, low, min(length, first + QB + SPAN) - low))
    return found


def gather_kernel(
    wqkv, wout, wff1, wff2, bqv, bff1,
    wt_all, wo_all, w1_all, w2_all, small_out,
    f_qkv, f_out, f_1, f_2, q_qkv, q_out, q_1, q_2, small,
    load_sem, local_sem, small_send, small_recv,
    sib_send, sib_recv, far_send, far_recv, side_send, side_recv, pass_send, pass_recv,
):
    t, d = lax.axis_index("tensor"), lax.axis_index("dp")
    y = d % 2
    sib, far, side = (d, flip(t, 1)), (d, flip(t, 2)), (flip(d, 1), t)
    loads = [
        pltpu.make_async_copy(src, dst, load_sem.at[i])
        for i, (src, dst) in enumerate(((wqkv, f_qkv), (wout, f_out), (wff1, f_1), (wff2, f_2)))
    ]
    for load in loads:
        load.start()
    peers = [sib, far, (d, flip(flip(t, 1), 2))]
    barrier = pltpu.get_barrier_semaphore()
    for peer in peers + [side]:
        pl.semaphore_signal(barrier, inc=1, device_id=peer, device_id_type=MESH)
    pl.semaphore_wait(barrier, 4)

    cols = f_qkv.shape[2]
    width = f_out.shape[1]
    for load in loads:
        load.wait()
    tops = [jnp.max(jnp.abs(f_qkv[j]), axis=(0, 1), keepdims=True) for j in range(3)]
    tops += [jnp.max(jnp.abs(f[...]), axis=(0, 1), keepdims=True) for f in (f_out, f_1, f_2)]
    zeros = jnp.zeros((8, width), F32)
    small[pl.ds(t, 1)] = zeros[None]
    small[pl.ds(t, 1), 0:1, :] = bff1[...][None]
    small[pl.ds(t, 1), 1:3, 0:cols] = bqv[...][None]
    row = jnp.concatenate([jnp.broadcast_to(top, (1, 128)) for top in tops], axis=1)
    small[pl.ds(t, 1), 3:4, :] = row[None]
    sends = []
    for i, peer in enumerate(peers):
        copy = pltpu.make_async_remote_copy(
            src_ref=small.at[t], dst_ref=small.at[t], send_sem=small_send.at[i],
            recv_sem=small_recv.at[i], device_id=peer, device_id_type=MESH,
        )
        copy.start()
        sends.append(copy)
    for copy in sends:
        copy.wait()
    top_row = jnp.max(small[:, 3:4, :], axis=0)
    small_out[...] = small[...]

    def weight(value, j):
        top = top_row[:, 128 * j : 128 * j + 1]
        return (stairs(value * (127.0 / top)) * (top / 127.0)).astype(BF16)

    def slot(full, i, s, half):
        if i == 0:
            part = cols // 2
            if half is None:
                return full.at[:, pl.ds(pl.multiple_of(s * cols, 16), cols)]
            return full.at[:, pl.ds(pl.multiple_of(s * cols + half * part, 16), part)]
        if i == 1:
            part = cols // 2
            if half is None:
                return full.at[pl.ds(pl.multiple_of(s * cols, 16), cols)]
            return full.at[pl.ds(pl.multiple_of(s * cols + half * part, 16), part)]
        if half is None:
            return full.at[s]
        part = full.shape[1] // 2
        return full.at[s, pl.ds(pl.multiple_of(half * part, 16), part)]

    def own_half(own, i, half):
        if i == 0:
            part = cols // 2
            return own.at[:, pl.ds(pl.multiple_of(half * part, 16), part)]
        part = own.shape[0] // 2
        return own.at[pl.ds(pl.multiple_of(half * part, 16), part)]

    fulls = (wt_all, wo_all, w1_all, w2_all)
    owns = (q_qkv, q_out, q_1, q_2)
    pending = []
    for i in range(4):
        if i == 0:
            for j in range(3):
                q_qkv[j] = jnp.transpose(
                    (stairs(f_qkv[j] * (127.0 / top_row[:, 128 * j : 128 * j + 1]))
                     * (top_row[:, 128 * j : 128 * j + 1] / 127.0))
                ).astype(BF16)
        elif i == 1:
            q_out[...] = weight(f_out[...], 3)
        elif i == 2:
            q_1[...] = weight(f_1[...], 4)
        else:
            q_2[...] = weight(f_2[...], 5)
        far_copy = pltpu.make_async_remote_copy(
            src_ref=own_half(owns[i], i, y), dst_ref=slot(fulls[i], i, t, y),
            send_sem=far_send.at[i], recv_sem=far_recv.at[i], device_id=far, device_id_type=MESH,
        )
        far_copy.start()
        sib_copy = pltpu.make_async_remote_copy(
            src_ref=owns[i], dst_ref=slot(fulls[i], i, t, None),
            send_sem=sib_send.at[i], recv_sem=sib_recv.at[i], device_id=sib, device_id_type=MESH,
        )
        sib_copy.start()
        local = pltpu.make_async_copy(owns[i], slot(fulls[i], i, t, None), local_sem.at[i])
        local.start()
        pending.append((far_copy, sib_copy, local))
    passed = []
    for i in range(4):
        far_copy, sib_copy, local = pending[i]
        far_copy.wait_recv()
        there = slot(fulls[i], i, flip(t, 2), y)
        side_copy = pltpu.make_async_remote_copy(
            src_ref=there, dst_ref=there, send_sem=side_send.at[i], recv_sem=side_recv.at[i],
            device_id=side, device_id_type=MESH,
        )
        side_copy.start()
        one = pltpu.make_async_remote_copy(
            src_ref=there, dst_ref=there, send_sem=pass_send.at[i], recv_sem=pass_recv.at[i],
            device_id=sib, device_id_type=MESH,
        )
        one.start()
        passed.append((side_copy, one))
    for i in range(4):
        side_copy, one = passed[i]
        side_copy.wait_recv()
        there = slot(fulls[i], i, flip(t, 2), 1 - y)
        two = pltpu.make_async_remote_copy(
            src_ref=there, dst_ref=there, send_sem=pass_send.at[4 + i],
            recv_sem=pass_recv.at[4 + i], device_id=sib, device_id_type=MESH,
        )
        two.start()
        passed[i] = (side_copy, one, two)
    for i in range(4):
        far_copy, sib_copy, local = pending[i]
        side_copy, one, two = passed[i]
        far_copy.wait_send()
        sib_copy.wait()
        local.wait()
        side_copy.wait_send()
        one.wait()
        two.wait()


def gather_weights(w_qkv, w_out, w_ff1, w_ff2, b_qv, b_ff1):
    _, width, cols = w_qkv.shape
    shards = 4
    hidden = w_ff1.shape[1]
    dma = pltpu.SemaphoreType.DMA
    return pl.pallas_call(
        gather_kernel,
        out_shape=(
            S((3, shards * cols, width), BF16),
            S((shards * cols, width), BF16),
            S((shards, width, hidden), BF16),
            S((shards, hidden, width), BF16),
            S((shards, 8, width), F32),
        ),
        in_specs=[ANY] * 4 + [VMEM] * 2,
        out_specs=(ANY,) * 4 + (VMEM,),
        scratch_shapes=[
            pltpu.VMEM((3, width, cols), F32),
            pltpu.VMEM((cols, width), F32),
            pltpu.VMEM((width, hidden), F32),
            pltpu.VMEM((hidden, width), F32),
            pltpu.VMEM((3, cols, width), BF16),
            pltpu.VMEM((cols, width), BF16),
            pltpu.VMEM((width, hidden), BF16),
            pltpu.VMEM((hidden, width), BF16),
            pltpu.VMEM((shards, 8, width), F32),
            dma((4,)), dma((4,)), dma((3,)), dma((3,)),
            dma((4,)), dma((4,)), dma((4,)), dma((4,)), dma((4,)), dma((4,)), dma((8,)), dma((8,)),
        ],
        compiler_params=pltpu.CompilerParams(
            collective_id=1, has_side_effects=True, vmem_limit_bytes=56 * MIB
        ),
        name="gather_weights",
    )(w_qkv, w_out, w_ff1, w_ff2, b_qv, b_ff1.reshape(1, -1))


def attend_kernel(
    place, x_ref, seg_ref, wt_ref, wo_ref, small_ref, gains, shifts, ranges,
    xq_ref, q_ref, k_ref, v_ref, p_ref, cq_ref, cs_ref, nq_ref, xh_ref, inv_ref,
    bias,
):
    length, width = x_ref.shape
    wins = windows(length)
    x = x_ref[...]
    xq = quantize(x, ranges[0])[0].astype(BF16)
    xq_ref[...] = xq
    cols = width // 4

    def both(row):
        parts = [small_ref[s, row : row + 1, 0:cols] for s in range(4)]
        return jnp.concatenate(parts, axis=1)

    q_ref[...] = (dot_nt(xq, wt_ref[0]) + both(1)).astype(BF16)
    k_ref[...] = dot_nt(xq, wt_ref[1]).astype(BF16)
    v_ref[...] = (dot_nt(xq, wt_ref[2]) + both(2)).astype(BF16)
    seg = seg_ref[0].astype(F32)
    seg_col = jnp.transpose(jnp.broadcast_to(seg, (128, length)))
    for b, (first, low, size) in enumerate(wins):
        for lane in range(0, size, 128):
            same = seg_col[first : first + QB] == seg[:, low + lane : low + lane + 128]
            bias[b, :, lane : lane + 128] = jnp.where(same, 0.0, MASKED)
    lanes = lax.broadcasted_iota(jnp.int32, (QB, 128), 1) < HD

    def pair(p, _):
        at = pl.ds(pl.multiple_of(p * 128, 128), 128)
        for b, (first, low, size) in enumerate(wins):
            queries = q_ref[first : first + QB, at].astype(F32) * 0.125
            keys = k_ref[low : low + size, at]
            values = v_ref[low : low + size, at]
            results = []
            for head in range(2):
                mine = lanes if head == 0 else jnp.logical_not(lanes)
                chosen = jnp.where(mine, queries, 0.0).astype(BF16)
                scores = dot_nt(chosen, keys) + bias[b]
                weights = jnp.exp(scores - jnp.max(scores, -1, keepdims=True))
                total = jnp.sum(weights, -1, keepdims=True)
                probs = (weights * (1.0 / total)).astype(BF16)
                p_ref[2 * p + head, first : first + QB, 0:size] = probs
                results.append(dot_nn(probs, values))
            context = jnp.where(lanes, results[0], results[1])
            coded, squash = quantize(context, ranges[1])
            cq_ref[first : first + QB, at] = coded.astype(BF16)
            cs_ref[first : first + QB, at] = (1.0 - squash * squash).astype(BF16)
        return 0

    lax.fori_loop(0, width // 128, pair, 0)
    attn = dot_nn(cq_ref[...], wo_ref[...]) + shifts[0:1]
    normed, inverse = norm(x_ref[...] + attn)
    xh_ref[...] = normed
    inv_ref[...] = jnp.broadcast_to(inverse, (length, 128))
    first_norm = normed * gains[0:1] + shifts[1:2]
    nq_ref[...] = quantize(first_norm, ranges[2])[0].astype(BF16)


def attend(place, inputs, segment_ids, wt, wo, small, gains, shifts, ranges):
    rows, length = segment_ids.shape
    tokens, width = inputs.shape
    mine = rows // 2
    half = tokens // 2
    size = max(w[2] for w in windows(length))
    by_row = lambda r, place: (r, 0)
    whole = lambda n: (lambda r, place: (0,) * n)
    return pl.pallas_call(
        attend_kernel,
        out_shape=(
            S((half, width), BF16),
            S((half, width), BF16),
            S((half, width), BF16),
            S((half, width), BF16),
            S((mine * (width // HD), length, size), BF16),
            S((half, width), BF16),
            S((half, width), BF16),
            S((half, width), BF16),
            S((half, width), F32),
            S((half, 128), F32),
        ),
        grid_spec=pltpu.PrefetchScalarGridSpec(
            num_scalar_prefetch=1,
            grid=(mine,),
            in_specs=[
                pl.BlockSpec((length, width), lambda r, place: (place[0] * mine + r, 0)),
                pl.BlockSpec((1, 1, length), lambda r, place: (place[0] * mine + r, 0, 0)),
                pl.BlockSpec(wt.shape, whole(3)),
                pl.BlockSpec(wo.shape, whole(2)),
                pl.BlockSpec(small.shape, whole(3)),
                pl.BlockSpec(gains.shape, whole(2)),
                pl.BlockSpec(shifts.shape, whole(2)),
                SMEM,
            ],
            out_specs=(
                pl.BlockSpec((length, width), by_row),
                pl.BlockSpec((length, width), by_row),
                pl.BlockSpec((length, width), by_row),
                pl.BlockSpec((length, width), by_row),
                pl.BlockSpec((width // HD, length, size), lambda r, place: (r, 0, 0)),
                pl.BlockSpec((length, width), by_row),
                pl.BlockSpec((length, width), by_row),
                pl.BlockSpec((length, width), by_row),
                pl.BlockSpec((length, width), by_row),
                pl.BlockSpec((length, 128), by_row),
            ),
            scratch_shapes=[pltpu.VMEM((length // QB, QB, size), F32)],
        ),
        compiler_params=pltpu.CompilerParams(vmem_limit_bytes=56 * MIB),
        name="attend",
    )(place, inputs, segment_ids.reshape(rows, 1, length), wt, wo, small, gains, shifts, ranges)


def feed_kernel(
    place, nq_ref, xh_hbm, inv_ref, cot_hbm, w1_ref, w2_ref, small_ref, gains, shifts, ranges,
    out_ref, g2_ref, g1_ref, da_ref, dh1_ref, sums_ref, gb1_ref,
    gq, factor, total, dl, xh, cot, dh2, do, load_sem,
):
    i = pl.program_id(0)
    tokens, width = nq_ref.shape
    blocks = tokens // QB
    shards = gq.shape[0]
    shard = place[1 + i % shards]

    def copies():
        return (
            pltpu.make_async_copy(xh_hbm, xh, load_sem.at[0]),
            pltpu.make_async_copy(
                cot_hbm.at[pl.ds(pl.multiple_of(place[0] * tokens, QB), tokens)], cot, load_sem.at[1]
            ),
        )

    @pl.when(i == 0)
    def _():
        for copy in copies():
            copy.start()
        total[...] = jnp.zeros_like(total)

    @pl.when(i < shards)
    def _():
        def block(b, _):
            rows = pl.ds(pl.multiple_of(b * QB, QB), QB)
            pre = dot_nn(nq_ref[rows], w1_ref[0]) + small_ref[0, 0:1]
            cdf = 0.5 * (1.0 + lax.erf(pre * ROOT_HALF))
            coded, squash = quantize(pre * cdf, ranges[3])
            slope = cdf + pre * jnp.exp(-0.5 * pre * pre) * INV_ROOT_TWO_PI
            factor[i, rows] = ((1.0 - squash * squash) * slope).astype(BF16)
            coded = coded.astype(BF16)
            gq[i, rows] = coded
            total[rows] += dot_nn(coded, w2_ref[0])
            return 0

        lax.fori_loop(0, blocks, block, 0)

    @pl.when(i == shards - 1)
    def _():
        for copy in copies():
            copy.wait()
        sums_ref[...] = jnp.zeros_like(sums_ref)

        def block(b, _):
            rows = pl.ds(pl.multiple_of(b * QB, QB), QB)
            first = xh[rows] * gains[0:1] + shifts[1:2]
            normed, inverse = norm(first + total[rows] + shifts[2:3])
            out_ref[rows] = normed * gains[1:2] + shifts[3:4]
            grad = cot[rows]
            back = norm_back(grad * gains[1:2], normed, inverse)
            dh2[rows] = back
            do[rows] = back.astype(BF16)
            sums_ref[1:2] += jnp.sum(grad * normed, 0, keepdims=True)
            sums_ref[4:5] += jnp.sum(back, 0, keepdims=True)
            sums_ref[5:6] += jnp.sum(grad, 0, keepdims=True)
            return 0

        lax.fori_loop(0, blocks, block, 0)
        total[...] = jnp.zeros_like(total)

    @pl.when(i >= shards)
    def _():
        def block(b, _):
            rows = pl.ds(pl.multiple_of(b * QB, QB), QB)
            back = dot_nt(do[rows], w2_ref[0]) * factor[i - shards, rows].astype(F32)
            low = back.astype(BF16)
            dl[rows] = low
            total[rows] += dot_nt(low, w1_ref[0])
            return jnp.sum(back, 0, keepdims=True)

        acc = block(0, 0)
        acc = lax.fori_loop(1, blocks, lambda b, a: a + block(b, 0), acc)

        @pl.when(i < shards + 2)
        def _():
            gb1_ref[0] = jnp.broadcast_to(acc, gb1_ref.shape[1:])
            g2_ref[0] = dot_tn(gq[i - shards], do[...]).astype(BF16)
            g1_ref[0] = dot_tn(nq_ref[...], dl[...]).astype(BF16)

    @pl.when(i == 2 * shards - 1)
    def _():
        def block(b, _):
            rows = pl.ds(pl.multiple_of(b * QB, QB), QB)
            normed = xh[rows]
            squash = jnp.tanh((normed * gains[0:1] + shifts[1:2]) * (1.0 / ranges[2]))
            grad = dh2[rows] + total[rows] * (1.0 - squash * squash)
            inverse = jnp.max(inv_ref[rows], axis=1, keepdims=True)
            back = norm_back(grad * gains[0:1], normed, inverse)
            dh1_ref[rows] = back
            da_ref[rows] = back.astype(BF16)
            sums_ref[0:1] += jnp.sum(grad * normed, 0, keepdims=True)
            sums_ref[2:3] += jnp.sum(back, 0, keepdims=True)
            sums_ref[3:4] += jnp.sum(grad, 0, keepdims=True)
            return 0

        lax.fori_loop(0, blocks, block, 0)


def feed(place, nq, xh, inv, cotangent, w1, w2, small, gains, shifts, ranges):
    tokens, width = nq.shape
    shards, _, hidden = w1.shape
    one = pl.Buffered(1)
    fixed = lambda shape: pl.BlockSpec(shape, lambda i, place: (0,) * len(shape), pipeline_mode=one)
    ours = lambda i, place: (jnp.clip(i - shards, 0, 1), 0, 0)
    turn = lambda i, place: (place[1 + i % shards], 0, 0)
    return pl.pallas_call(
        feed_kernel,
        out_shape=(
            S((tokens, width), F32),
            S((2, hidden, width), BF16),
            S((2, width, hidden), BF16),
            S((tokens, width), BF16),
            S((tokens, width), F32),
            S((8, width), F32),
            S((2, 8, hidden), F32),
        ),
        grid_spec=pltpu.PrefetchScalarGridSpec(
            num_scalar_prefetch=1,
            grid=(2 * shards,),
            in_specs=[
                fixed(nq.shape),
                ANY,
                fixed(inv.shape),
                ANY,
                pl.BlockSpec((1, width, hidden), turn),
                pl.BlockSpec((1, hidden, width), turn),
                pl.BlockSpec((1, 8, width), turn),
                fixed(gains.shape),
                fixed(shifts.shape),
                SMEM,
            ],
            out_specs=(
                fixed((tokens, width)),
                pl.BlockSpec((1, hidden, width), ours),
                pl.BlockSpec((1, width, hidden), ours),
                fixed((tokens, width)),
                fixed((tokens, width)),
                fixed((8, width)),
                pl.BlockSpec((1, 8, hidden), ours),
            ),
            scratch_shapes=[
                pltpu.VMEM((shards, tokens, hidden), BF16),
                pltpu.VMEM((shards, tokens, hidden), BF16),
                pltpu.VMEM((tokens, width), F32),
                pltpu.VMEM((tokens, hidden), BF16),
                pltpu.VMEM((tokens, width), F32),
                pltpu.VMEM((tokens, width), F32),
                pltpu.VMEM((tokens, width), F32),
                pltpu.VMEM((tokens, width), BF16),
                pltpu.SemaphoreType.DMA((2,)),
            ],
        ),
        compiler_params=pltpu.CompilerParams(vmem_limit_bytes=60 * MIB),
        name="feed",
    )(place, nq, xh, inv, cotangent, w1, w2, small, gains, shifts, ranges)


def attend_back_kernel(
    place, x_ref, xq_ref, q_ref, k_ref, v_ref, p_ref, cq_ref, cs_ref, da_ref, dh1_ref, wt_ref, wo_ref,
    ranges, dx_ref, go_ref, gq_ref, gb_ref, dc, dq, dk, dv, acc_o, acc_q,
):
    r = pl.program_id(0)
    length, width = x_ref.shape
    wins = windows(length)
    side = width // 2
    mine = pl.ds(pl.multiple_of(place[1] // 2 * side, 128), side)
    dc[...] = (dot_nt(da_ref[...], wo_ref[...]) * cs_ref[...].astype(F32)).astype(BF16)
    lanes = lax.broadcasted_iota(jnp.int32, (QB, 128), 1) < HD

    def pair(p, _):
        at = pl.ds(pl.multiple_of(p * 128, 128), 128)
        d_keys, d_values = [], []
        for b, (first, low, size) in enumerate(wins):
            wide = lax.broadcasted_iota(jnp.int32, (size, 128), 1) < HD
            queries = q_ref[first : first + QB, at]
            keys = k_ref[low : low + size, at]
            values = v_ref[low : low + size, at]
            context = dc[first : first + QB, at]
            got = []
            for head in range(2):
                own = lanes if head == 0 else jnp.logical_not(lanes)
                chosen = jnp.where(own, context.astype(F32), 0.0).astype(BF16)
                probs = p_ref[2 * p + head, first : first + QB, 0:size]
                d_probs = dot_nt(chosen, values)
                exact = probs.astype(F32)
                both = exact * d_probs
                d_low = (both - exact * jnp.sum(both, -1, keepdims=True)).astype(BF16)
                got.append(
                    (dot_nn(d_low, keys), dot_tn(d_low, queries), dot_tn(probs, context))
                )
            dq[first : first + QB, at] = (jnp.where(lanes, got[0][0], got[1][0]) * 0.125).astype(BF16)
            d_keys.append(jnp.where(wide, got[0][1], got[1][1]))
            d_values.append(jnp.where(wide, got[0][2], got[1][2]))
        for ref, parts, scale in ((dk, d_keys, 0.125), (dv, d_values, 1.0)):
            for lane in range(0, length, SPAN):
                terms = [
                    part[lane - low : lane - low + SPAN]
                    for part, (_, low, size) in zip(parts, wins)
                    if low <= lane < low + size
                ]
                ref[lane : lane + SPAN, at] = (sum(terms[1:], terms[0]) * scale).astype(BF16)
        return 0

    lax.fori_loop(0, width // 128, pair, 0)
    squash = jnp.tanh(x_ref[...] * (1.0 / ranges[0]))
    back = dot_nn(dq[...], wt_ref[0]) + dot_nn(dk[...], wt_ref[1]) + dot_nn(dv[...], wt_ref[2])
    dx_ref[...] = dh1_ref[...] + back * (1.0 - squash * squash)

    def sums(ref):
        return jnp.sum(ref[:, mine].astype(F32), 0, keepdims=True)

    @pl.when(r == 0)
    def _():
        acc_o[...] = jnp.zeros_like(acc_o)
        acc_q[...] = jnp.zeros_like(acc_q)
        gb_ref[...] = jnp.zeros_like(gb_ref)

    acc_o[...] += dot_tn(cq_ref[:, mine], da_ref[...])
    for j, ref in enumerate((dq, dk, dv)):
        acc_q[j] += dot_tn(ref[:, mine], xq_ref[...])
    gb_ref[0:1] += sums(dq)
    gb_ref[1:2] += sums(dv)

    @pl.when(r == pl.num_programs(0) - 1)
    def _():
        go_ref[...] = acc_o[...].astype(BF16)
        gq_ref[...] = acc_q[...].astype(BF16)


def attend_back(place, inputs, xq, q, k, v, probs, cq, cs, da, dh1, wt, wo, ranges, rows, length):
    tokens, width = inputs.shape
    mine = rows // 2
    half = tokens // 2
    size = probs.shape[2]
    side = width // 2
    by_row = lambda r, place: (r, 0)
    whole = lambda n: (lambda r, place: (0,) * n)
    one = pl.Buffered(1)
    return pl.pallas_call(
        attend_back_kernel,
        out_shape=(
            S((half, width), F32),
            S((side, width), BF16),
            S((3, side, width), BF16),
            S((8, side), F32),
        ),
        grid_spec=pltpu.PrefetchScalarGridSpec(
            num_scalar_prefetch=1,
            grid=(mine,),
            in_specs=[
                pl.BlockSpec((length, width), lambda r, place: (place[0] * mine + r, 0)),
                *[pl.BlockSpec((length, width), by_row)] * 4,
                pl.BlockSpec((width // HD, length, size), lambda r, place: (r, 0, 0)),
                *[pl.BlockSpec((length, width), by_row)] * 4,
                pl.BlockSpec(wt.shape, whole(3), pipeline_mode=one),
                pl.BlockSpec(wo.shape, whole(2), pipeline_mode=one),
                SMEM,
            ],
            out_specs=(
                pl.BlockSpec((length, width), by_row),
                pl.BlockSpec((side, width), whole(2), pipeline_mode=one),
                pl.BlockSpec((3, side, width), whole(3), pipeline_mode=one),
                pl.BlockSpec((8, side), whole(2)),
            ),
            scratch_shapes=[
                pltpu.VMEM((length, width), BF16),
                pltpu.VMEM((length, width), BF16),
                pltpu.VMEM((length, width), BF16),
                pltpu.VMEM((length, width), BF16),
                pltpu.VMEM((side, width), F32),
                pltpu.VMEM((3, side, width), F32),
            ],
        ),
        compiler_params=pltpu.CompilerParams(vmem_limit_bytes=60 * MIB),
        name="attend_back",
    )(place, inputs, xq, q, k, v, probs, cq, cs, da, dh1, wt, wo, ranges)


CHUNK = 192


def reduce_kernel(
    extra, g2, g1, go, gq, smalls, lo_half, dx_half,
    result, small_out, lo_full, dx_full,
    mine, theirs, got_core, own, got_y, part, got_1, got_2, got_x, small_own, small_got,
    load_sem, core_send, core_recv, y_send, y_recv, z1_send, z1_recv, z2_send, z2_recv,
    x_send, x_recv, z3_send, z3_recv, ag_send, ag_recv, big_sem, big_send, big_recv,
    small_send, small_recv,
):
    t, d = lax.axis_index("tensor"), lax.axis_index("dp")
    c = t % 2
    y = d % 2
    z = (d // 2) % 4
    end = jnp.logical_or(z == 0, z == 3)
    middle = jnp.logical_not(end)
    sib = (d, flip(t, 1))
    side = (flip(d, 1), t)
    inner = (flip(d, 2), t)
    across = (d - 2 * z + 2 * (3 - z), t)
    others = [(flip(d, 8 << b), t) for b in range(extra)]
    rows, width = own.shape
    chunks = rows // CHUNK
    half = CHUNK // 2

    barrier = pltpu.get_barrier_semaphore()
    peers = [sib, side, inner, across] + others
    for peer in peers:
        pl.semaphore_signal(barrier, inc=1, device_id=peer, device_id_type=MESH)
    pl.semaphore_wait(barrier, len(peers))

    def remote(src, dst, send, recv, to):
        return pltpu.make_async_remote_copy(
            src_ref=src, dst_ref=dst, send_sem=send, recv_sem=recv, device_id=to, device_id_type=MESH
        )

    tokens = lo_half.shape[0]
    at = pl.ds(pl.multiple_of(c * tokens, 256), tokens)
    big = []
    for i, (src, dst) in enumerate(((lo_half, lo_full), (dx_half, dx_full))):
        copy = pltpu.make_async_copy(src, dst.at[at], big_sem.at[i])
        copy.start()
        other = remote(src, dst.at[at], big_send.at[i], big_recv.at[i], sib)
        other.start()
        big += [copy, other]

    loads = []
    hidden = g2.shape[1]
    cols = go.shape[0] // 2
    for which, (buffer, core) in enumerate(((mine, c), (theirs, 1 - c))):
        places = [
            (g2.at[core], buffer.at[0:hidden]),
            (g1.at[core], buffer.at[hidden : 2 * hidden]),
            (
                go.at[pl.ds(pl.multiple_of(core * cols, 16), cols)],
                buffer.at[2 * hidden : 2 * hidden + cols],
            ),
        ]
        for j in range(3):
            base = 2 * hidden + (j + 1) * cols
            places.append(
                (
                    gq.at[j, pl.ds(pl.multiple_of(core * cols, 16), cols)],
                    buffer.at[base : base + cols],
                )
            )
        for i, (src, dst) in enumerate(places):
            copy = pltpu.make_async_copy(src, dst, load_sem.at[which * 6 + i])
            copy.start()
            loads.append(copy)
    for copy in loads:
        copy.wait()

    small_own[...] = smalls[...]
    steps = [sib, side, inner, across] + others
    for i, peer in enumerate(steps):
        copy = remote(small_own, small_got.at[i], small_send.at[i], small_recv.at[i], peer)
        copy.start()
        copy.wait()
        small_own[...] = small_own[...] + small_got[i]
    small_out[...] = small_own[...]

    def span(k):
        return pl.ds(k * CHUNK, CHUNK)

    def part_of(k, which):
        return pl.ds(pl.multiple_of(k * CHUNK + which * half, 16), half)

    def core_copy(k):
        return remote(theirs.at[span(k)], got_core.at[span(k)], core_send.at[k], core_recv.at[k], sib)

    def y_copy(k):
        return remote(own.at[part_of(k, 1 - y)], got_y.at[k], y_send.at[k], y_recv.at[k], side)

    def z1_copy(k):
        return remote(part.at[k], got_1.at[k], z1_send.at[k], z1_recv.at[k], inner)

    def z2_copy(k):
        return remote(part.at[k], got_2.at[k], z2_send.at[k], z2_recv.at[k], across)

    def x_copy(k, b):
        return remote(part.at[k], got_x.at[b, k], x_send.at[b, k], x_recv.at[b, k], others[b])

    def z3_copy(k):
        there = result.at[part_of(k, y)]
        return remote(there, there, z3_send.at[k], z3_recv.at[k], inner)

    def ag_copy(k):
        there = result.at[part_of(k, y)]
        return remote(there, there, ag_send.at[k], ag_recv.at[k], side)

    def stage(s, k):
        if s == 0:
            core_copy(k).start()
        if s == 1:
            core_copy(k).wait()
            own[span(k)] = (mine[span(k)].astype(F32) + got_core[span(k)].astype(F32)).astype(BF16)
            y_copy(k).start()
        if s == 2:
            y_copy(k).wait()
            part[k] = (own[part_of(k, y)].astype(F32) + got_y[k].astype(F32)).astype(BF16)

            @pl.when(end)
            def _():
                z1_copy(k).start()

        if s == 3:

            @pl.when(middle)
            def _():
                z1_copy(k).wait_recv()
                part[k] = (part[k].astype(F32) + got_1[k].astype(F32)).astype(BF16)
                z2_copy(k).start()

        if s == 4:

            @pl.when(middle)
            def _():
                z2_copy(k).wait()
                part[k] = (part[k].astype(F32) + got_2[k].astype(F32)).astype(BF16)
                for b in range(extra):
                    copy = x_copy(k, b)
                    copy.start()
                    copy.wait()
                    part[k] = (part[k].astype(F32) + got_x[b, k].astype(F32)).astype(BF16)
                result[part_of(k, y)] = part[k]
                z3_copy(k).start()
                ag_copy(k).start()

        if s == 5:

            @pl.when(end)
            def _():
                z3_copy(k).wait_recv()
                ag_copy(k).start()

        if s == 6:
            ag_copy(k).wait()

            @pl.when(end)
            def _():
                z1_copy(k).wait_send()

            @pl.when(middle)
            def _():
                z3_copy(k).wait_send()

    for step in range(chunks + 6):
        for s in range(7):
            if 0 <= step - s < chunks:
                stage(s, step - s)
    for copy in big:
        copy.wait()


def reduce_grads(nd, g2, g1, go, gq, smalls, lo_half, dx_half):
    hidden, width = g2.shape[1:]
    cols = go.shape[0] // 2
    rows = 2 * hidden + 4 * cols
    chunks = rows // CHUNK
    half = CHUNK // 2
    extra = (nd // 8).bit_length() - 1
    tokens = lo_half.shape[0]
    dma = pltpu.SemaphoreType.DMA
    buf = lambda *shape: pltpu.VMEM(shape, BF16)
    count = max(extra, 1)
    return pl.pallas_call(
        functools.partial(reduce_kernel, extra),
        out_shape=(
            S((rows, width), BF16),
            S(smalls.shape, F32),
            S((2 * tokens, width), F32),
            S((2 * tokens, width), F32),
        ),
        in_specs=[ANY] * 4 + [VMEM] + [ANY] * 2,
        out_specs=(VMEM, VMEM, ANY, ANY),
        scratch_shapes=[
            buf(rows, width), buf(rows, width), buf(rows, width), buf(rows, width),
            buf(chunks, half, width), buf(chunks, half, width),
            buf(chunks, half, width), buf(chunks, half, width), buf(count, chunks, half, width),
            pltpu.VMEM(smalls.shape, F32),
            pltpu.VMEM((4 + extra,) + smalls.shape, F32),
            dma((12,)),
            dma((chunks,)), dma((chunks,)), dma((chunks,)), dma((chunks,)),
            dma((chunks,)), dma((chunks,)), dma((chunks,)), dma((chunks,)),
            dma((count, chunks)), dma((count, chunks)),
            dma((chunks,)), dma((chunks,)), dma((chunks,)), dma((chunks,)),
            dma((2,)), dma((2,)), dma((2,)),
            dma((4 + extra,)), dma((4 + extra,)),
        ],
        compiler_params=pltpu.CompilerParams(
            collective_id=2, has_side_effects=True, vmem_limit_bytes=60 * MIB
        ),
        name="reduce_grads",
    )(g2, g1, go, gq, smalls, lo_half, dx_half)


def per_device(
    nd, inputs, segment_ids, w_qkv, b_qv, w_out, w_ff1, b_ff1, w_ff2, norm_gains, shift_biases,
    act_ranges, cotangent,
):
    t = lax.axis_index("tensor")
    c, pair = t % 2, t // 2
    rows, length = segment_ids.shape
    width = inputs.shape[1]
    cols = w_qkv.shape[2]
    hidden = w_ff1.shape[1]
    order = [(2 * pair + i) % 4 for i in range(4)]
    place = jnp.stack([c] + order).astype(jnp.int32)
    wt, wo, w1, w2, small = gather_weights(w_qkv, w_out, w_ff1, w_ff2, b_qv, b_ff1)
    weight_max = jnp.max(small[:, 3, ::128], axis=0)
    xq, q, k, v, probs, cq, cs, nq, xh, inv = attend(
        place, inputs, segment_ids, wt, wo, small, norm_gains, shift_biases, act_ranges
    )
    lo_half, g2, g1, da, dh1, sums, gb1 = feed(
        place, nq, xh, inv, cotangent, w1, w2, small, norm_gains, shift_biases, act_ranges
    )
    dx_half, go, gq, gb = attend_back(
        place, inputs, xq, q, k, v, probs, cq, cs, da, dh1, wt, wo, act_ranges, rows, length
    )
    smalls = jnp.concatenate(
        [sums[:6], gb1[:, 0], jnp.pad(gb[:2], ((0, 6), (0, width - gb.shape[1])))], axis=0
    )
    grads, smalls, layer_out, input_grad = reduce_grads(nd, g2, g1, go, gq, smalls, lo_half, dx_half)
    grads = grads.astype(F32)
    grad_ff2 = grads[:hidden]
    grad_ff1 = grads[hidden : 2 * hidden]
    grad_out = grads[2 * hidden : 2 * hidden + cols]
    grad_qkv = grads[2 * hidden + cols :].reshape(3, cols, width).transpose(0, 2, 1)
    share = lax.dynamic_slice_in_dim(smalls[:6], t * cols, cols, 1)
    grad_gains, grad_shifts = share[:2], share[2:6]
    grad_bff1 = lax.dynamic_slice_in_dim(smalls, 6 + c, 1, 0)[0]
    grad_bqv = lax.dynamic_slice_in_dim(smalls[8:10], c * cols, cols, 1)
    return (
        layer_out, input_grad, grad_qkv, grad_bqv, grad_out, grad_ff1, grad_bff1, grad_ff2,
        grad_gains, grad_shifts, weight_max,
    )


def solution(mesh):
    return jax.shard_map(
        functools.partial(per_device, mesh.shape["dp"]),
        mesh=mesh,
        in_specs=(
            P("dp", None),
            P("dp", None),
            P(None, None, "tensor"),
            P(None, "tensor"),
            P("tensor", None),
            P(None, "tensor"),
            P("tensor"),
            P("tensor", None),
            P(),
            P(),
            P(),
            P("dp", None),
        ),
        out_specs=(
            P("dp", None),
            P("dp", None),
            P(None, None, "tensor"),
            P(None, "tensor"),
            P("tensor", None),
            P(None, "tensor"),
            P("tensor"),
            P("tensor", None),
            P(None, "tensor"),
            P(None, "tensor"),
            P(),
        ),
        check_vma=False,
    )
```

```python
import functools
import math

import jax
import jax.numpy as jnp
from jax import lax
from jax.experimental import pallas as pl
from jax.experimental.pallas import tpu as pltpu
from jax.sharding import PartitionSpec as P

HD = 64
SPAN = 128
QB = 256
MASKED = -1e30
EPSILON = 1e-06
ROOT_HALF = 0.7071067811865476
INV_ROOT_TWO_PI = 0.3989422804014327
STAIR = (
    6.579734980213376,
    -12.987641368031495,
    12.20087719668052,
    -6.61489684889321,
    2.04264519055443,
)
MIB = 1 << 20
MESH = pl.DeviceIdType.MESH
F32 = jnp.float32
BF16 = jnp.bfloat16
ANY = pl.BlockSpec(memory_space=pl.ANY)
VMEM = pl.BlockSpec(memory_space=pltpu.VMEM)
SMEM = pl.BlockSpec(memory_space=pltpu.SMEM)
S = jax.ShapeDtypeStruct


def flip(value, bit):
    return value + bit - 2 * bit * ((value // bit) % 2)


def dot_nn(left, right):
    return lax.dot_general(left, right, (((1,), (0,)), ((), ())), preferred_element_type=F32)


def dot_nt(left, right):
    return lax.dot_general(left, right, (((1,), (1,)), ((), ())), preferred_element_type=F32)


def dot_tn(left, right):
    return lax.dot_general(left, right, (((0,), (0,)), ((), ())), preferred_element_type=F32)


def stairs(levels):
    whole = jnp.round(levels)
    rest = levels - whole
    square = rest * rest
    curve = STAIR[4]
    for factor in STAIR[3::-1]:
        curve = curve * square + factor
    return whole + rest * square * curve


def quantize(values, bound):
    squash = jnp.tanh(values * (1.0 / bound))
    return stairs(127.0 * squash) * (bound / 127.0), squash


def norm(hidden):
    centred = hidden - jnp.mean(hidden, -1, keepdims=True)
    inverse = lax.rsqrt(jnp.mean(centred * centred, -1, keepdims=True) + EPSILON)
    return centred * inverse, inverse


def norm_back(scaled, normed, inverse):
    return inverse * (
        scaled
        - jnp.mean(scaled, -1, keepdims=True)
        - normed * jnp.mean(scaled * normed, -1, keepdims=True)
    )


def windows(length):
    found = []
    for first in range(0, length, QB):
        low = max(0, first - SPAN)
        found.append((first, low, min(length, first + QB + SPAN) - low))
    return found


def gather_kernel(
    wqkv, wout, wff1, wff2, bqv, bff1,
    wt_all, wo_all, w1_all, w2_all, small_out,
    f_qkv, f_out, f_1, f_2, q_qkv, q_out, q_1, q_2, small,
    load_sem, local_sem, small_send, small_recv,
    sib_send, sib_recv, far_send, far_recv, side_send, side_recv, pass_send, pass_recv,
):
    t, d = lax.axis_index("tensor"), lax.axis_index("dp")
    y = d % 2
    sib, far, side = (d, flip(t, 1)), (d, flip(t, 2)), (flip(d, 1), t)
    loads = [
        pltpu.make_async_copy(src, dst, load_sem.at[i])
        for i, (src, dst) in enumerate(((wqkv, f_qkv), (wout, f_out), (wff1, f_1), (wff2, f_2)))
    ]
    for load in loads:
        load.start()
    peers = [sib, far, (d, flip(flip(t, 1), 2))]
    barrier = pltpu.get_barrier_semaphore()
    for peer in peers + [side]:
        pl.semaphore_signal(barrier, inc=1, device_id=peer, device_id_type=MESH)
    pl.semaphore_wait(barrier, 4)

    cols = f_qkv.shape[2]
    width = f_out.shape[1]
    for load in loads:
        load.wait()
    tops = [jnp.max(jnp.abs(f_qkv[j]), axis=(0, 1), keepdims=True) for j in range(3)]
    tops += [jnp.max(jnp.abs(f[...]), axis=(0, 1), keepdims=True) for f in (f_out, f_1, f_2)]
    zeros = jnp.zeros((8, width), F32)
    small[pl.ds(t, 1)] = zeros[None]
    small[pl.ds(t, 1), 0:1, :] = bff1[...][None]
    small[pl.ds(t, 1), 1:3, 0:cols] = bqv[...][None]
    row = jnp.concatenate([jnp.broadcast_to(top, (1, 128)) for top in tops], axis=1)
    small[pl.ds(t, 1), 3:4, :] = row[None]
    sends = []
    for i, peer in enumerate(peers):
        copy = pltpu.make_async_remote_copy(
            src_ref=small.at[t], dst_ref=small.at[t], send_sem=small_send.at[i],
            recv_sem=small_recv.at[i], device_id=peer, device_id_type=MESH,
        )
        copy.start()
        sends.append(copy)
    for copy in sends:
        copy.wait()
    top_row = jnp.max(small[:, 3:4, :], axis=0)
    small_out[...] = small[...]

    def weight(value, j):
        top = top_row[:, 128 * j : 128 * j + 1]
        return (stairs(value * (127.0 / top)) * (top / 127.0)).astype(BF16)

    def slot(full, i, s, half):
        if i == 0:
            part = cols // 2
            if half is None:
                return full.at[:, pl.ds(pl.multiple_of(s * cols, 16), cols)]
            return full.at[:, pl.ds(pl.multiple_of(s * cols + half * part, 16), part)]
        if i == 1:
            part = cols // 2
            if half is None:
                return full.at[pl.ds(pl.multiple_of(s * cols, 16), cols)]
            return full.at[pl.ds(pl.multiple_of(s * cols + half * part, 16), part)]
        if half is None:
            return full.at[s]
        part = full.shape[1] // 2
        return full.at[s, pl.ds(pl.multiple_of(half * part, 16), part)]

    def own_half(own, i, half):
        if i == 0:
            part = cols // 2
            return own.at[:, pl.ds(pl.multiple_of(half * part, 16), part)]
        part = own.shape[0] // 2
        return own.at[pl.ds(pl.multiple_of(half * part, 16), part)]

    fulls = (wt_all, wo_all, w1_all, w2_all)
    owns = (q_qkv, q_out, q_1, q_2)
    pending = []
    for i in range(4):
        if i == 0:
            for j in range(3):
                q_qkv[j] = jnp.transpose(
                    (stairs(f_qkv[j] * (127.0 / top_row[:, 128 * j : 128 * j + 1]))
                     * (top_row[:, 128 * j : 128 * j + 1] / 127.0))
                ).astype(BF16)
        elif i == 1:
            q_out[...] = weight(f_out[...], 3)
        elif i == 2:
            q_1[...] = weight(f_1[...], 4)
        else:
            q_2[...] = weight(f_2[...], 5)
        far_copy = pltpu.make_async_remote_copy(
            src_ref=own_half(owns[i], i, y), dst_ref=slot(fulls[i], i, t, y),
            send_sem=far_send.at[i], recv_sem=far_recv.at[i], device_id=far, device_id_type=MESH,
        )
        far_copy.start()
        sib_copy = pltpu.make_async_remote_copy(
            src_ref=owns[i], dst_ref=slot(fulls[i], i, t, None),
            send_sem=sib_send.at[i], recv_sem=sib_recv.at[i], device_id=sib, device_id_type=MESH,
        )
        sib_copy.start()
        local = pltpu.make_async_copy(owns[i], slot(fulls[i], i, t, None), local_sem.at[i])
        local.start()
        pending.append((far_copy, sib_copy, local))
    passed = []
    for i in range(4):
        far_copy, sib_copy, local = pending[i]
        far_copy.wait_recv()
        there = slot(fulls[i], i, flip(t, 2), y)
        side_copy = pltpu.make_async_remote_copy(
            src_ref=there, dst_ref=there, send_sem=side_send.at[i], recv_sem=side_recv.at[i],
            device_id=side, device_id_type=MESH,
        )
        side_copy.start()
        one = pltpu.make_async_remote_copy(
            src_ref=there, dst_ref=there, send_sem=pass_send.at[i], recv_sem=pass_recv.at[i],
            device_id=sib, device_id_type=MESH,
        )
        one.start()
        passed.append((side_copy, one))
    for i in range(4):
        side_copy, one = passed[i]
        side_copy.wait_recv()
        there = slot(fulls[i], i, flip(t, 2), 1 - y)
        two = pltpu.make_async_remote_copy(
            src_ref=there, dst_ref=there, send_sem=pass_send.at[4 + i],
            recv_sem=pass_recv.at[4 + i], device_id=sib, device_id_type=MESH,
        )
        two.start()
        passed[i] = (side_copy, one, two)
    for i in range(4):
        far_copy, sib_copy, local = pending[i]
        side_copy, one, two = passed[i]
        far_copy.wait_send()
        sib_copy.wait()
        local.wait()
        side_copy.wait_send()
        one.wait()
        two.wait()


def gather_weights(w_qkv, w_out, w_ff1, w_ff2, b_qv, b_ff1):
    _, width, cols = w_qkv.shape
    shards = 4
    hidden = w_ff1.shape[1]
    dma = pltpu.SemaphoreType.DMA
    return pl.pallas_call(
        gather_kernel,
        out_shape=(
            S((3, shards * cols, width), BF16),
            S((shards * cols, width), BF16),
            S((shards, width, hidden), BF16),
            S((shards, hidden, width), BF16),
            S((shards, 8, width), F32),
        ),
        in_specs=[ANY] * 4 + [VMEM] * 2,
        out_specs=(ANY,) * 4 + (VMEM,),
        scratch_shapes=[
            pltpu.VMEM((3, width, cols), F32),
            pltpu.VMEM((cols, width), F32),
            pltpu.VMEM((width, hidden), F32),
            pltpu.VMEM((hidden, width), F32),
            pltpu.VMEM((3, cols, width), BF16),
            pltpu.VMEM((cols, width), BF16),
            pltpu.VMEM((width, hidden), BF16),
            pltpu.VMEM((hidden, width), BF16),
            pltpu.VMEM((shards, 8, width), F32),
            dma((4,)), dma((4,)), dma((3,)), dma((3,)),
            dma((4,)), dma((4,)), dma((4,)), dma((4,)), dma((4,)), dma((4,)), dma((8,)), dma((8,)),
        ],
        compiler_params=pltpu.CompilerParams(
            collective_id=1, has_side_effects=True, vmem_limit_bytes=56 * MIB
        ),
        name="gather_weights",
    )(w_qkv, w_out, w_ff1, w_ff2, b_qv, b_ff1.reshape(1, -1))


def attend_kernel(
    place, x_ref, seg_ref, wt_ref, wo_ref, small_ref, gains, shifts, ranges,
    xq_ref, q_ref, k_ref, v_ref, p_ref, cq_ref, cs_ref, nq_ref, xh_ref, inv_ref,
    bias,
):
    length, width = x_ref.shape
    wins = windows(length)
    x = x_ref[...]
    xq = quantize(x, ranges[0])[0].astype(BF16)
    xq_ref[...] = xq
    cols = width // 4

    def both(row):
        parts = [small_ref[s, row : row + 1, 0:cols] for s in range(4)]
        return jnp.concatenate(parts, axis=1)

    q_ref[...] = (dot_nt(xq, wt_ref[0]) + both(1)).astype(BF16)
    k_ref[...] = dot_nt(xq, wt_ref[1]).astype(BF16)
    v_ref[...] = (dot_nt(xq, wt_ref[2]) + both(2)).astype(BF16)
    seg = seg_ref[0].astype(F32)
    seg_col = jnp.transpose(jnp.broadcast_to(seg, (128, length)))
    for b, (first, low, size) in enumerate(wins):
        for lane in range(0, size, 128):
            same = seg_col[first : first + QB] == seg[:, low + lane : low + lane + 128]
            bias[b, :, lane : lane + 128] = jnp.where(same, 0.0, MASKED)
    lanes = lax.broadcasted_iota(jnp.int32, (QB, 128), 1) < HD

    def pair(p, _):
        at = pl.ds(pl.multiple_of(p * 128, 128), 128)
        for b, (first, low, size) in enumerate(wins):
            queries = q_ref[first : first + QB, at].astype(F32) * 0.125
            keys = k_ref[low : low + size, at]
            values = v_ref[low : low + size, at]
            results = []
            for head in range(2):
                mine = lanes if head == 0 else jnp.logical_not(lanes)
                chosen = jnp.where(mine, queries, 0.0).astype(BF16)
                scores = dot_nt(chosen, keys) + bias[b]
                weights = jnp.exp(scores - jnp.max(scores, -1, keepdims=True))
                total = jnp.sum(weights, -1, keepdims=True)
                probs = (weights * (1.0 / total)).astype(BF16)
                p_ref[2 * p + head, first : first + QB, 0:size] = probs
                results.append(dot_nn(probs, values))
            context = jnp.where(lanes, results[0], results[1])
            coded, squash = quantize(context, ranges[1])
            cq_ref[first : first + QB, at] = coded.astype(BF16)
            cs_ref[first : first + QB, at] = (1.0 - squash * squash).astype(BF16)
        return 0

    lax.fori_loop(0, width // 128, pair, 0)
    attn = dot_nn(cq_ref[...], wo_ref[...]) + shifts[0:1]
    normed, inverse = norm(x_ref[...] + attn)
    xh_ref[...] = normed
    inv_ref[...] = jnp.broadcast_to(inverse, (length, 128))
    first_norm = normed * gains[0:1] + shifts[1:2]
    nq_ref[...] = quantize(first_norm, ranges[2])[0].astype(BF16)


def attend(place, inputs, segment_ids, wt, wo, small, gains, shifts, ranges):
    rows, length = segment_ids.shape
    tokens, width = inputs.shape
    mine = rows // 2
    half = tokens // 2
    size = max(w[2] for w in windows(length))
    by_row = lambda r, place: (r, 0)
    whole = lambda n: (lambda r, place: (0,) * n)
    return pl.pallas_call(
        attend_kernel,
        out_shape=(
            S((half, width), BF16),
            S((half, width), BF16),
            S((half, width), BF16),
            S((half, width), BF16),
            S((mine * (width // HD), length, size), BF16),
            S((half, width), BF16),
            S((half, width), BF16),
            S((half, width), BF16),
            S((half, width), F32),
            S((half, 128), F32),
        ),
        grid_spec=pltpu.PrefetchScalarGridSpec(
            num_scalar_prefetch=1,
            grid=(mine,),
            in_specs=[
                pl.BlockSpec((length, width), lambda r, place: (place[0] * mine + r, 0)),
                pl.BlockSpec((1, 1, length), lambda r, place: (place[0] * mine + r, 0, 0)),
                pl.BlockSpec(wt.shape, whole(3)),
                pl.BlockSpec(wo.shape, whole(2)),
                pl.BlockSpec(small.shape, whole(3)),
                pl.BlockSpec(gains.shape, whole(2)),
                pl.BlockSpec(shifts.shape, whole(2)),
                SMEM,
            ],
            out_specs=(
                pl.BlockSpec((length, width), by_row),
                pl.BlockSpec((length, width), by_row),
                pl.BlockSpec((length, width), by_row),
                pl.BlockSpec((length, width), by_row),
                pl.BlockSpec((width // HD, length, size), lambda r, place: (r, 0, 0)),
                pl.BlockSpec((length, width), by_row),
                pl.BlockSpec((length, width), by_row),
                pl.BlockSpec((length, width), by_row),
                pl.BlockSpec((length, width), by_row),
                pl.BlockSpec((length, 128), by_row),
            ),
            scratch_shapes=[pltpu.VMEM((length // QB, QB, size), F32)],
        ),
        compiler_params=pltpu.CompilerParams(vmem_limit_bytes=56 * MIB),
        name="attend",
    )(place, inputs, segment_ids.reshape(rows, 1, length), wt, wo, small, gains, shifts, ranges)


def feed_kernel(
    place, nq_ref, xh_hbm, inv_ref, cot_hbm, w1_ref, w2_ref, small_ref, gains, shifts, ranges,
    out_ref, g2_ref, g1_ref, da_ref, dh1_ref, sums_ref, gb1_ref,
    gq, factor, total, dl, xh, cot, dh2, do, load_sem,
):
    i = pl.program_id(0)
    tokens, width = nq_ref.shape
    blocks = tokens // QB
    shards = gq.shape[0]
    shard = place[1 + i % shards]

    def copies():
        return (
            pltpu.make_async_copy(xh_hbm, xh, load_sem.at[0]),
            pltpu.make_async_copy(
                cot_hbm.at[pl.ds(pl.multiple_of(place[0] * tokens, QB), tokens)], cot, load_sem.at[1]
            ),
        )

    @pl.when(i == 0)
    def _():
        for copy in copies():
            copy.start()
        total[...] = jnp.zeros_like(total)

    @pl.when(i < shards)
    def _():
        def block(b, _):
            rows = pl.ds(pl.multiple_of(b * QB, QB), QB)
            pre = dot_nn(nq_ref[rows], w1_ref[0]) + small_ref[0, 0:1]
            cdf = 0.5 * (1.0 + lax.erf(pre * ROOT_HALF))
            coded, squash = quantize(pre * cdf, ranges[3])
            slope = cdf + pre * jnp.exp(-0.5 * pre * pre) * INV_ROOT_TWO_PI
            factor[i, rows] = ((1.0 - squash * squash) * slope).astype(BF16)
            coded = coded.astype(BF16)
            gq[i, rows] = coded
            total[rows] += dot_nn(coded, w2_ref[0])
            return 0

        lax.fori_loop(0, blocks, block, 0)

    @pl.when(i == shards - 1)
    def _():
        for copy in copies():
            copy.wait()
        sums_ref[...] = jnp.zeros_like(sums_ref)

        def block(b, _):
            rows = pl.ds(pl.multiple_of(b * QB, QB), QB)
            first = xh[rows] * gains[0:1] + shifts[1:2]
            normed, inverse = norm(first + total[rows] + shifts[2:3])
            out_ref[rows] = normed * gains[1:2] + shifts[3:4]
            grad = cot[rows]
            back = norm_back(grad * gains[1:2], normed, inverse)
            dh2[rows] = back
            do[rows] = back.astype(BF16)
            sums_ref[1:2] += jnp.sum(grad * normed, 0, keepdims=True)
            sums_ref[4:5] += jnp.sum(back, 0, keepdims=True)
            sums_ref[5:6] += jnp.sum(grad, 0, keepdims=True)
            return 0

        lax.fori_loop(0, blocks, block, 0)
        total[...] = jnp.zeros_like(total)

    @pl.when(i >= shards)
    def _():
        def block(b, _):
            rows = pl.ds(pl.multiple_of(b * QB, QB), QB)
            back = dot_nt(do[rows], w2_ref[0]) * factor[i - shards, rows].astype(F32)
            low = back.astype(BF16)
            dl[rows] = low
            total[rows] += dot_nt(low, w1_ref[0])
            return jnp.sum(back, 0, keepdims=True)

        acc = block(0, 0)
        acc = lax.fori_loop(1, blocks, lambda b, a: a + block(b, 0), acc)

        @pl.when(i < shards + 2)
        def _():
            gb1_ref[0] = jnp.broadcast_to(acc, gb1_ref.shape[1:])
            g2_ref[0] = dot_tn(gq[i - shards], do[...]).astype(BF16)
            g1_ref[0] = dot_tn(nq_ref[...], dl[...]).astype(BF16)

    @pl.when(i == 2 * shards - 1)
    def _():
        def block(b, _):
            rows = pl.ds(pl.multiple_of(b * QB, QB), QB)
            normed = xh[rows]
            squash = jnp.tanh((normed * gains[0:1] + shifts[1:2]) * (1.0 / ranges[2]))
            grad = dh2[rows] + total[rows] * (1.0 - squash * squash)
            inverse = jnp.max(inv_ref[rows], axis=1, keepdims=True)
            back = norm_back(grad * gains[0:1], normed, inverse)
            dh1_ref[rows] = back
            da_ref[rows] = back.astype(BF16)
            sums_ref[0:1] += jnp.sum(grad * normed, 0, keepdims=True)
            sums_ref[2:3] += jnp.sum(back, 0, keepdims=True)
            sums_ref[3:4] += jnp.sum(grad, 0, keepdims=True)
            return 0

        lax.fori_loop(0, blocks, block, 0)


def feed(place, nq, xh, inv, cotangent, w1, w2, small, gains, shifts, ranges):
    tokens, width = nq.shape
    shards, _, hidden = w1.shape
    one = pl.Buffered(1)
    fixed = lambda shape: pl.BlockSpec(shape, lambda i, place: (0,) * len(shape), pipeline_mode=one)
    ours = lambda i, place: (jnp.clip(i - shards, 0, 1), 0, 0)
    turn = lambda i, place: (place[1 + i % shards], 0, 0)
    return pl.pallas_call(
        feed_kernel,
        out_shape=(
            S((tokens, width), F32),
            S((2, hidden, width), BF16),
            S((2, width, hidden), BF16),
            S((tokens, width), BF16),
            S((tokens, width), F32),
            S((8, width), F32),
            S((2, 8, hidden), F32),
        ),
        grid_spec=pltpu.PrefetchScalarGridSpec(
            num_scalar_prefetch=1,
            grid=(2 * shards,),
            in_specs=[
                fixed(nq.shape),
                ANY,
                fixed(inv.shape),
                ANY,
                pl.BlockSpec((1, width, hidden), turn),
                pl.BlockSpec((1, hidden, width), turn),
                pl.BlockSpec((1, 8, width), turn),
                fixed(gains.shape),
                fixed(shifts.shape),
                SMEM,
            ],
            out_specs=(
                fixed((tokens, width)),
                pl.BlockSpec((1, hidden, width), ours),
                pl.BlockSpec((1, width, hidden), ours),
                fixed((tokens, width)),
                fixed((tokens, width)),
                fixed((8, width)),
                pl.BlockSpec((1, 8, hidden), ours),
            ),
            scratch_shapes=[
                pltpu.VMEM((shards, tokens, hidden), BF16),
                pltpu.VMEM((shards, tokens, hidden), BF16),
                pltpu.VMEM((tokens, width), F32),
                pltpu.VMEM((tokens, hidden), BF16),
                pltpu.VMEM((tokens, width), F32),
                pltpu.VMEM((tokens, width), F32),
                pltpu.VMEM((tokens, width), F32),
                pltpu.VMEM((tokens, width), BF16),
                pltpu.SemaphoreType.DMA((2,)),
            ],
        ),
        compiler_params=pltpu.CompilerParams(vmem_limit_bytes=60 * MIB),
        name="feed",
    )(place, nq, xh, inv, cotangent, w1, w2, small, gains, shifts, ranges)


def attend_back_kernel(
    place, x_ref, xq_ref, q_ref, k_ref, v_ref, p_ref, cq_ref, cs_ref, da_ref, dh1_ref, wt_ref, wo_ref,
    ranges, dx_ref, go_ref, gq_ref, gb_ref, dc, dq, dk, dv, acc_o, acc_q,
):
    r = pl.program_id(0)
    length, width = x_ref.shape
    wins = windows(length)
    side = width // 2
    mine = pl.ds(pl.multiple_of(place[1] // 2 * side, 128), side)
    dc[...] = (dot_nt(da_ref[...], wo_ref[...]) * cs_ref[...].astype(F32)).astype(BF16)
    lanes = lax.broadcasted_iota(jnp.int32, (QB, 128), 1) < HD

    def pair(p, _):
        at = pl.ds(pl.multiple_of(p * 128, 128), 128)
        d_keys, d_values = [], []
        for b, (first, low, size) in enumerate(wins):
            wide = lax.broadcasted_iota(jnp.int32, (size, 128), 1) < HD
            queries = q_ref[first : first + QB, at]
            keys = k_ref[low : low + size, at]
            values = v_ref[low : low + size, at]
            context = dc[first : first + QB, at]
            got = []
            for head in range(2):
                own = lanes if head == 0 else jnp.logical_not(lanes)
                chosen = jnp.where(own, context.astype(F32), 0.0).astype(BF16)
                probs = p_ref[2 * p + head, first : first + QB, 0:size]
                d_probs = dot_nt(chosen, values)
                exact = probs.astype(F32)
                both = exact * d_probs
                d_low = (both - exact * jnp.sum(both, -1, keepdims=True)).astype(BF16)
                got.append(
                    (dot_nn(d_low, keys), dot_tn(d_low, queries), dot_tn(probs, context))
                )
            dq[first : first + QB, at] = (jnp.where(lanes, got[0][0], got[1][0]) * 0.125).astype(BF16)
            d_keys.append(jnp.where(wide, got[0][1], got[1][1]))
            d_values.append(jnp.where(wide, got[0][2], got[1][2]))
        for ref, parts, scale in ((dk, d_keys, 0.125), (dv, d_values, 1.0)):
            for lane in range(0, length, SPAN):
                terms = [
                    part[lane - low : lane - low + SPAN]
                    for part, (_, low, size) in zip(parts, wins)
                    if low <= lane < low + size
                ]
                ref[lane : lane + SPAN, at] = (sum(terms[1:], terms[0]) * scale).astype(BF16)
        return 0

    lax.fori_loop(0, width // 128, pair, 0)
    squash = jnp.tanh(x_ref[...] * (1.0 / ranges[0]))
    back = dot_nn(dq[...], wt_ref[0]) + dot_nn(dk[...], wt_ref[1]) + dot_nn(dv[...], wt_ref[2])
    dx_ref[...] = dh1_ref[...] + back * (1.0 - squash * squash)

    def sums(ref):
        return jnp.sum(ref[:, mine].astype(F32), 0, keepdims=True)

    @pl.when(r == 0)
    def _():
        acc_o[...] = jnp.zeros_like(acc_o)
        acc_q[...] = jnp.zeros_like(acc_q)
        gb_ref[...] = jnp.zeros_like(gb_ref)

    acc_o[...] += dot_tn(cq_ref[:, mine], da_ref[...])
    for j, ref in enumerate((dq, dk, dv)):
        acc_q[j] += dot_tn(ref[:, mine], xq_ref[...])
    gb_ref[0:1] += sums(dq)
    gb_ref[1:2] += sums(dv)

    @pl.when(r == pl.num_programs(0) - 1)
    def _():
        go_ref[...] = acc_o[...].astype(BF16)
        gq_ref[...] = acc_q[...].astype(BF16)


def attend_back(place, inputs, xq, q, k, v, probs, cq, cs, da, dh1, wt, wo, ranges, rows, length):
    tokens, width = inputs.shape
    mine = rows // 2
    half = tokens // 2
    size = probs.shape[2]
    side = width // 2
    by_row = lambda r, place: (r, 0)
    whole = lambda n: (lambda r, place: (0,) * n)
    one = pl.Buffered(1)
    return pl.pallas_call(
        attend_back_kernel,
        out_shape=(
            S((half, width), F32),
            S((side, width), BF16),
            S((3, side, width), BF16),
            S((8, side), F32),
        ),
        grid_spec=pltpu.PrefetchScalarGridSpec(
            num_scalar_prefetch=1,
            grid=(mine,),
            in_specs=[
                pl.BlockSpec((length, width), lambda r, place: (place[0] * mine + r, 0)),
                *[pl.BlockSpec((length, width), by_row)] * 4,
                pl.BlockSpec((width // HD, length, size), lambda r, place: (r, 0, 0)),
                *[pl.BlockSpec((length, width), by_row)] * 4,
                pl.BlockSpec(wt.shape, whole(3), pipeline_mode=one),
                pl.BlockSpec(wo.shape, whole(2), pipeline_mode=one),
                SMEM,
            ],
            out_specs=(
                pl.BlockSpec((length, width), by_row),
                pl.BlockSpec((side, width), whole(2), pipeline_mode=one),
                pl.BlockSpec((3, side, width), whole(3), pipeline_mode=one),
                pl.BlockSpec((8, side), whole(2)),
            ),
            scratch_shapes=[
                pltpu.VMEM((length, width), BF16),
                pltpu.VMEM((length, width), BF16),
                pltpu.VMEM((length, width), BF16),
                pltpu.VMEM((length, width), BF16),
                pltpu.VMEM((side, width), F32),
                pltpu.VMEM((3, side, width), F32),
            ],
        ),
        compiler_params=pltpu.CompilerParams(vmem_limit_bytes=60 * MIB),
        name="attend_back",
    )(place, inputs, xq, q, k, v, probs, cq, cs, da, dh1, wt, wo, ranges)


GROUP = 192
QUARTER = GROUP // 4
HOPS = ("core", "y", "z1", "z2", "z3", "ag")
LINE_HOPS = ("zs1", "zs2", "zy", "zb1", "zb2", "zb3")


def sum_scratch(groups, width, extra, small_shape):
    count = max(extra, 1)
    dma = pltpu.SemaphoreType.DMA
    buf = lambda *shape: pltpu.VMEM(shape + (width,), BF16)
    kinds = dict(
        own=buf(groups * GROUP), got_y=buf(groups, QUARTER), part=buf(groups, QUARTER),
        got_1=buf(groups, QUARTER), got_2=buf(groups, QUARTER), got_x=buf(count, groups, QUARTER),
        line_1=buf(groups, 2, QUARTER), line_2=buf(groups, 2, QUARTER), line_y=buf(groups, 2, QUARTER),
        line_x=buf(count, groups, 2, QUARTER),
        small_own=pltpu.VMEM(small_shape, F32), small_got=pltpu.VMEM((4 + extra,) + small_shape, F32),
        x_s=dma((count, groups)), x_r=dma((count, groups)),
        lx_s=dma((count, groups, 2)), lx_r=dma((count, groups, 2)),
        small_s=dma((4 + extra,)), small_r=dma((4 + extra,)),
    )
    for hop in HOPS:
        kinds[hop + "_s"], kinds[hop + "_r"] = dma((groups,)), dma((groups,))
    for hop in LINE_HOPS:
        kinds[hop + "_s"], kinds[hop + "_r"] = dma((groups, 2)), dma((groups, 2))
    return list(kinds), list(kinds.values())


class GradientSum:
    STAGES = 7

    def __init__(self, extra, mine, theirs, result, refs):
        self.__dict__.update(refs)
        self.extra, self.mine, self.theirs, self.result = extra, mine, theirs, result
        t, d = lax.axis_index("tensor"), lax.axis_index("dp")
        self.y = d % 2
        self.z = (d // 2) % 4
        self.end = jnp.logical_or(self.z == 0, self.z == 3)
        self.middle = jnp.logical_not(self.end)
        self.sib = (d, flip(t, 1))
        self.side = (flip(d, 1), t)
        self.inner = (flip(d, 2), t)
        self.across = (d + 2 * (3 - 2 * self.z), t)
        self.others = [(flip(d, 8 << b), t) for b in range(extra)]
        self.peers = [self.sib, self.side, self.inner, self.across] + self.others
        self.groups = self.own.shape[0] // GROUP

    def enter(self):
        barrier = pltpu.get_barrier_semaphore()
        for peer in self.peers:
            pl.semaphore_signal(barrier, inc=1, device_id=peer, device_id_type=MESH)
        pl.semaphore_wait(barrier, len(self.peers))

    def remote(self, src, dst, hop, at, to):
        return pltpu.make_async_remote_copy(
            src_ref=src, dst_ref=dst, send_sem=getattr(self, hop + "_s").at[at],
            recv_sem=getattr(self, hop + "_r").at[at], device_id=to, device_id_type=MESH,
        )

    def small(self, i):
        copy = self.remote(self.small_own, self.small_got.at[i], "small", i, self.peers[i])
        return copy

    def small_step(self, i):
        if i > 0:
            self.small(i - 1).wait()
            self.small_own[...] = self.small_own[...] + self.small_got[i - 1]
        if i < len(self.peers):
            self.small(i).start()

    def span(self, g):
        return pl.ds(g * GROUP, GROUP)

    def half(self, g, which):
        return pl.ds(pl.multiple_of(g * GROUP + which * QUARTER, 16), QUARTER)

    def line(self, g, i):
        return pl.ds(g * GROUP + (2 + i) * QUARTER, QUARTER)

    def core(self, g):
        return self.remote(self.theirs.at[self.span(g)], self.own.at[self.span(g)], "core", g, self.sib)

    def hop(self, name, g):
        if name == "y":
            return self.remote(self.own.at[self.half(g, 1 - self.y)], self.got_y.at[g], "y", g, self.side)
        if name == "z1":
            return self.remote(self.part.at[g], self.got_1.at[g], "z1", g, self.inner)
        if name == "z2":
            return self.remote(self.part.at[g], self.got_2.at[g], "z2", g, self.across)
        there = self.result.at[self.half(g, self.y)]
        return self.remote(there, there, name, g, self.inner if name == "z3" else self.side)

    def line_hop(self, name, g, i):
        mine = self.own.at[self.line(g, i)]
        if name == "zs1":
            return self.remote(mine, self.line_1.at[g, i], name, (g, i), self.inner)
        if name == "zs2":
            return self.remote(mine, self.line_2.at[g, i], name, (g, i), self.across)
        if name == "zy":
            return self.remote(mine, self.line_y.at[g, i], name, (g, i), self.side)
        there = self.result.at[self.line(g, i)]
        return self.remote(there, there, name, (g, i), self.across if name == "zb2" else self.inner)

    def stage(self, s, g):
        add = lambda a, b: (a.astype(F32) + b.astype(F32)).astype(BF16)
        when = lambda condition, body: pl.when(condition)(body)
        root = [self.z == 1, self.z == 2]
        passer = [self.z == 2, self.z == 1]
        near = [self.z == 0, self.z == 3]
        far = [self.z == 3, self.z == 0]
        if s == 0:
            self.core(g).start()
        if s == 1:
            self.core(g).wait()
            self.own[self.span(g)] = add(self.own[self.span(g)], self.mine[self.span(g)])
            self.hop("y", g).start()
            when(self.end, lambda: [self.line_hop("zs1", g, i).start() for i in range(2)] and None)
        if s == 2:
            self.hop("y", g).wait()
            self.part[g] = add(self.own[self.half(g, self.y)], self.got_y[g])
            when(self.end, lambda: self.hop("z1", g).start())
            for i in range(2):

                def gather(i=i):
                    self.line_hop("zs1", g, i).wait_recv()
                    rows = self.line(g, i)
                    self.own[rows] = add(self.own[rows], self.line_1[g, i])
                    when(passer[i], lambda: self.line_hop("zs2", g, i).start())

                when(self.middle, gather)
        if s == 3:

            def middle():
                self.hop("z1", g).wait_recv()
                self.part[g] = add(self.part[g], self.got_1[g])
                self.hop("z2", g).start()

            when(self.middle, middle)
            for i in range(2):

                def at_root(i=i):
                    self.line_hop("zs2", g, i).wait_recv()
                    rows = self.line(g, i)
                    self.own[rows] = add(self.own[rows], self.line_2[g, i])
                    self.line_hop("zy", g, i).start()

                when(root[i], at_root)
        if s == 4:

            def total():
                self.hop("z2", g).wait()
                self.part[g] = add(self.part[g], self.got_2[g])
                for b in range(self.extra):
                    copy = self.remote(self.part.at[g], self.got_x.at[b, g], "x", (b, g), self.others[b])
                    copy.start()
                    copy.wait()
                    self.part[g] = add(self.part[g], self.got_x[b, g])
                self.result[self.half(g, self.y)] = self.part[g]
                self.hop("ag", g).start()
                self.hop("z3", g).start()

            when(self.middle, total)
            for i in range(2):

                def spread(i=i):
                    self.line_hop("zy", g, i).wait()
                    rows = self.line(g, i)
                    self.own[rows] = add(self.own[rows], self.line_y[g, i])
                    for b in range(self.extra):
                        copy = self.remote(
                            self.own.at[rows], self.line_x.at[b, g, i], "lx", (b, g, i), self.others[b]
                        )
                        copy.start()
                        copy.wait()
                        self.own[rows] = add(self.own[rows], self.line_x[b, g, i])
                    self.result[rows] = self.own[rows]
                    self.line_hop("zb2", g, i).start()
                    self.line_hop("zb1", g, i).start()

                when(root[i], spread)
        if s == 5:

            def outer():
                self.hop("z3", g).wait_recv()
                self.hop("ag", g).start()

            when(self.end, outer)
            for i in range(2):

                def onward(i=i):
                    self.line_hop("zb2", g, i).wait_recv()
                    self.line_hop("zb3", g, i).start()

                when(passer[i], onward)
        if s == 6:
            self.hop("ag", g).wait()
            for i in range(2):
                when(near[i], lambda i=i: self.line_hop("zb1", g, i).wait_recv())
                when(far[i], lambda i=i: self.line_hop("zb3", g, i).wait_recv())

                def sent_root(i=i):
                    self.line_hop("zb1", g, i).wait_send()
                    self.line_hop("zb2", g, i).wait_send()

                def sent_passer(i=i):
                    self.line_hop("zs2", g, i).wait_send()
                    self.line_hop("zb3", g, i).wait_send()

                when(root[i], sent_root)
                when(passer[i], sent_passer)

            def sent_end():
                self.hop("z1", g).wait_send()
                for i in range(2):
                    self.line_hop("zs1", g, i).wait_send()

            when(self.end, sent_end)
            when(self.middle, lambda: self.hop("z3", g).wait_send())

    def tick(self, n):
        for s in reversed(range(self.STAGES)):
            if 0 <= n - s < self.groups:
                self.stage(s, n - s)

    def ticks(self):
        return self.groups + self.STAGES - 1


def reduce_kernel(
    extra, names, g2, g1, go, gq, smalls, lo_half, dx_half, result, small_out, lo_full, dx_full,
    mine, theirs, bounce, load_sem, big_sem, big_send, big_recv, *refs,
):
    t, d = lax.axis_index("tensor"), lax.axis_index("dp")
    c = t % 2
    engine = GradientSum(extra, mine, theirs, result, dict(zip(names, refs)))
    engine.enter()
    tokens = lo_half.shape[0]
    at = pl.ds(pl.multiple_of(c * tokens, 256), tokens)
    big = []
    bounces = []
    for i, (src, dst) in enumerate(((lo_half, lo_full), (dx_half, dx_full))):
        copy = pltpu.make_async_copy(src, bounce.at[i], big_sem.at[i])
        copy.start()
        bounces.append((copy, pltpu.make_async_copy(bounce.at[i], dst.at[at], big_sem.at[i])))
        other = pltpu.make_async_remote_copy(
            src_ref=src, dst_ref=dst.at[at], send_sem=big_send.at[i], recv_sem=big_recv.at[i],
            device_id=engine.sib, device_id_type=MESH,
        )
        other.start()
        big.append(other)

    loads = []
    hidden = g2.shape[1]
    cols = go.shape[0] // 2
    for which, (buffer, core) in enumerate(((mine, c), (theirs, 1 - c))):
        places = [
            (g2.at[core], buffer.at[0:hidden]),
            (g1.at[core], buffer.at[hidden : 2 * hidden]),
            (
                go.at[pl.ds(pl.multiple_of(core * cols, 16), cols)],
                buffer.at[2 * hidden : 2 * hidden + cols],
            ),
        ]
        for j in range(3):
            base = 2 * hidden + (j + 1) * cols
            places.append(
                (
                    gq.at[j, pl.ds(pl.multiple_of(core * cols, 16), cols)],
                    buffer.at[base : base + cols],
                )
            )
        for i, (src, dst) in enumerate(places):
            copy = pltpu.make_async_copy(src, dst, load_sem.at[which * 6 + i])
            copy.start()
            loads.append(copy)
    engine.small_own[...] = smalls[...]
    for into, out in bounces:
        into.wait()
        out.start()
        big.append(out)
    for copy in loads:
        copy.wait()
    for n in range(engine.ticks()):
        if n <= len(engine.peers):
            engine.small_step(n)
        engine.tick(n)
    small_out[...] = engine.small_own[...]
    for copy in big:
        copy.wait()


def reduce_grads(nd, g2, g1, go, gq, smalls, lo_half, dx_half):
    hidden, width = g2.shape[1:]
    cols = go.shape[0] // 2
    rows = 2 * hidden + 4 * cols
    extra = (nd // 8).bit_length() - 1
    tokens = lo_half.shape[0]
    dma = pltpu.SemaphoreType.DMA
    names, scratch = sum_scratch(rows // GROUP, width, extra, smalls.shape)
    return pl.pallas_call(
        functools.partial(reduce_kernel, extra, names),
        out_shape=(
            S((rows, width), BF16),
            S(smalls.shape, F32),
            S((2 * tokens, width), F32),
            S((2 * tokens, width), F32),
        ),
        in_specs=[ANY] * 4 + [VMEM] + [ANY] * 2,
        out_specs=(VMEM, VMEM, ANY, ANY),
        scratch_shapes=[
            pltpu.VMEM((rows, width), BF16),
            pltpu.VMEM((rows, width), BF16),
            pltpu.VMEM((2, tokens, width), F32),
            dma((12,)),
            dma((2,)), dma((2,)), dma((2,)),
            *scratch,
        ],
        compiler_params=pltpu.CompilerParams(
            collective_id=2, has_side_effects=True, vmem_limit_bytes=60 * MIB
        ),
        name="reduce_grads",
    )(g2, g1, go, gq, smalls, lo_half, dx_half)


def per_device(
    nd, inputs, segment_ids, w_qkv, b_qv, w_out, w_ff1, b_ff1, w_ff2, norm_gains, shift_biases,
    act_ranges, cotangent,
):
    t = lax.axis_index("tensor")
    c, pair = t % 2, t // 2
    rows, length = segment_ids.shape
    width = inputs.shape[1]
    cols = w_qkv.shape[2]
    hidden = w_ff1.shape[1]
    order = [(2 * pair + i) % 4 for i in range(4)]
    place = jnp.stack([c] + order).astype(jnp.int32)
    wt, wo, w1, w2, small = gather_weights(w_qkv, w_out, w_ff1, w_ff2, b_qv, b_ff1)
    weight_max = jnp.max(small[:, 3, ::128], axis=0)
    xq, q, k, v, probs, cq, cs, nq, xh, inv = attend(
        place, inputs, segment_ids, wt, wo, small, norm_gains, shift_biases, act_ranges
    )
    lo_half, g2, g1, da, dh1, sums, gb1 = feed(
        place, nq, xh, inv, cotangent, w1, w2, small, norm_gains, shift_biases, act_ranges
    )
    dx_half, go, gq, gb = attend_back(
        place, inputs, xq, q, k, v, probs, cq, cs, da, dh1, wt, wo, act_ranges, rows, length
    )
    smalls = jnp.concatenate(
        [sums[:6], gb1[:, 0], jnp.pad(gb[:2], ((0, 6), (0, width - gb.shape[1])))], axis=0
    )
    grads, smalls, layer_out, input_grad = reduce_grads(nd, g2, g1, go, gq, smalls, lo_half, dx_half)
    grads = grads.astype(F32)
    grad_ff2 = grads[:hidden]
    grad_ff1 = grads[hidden : 2 * hidden]
    grad_out = grads[2 * hidden : 2 * hidden + cols]
    grad_qkv = grads[2 * hidden + cols :].reshape(3, cols, width).transpose(0, 2, 1)
    share = lax.dynamic_slice_in_dim(smalls[:6], t * cols, cols, 1)
    grad_gains, grad_shifts = share[:2], share[2:6]
    grad_bff1 = lax.dynamic_slice_in_dim(smalls, 6 + c, 1, 0)[0]
    grad_bqv = lax.dynamic_slice_in_dim(smalls[8:10], c * cols, cols, 1)
    return (
        layer_out, input_grad, grad_qkv, grad_bqv, grad_out, grad_ff1, grad_bff1, grad_ff2,
        grad_gains, grad_shifts, weight_max,
    )


def solution(mesh):
    return jax.shard_map(
        functools.partial(per_device, mesh.shape["dp"]),
        mesh=mesh,
        in_specs=(
            P("dp", None),
            P("dp", None),
            P(None, None, "tensor"),
            P(None, "tensor"),
            P("tensor", None),
            P(None, "tensor"),
            P("tensor"),
            P("tensor", None),
            P(),
            P(),
            P(),
            P("dp", None),
        ),
        out_specs=(
            P("dp", None),
            P("dp", None),
            P(None, None, "tensor"),
            P(None, "tensor"),
            P("tensor", None),
            P(None, "tensor"),
            P("tensor"),
            P("tensor", None),
            P(None, "tensor"),
            P(None, "tensor"),
            P(),
        ),
        check_vma=False,
    )
```

```python
import functools
import math

import jax
import jax.numpy as jnp
from jax import lax
from jax.experimental import pallas as pl
from jax.experimental.pallas import tpu as pltpu
from jax.sharding import PartitionSpec as P

HD = 64
SPAN = 128
QB = 256
MASKED = -1e30
EPSILON = 1e-06
ROOT_HALF = 0.7071067811865476
INV_ROOT_TWO_PI = 0.3989422804014327
STAIR = (
    6.579734980213376,
    -12.987641368031495,
    12.20087719668052,
    -6.61489684889321,
    2.04264519055443,
)
MIB = 1 << 20
MESH = pl.DeviceIdType.MESH
F32 = jnp.float32
BF16 = jnp.bfloat16
ANY = pl.BlockSpec(memory_space=pl.ANY)
VMEM = pl.BlockSpec(memory_space=pltpu.VMEM)
SMEM = pl.BlockSpec(memory_space=pltpu.SMEM)
S = jax.ShapeDtypeStruct


def flip(value, bit):
    return value + bit - 2 * bit * ((value // bit) % 2)


def dot_nn(left, right):
    return lax.dot_general(left, right, (((1,), (0,)), ((), ())), preferred_element_type=F32)


def dot_nt(left, right):
    return lax.dot_general(left, right, (((1,), (1,)), ((), ())), preferred_element_type=F32)


def dot_tn(left, right):
    return lax.dot_general(left, right, (((0,), (0,)), ((), ())), preferred_element_type=F32)


def stairs(levels):
    whole = jnp.round(levels)
    rest = levels - whole
    square = rest * rest
    curve = STAIR[4]
    for factor in STAIR[3::-1]:
        curve = curve * square + factor
    return whole + rest * square * curve


def quantize(values, bound):
    squash = jnp.tanh(values * (1.0 / bound))
    return stairs(127.0 * squash) * (bound / 127.0), squash


def norm(hidden):
    centred = hidden - jnp.mean(hidden, -1, keepdims=True)
    inverse = lax.rsqrt(jnp.mean(centred * centred, -1, keepdims=True) + EPSILON)
    return centred * inverse, inverse


def norm_back(scaled, normed, inverse):
    return inverse * (
        scaled
        - jnp.mean(scaled, -1, keepdims=True)
        - normed * jnp.mean(scaled * normed, -1, keepdims=True)
    )


def windows(length):
    found = []
    for first in range(0, length, QB):
        low = max(0, first - SPAN)
        found.append((first, low, min(length, first + QB + SPAN) - low))
    return found


def gather_kernel(
    wqkv, wout, wff1, wff2, bqv, bff1,
    wt_all, wo_all, w1_all, w2_all, small_out,
    f_qkv, f_out, f_1, f_2, q_qkv, q_out, q_1, q_2, small,
    load_sem, local_sem, small_send, small_recv,
    sib_send, sib_recv, far_send, far_recv, side_send, side_recv, pass_send, pass_recv,
):
    t, d = lax.axis_index("tensor"), lax.axis_index("dp")
    y = d % 2
    sib, far, side = (d, flip(t, 1)), (d, flip(t, 2)), (flip(d, 1), t)
    loads = [
        pltpu.make_async_copy(src, dst, load_sem.at[i])
        for i, (src, dst) in enumerate(((wqkv, f_qkv), (wout, f_out), (wff1, f_1), (wff2, f_2)))
    ]
    for load in loads:
        load.start()
    peers = [sib, far, (d, flip(flip(t, 1), 2))]
    barrier = pltpu.get_barrier_semaphore()
    for peer in peers + [side]:
        pl.semaphore_signal(barrier, inc=1, device_id=peer, device_id_type=MESH)
    pl.semaphore_wait(barrier, 4)

    cols = f_qkv.shape[2]
    width = f_out.shape[1]
    for load in loads:
        load.wait()
    tops = [jnp.max(jnp.abs(f_qkv[j]), axis=(0, 1), keepdims=True) for j in range(3)]
    tops += [jnp.max(jnp.abs(f[...]), axis=(0, 1), keepdims=True) for f in (f_out, f_1, f_2)]
    zeros = jnp.zeros((8, width), F32)
    small[pl.ds(t, 1)] = zeros[None]
    small[pl.ds(t, 1), 0:1, :] = bff1[...][None]
    small[pl.ds(t, 1), 1:3, 0:cols] = bqv[...][None]
    row = jnp.concatenate([jnp.broadcast_to(top, (1, 128)) for top in tops], axis=1)
    small[pl.ds(t, 1), 3:4, :] = row[None]
    sends = []
    for i, peer in enumerate(peers):
        copy = pltpu.make_async_remote_copy(
            src_ref=small.at[t], dst_ref=small.at[t], send_sem=small_send.at[i],
            recv_sem=small_recv.at[i], device_id=peer, device_id_type=MESH,
        )
        copy.start()
        sends.append(copy)
    for copy in sends:
        copy.wait()
    top_row = jnp.max(small[:, 3:4, :], axis=0)
    small_out[...] = small[...]

    def weight(value, j):
        top = top_row[:, 128 * j : 128 * j + 1]
        return (stairs(value * (127.0 / top)) * (top / 127.0)).astype(BF16)

    def slot(full, i, s, half):
        if i == 0:
            part = cols // 2
            if half is None:
                return full.at[:, pl.ds(pl.multiple_of(s * cols, 16), cols)]
            return full.at[:, pl.ds(pl.multiple_of(s * cols + half * part, 16), part)]
        if i == 1:
            part = cols // 2
            if half is None:
                return full.at[pl.ds(pl.multiple_of(s * cols, 16), cols)]
            return full.at[pl.ds(pl.multiple_of(s * cols + half * part, 16), part)]
        if half is None:
            return full.at[s]
        part = full.shape[1] // 2
        return full.at[s, pl.ds(pl.multiple_of(half * part, 16), part)]

    def own_half(own, i, half):
        if i == 0:
            part = cols // 2
            return own.at[:, pl.ds(pl.multiple_of(half * part, 16), part)]
        part = own.shape[0] // 2
        return own.at[pl.ds(pl.multiple_of(half * part, 16), part)]

    fulls = (wt_all, wo_all, w1_all, w2_all)
    owns = (q_qkv, q_out, q_1, q_2)
    pending = []
    for i in range(4):
        if i == 0:
            for j in range(3):
                q_qkv[j] = jnp.transpose(
                    (stairs(f_qkv[j] * (127.0 / top_row[:, 128 * j : 128 * j + 1]))
                     * (top_row[:, 128 * j : 128 * j + 1] / 127.0))
                ).astype(BF16)
        elif i == 1:
            q_out[...] = weight(f_out[...], 3)
        elif i == 2:
            q_1[...] = weight(f_1[...], 4)
        else:
            q_2[...] = weight(f_2[...], 5)
        far_copy = pltpu.make_async_remote_copy(
            src_ref=own_half(owns[i], i, y), dst_ref=slot(fulls[i], i, t, y),
            send_sem=far_send.at[i], recv_sem=far_recv.at[i], device_id=far, device_id_type=MESH,
        )
        far_copy.start()
        sib_copy = pltpu.make_async_remote_copy(
            src_ref=owns[i], dst_ref=slot(fulls[i], i, t, None),
            send_sem=sib_send.at[i], recv_sem=sib_recv.at[i], device_id=sib, device_id_type=MESH,
        )
        sib_copy.start()
        local = pltpu.make_async_copy(owns[i], slot(fulls[i], i, t, None), local_sem.at[i])
        local.start()
        pending.append((far_copy, sib_copy, local))
    passed = []
    for i in range(4):
        far_copy, sib_copy, local = pending[i]
        far_copy.wait_recv()
        there = slot(fulls[i], i, flip(t, 2), y)
        side_copy = pltpu.make_async_remote_copy(
            src_ref=there, dst_ref=there, send_sem=side_send.at[i], recv_sem=side_recv.at[i],
            device_id=side, device_id_type=MESH,
        )
        side_copy.start()
        one = pltpu.make_async_remote_copy(
            src_ref=there, dst_ref=there, send_sem=pass_send.at[i], recv_sem=pass_recv.at[i],
            device_id=sib, device_id_type=MESH,
        )
        one.start()
        passed.append((side_copy, one))
    for i in range(4):
        side_copy, one = passed[i]
        side_copy.wait_recv()
        there = slot(fulls[i], i, flip(t, 2), 1 - y)
        two = pltpu.make_async_remote_copy(
            src_ref=there, dst_ref=there, send_sem=pass_send.at[4 + i],
            recv_sem=pass_recv.at[4 + i], device_id=sib, device_id_type=MESH,
        )
        two.start()
        passed[i] = (side_copy, one, two)
    for i in range(4):
        far_copy, sib_copy, local = pending[i]
        side_copy, one, two = passed[i]
        far_copy.wait_send()
        sib_copy.wait()
        local.wait()
        side_copy.wait_send()
        one.wait()
        two.wait()


def gather_weights(w_qkv, w_out, w_ff1, w_ff2, b_qv, b_ff1):
    _, width, cols = w_qkv.shape
    shards = 4
    hidden = w_ff1.shape[1]
    dma = pltpu.SemaphoreType.DMA
    return pl.pallas_call(
        gather_kernel,
        out_shape=(
            S((3, shards * cols, width), BF16),
            S((shards * cols, width), BF16),
            S((shards, width, hidden), BF16),
            S((shards, hidden, width), BF16),
            S((shards, 8, width), F32),
        ),
        in_specs=[ANY] * 4 + [VMEM] * 2,
        out_specs=(ANY,) * 4 + (VMEM,),
        scratch_shapes=[
            pltpu.VMEM((3, width, cols), F32),
            pltpu.VMEM((cols, width), F32),
            pltpu.VMEM((width, hidden), F32),
            pltpu.VMEM((hidden, width), F32),
            pltpu.VMEM((3, cols, width), BF16),
            pltpu.VMEM((cols, width), BF16),
            pltpu.VMEM((width, hidden), BF16),
            pltpu.VMEM((hidden, width), BF16),
            pltpu.VMEM((shards, 8, width), F32),
            dma((4,)), dma((4,)), dma((3,)), dma((3,)),
            dma((4,)), dma((4,)), dma((4,)), dma((4,)), dma((4,)), dma((4,)), dma((8,)), dma((8,)),
        ],
        compiler_params=pltpu.CompilerParams(
            collective_id=1, has_side_effects=True, vmem_limit_bytes=56 * MIB
        ),
        name="gather_weights",
    )(w_qkv, w_out, w_ff1, w_ff2, b_qv, b_ff1.reshape(1, -1))


def attend_kernel(
    place, x_ref, seg_ref, wt_ref, wo_ref, small_ref, gains, shifts, ranges,
    xq_ref, xs_ref, q_ref, k_ref, v_ref, p_ref, cq_ref, cs_ref, nq_ref, xh_ref, inv_ref,
    bias,
):
    length, width = x_ref.shape
    wins = windows(length)
    x = x_ref[...]
    coded, squash = quantize(x, ranges[0])
    xq = coded.astype(BF16)
    xq_ref[...] = xq
    xs_ref[...] = (1.0 - squash * squash).astype(BF16)
    cols = width // 4

    def both(row):
        parts = [small_ref[s, row : row + 1, 0:cols] for s in range(4)]
        return jnp.concatenate(parts, axis=1)

    q_ref[...] = (dot_nt(xq, wt_ref[0]) + both(1)).astype(BF16)
    k_ref[...] = dot_nt(xq, wt_ref[1]).astype(BF16)
    v_ref[...] = (dot_nt(xq, wt_ref[2]) + both(2)).astype(BF16)
    seg = seg_ref[0].astype(F32)
    seg_col = jnp.transpose(jnp.broadcast_to(seg, (128, length)))
    for b, (first, low, size) in enumerate(wins):
        for lane in range(0, size, 128):
            same = seg_col[first : first + QB] == seg[:, low + lane : low + lane + 128]
            bias[b, :, lane : lane + 128] = jnp.where(same, 0.0, MASKED)
    lanes = lax.broadcasted_iota(jnp.int32, (QB, 128), 1) < HD

    def pair(p, _):
        at = pl.ds(pl.multiple_of(p * 128, 128), 128)
        for b, (first, low, size) in enumerate(wins):
            queries = q_ref[first : first + QB, at].astype(F32) * 0.125
            keys = k_ref[low : low + size, at]
            values = v_ref[low : low + size, at]
            results = []
            for head in range(2):
                mine = lanes if head == 0 else jnp.logical_not(lanes)
                chosen = jnp.where(mine, queries, 0.0).astype(BF16)
                scores = dot_nt(chosen, keys) + bias[b]
                weights = jnp.exp(scores - jnp.max(scores, -1, keepdims=True))
                total = jnp.sum(weights, -1, keepdims=True)
                probs = (weights * (1.0 / total)).astype(BF16)
                p_ref[p, first : first + QB, head * size : (head + 1) * size] = probs
                results.append(dot_nn(probs, values))
            context = jnp.where(lanes, results[0], results[1])
            coded, squash = quantize(context, ranges[1])
            cq_ref[first : first + QB, at] = coded.astype(BF16)
            cs_ref[first : first + QB, at] = (1.0 - squash * squash).astype(BF16)
        return 0

    lax.fori_loop(0, width // 128, pair, 0)
    attn = dot_nn(cq_ref[...], wo_ref[...]) + shifts[0:1]
    normed, inverse = norm(x_ref[...] + attn)
    xh_ref[...] = normed
    inv_ref[...] = jnp.broadcast_to(inverse, (length, 128))
    first_norm = normed * gains[0:1] + shifts[1:2]
    nq_ref[...] = quantize(first_norm, ranges[2])[0].astype(BF16)


def attend(place, inputs, segment_ids, wt, wo, small, gains, shifts, ranges):
    rows, length = segment_ids.shape
    tokens, width = inputs.shape
    mine = rows // 2
    half = tokens // 2
    size = max(w[2] for w in windows(length))
    by_row = lambda r, place: (r, 0)
    whole = lambda n: (lambda r, place: (0,) * n)
    return pl.pallas_call(
        attend_kernel,
        out_shape=(
            S((half, width), BF16),
            S((half, width), BF16),
            S((half, width), BF16),
            S((half, width), BF16),
            S((half, width), BF16),
            S((mine * (width // 128), length, 2 * size), BF16),
            S((half, width), BF16),
            S((half, width), BF16),
            S((half, width), BF16),
            S((half, width), F32),
            S((half, 128), F32),
        ),
        grid_spec=pltpu.PrefetchScalarGridSpec(
            num_scalar_prefetch=1,
            grid=(mine,),
            in_specs=[
                pl.BlockSpec((length, width), lambda r, place: (place[0] * mine + r, 0)),
                pl.BlockSpec((1, 1, length), lambda r, place: (place[0] * mine + r, 0, 0)),
                pl.BlockSpec(wt.shape, whole(3)),
                pl.BlockSpec(wo.shape, whole(2)),
                pl.BlockSpec(small.shape, whole(3)),
                pl.BlockSpec(gains.shape, whole(2)),
                pl.BlockSpec(shifts.shape, whole(2)),
                SMEM,
            ],
            out_specs=(
                pl.BlockSpec((length, width), by_row),
                pl.BlockSpec((length, width), by_row),
                pl.BlockSpec((length, width), by_row),
                pl.BlockSpec((length, width), by_row),
                pl.BlockSpec((length, width), by_row),
                pl.BlockSpec((width // 128, length, 2 * size), lambda r, place: (r, 0, 0)),
                pl.BlockSpec((length, width), by_row),
                pl.BlockSpec((length, width), by_row),
                pl.BlockSpec((length, width), by_row),
                pl.BlockSpec((length, width), by_row),
                pl.BlockSpec((length, 128), by_row),
            ),
            scratch_shapes=[pltpu.VMEM((length // QB, QB, size), F32)],
        ),
        compiler_params=pltpu.CompilerParams(vmem_limit_bytes=56 * MIB),
        name="attend",
    )(place, inputs, segment_ids.reshape(rows, 1, length), wt, wo, small, gains, shifts, ranges)


def feed_kernel(
    place, nq_ref, xh_hbm, cot_hbm, w1_ref, w2_ref, small_ref, gains, shifts, ranges,
    out_ref, gq_ref, factor_ref, dh2_ref, do_ref, sums_ref, total, xh, cot, load_sem,
):
    i = pl.program_id(0)
    tokens, width = nq_ref.shape
    blocks = tokens // QB
    shards = pl.num_programs(0)

    def copies():
        return (
            pltpu.make_async_copy(xh_hbm, xh, load_sem.at[0]),
            pltpu.make_async_copy(
                cot_hbm.at[pl.ds(pl.multiple_of(place[0] * tokens, QB), tokens)], cot, load_sem.at[1]
            ),
        )

    @pl.when(i == 0)
    def _():
        for copy in copies():
            copy.start()

    def block(b, _):
        rows = pl.ds(pl.multiple_of(b * QB, QB), QB)
        pre = dot_nn(nq_ref[rows], w1_ref[0]) + small_ref[0, 0:1]
        cdf = 0.5 * (1.0 + lax.erf(pre * ROOT_HALF))
        coded, squash = quantize(pre * cdf, ranges[3])
        slope = cdf + pre * jnp.exp(-0.5 * pre * pre) * INV_ROOT_TWO_PI
        factor_ref[0, rows] = ((1.0 - squash * squash) * slope).astype(BF16)
        coded = coded.astype(BF16)

        @pl.when(i < 2)
        def _():
            gq_ref[0, rows] = coded

        part = dot_nn(coded, w2_ref[0])

        @pl.when(i % 2 == 0)
        def _():
            total[i // 2, rows] = part

        @pl.when(i % 2 == 1)
        def _():
            total[i // 2, rows] += part

        return 0

    lax.fori_loop(0, blocks, block, 0)

    @pl.when(i == shards - 1)
    def _():
        for copy in copies():
            copy.wait()
        sums_ref[...] = jnp.zeros_like(sums_ref)

        def block(b, _):
            rows = pl.ds(pl.multiple_of(b * QB, QB), QB)
            first = xh[rows] * gains[0:1] + shifts[1:2]
            normed, inverse = norm(first + (total[0, rows] + total[1, rows]) + shifts[2:3])
            out_ref[rows] = normed * gains[1:2] + shifts[3:4]
            grad = cot[rows]
            back = norm_back(grad * gains[1:2], normed, inverse)
            dh2_ref[rows] = back
            do_ref[rows] = back.astype(BF16)
            sums_ref[1:2] += jnp.sum(grad * normed, 0, keepdims=True)
            sums_ref[4:5] += jnp.sum(back, 0, keepdims=True)
            sums_ref[5:6] += jnp.sum(grad, 0, keepdims=True)
            return 0

        lax.fori_loop(0, blocks, block, 0)


def feed(place, nq, xh, cotangent, w1, w2, small, gains, shifts, ranges):
    tokens, width = nq.shape
    shards, _, hidden = w1.shape
    one = pl.Buffered(1)
    fixed = lambda shape: pl.BlockSpec(shape, lambda i, place: (0,) * len(shape), pipeline_mode=one)
    turn = lambda i, place: (place[1 + i], 0, 0)
    return pl.pallas_call(
        feed_kernel,
        out_shape=(
            S((tokens, width), F32),
            S((2, tokens, hidden), BF16),
            S((shards, tokens, hidden), BF16),
            S((tokens, width), F32),
            S((tokens, width), BF16),
            S((8, width), F32),
        ),
        grid_spec=pltpu.PrefetchScalarGridSpec(
            num_scalar_prefetch=1,
            grid=(shards,),
            in_specs=[
                fixed(nq.shape),
                ANY,
                ANY,
                pl.BlockSpec((1, width, hidden), turn),
                pl.BlockSpec((1, hidden, width), turn),
                pl.BlockSpec((1, 8, width), turn),
                fixed(gains.shape),
                fixed(shifts.shape),
                SMEM,
            ],
            out_specs=(
                fixed((tokens, width)),
                pl.BlockSpec((1, tokens, hidden), lambda i, place: (jnp.minimum(i, 1), 0, 0)),
                pl.BlockSpec((1, tokens, hidden), lambda i, place: (i, 0, 0)),
                fixed((tokens, width)),
                fixed((tokens, width)),
                fixed((8, width)),
            ),
            scratch_shapes=[
                pltpu.VMEM((2, tokens, width), F32),
                pltpu.VMEM((tokens, width), F32),
                pltpu.VMEM((tokens, width), F32),
                pltpu.SemaphoreType.DMA((2,)),
            ],
        ),
        compiler_params=pltpu.CompilerParams(vmem_limit_bytes=60 * MIB),
        name="feed",
    )(place, nq, xh, cotangent, w1, w2, small, gains, shifts, ranges)


GROUP = 192
QUARTER = GROUP // 4
HOPS = ("core", "y", "z1", "z2", "z3", "ag")
LINE_HOPS = ("zs1", "zs2", "zy", "zb1", "zb2", "zb3")


def sum_scratch(groups, width, extra, small_shape):
    count = max(extra, 1)
    dma = pltpu.SemaphoreType.DMA
    buf = lambda *shape: pltpu.VMEM(shape + (width,), BF16)
    kinds = dict(
        own=buf(groups * GROUP), got_y=buf(groups, QUARTER), part=buf(groups, QUARTER),
        got_1=buf(groups, QUARTER), got_2=buf(groups, QUARTER), got_x=buf(count, 2, QUARTER),
        line_1=buf(groups, 2, QUARTER), line_2=buf(groups, 2, QUARTER), line_y=buf(groups, 2, QUARTER),
        line_x=buf(count, 2, 2, QUARTER),
        small_own=pltpu.VMEM(small_shape, F32), small_got=pltpu.VMEM((4 + extra,) + small_shape, F32),
        x_s=dma((count, groups)), x_r=dma((count, groups)),
        lx_s=dma((count, groups, 2)), lx_r=dma((count, groups, 2)),
        small_s=dma((4 + extra,)), small_r=dma((4 + extra,)),
    )
    for hop in HOPS:
        kinds[hop + "_s"], kinds[hop + "_r"] = dma((groups,)), dma((groups,))
    for hop in LINE_HOPS:
        kinds[hop + "_s"], kinds[hop + "_r"] = dma((groups, 2)), dma((groups, 2))
    return list(kinds), list(kinds.values())


class GradientSum:
    STAGES = 7

    def __init__(self, extra, mine, theirs, result, refs):
        self.__dict__.update(refs)
        self.extra, self.mine, self.theirs, self.result = extra, mine, theirs, result
        t, d = lax.axis_index("tensor"), lax.axis_index("dp")
        self.y = d % 2
        self.z = (d // 2) % 4
        self.end = jnp.logical_or(self.z == 0, self.z == 3)
        self.middle = jnp.logical_not(self.end)
        self.sib = (d, flip(t, 1))
        self.side = (flip(d, 1), t)
        self.inner = (flip(d, 2), t)
        self.across = (d + 2 * (3 - 2 * self.z), t)
        self.others = [(flip(d, 8 << b), t) for b in range(extra)]
        self.peers = [self.sib, self.side, self.inner, self.across] + self.others
        self.groups = self.own.shape[0] // GROUP

    def enter(self):
        barrier = pltpu.get_barrier_semaphore()
        for peer in self.peers:
            pl.semaphore_signal(barrier, inc=1, device_id=peer, device_id_type=MESH)
        pl.semaphore_wait(barrier, len(self.peers))

    def remote(self, src, dst, hop, at, to):
        return pltpu.make_async_remote_copy(
            src_ref=src, dst_ref=dst, send_sem=getattr(self, hop + "_s").at[at],
            recv_sem=getattr(self, hop + "_r").at[at], device_id=to, device_id_type=MESH,
        )

    def small(self, i):
        copy = self.remote(self.small_own, self.small_got.at[i], "small", i, self.peers[i])
        return copy

    def small_step(self, i):
        if i > 0:
            self.small(i - 1).wait()
            self.small_own[...] = self.small_own[...] + self.small_got[i - 1]
        if i < len(self.peers):
            self.small(i).start()

    def span(self, g):
        return pl.ds(pl.multiple_of(g * GROUP, 16), GROUP)

    def half(self, g, which):
        return pl.ds(pl.multiple_of(g * GROUP + which * QUARTER, 16), QUARTER)

    def line(self, g, i):
        return pl.ds(pl.multiple_of(g * GROUP + (2 + i) * QUARTER, 16), QUARTER)

    def core(self, g):
        return self.remote(self.theirs.at[self.span(g)], self.own.at[self.span(g)], "core", g, self.sib)

    def hop(self, name, g):
        if name == "y":
            return self.remote(self.own.at[self.half(g, 1 - self.y)], self.got_y.at[g], "y", g, self.side)
        if name == "z1":
            return self.remote(self.part.at[g], self.got_1.at[g], "z1", g, self.inner)
        if name == "z2":
            return self.remote(self.part.at[g], self.got_2.at[g], "z2", g, self.across)
        there = self.result.at[self.half(g, self.y)]
        return self.remote(there, there, name, g, self.inner if name == "z3" else self.side)

    def line_hop(self, name, g, i):
        mine = self.own.at[self.line(g, i)]
        if name == "zs1":
            return self.remote(mine, self.line_1.at[g, i], name, (g, i), self.inner)
        if name == "zs2":
            return self.remote(mine, self.line_2.at[g, i], name, (g, i), self.across)
        if name == "zy":
            return self.remote(mine, self.line_y.at[g, i], name, (g, i), self.side)
        there = self.result.at[self.line(g, i)]
        return self.remote(there, there, name, (g, i), self.across if name == "zb2" else self.inner)

    def stage(self, s, g):
        add = lambda a, b: (a.astype(F32) + b.astype(F32)).astype(BF16)
        when = lambda condition, body: pl.when(condition)(body)
        root = [self.z == 1, self.z == 2]
        passer = [self.z == 2, self.z == 1]
        near = [self.z == 0, self.z == 3]
        far = [self.z == 3, self.z == 0]
        if s == 0:
            self.core(g).start()
        if s == 1:
            self.core(g).wait()
            self.own[self.span(g)] = add(self.own[self.span(g)], self.mine[self.span(g)])
            self.hop("y", g).start()
            when(self.end, lambda: [self.line_hop("zs1", g, i).start() for i in range(2)] and None)
        if s == 2:
            self.hop("y", g).wait()
            self.part[g] = add(self.own[self.half(g, self.y)], self.got_y[g])
            when(self.end, lambda: self.hop("z1", g).start())
            for i in range(2):

                def gather(i=i):
                    self.line_hop("zs1", g, i).wait_recv()
                    rows = self.line(g, i)
                    self.own[rows] = add(self.own[rows], self.line_1[g, i])
                    when(passer[i], lambda: self.line_hop("zs2", g, i).start())

                when(self.middle, gather)
        if s == 3:

            def middle():
                self.hop("z1", g).wait_recv()
                self.part[g] = add(self.part[g], self.got_1[g])
                self.hop("z2", g).start()

            when(self.middle, middle)
            for i in range(2):

                def at_root(i=i):
                    self.line_hop("zs2", g, i).wait_recv()
                    rows = self.line(g, i)
                    self.own[rows] = add(self.own[rows], self.line_2[g, i])
                    self.line_hop("zy", g, i).start()

                when(root[i], at_root)
        if s == 4:

            def total():
                self.hop("z2", g).wait()
                self.part[g] = add(self.part[g], self.got_2[g])
                for b in range(self.extra):
                    copy = self.remote(self.part.at[g], self.got_x.at[b, g % 2], "x", (b, g), self.others[b])
                    copy.start()
                    copy.wait()
                    self.part[g] = add(self.part[g], self.got_x[b, g % 2])
                self.result[self.half(g, self.y)] = self.part[g]
                self.hop("ag", g).start()
                self.hop("z3", g).start()

            when(self.middle, total)
            for i in range(2):

                def spread(i=i):
                    self.line_hop("zy", g, i).wait()
                    rows = self.line(g, i)
                    self.own[rows] = add(self.own[rows], self.line_y[g, i])
                    for b in range(self.extra):
                        copy = self.remote(
                            self.own.at[rows], self.line_x.at[b, g % 2, i], "lx", (b, g, i), self.others[b]
                        )
                        copy.start()
                        copy.wait()
                        self.own[rows] = add(self.own[rows], self.line_x[b, g % 2, i])
                    self.result[rows] = self.own[rows]
                    self.line_hop("zb2", g, i).start()
                    self.line_hop("zb1", g, i).start()

                when(root[i], spread)
        if s == 5:

            def outer():
                self.hop("z3", g).wait_recv()
                self.hop("ag", g).start()

            when(self.end, outer)
            for i in range(2):

                def onward(i=i):
                    self.line_hop("zb2", g, i).wait_recv()
                    self.line_hop("zb3", g, i).start()

                when(passer[i], onward)
        if s == 6:
            self.hop("ag", g).wait()
            for i in range(2):
                when(near[i], lambda i=i: self.line_hop("zb1", g, i).wait_recv())
                when(far[i], lambda i=i: self.line_hop("zb3", g, i).wait_recv())

                def sent_root(i=i):
                    self.line_hop("zb1", g, i).wait_send()
                    self.line_hop("zb2", g, i).wait_send()

                def sent_passer(i=i):
                    self.line_hop("zs2", g, i).wait_send()
                    self.line_hop("zb3", g, i).wait_send()

                when(root[i], sent_root)
                when(passer[i], sent_passer)

            def sent_end():
                self.hop("z1", g).wait_send()
                for i in range(2):
                    self.line_hop("zs1", g, i).wait_send()

            when(self.end, sent_end)
            when(self.middle, lambda: self.hop("z3", g).wait_send())

    def tick(self, n, first, last):
        for s in reversed(range(self.STAGES)):
            if isinstance(n, int):
                if first <= n - s < last:
                    self.stage(s, n - s)
            else:
                g = n - s
                pl.when(jnp.logical_and(g >= first, g < last))(functools.partial(self.stage, s, g))


def back_kernel(
    extra, names,
    do_hbm, gq_hbm, factor_hbm, nq_hbm, w1_hbm, w2_hbm, dh2_hbm, xh_hbm, inv_ref, sums_ref, lo_hbm,
    wo_hbm, cs_hbm, cq_hbm, q_hbm, k_hbm, v_hbm, p_hbm, xq_hbm, xs_hbm, wt_hbm, gains, ranges,
    result, small_out, lo_full, dx_full,
    grads, do, weights, gq, factor, nq, low, total, dh, xh, wo, cq, dproj, sem, lo_send, lo_recv,
    *refs,
):
    t, d = lax.axis_index("tensor"), lax.axis_index("dp")
    c, pair = t % 2, t // 2
    engine = GradientSum(extra, grads.at[c], grads.at[1 - c], result, dict(zip(names, refs)))
    tokens, width = do.shape
    hidden = w1_hbm.shape[2]
    side = width // 2
    cols = side // 2
    length = p_hbm.shape[1]
    heads = width // 128 // 2
    wins = windows(length)
    size = wins[0][2]
    blocks = tokens // QB
    slots = factor.shape[0] // length

    def load(i, src, dst):
        copy = pltpu.make_async_copy(src, dst, sem.at[i])
        copy.start()
        return copy

    def shard_at(i):
        return (2 * pair + i) % 4

    first_loads = [load(0, do_hbm, do)]
    first_loads += [load(1 + i, gq_hbm.at[i], gq.at[i * tokens : (i + 1) * tokens]) for i in range(2)]

    def load_pair(base):
        copies = []
        for i in range(2):
            s = shard_at(base + i)
            at = pl.ds(i * tokens, tokens)
            copies.append(load(3 + i, w2_hbm.at[s], weights.at[(2 + i) * width : (3 + i) * width]))
            copies.append(load(5 + i, w1_hbm.at[s], weights.at[i * width : (i + 1) * width]))
            copies.append(load(7 + i, factor_hbm.at[base + i], factor.at[at]))
        return copies

    pair_loads = load_pair(0)
    nq_load = load(9, nq_hbm, nq)
    norm_loads = [load(10, dh2_hbm, dh), load(11, xh_hbm, xh)]
    wo_load = load(12, wo_hbm, wo)
    mine = pl.ds(pl.multiple_of(pair * side, 128), side)
    cq_load = load(13, cq_hbm.at[:, mine], cq)
    engine.enter()
    at = pl.ds(pl.multiple_of(c * tokens, 256), tokens)
    lo_copy = pltpu.make_async_remote_copy(
        src_ref=lo_hbm, dst_ref=lo_full.at[at], send_sem=lo_send.at[0], recv_sem=lo_recv.at[0],
        device_id=engine.sib, device_id_type=MESH,
    )
    lo_copy.start()
    engine.small_own[...] = jnp.zeros_like(engine.small_own)
    engine.small_own[0:8] = sums_ref[...]

    def tick(n):
        engine.tick(n, 0, 9)

    for copy in first_loads:
        copy.wait()
    for i in range(2):
        grads[i, 0:hidden] = dot_tn(gq[i * tokens : (i + 1) * tokens], do[...]).astype(BF16)
    wt_loads = [load(14 + j, wt_hbm.at[j], gq.at[j * width : (j + 1) * width]) for j in range(3)]
    tick(0)
    for copy in pair_loads:
        copy.wait()

    def feed_block(own, b):
        rows = pl.ds(pl.multiple_of(b * QB, QB), QB)
        grad = do[rows]
        lows = []
        for i in range(2):
            spot = pl.ds(pl.multiple_of(i * tokens + b * QB, QB), QB)
            back = dot_nt(grad, weights[(2 + i) * width : (3 + i) * width]) * factor[spot].astype(F32)
            if own:
                engine.small_own[6 + i : 7 + i] += jnp.sum(back, 0, keepdims=True)
                low[spot] = back.astype(BF16)
            lows.append(back.astype(BF16))
        part = dot_nt(lows[0], weights[0:width]) + dot_nt(lows[1], weights[width : 2 * width])
        total[rows] = part if own else total[rows] + part

    def feed_blocks(own, begin, end):
        lax.fori_loop(begin, end, lambda b, _: (feed_block(own, b), 0)[1], 0)

    engine.small_own[6:8] = jnp.zeros_like(engine.small_own[6:8])
    feed_blocks(True, 0, blocks // 2)
    tick(1)
    feed_blocks(True, blocks // 2, blocks)
    tick(2)
    pair_loads = load_pair(2)
    nq_load.wait()
    grads[0, hidden : 2 * hidden] = dot_tn(nq[...], low[0:tokens]).astype(BF16)
    grads[1, hidden : 2 * hidden] = dot_tn(nq[...], low[tokens : 2 * tokens]).astype(BF16)
    cs_load = load(9, cs_hbm, nq)
    xq_load = load(17, xq_hbm, low.at[tokens : 2 * tokens])
    tick(3)
    for copy in pair_loads:
        copy.wait()
    feed_blocks(False, 0, blocks // 2)
    tick(4)
    feed_blocks(False, blocks // 2, blocks)
    qkv_loads = [
        load(18 + j, src, weights.at[j * tokens : (j + 1) * tokens])
        for j, src in enumerate((q_hbm, k_hbm, v_hbm))
    ]
    xs_load = load(21, xs_hbm, do)

    def unit_at(own, u):
        half = pair if own else 1 - pair
        return u // heads, half * heads + u % heads

    def probs_load(own, u):
        row, which = unit_at(own, u)
        slot = u % slots
        return pltpu.make_async_copy(
            p_hbm.at[row * 2 * heads + which],
            factor.at[pl.ds(pl.multiple_of(slot * length, length), length)],
            sem.at[22 + slot],
        )

    units = 2 * heads
    for u in range(slots - 1):
        probs_load(True, u).start()
    tick(5)

    for copy in norm_loads:
        copy.wait()

    def norm_block(b, _):
        rows = pl.ds(pl.multiple_of(b * QB, QB), QB)
        normed = xh[rows]
        squash = jnp.tanh((normed * gains[0:1] + gains[2:3]) * (1.0 / ranges[2]))
        grad = dh[rows] + total[rows] * (1.0 - squash * squash)
        inverse = jnp.max(inv_ref[rows], axis=1, keepdims=True)
        back = norm_back(grad * gains[0:1], normed, inverse)
        dh[rows] = back
        low[rows] = back.astype(BF16)
        engine.small_own[0:1] += jnp.sum(grad * normed, 0, keepdims=True)
        engine.small_own[2:3] += jnp.sum(back, 0, keepdims=True)
        engine.small_own[3:4] += jnp.sum(grad, 0, keepdims=True)
        return 0

    lax.fori_loop(0, blocks, norm_block, 0)
    tick(6)
    lo_in = load(26, lo_hbm, xh)
    wo_load.wait()
    cq_load.wait()
    cs_load.wait()
    d_attn = low.at[0:tokens]
    part = dot_tn(cq[...], d_attn[...]).astype(BF16)
    for i in range(2):
        grads[i, 2 * hidden : 2 * hidden + cols] = part[i * cols : (i + 1) * cols]

    def context_block(b, _):
        rows = pl.ds(pl.multiple_of(b * QB, QB), QB)
        nq[rows] = (dot_nt(d_attn[rows], wo[...]) * nq[rows].astype(F32)).astype(BF16)
        return 0

    lax.fori_loop(0, blocks, context_block, 0)
    lo_in.wait()
    lo_out = load(26, xh, lo_full.at[at])
    tick(7)

    for copy in qkv_loads:
        copy.wait()
    lanes = lax.broadcasted_iota(jnp.int32, (QB, 128), 1) < HD

    def attention(own, u):
        row, which = unit_at(own, u)
        probs_load(own, u).wait()

        @pl.when(u + slots - 1 < units)
        def _():
            probs_load(own, u + slots - 1).start()

        lane = pl.ds(pl.multiple_of(which * 128, 128), 128)
        here = pl.ds(pl.multiple_of((u % heads) * 128, 128), 128)
        slot = pl.multiple_of((u % slots) * length, length)
        base = pl.multiple_of(row * length, length)
        d_keys, d_values = [], []
        for b, (first, begin, _) in enumerate(wins):
            wide = lax.broadcasted_iota(jnp.int32, (size, 128), 1) < HD
            rows = pl.ds(base + first, QB)
            queries = weights[rows, lane]
            keys = weights[pl.ds(tokens + base + begin, size), lane]
            values = weights[pl.ds(2 * tokens + base + begin, size), lane]
            context = nq[rows, lane]
            got = []
            for head in range(2):
                own_lanes = lanes if head == 0 else jnp.logical_not(lanes)
                chosen = jnp.where(own_lanes, context.astype(F32), 0.0).astype(BF16)
                probs = factor[pl.ds(slot + first, QB), head * size : (head + 1) * size]
                d_probs = dot_nt(chosen, values)
                exact = probs.astype(F32)
                both = exact * d_probs
                d_low = (both - exact * jnp.sum(both, -1, keepdims=True)).astype(BF16)
                got.append((dot_nn(d_low, keys), dot_tn(d_low, queries), dot_tn(probs, context)))
            dproj[0, rows, here] = (jnp.where(lanes, got[0][0], got[1][0]) * 0.125).astype(BF16)
            d_keys.append(jnp.where(wide, got[0][1], got[1][1]))
            d_values.append(jnp.where(wide, got[0][2], got[1][2]))
        for j, parts, scale in ((1, d_keys, 0.125), (2, d_values, 1.0)):
            for spot in range(0, length, SPAN):
                terms = [
                    part[spot - begin : spot - begin + SPAN]
                    for part, (_, begin, _) in zip(parts, wins)
                    if begin <= spot < begin + size
                ]
                dproj[j, pl.ds(base + spot, SPAN), here] = (sum(terms[1:], terms[0]) * scale).astype(BF16)

    def back_through(own):
        half = pair if own else 1 - pair
        terms = [
            dot_nn(dproj[j], gq[pl.ds(pl.multiple_of(j * width + half * side, 128), side)])
            for j in range(3)
        ]
        return terms[0] + terms[1] + terms[2]

    def own_unit(u, _):
        attention(True, u)
        engine.tick(u + 8, 0, 9)
        return 0

    lax.fori_loop(0, units, own_unit, 0)
    for u in range(slots - 1):
        probs_load(False, u).start()
    for copy in wt_loads:
        copy.wait()
    xq_load.wait()
    for j in range(3):
        part = dot_tn(dproj[j], low[tokens : 2 * tokens]).astype(BF16)
        base = 2 * hidden + (j + 1) * cols
        for i in range(2):
            grads[i, base : base + cols] = part[i * cols : (i + 1) * cols]
    engine.small_own[8:9, 0:side] = jnp.sum(dproj[0].astype(F32), 0, keepdims=True)
    engine.small_own[9:10, 0:side] = jnp.sum(dproj[2].astype(F32), 0, keepdims=True)
    engine.tick(14, 0, 9)
    engine.tick(9, 9, 12)
    engine.small_step(0)
    total[...] = back_through(True)
    engine.tick(10, 9, 12)
    engine.small_step(1)

    def other_unit(u, _):
        attention(False, u)
        engine.tick(u + 11, 9, 12)
        return 0

    steps = list(range(2, len(engine.peers) + 1))
    lax.fori_loop(0, 2, other_unit, 0)
    engine.small_step(steps.pop(0))
    lax.fori_loop(2, 4, other_unit, 0)
    engine.small_step(steps.pop(0))
    lax.fori_loop(4, units, other_unit, 0)
    for step in steps:
        engine.small_step(step)
    small_out[...] = engine.small_own[...]
    xs_load.wait()
    lo_out.wait()
    other = back_through(False)
    xh[...] = dh[...] + (total[...] + other) * do[...].astype(F32)
    dx_copy = pltpu.make_async_remote_copy(
        src_ref=xh, dst_ref=dx_full.at[at], send_sem=lo_send.at[1], recv_sem=lo_recv.at[1],
        device_id=engine.sib, device_id_type=MESH,
    )
    dx_copy.start()
    dx_out = load(26, xh, dx_full.at[at])
    for n in range(units + 11, 18):
        engine.tick(n, 9, 12)
    lo_copy.wait()
    dx_copy.wait()
    dx_out.wait()


def back(
    nd, do, gq, factor, nq, w1, w2, dh2, xh, inv, sums, lo_half, wo, cs, cq, q, k, v, probs, xq, xs, wt,
    gains, shifts, ranges,
):
    tokens, width = do.shape
    hidden = w1.shape[2]
    cols = width // 4
    rows = 2 * hidden + 4 * cols
    extra = (nd // 8).bit_length() - 1
    dma = pltpu.SemaphoreType.DMA
    names, scratch = sum_scratch(rows // GROUP, width, extra, (16, width))
    length = probs.shape[1]
    buf = lambda *shape: pltpu.VMEM(shape, BF16)
    table = jnp.concatenate([gains, shifts[1:2]], axis=0)
    return pl.pallas_call(
        functools.partial(back_kernel, extra, names),
        out_shape=(
            S((rows, width), BF16),
            S((16, width), F32),
            S((2 * tokens, width), F32),
            S((2 * tokens, width), F32),
        ),
        in_specs=[ANY] * 8 + [VMEM] * 2 + [ANY] * 11 + [VMEM, SMEM],
        out_specs=(VMEM, VMEM, ANY, ANY),
        scratch_shapes=[
            buf(2, rows, width),
            buf(tokens, width),
            buf(max(4 * width, 3 * tokens), width),
            buf(max(3 * width, 2 * tokens), width),
            buf(2 * tokens, width),
            buf(tokens, width),
            buf(2 * tokens, width),
            pltpu.VMEM((tokens, width), F32),
            pltpu.VMEM((tokens, width), F32),
            pltpu.VMEM((tokens, width), F32),
            buf(width, width),
            buf(tokens, width // 2),
            buf(3, tokens, width // 2),
            dma((27,)),
            dma((2,)),
            dma((2,)),
            *scratch,
        ],
        compiler_params=pltpu.CompilerParams(
            collective_id=2, has_side_effects=True, vmem_limit_bytes=62 * MIB
        ),
        name="back",
    )(
        do, gq, factor, nq, w1, w2, dh2, xh, inv, sums, lo_half, wo, cs, cq, q, k, v, probs, xq, xs, wt,
        table, ranges,
    )


def per_device(
    nd, inputs, segment_ids, w_qkv, b_qv, w_out, w_ff1, b_ff1, w_ff2, norm_gains, shift_biases,
    act_ranges, cotangent,
):
    t = lax.axis_index("tensor")
    c, pair = t % 2, t // 2
    rows, length = segment_ids.shape
    width = inputs.shape[1]
    cols = w_qkv.shape[2]
    hidden = w_ff1.shape[1]
    order = [(2 * pair + i) % 4 for i in range(4)]
    place = jnp.stack([c] + order).astype(jnp.int32)
    wt, wo, w1, w2, small = gather_weights(w_qkv, w_out, w_ff1, w_ff2, b_qv, b_ff1)
    weight_max = jnp.max(small[:, 3, ::128], axis=0)
    xq, xs, q, k, v, probs, cq, cs, nq, xh, inv = attend(
        place, inputs, segment_ids, wt, wo, small, norm_gains, shift_biases, act_ranges
    )
    lo_half, gq, factor, dh2, do, sums = feed(
        place, nq, xh, cotangent, w1, w2, small, norm_gains, shift_biases, act_ranges
    )
    grads, smalls, layer_out, input_grad = back(
        nd, do, gq, factor, nq, w1, w2, dh2, xh, inv, sums, lo_half, wo, cs, cq, q, k, v, probs, xq, xs,
        wt, norm_gains, shift_biases, act_ranges,
    )
    grads = grads.astype(F32)
    grad_ff2 = grads[:hidden]
    grad_ff1 = grads[hidden : 2 * hidden]
    grad_out = grads[2 * hidden : 2 * hidden + cols]
    grad_qkv = grads[2 * hidden + cols :].reshape(3, cols, width).transpose(0, 2, 1)
    share = lax.dynamic_slice_in_dim(smalls[:6], t * cols, cols, 1)
    grad_gains, grad_shifts = share[:2], share[2:6]
    grad_bff1 = lax.dynamic_slice_in_dim(smalls, 6 + c, 1, 0)[0]
    grad_bqv = lax.dynamic_slice_in_dim(smalls[8:10], c * cols, cols, 1)
    return (
        layer_out, input_grad, grad_qkv, grad_bqv, grad_out, grad_ff1, grad_bff1, grad_ff2,
        grad_gains, grad_shifts, weight_max,
    )


def solution(mesh):
    return jax.shard_map(
        functools.partial(per_device, mesh.shape["dp"]),
        mesh=mesh,
        in_specs=(
            P("dp", None),
            P("dp", None),
            P(None, None, "tensor"),
            P(None, "tensor"),
            P("tensor", None),
            P(None, "tensor"),
            P("tensor"),
            P("tensor", None),
            P(),
            P(),
            P(),
            P("dp", None),
        ),
        out_specs=(
            P("dp", None),
            P("dp", None),
            P(None, None, "tensor"),
            P(None, "tensor"),
            P("tensor", None),
            P(None, "tensor"),
            P("tensor"),
            P("tensor", None),
            P(None, "tensor"),
            P(None, "tensor"),
            P(),
        ),
        check_vma=False,
    )
```

```python
import functools
import math

import jax
import jax.numpy as jnp
from jax import lax
from jax.experimental import pallas as pl
from jax.experimental.pallas import tpu as pltpu
from jax.sharding import PartitionSpec as P

HD = 64
SPAN = 128
QB = 256
MASKED = -1e30
EPSILON = 1e-06
ROOT_HALF = 0.7071067811865476
INV_ROOT_TWO_PI = 0.3989422804014327
STAIR = (
    6.579734980213376,
    -12.987641368031495,
    12.20087719668052,
    -6.61489684889321,
    2.04264519055443,
)
MIB = 1 << 20
MESH = pl.DeviceIdType.MESH
F32 = jnp.float32
BF16 = jnp.bfloat16
ANY = pl.BlockSpec(memory_space=pl.ANY)
VMEM = pl.BlockSpec(memory_space=pltpu.VMEM)
SMEM = pl.BlockSpec(memory_space=pltpu.SMEM)
S = jax.ShapeDtypeStruct


def flip(value, bit):
    return value + bit - 2 * bit * ((value // bit) % 2)


def dot_nn(left, right):
    return lax.dot_general(left, right, (((1,), (0,)), ((), ())), preferred_element_type=F32)


def dot_nt(left, right):
    return lax.dot_general(left, right, (((1,), (1,)), ((), ())), preferred_element_type=F32)


def dot_tn(left, right):
    return lax.dot_general(left, right, (((0,), (0,)), ((), ())), preferred_element_type=F32)


def stairs(levels):
    whole = jnp.round(levels)
    rest = levels - whole
    square = rest * rest
    curve = STAIR[4]
    for factor in STAIR[3::-1]:
        curve = curve * square + factor
    return whole + rest * square * curve


def quantize(values, bound):
    squash = jnp.tanh(values * (1.0 / bound))
    return stairs(127.0 * squash) * (bound / 127.0), squash


def norm(hidden):
    centred = hidden - jnp.mean(hidden, -1, keepdims=True)
    inverse = lax.rsqrt(jnp.mean(centred * centred, -1, keepdims=True) + EPSILON)
    return centred * inverse, inverse


def norm_back(scaled, normed, inverse):
    return inverse * (
        scaled
        - jnp.mean(scaled, -1, keepdims=True)
        - normed * jnp.mean(scaled * normed, -1, keepdims=True)
    )


def windows(length):
    found = []
    for first in range(0, length, QB):
        low = max(0, first - SPAN)
        found.append((first, low, min(length, first + QB + SPAN) - low))
    return found


def forward_kernel(
    wqkv, wout, wff1, wff2, bqv, bff1, x_hbm, cot_hbm, seg_ref, gains, shifts, ranges,
    bank_out, top_out, xq_out, xs_out, q_out, k_out, v_out, p_out, cq_out, cs_out, nq_out, xh_out,
    inv_out, lo_out, gq_out, factor_out, dh2_out, do_out, sums_out,
    bank, flat, x, xq, xs, qkv, probs, cq, cs, total, bias, xh, nq, inv, small,
    sem, out_sem, p_sem, f_sem, small_s, small_r, sib_s, sib_r, far_s, far_r, side_s, side_r,
    one_s, one_r, two_s, two_r,
):
    t, d = lax.axis_index("tensor"), lax.axis_index("dp")
    c, pair, y = t % 2, t // 2, d % 2
    sib, far, side = (d, flip(t, 1)), (d, flip(t, 2)), (flip(d, 1), t)
    diagonal = (d, flip(flip(t, 1), 2))
    cols, width = wout.shape
    hidden = wff1.shape[1]
    tokens = x.shape[0]
    length = seg_ref.shape[1]
    rows_here = tokens // length
    lanes_half = width // 2
    wins = windows(length)
    size = wins[0][2]
    blocks = tokens // QB
    heads = width // 256
    units = rows_here * heads
    piece = cols
    pieces = bank.shape[1] // piece

    def load(i, src, dst):
        copy = pltpu.make_async_copy(src, dst, sem.at[i])
        copy.start()
        return copy

    mine = pl.ds(pl.multiple_of(c * tokens, QB), tokens)
    loads = [load(j, wqkv.at[j], flat.at[j * cols : (j + 1) * cols]) for j in range(3)]
    loads.append(load(3, wout, flat.at[3 * cols : 4 * cols]))
    loads.append(load(4, wff1, flat.at[4 * cols : 4 * cols + width]))
    loads.append(load(5, wff2, flat.at[4 * cols + width : 4 * cols + width + hidden]))
    x_load = load(6, x_hbm.at[mine], x)
    spans = [(j * cols, cols) for j in range(4)]
    spans += [(4 * cols, width), (4 * cols + width, hidden)]

    barrier = pltpu.get_barrier_semaphore()
    for peer in (sib, far, diagonal, side):
        pl.semaphore_signal(barrier, inc=1, device_id=peer, device_id_type=MESH)
    small[pl.ds(t, 1)] = jnp.zeros((1, 8, width), F32)
    small[pl.ds(t, 1), 0:1, 0:hidden] = bff1[...][None]
    small[pl.ds(t, 1), 1:3, 0:cols] = bqv[...][None]
    for j, (begin, count) in enumerate(spans):
        loads[j].wait()
        top = jnp.max(jnp.abs(flat[begin : begin + count]), axis=(0, 1), keepdims=True)
        small[pl.ds(t, 1), 3:4, 128 * j : 128 * (j + 1)] = jnp.broadcast_to(top, (1, 128))[None]
    pl.semaphore_wait(barrier, 4)
    sends = []
    for i, peer in enumerate((sib, far, diagonal)):
        copy = pltpu.make_async_remote_copy(
            src_ref=small.at[t], dst_ref=small.at[t], send_sem=small_s.at[i],
            recv_sem=small_r.at[i], device_id=peer, device_id_type=MESH,
        )
        copy.start()
        sends.append(copy)

    x_load.wait()

    def input_block(b, _):
        rows = pl.ds(pl.multiple_of(b * QB, QB), QB)
        coded, squash = quantize(x[rows], ranges[0])
        xq[rows] = coded.astype(BF16)
        xs[rows] = (1.0 - squash * squash).astype(BF16)
        return 0

    lax.fori_loop(0, blocks, input_block, 0)
    outs = []

    def put(src, dst):
        copy = pltpu.make_async_copy(src, dst, out_sem.at[len(outs)])
        copy.start()
        outs.append(copy)
        return copy

    for copy in sends:
        copy.wait()
    top_row = jnp.max(small[:, 3:4, :], axis=0)
    top_out[...] = top_row

    def far_copy(p):
        at = pl.ds(pl.multiple_of(p * piece + y * (piece // 2), 16), piece // 2)
        return pltpu.make_async_remote_copy(
            src_ref=bank.at[t, at], dst_ref=bank.at[t, at], send_sem=far_s.at[p], recv_sem=far_r.at[p],
            device_id=far, device_id_type=MESH,
        )

    def sib_copy(p):
        at = pl.ds(pl.multiple_of(p * piece, 16), piece)
        return pltpu.make_async_remote_copy(
            src_ref=bank.at[t, at], dst_ref=bank.at[t, at], send_sem=sib_s.at[p], recv_sem=sib_r.at[p],
            device_id=sib, device_id_type=MESH,
        )

    def onward(p, half, send, recv, to):
        at = pl.ds(pl.multiple_of(p * piece + half * (piece // 2), 16), piece // 2)
        there = bank.at[flip(t, 2), at]
        return pltpu.make_async_remote_copy(
            src_ref=there, dst_ref=there, send_sem=send.at[p], recv_sem=recv.at[p],
            device_id=to, device_id_type=MESH,
        )

    side_copy = lambda p: onward(p, y, side_s, side_r, side)
    one_copy = lambda p: onward(p, y, one_s, one_r, sib)
    two_copy = lambda p: onward(p, 1 - y, two_s, two_r, sib)

    for j, (begin, count) in enumerate(spans):
        top = top_row[:, 128 * j : 128 * j + 1]
        up, down = 127.0 / top, top / 127.0

        def code(p, _, up=up, down=down):
            at = pl.ds(pl.multiple_of(p * piece, 16), piece)
            bank[t, at] = (stairs(flat[at] * up) * down).astype(BF16)
            far_copy(p).start()
            sib_copy(p).start()
            return 0

        lax.fori_loop(begin // piece, (begin + count) // piece, code, 0)
    put(xq, xq_out)
    put(xs, xs_out)

    def first_step(p):
        far_copy(p).wait_recv()
        side_copy(p).start()
        one_copy(p).start()

    def second_step(p):
        side_copy(p).wait_recv()
        two_copy(p).start()

    def tick(n):
        if isinstance(n, int):
            if n < pieces:
                first_step(n)
            if 0 <= n - 3 < pieces:
                second_step(n - 3)
            return
        pl.when(n < pieces)(lambda: first_step(n))
        pl.when(jnp.logical_and(n >= 3, n < pieces + 3))(lambda: second_step(n - 3))

    def arrived(own, p):
        if own:
            sib_copy(p).wait_recv()
        else:
            one_copy(p).wait_recv()
            two_copy(p).wait_recv()

    def shard_rows(own, begin, count):
        first = 2 * pair if own else 2 - 2 * pair
        return jnp.concatenate(
            [bank[first, begin : begin + count], bank[first + 1, begin : begin + count]], axis=0
        )

    def half_lanes(own):
        return pl.ds(pl.multiple_of((pair if own else 1 - pair) * lanes_half, 128), lanes_half)

    for r in range(rows_here):
        seg = seg_ref[pl.ds(c * rows_here + r, 1)].astype(F32)
        seg_col = jnp.transpose(jnp.broadcast_to(seg, (128, length)))
        for b, (first, low, _) in enumerate(wins):
            for lane in range(0, size, 128):
                same = seg_col[first : first + QB] == seg[:, low + lane : low + lane + 128]
                bias[r, b, :, lane : lane + 128] = jnp.where(same, 0.0, MASKED)
    lanes = lax.broadcasted_iota(jnp.int32, (QB, 128), 1) < HD

    def project(own):
        first = 2 * pair if own else 2 - 2 * pair
        at = half_lanes(own)
        for j in range(3):
            value = dot_nt(xq[...], shard_rows(own, j * cols, cols))
            if j != 1:
                row = 1 if j == 0 else 2
                value += jnp.concatenate(
                    [small[first + i, row : row + 1, 0:cols] for i in range(2)], axis=1
                )
            qkv[j * tokens : (j + 1) * tokens, at] = value.astype(BF16)

    def p_copy(own, u):
        n = u if own else u + units
        slot = n % 4
        which = (pair if own else 1 - pair) * heads + u % heads
        return pltpu.make_async_copy(
            probs.at[pl.ds(pl.multiple_of(slot * length, length), length)],
            p_out.at[u // heads * 2 * heads + which],
            p_sem.at[slot],
        )

    def attention(own, u):
        n = u if own else u + units
        row = u // heads
        which = (pair if own else 1 - pair) * heads + u % heads
        at = pl.ds(pl.multiple_of(which * 128, 128), 128)
        base = pl.multiple_of(row * length, length)
        slot = pl.multiple_of((n % 4) * length, length)
        if own:
            pl.when(u >= 4)(lambda: p_copy(True, u - 4).wait())
        else:
            pl.when(u < 4)(lambda: p_copy(True, u + units - 4).wait())
            pl.when(u >= 4)(lambda: p_copy(False, u - 4).wait())
        for b, (first, low, _) in enumerate(wins):
            rows = pl.ds(base + first, QB)
            queries = qkv[rows, at].astype(F32) * 0.125
            keys = qkv[pl.ds(tokens + base + low, size), at]
            values = qkv[pl.ds(2 * tokens + base + low, size), at]
            results = []
            for head in range(2):
                inside = lanes if head == 0 else jnp.logical_not(lanes)
                chosen = jnp.where(inside, queries, 0.0).astype(BF16)
                scores = dot_nt(chosen, keys) + bias[row, b]
                weights = jnp.exp(scores - jnp.max(scores, -1, keepdims=True))
                share = 1.0 / jnp.sum(weights, -1, keepdims=True)
                low_probs = (weights * share).astype(BF16)
                probs[pl.ds(slot + first, QB), head * size : (head + 1) * size] = low_probs
                results.append(dot_nn(low_probs, values))
            coded, squash = quantize(jnp.where(lanes, results[0], results[1]), ranges[1])
            cq[rows, at] = coded.astype(BF16)
            cs[rows, at] = (1.0 - squash * squash).astype(BF16)
        p_copy(own, u).start()

    for p in range(3):
        arrived(True, p)
    project(True)

    def own_unit(u, _):
        attention(True, u)
        pl.when(u > 0)(lambda: tick(u - 1))
        return 0

    lax.fori_loop(0, units, own_unit, 0)
    arrived(True, 3)
    total[...] = dot_nn(cq[:, half_lanes(True)], shard_rows(True, 3 * cols, cols))
    tick(units - 1)

    for p in range(3):
        arrived(False, p)
    project(False)

    def other_unit(u, _):
        attention(False, u)
        tick(u + units)
        return 0

    lax.fori_loop(0, units, other_unit, 0)
    put(qkv.at[0:tokens], q_out)
    put(qkv.at[tokens : 2 * tokens], k_out)
    put(qkv.at[2 * tokens : 3 * tokens], v_out)
    put(cq, cq_out)
    put(cs, cs_out)
    arrived(False, 3)

    def norm_block(b, _):
        rows = pl.ds(pl.multiple_of(b * QB, QB), QB)
        attn = total[rows] + dot_nn(cq[rows, half_lanes(False)], shard_rows(False, 3 * cols, cols))
        normed, inverse = norm(x[rows] + (attn + shifts[0:1]))
        xh[rows] = normed
        inv[rows] = jnp.broadcast_to(inverse, (QB, 128))
        nq[rows] = quantize(normed * gains[0:1] + shifts[1:2], ranges[2])[0].astype(BF16)
        pl.when(b < 3)(lambda: tick(b + 2 * units))
        return 0

    lax.fori_loop(0, blocks, norm_block, 0)
    xh_put = put(xh, xh_out)
    put(inv, inv_out)
    nq_put = put(nq, nq_out)
    cot_load = load(6, cot_hbm.at[mine], x)

    for u in range(units - 4, units):
        p_copy(False, u).wait()
    for copy in outs[2:5]:
        copy.wait()

    def feed_copies(i, b, with_gq):
        rows = pl.ds(pl.multiple_of(b * QB, QB), QB)
        found = [
            pltpu.make_async_copy(
                qkv.at[pl.ds(pl.multiple_of(b * QB, QB), QB)], factor_out.at[i, rows], f_sem.at[0, b]
            )
        ]
        if with_gq:
            found.append(
                pltpu.make_async_copy(
                    qkv.at[pl.ds(pl.multiple_of(tokens + b * QB, QB), QB)], gq_out.at[i, rows],
                    f_sem.at[1, b],
                )
            )
        return found

    for i in range(4):
        own = i < 2
        shard = (2 * pair + i) % 4
        for p in range(4, pieces):
            if i == 0:
                arrived(True, p)
            if i == 2:
                arrived(False, p)

        def block(b, _, i=i, own=own, shard=shard):
            rows = pl.ds(pl.multiple_of(b * QB, QB), QB)
            pre = dot_nn(nq[rows], bank[shard, 4 * cols : 4 * cols + width]) + small[shard, 0:1, 0:hidden]
            cdf = 0.5 * (1.0 + lax.erf(pre * ROOT_HALF))
            coded, squash = quantize(pre * cdf, ranges[3])
            slope = cdf + pre * jnp.exp(-0.5 * pre * pre) * INV_ROOT_TWO_PI
            slope = ((1.0 - squash * squash) * slope).astype(BF16)
            coded = coded.astype(BF16)
            if i > 0:
                for copy in feed_copies(i - 1, b, i <= 2):
                    copy.wait()
            qkv[rows] = slope
            if own:
                qkv[pl.ds(pl.multiple_of(tokens + b * QB, QB), QB)] = coded
            for copy in feed_copies(i, b, own):
                copy.start()
            part = dot_nn(coded, bank[shard, 4 * cols + width : 4 * cols + width + hidden])
            spot = pl.ds(pl.multiple_of((i // 2) * tokens + b * QB, QB), QB)
            flat[spot] = part if i % 2 == 0 else flat[spot] + part
            return 0

        lax.fori_loop(0, blocks, block, 0)
        if i == 2:
            for s in range(4):
                put(bank.at[s], bank_out.at[s])

    cot_load.wait()
    xh_put.wait()
    nq_put.wait()
    sums_out[...] = jnp.zeros_like(sums_out)

    def last_block(b, _):
        rows = pl.ds(pl.multiple_of(b * QB, QB), QB)
        first = xh[rows] * gains[0:1] + shifts[1:2]
        feed = flat[rows] + flat[pl.ds(pl.multiple_of(tokens + b * QB, QB), QB)]
        normed, inverse = norm(first + (feed + shifts[2:3]))
        xh[rows] = normed * gains[1:2] + shifts[3:4]
        grad = x[rows]
        back = norm_back(grad * gains[1:2], normed, inverse)
        total[rows] = back
        nq[rows] = back.astype(BF16)
        sums_out[1:2] += jnp.sum(grad * normed, 0, keepdims=True)
        sums_out[4:5] += jnp.sum(back, 0, keepdims=True)
        sums_out[5:6] += jnp.sum(grad, 0, keepdims=True)
        return 0

    lax.fori_loop(0, blocks, last_block, 0)
    put(xh, lo_out)
    put(total, dh2_out)
    put(nq, do_out)
    for b in range(blocks):
        for copy in feed_copies(3, b, False):
            copy.wait()

    def sent(p, _):
        far_copy(p).wait_send()
        sib_copy(p).wait_send()
        side_copy(p).wait_send()
        one_copy(p).wait_send()
        two_copy(p).wait_send()
        return 0

    lax.fori_loop(0, pieces, sent, 0)
    for k, copy in enumerate(outs):
        if k not in (2, 3, 4) and copy is not xh_put and copy is not nq_put:
            copy.wait()


def forward(inputs, segment_ids, w_qkv, b_qv, w_out, w_ff1, b_ff1, w_ff2, gains, shifts, ranges, cotangent):
    cols, width = w_out.shape
    hidden = w_ff1.shape[1]
    rows, length = segment_ids.shape
    tokens = inputs.shape[0] // 2
    size = windows(length)[0][2]
    units = rows // 2 * (width // 128)
    bank_rows = 4 * cols + width + hidden
    pieces = bank_rows // cols
    dma = pltpu.SemaphoreType.DMA
    low = lambda *shape: pltpu.VMEM(shape, BF16)
    full = lambda *shape: pltpu.VMEM(shape, F32)
    wide = S((tokens, width), BF16)
    deep = S((tokens, width), F32)
    return pl.pallas_call(
        forward_kernel,
        out_shape=(
            S((4, bank_rows, width), BF16),
            S((1, width), F32),
            wide, wide, wide, wide, wide,
            S((units, length, 2 * size), BF16),
            wide, wide, wide, deep,
            S((tokens, 128), F32),
            deep,
            S((2, tokens, hidden), BF16),
            S((4, tokens, hidden), BF16),
            deep, wide,
            S((8, width), F32),
        ),
        in_specs=[ANY] * 4 + [VMEM] * 2 + [ANY] * 2 + [VMEM] * 3 + [SMEM],
        out_specs=(ANY, VMEM) + (ANY,) * 16 + (VMEM,),
        scratch_shapes=[
            low(4, bank_rows, width),
            full(max(bank_rows, 2 * tokens), width),
            full(tokens, width),
            low(tokens, width),
            low(tokens, width),
            low(3 * tokens, width),
            low(4 * length, 2 * size),
            low(tokens, width),
            low(tokens, width),
            full(tokens, width),
            full(tokens // length, length // QB, QB, size),
            full(tokens, width),
            low(tokens, width),
            full(tokens, 128),
            full(4, 8, width),
            dma((7,)), dma((24,)), dma((4,)), dma((2, tokens // QB)), dma((3,)), dma((3,)),
            *[dma((pieces,))] * 10,
        ],
        compiler_params=pltpu.CompilerParams(
            collective_id=1, has_side_effects=True, vmem_limit_bytes=62 * MIB
        ),
        name="forward",
    )(
        jnp.swapaxes(w_qkv, 1, 2), w_out, w_ff1, w_ff2, b_qv, b_ff1.reshape(1, -1), inputs, cotangent,
        segment_ids, gains, shifts, ranges,
    )


GROUP = 192
QUARTER = GROUP // 4
HOPS = ("core", "y", "z1", "z2", "z3", "ag")
LINE_HOPS = ("zs1", "zs2", "zy", "zb1", "zb2", "zb3")


def sum_scratch(groups, width, extra, small_shape):
    count = max(extra, 1)
    dma = pltpu.SemaphoreType.DMA
    buf = lambda *shape: pltpu.VMEM(shape + (width,), BF16)
    kinds = dict(
        own=buf(groups * GROUP), got_y=buf(groups, QUARTER), part=buf(groups, QUARTER),
        got_1=buf(groups, QUARTER), got_2=buf(groups, QUARTER), got_x=buf(count, 2, QUARTER),
        line_1=buf(groups, 2, QUARTER), line_2=buf(groups, 2, QUARTER), line_y=buf(groups, 2, QUARTER),
        line_x=buf(count, 2, 2, QUARTER),
        small_own=pltpu.VMEM(small_shape, F32), small_got=pltpu.VMEM((4 + extra,) + small_shape, F32),
        x_s=dma((count, groups)), x_r=dma((count, groups)),
        lx_s=dma((count, groups, 2)), lx_r=dma((count, groups, 2)),
        small_s=dma((4 + extra,)), small_r=dma((4 + extra,)),
    )
    for hop in HOPS:
        kinds[hop + "_s"], kinds[hop + "_r"] = dma((groups,)), dma((groups,))
    for hop in LINE_HOPS:
        kinds[hop + "_s"], kinds[hop + "_r"] = dma((groups, 2)), dma((groups, 2))
    return list(kinds), list(kinds.values())


class GradientSum:
    STAGES = 7

    def __init__(self, extra, mine, theirs, result, refs):
        self.__dict__.update(refs)
        self.extra, self.mine, self.theirs, self.result = extra, mine, theirs, result
        t, d = lax.axis_index("tensor"), lax.axis_index("dp")
        self.y = d % 2
        self.z = (d // 2) % 4
        self.end = jnp.logical_or(self.z == 0, self.z == 3)
        self.middle = jnp.logical_not(self.end)
        self.sib = (d, flip(t, 1))
        self.side = (flip(d, 1), t)
        self.inner = (flip(d, 2), t)
        self.across = (d + 2 * (3 - 2 * self.z), t)
        self.others = [(flip(d, 8 << b), t) for b in range(extra)]
        self.peers = [self.sib, self.side, self.inner, self.across] + self.others
        self.groups = self.own.shape[0] // GROUP

    def enter(self):
        barrier = pltpu.get_barrier_semaphore()
        for peer in self.peers:
            pl.semaphore_signal(barrier, inc=1, device_id=peer, device_id_type=MESH)
        pl.semaphore_wait(barrier, len(self.peers))

    def remote(self, src, dst, hop, at, to):
        return pltpu.make_async_remote_copy(
            src_ref=src, dst_ref=dst, send_sem=getattr(self, hop + "_s").at[at],
            recv_sem=getattr(self, hop + "_r").at[at], device_id=to, device_id_type=MESH,
        )

    def small(self, i):
        copy = self.remote(self.small_own, self.small_got.at[i], "small", i, self.peers[i])
        return copy

    def small_step(self, i):
        if i > 0:
            self.small(i - 1).wait()
            self.small_own[...] = self.small_own[...] + self.small_got[i - 1]
        if i < len(self.peers):
            self.small(i).start()

    def span(self, g):
        return pl.ds(pl.multiple_of(g * GROUP, 16), GROUP)

    def half(self, g, which):
        return pl.ds(pl.multiple_of(g * GROUP + which * QUARTER, 16), QUARTER)

    def line(self, g, i):
        return pl.ds(pl.multiple_of(g * GROUP + (2 + i) * QUARTER, 16), QUARTER)

    def core(self, g):
        return self.remote(self.theirs.at[self.span(g)], self.own.at[self.span(g)], "core", g, self.sib)

    def hop(self, name, g):
        if name == "y":
            return self.remote(self.own.at[self.half(g, 1 - self.y)], self.got_y.at[g], "y", g, self.side)
        if name == "z1":
            return self.remote(self.part.at[g], self.got_1.at[g], "z1", g, self.inner)
        if name == "z2":
            return self.remote(self.part.at[g], self.got_2.at[g], "z2", g, self.across)
        there = self.result.at[self.half(g, self.y)]
        return self.remote(there, there, name, g, self.inner if name == "z3" else self.side)

    def line_hop(self, name, g, i):
        mine = self.own.at[self.line(g, i)]
        if name == "zs1":
            return self.remote(mine, self.line_1.at[g, i], name, (g, i), self.inner)
        if name == "zs2":
            return self.remote(mine, self.line_2.at[g, i], name, (g, i), self.across)
        if name == "zy":
            return self.remote(mine, self.line_y.at[g, i], name, (g, i), self.side)
        there = self.result.at[self.line(g, i)]
        return self.remote(there, there, name, (g, i), self.across if name == "zb2" else self.inner)

    def stage(self, s, g):
        add = lambda a, b: (a.astype(F32) + b.astype(F32)).astype(BF16)
        when = lambda condition, body: pl.when(condition)(body)
        root = [self.z == 1, self.z == 2]
        passer = [self.z == 2, self.z == 1]
        near = [self.z == 0, self.z == 3]
        far = [self.z == 3, self.z == 0]
        if s == 0:
            self.core(g).start()
        if s == 1:
            self.core(g).wait()
            self.own[self.span(g)] = add(self.own[self.span(g)], self.mine[self.span(g)])
            self.hop("y", g).start()
            when(self.end, lambda: [self.line_hop("zs1", g, i).start() for i in range(2)] and None)
        if s == 2:
            self.hop("y", g).wait()
            self.part[g] = add(self.own[self.half(g, self.y)], self.got_y[g])
            when(self.end, lambda: self.hop("z1", g).start())
            for i in range(2):

                def gather(i=i):
                    self.line_hop("zs1", g, i).wait_recv()
                    rows = self.line(g, i)
                    self.own[rows] = add(self.own[rows], self.line_1[g, i])
                    when(passer[i], lambda: self.line_hop("zs2", g, i).start())

                when(self.middle, gather)
        if s == 3:

            def middle():
                self.hop("z1", g).wait_recv()
                self.part[g] = add(self.part[g], self.got_1[g])
                self.hop("z2", g).start()

            when(self.middle, middle)
            for i in range(2):

                def at_root(i=i):
                    self.line_hop("zs2", g, i).wait_recv()
                    rows = self.line(g, i)
                    self.own[rows] = add(self.own[rows], self.line_2[g, i])
                    self.line_hop("zy", g, i).start()

                when(root[i], at_root)
        if s == 4:

            def total():
                self.hop("z2", g).wait()
                self.part[g] = add(self.part[g], self.got_2[g])
                for b in range(self.extra):
                    copy = self.remote(self.part.at[g], self.got_x.at[b, g % 2], "x", (b, g), self.others[b])
                    copy.start()
                    copy.wait()
                    self.part[g] = add(self.part[g], self.got_x[b, g % 2])
                self.result[self.half(g, self.y)] = self.part[g]
                self.hop("ag", g).start()
                self.hop("z3", g).start()

            when(self.middle, total)
            for i in range(2):

                def spread(i=i):
                    self.line_hop("zy", g, i).wait()
                    rows = self.line(g, i)
                    self.own[rows] = add(self.own[rows], self.line_y[g, i])
                    for b in range(self.extra):
                        copy = self.remote(
                            self.own.at[rows], self.line_x.at[b, g % 2, i], "lx", (b, g, i), self.others[b]
                        )
                        copy.start()
                        copy.wait()
                        self.own[rows] = add(self.own[rows], self.line_x[b, g % 2, i])
                    self.result[rows] = self.own[rows]
                    self.line_hop("zb2", g, i).start()
                    self.line_hop("zb1", g, i).start()

                when(root[i], spread)
        if s == 5:

            def outer():
                self.hop("z3", g).wait_recv()
                self.hop("ag", g).start()

            when(self.end, outer)
            for i in range(2):

                def onward(i=i):
                    self.line_hop("zb2", g, i).wait_recv()
                    self.line_hop("zb3", g, i).start()

                when(passer[i], onward)
        if s == 6:
            self.hop("ag", g).wait()
            for i in range(2):
                when(near[i], lambda i=i: self.line_hop("zb1", g, i).wait_recv())
                when(far[i], lambda i=i: self.line_hop("zb3", g, i).wait_recv())

                def sent_root(i=i):
                    self.line_hop("zb1", g, i).wait_send()
                    self.line_hop("zb2", g, i).wait_send()

                def sent_passer(i=i):
                    self.line_hop("zs2", g, i).wait_send()
                    self.line_hop("zb3", g, i).wait_send()

                when(root[i], sent_root)
                when(passer[i], sent_passer)

            def sent_end():
                self.hop("z1", g).wait_send()
                for i in range(2):
                    self.line_hop("zs1", g, i).wait_send()

            when(self.end, sent_end)
            when(self.middle, lambda: self.hop("z3", g).wait_send())

    def tick(self, n, first, last):
        for s in reversed(range(self.STAGES)):
            if isinstance(n, int):
                if first <= n - s < last:
                    self.stage(s, n - s)
            else:
                g = n - s
                pl.when(jnp.logical_and(g >= first, g < last))(functools.partial(self.stage, s, g))


def back_kernel(
    extra, names,
    do_hbm, gq_hbm, factor_hbm, nq_hbm, bank, dh2_hbm, xh_hbm, inv_ref, sums_ref, lo_hbm,
    cs_hbm, cq_hbm, q_hbm, k_hbm, v_hbm, p_hbm, xq_hbm, xs_hbm, gains, ranges,
    result, small_out, lo_full, dx_full,
    grads, do, weights, gq, factor, nq, low, total, dh, xh, wo, cq, dproj, sem, lo_send, lo_recv,
    *refs,
):
    t, d = lax.axis_index("tensor"), lax.axis_index("dp")
    c, pair = t % 2, t // 2
    engine = GradientSum(extra, grads.at[c], grads.at[1 - c], result, dict(zip(names, refs)))
    tokens, width = do.shape
    hidden = gq_hbm.shape[2]
    side = width // 2
    cols = side // 2
    length = p_hbm.shape[1]
    heads = width // 128 // 2
    wins = windows(length)
    size = wins[0][2]
    blocks = tokens // QB
    slots = factor.shape[0] // length

    def load(i, src, dst):
        copy = pltpu.make_async_copy(src, dst, sem.at[i])
        copy.start()
        return copy

    def shard_at(i):
        return (2 * pair + i) % 4

    first_loads = [load(0, do_hbm, do)]
    first_loads += [load(1 + i, gq_hbm.at[i], gq.at[i * tokens : (i + 1) * tokens]) for i in range(2)]

    def load_pair(base):
        copies = []
        for i in range(2):
            s = shard_at(base + i)
            at = pl.ds(i * tokens, tokens)
            for j in range(2):
                spot = weights.at[(2 * j + i) * width : (2 * j + i + 1) * width]
                copies.append(load(3 + 2 * j + i, bank.at[s, 4 * cols + j * width : 4 * cols + (j + 1) * width], spot))
            copies.append(load(7 + i, factor_hbm.at[base + i], factor.at[at]))
        return copies

    pair_loads = load_pair(0)
    nq_load = load(9, nq_hbm, nq)
    norm_loads = [load(10, dh2_hbm, dh), load(11, xh_hbm, xh)]
    wo_loads = [
        load(27 + s, bank.at[s, 3 * cols : 4 * cols], wo.at[s * cols : (s + 1) * cols]) for s in range(4)
    ]
    mine = pl.ds(pl.multiple_of(pair * side, 128), side)
    cq_load = load(13, cq_hbm.at[:, mine], cq)
    engine.enter()
    at = pl.ds(pl.multiple_of(c * tokens, 256), tokens)
    lo_copy = pltpu.make_async_remote_copy(
        src_ref=lo_hbm, dst_ref=lo_full.at[at], send_sem=lo_send.at[0], recv_sem=lo_recv.at[0],
        device_id=engine.sib, device_id_type=MESH,
    )
    lo_copy.start()
    engine.small_own[...] = jnp.zeros_like(engine.small_own)
    engine.small_own[0:8] = sums_ref[...]

    def tick(n):
        engine.tick(n, 0, 9)

    for copy in first_loads:
        copy.wait()
    for i in range(2):
        grads[i, 0:hidden] = dot_tn(gq[i * tokens : (i + 1) * tokens], do[...]).astype(BF16)
    wt_loads = [
        load(31 + s, bank.at[s, 0 : 3 * cols], gq.at[3 * s * cols : 3 * (s + 1) * cols]) for s in range(4)
    ]
    tick(0)
    for copy in pair_loads:
        copy.wait()

    def feed_block(own, b):
        rows = pl.ds(pl.multiple_of(b * QB, QB), QB)
        grad = do[rows]
        lows = []
        for i in range(2):
            spot = pl.ds(pl.multiple_of(i * tokens + b * QB, QB), QB)
            back = dot_nt(grad, weights[(2 + i) * width : (3 + i) * width]) * factor[spot].astype(F32)
            if own:
                engine.small_own[6 + i : 7 + i] += jnp.sum(back, 0, keepdims=True)
                low[spot] = back.astype(BF16)
            lows.append(back.astype(BF16))
        part = dot_nt(lows[0], weights[0:width]) + dot_nt(lows[1], weights[width : 2 * width])
        total[rows] = part if own else total[rows] + part

    def feed_blocks(own, begin, end):
        lax.fori_loop(begin, end, lambda b, _: (feed_block(own, b), 0)[1], 0)

    engine.small_own[6:8] = jnp.zeros_like(engine.small_own[6:8])
    feed_blocks(True, 0, blocks // 2)
    tick(1)
    feed_blocks(True, blocks // 2, blocks)
    tick(2)
    pair_loads = load_pair(2)
    nq_load.wait()
    grads[0, hidden : 2 * hidden] = dot_tn(nq[...], low[0:tokens]).astype(BF16)
    grads[1, hidden : 2 * hidden] = dot_tn(nq[...], low[tokens : 2 * tokens]).astype(BF16)
    cs_load = load(9, cs_hbm, nq)
    xq_load = load(17, xq_hbm, low.at[tokens : 2 * tokens])
    tick(3)
    for copy in pair_loads:
        copy.wait()
    feed_blocks(False, 0, blocks // 2)
    tick(4)
    feed_blocks(False, blocks // 2, blocks)
    qkv_loads = [
        load(18 + j, src, weights.at[j * tokens : (j + 1) * tokens])
        for j, src in enumerate((q_hbm, k_hbm, v_hbm))
    ]
    xs_load = load(21, xs_hbm, do)

    def unit_at(own, u):
        half = pair if own else 1 - pair
        return u // heads, half * heads + u % heads

    def probs_load(own, u):
        row, which = unit_at(own, u)
        slot = u % slots
        return pltpu.make_async_copy(
            p_hbm.at[row * 2 * heads + which],
            factor.at[pl.ds(pl.multiple_of(slot * length, length), length)],
            sem.at[22 + slot],
        )

    units = 2 * heads
    for u in range(slots - 1):
        probs_load(True, u).start()
    tick(5)

    for copy in norm_loads:
        copy.wait()

    def norm_block(b, _):
        rows = pl.ds(pl.multiple_of(b * QB, QB), QB)
        normed = xh[rows]
        squash = jnp.tanh((normed * gains[0:1] + gains[2:3]) * (1.0 / ranges[2]))
        grad = dh[rows] + total[rows] * (1.0 - squash * squash)
        inverse = jnp.max(inv_ref[rows], axis=1, keepdims=True)
        back = norm_back(grad * gains[0:1], normed, inverse)
        dh[rows] = back
        low[rows] = back.astype(BF16)
        engine.small_own[0:1] += jnp.sum(grad * normed, 0, keepdims=True)
        engine.small_own[2:3] += jnp.sum(back, 0, keepdims=True)
        engine.small_own[3:4] += jnp.sum(grad, 0, keepdims=True)
        return 0

    lax.fori_loop(0, blocks, norm_block, 0)
    tick(6)
    lo_in = load(26, lo_hbm, xh)
    for copy in wo_loads:
        copy.wait()
    cq_load.wait()
    cs_load.wait()
    d_attn = low.at[0:tokens]
    part = dot_tn(cq[...], d_attn[...]).astype(BF16)
    for i in range(2):
        grads[i, 2 * hidden : 2 * hidden + cols] = part[i * cols : (i + 1) * cols]

    def context_block(b, _):
        rows = pl.ds(pl.multiple_of(b * QB, QB), QB)
        nq[rows] = (dot_nt(d_attn[rows], wo[...]) * nq[rows].astype(F32)).astype(BF16)
        return 0

    lax.fori_loop(0, blocks, context_block, 0)
    lo_in.wait()
    lo_out = load(26, xh, lo_full.at[at])
    tick(7)

    for copy in qkv_loads:
        copy.wait()
    lanes = lax.broadcasted_iota(jnp.int32, (QB, 128), 1) < HD

    def attention(own, u):
        row, which = unit_at(own, u)
        probs_load(own, u).wait()

        @pl.when(u + slots - 1 < units)
        def _():
            probs_load(own, u + slots - 1).start()

        lane = pl.ds(pl.multiple_of(which * 128, 128), 128)
        here = pl.ds(pl.multiple_of((u % heads) * 128, 128), 128)
        slot = pl.multiple_of((u % slots) * length, length)
        base = pl.multiple_of(row * length, length)
        d_keys, d_values = [], []
        for b, (first, begin, _) in enumerate(wins):
            wide = lax.broadcasted_iota(jnp.int32, (size, 128), 1) < HD
            rows = pl.ds(base + first, QB)
            queries = weights[rows, lane]
            keys = weights[pl.ds(tokens + base + begin, size), lane]
            values = weights[pl.ds(2 * tokens + base + begin, size), lane]
            context = nq[rows, lane]
            got = []
            for head in range(2):
                own_lanes = lanes if head == 0 else jnp.logical_not(lanes)
                chosen = jnp.where(own_lanes, context.astype(F32), 0.0).astype(BF16)
                probs = factor[pl.ds(slot + first, QB), head * size : (head + 1) * size]
                d_probs = dot_nt(chosen, values)
                exact = probs.astype(F32)
                both = exact * d_probs
                d_low = (both - exact * jnp.sum(both, -1, keepdims=True)).astype(BF16)
                got.append((dot_nn(d_low, keys), dot_tn(d_low, queries), dot_tn(probs, context)))
            dproj[0, rows, here] = (jnp.where(lanes, got[0][0], got[1][0]) * 0.125).astype(BF16)
            d_keys.append(jnp.where(wide, got[0][1], got[1][1]))
            d_values.append(jnp.where(wide, got[0][2], got[1][2]))
        for j, parts, scale in ((1, d_keys, 0.125), (2, d_values, 1.0)):
            for spot in range(0, length, SPAN):
                terms = [
                    part[spot - begin : spot - begin + SPAN]
                    for part, (_, begin, _) in zip(parts, wins)
                    if begin <= spot < begin + size
                ]
                dproj[j, pl.ds(base + spot, SPAN), here] = (sum(terms[1:], terms[0]) * scale).astype(BF16)

    def back_through(own):
        first = 2 * pair if own else 2 - 2 * pair

        def rows(j):
            found = [
                gq[pl.ds(pl.multiple_of(((first + i) * 3 + j) * cols, 16), cols)] for i in range(2)
            ]
            return jnp.concatenate(found, axis=0)

        terms = [dot_nn(dproj[j], rows(j)) for j in range(3)]
        return terms[0] + terms[1] + terms[2]

    def own_unit(u, _):
        attention(True, u)
        engine.tick(u + 8, 0, 9)
        return 0

    lax.fori_loop(0, units, own_unit, 0)
    for u in range(slots - 1):
        probs_load(False, u).start()
    for copy in wt_loads:
        copy.wait()
    xq_load.wait()
    for j in range(3):
        part = dot_tn(dproj[j], low[tokens : 2 * tokens]).astype(BF16)
        base = 2 * hidden + (j + 1) * cols
        for i in range(2):
            grads[i, base : base + cols] = part[i * cols : (i + 1) * cols]
    engine.small_own[8:9, 0:side] = jnp.sum(dproj[0].astype(F32), 0, keepdims=True)
    engine.small_own[9:10, 0:side] = jnp.sum(dproj[2].astype(F32), 0, keepdims=True)
    engine.tick(14, 0, 9)
    engine.tick(9, 9, 12)
    engine.small_step(0)
    total[...] = back_through(True)
    engine.tick(10, 9, 12)
    engine.small_step(1)

    def other_unit(u, _):
        attention(False, u)
        engine.tick(u + 11, 9, 12)
        return 0

    steps = list(range(2, len(engine.peers) + 1))
    lax.fori_loop(0, 2, other_unit, 0)
    engine.small_step(steps.pop(0))
    lax.fori_loop(2, 4, other_unit, 0)
    engine.small_step(steps.pop(0))
    lax.fori_loop(4, units, other_unit, 0)
    for step in steps:
        engine.small_step(step)
    small_out[...] = engine.small_own[...]
    xs_load.wait()
    lo_out.wait()
    other = back_through(False)
    xh[...] = dh[...] + (total[...] + other) * do[...].astype(F32)
    dx_copy = pltpu.make_async_remote_copy(
        src_ref=xh, dst_ref=dx_full.at[at], send_sem=lo_send.at[1], recv_sem=lo_recv.at[1],
        device_id=engine.sib, device_id_type=MESH,
    )
    dx_copy.start()
    dx_out = load(26, xh, dx_full.at[at])
    for n in range(units + 11, 18):
        engine.tick(n, 9, 12)
    lo_copy.wait()
    dx_copy.wait()
    dx_out.wait()


def back(
    nd, do, gq, factor, nq, bank, dh2, xh, inv, sums, lo_half, cs, cq, q, k, v, probs, xq, xs,
    gains, shifts, ranges,
):
    tokens, width = do.shape
    hidden = gq.shape[2]
    cols = width // 4
    rows = 2 * hidden + 4 * cols
    extra = (nd // 8).bit_length() - 1
    dma = pltpu.SemaphoreType.DMA
    names, scratch = sum_scratch(rows // GROUP, width, extra, (16, width))
    length = probs.shape[1]
    buf = lambda *shape: pltpu.VMEM(shape, BF16)
    table = jnp.concatenate([gains, shifts[1:2]], axis=0)
    return pl.pallas_call(
        functools.partial(back_kernel, extra, names),
        out_shape=(
            S((rows, width), BF16),
            S((16, width), F32),
            S((2 * tokens, width), F32),
            S((2 * tokens, width), F32),
        ),
        in_specs=[ANY] * 7 + [VMEM] * 2 + [ANY] * 9 + [VMEM, SMEM],
        out_specs=(VMEM, VMEM, ANY, ANY),
        scratch_shapes=[
            buf(2, rows, width),
            buf(tokens, width),
            buf(max(4 * width, 3 * tokens), width),
            buf(max(3 * width, 2 * tokens), width),
            buf(2 * tokens, width),
            buf(tokens, width),
            buf(2 * tokens, width),
            pltpu.VMEM((tokens, width), F32),
            pltpu.VMEM((tokens, width), F32),
            pltpu.VMEM((tokens, width), F32),
            buf(width, width),
            buf(tokens, width // 2),
            buf(3, tokens, width // 2),
            dma((35,)),
            dma((2,)),
            dma((2,)),
            *scratch,
        ],
        compiler_params=pltpu.CompilerParams(
            collective_id=2, has_side_effects=True, vmem_limit_bytes=62 * MIB
        ),
        name="back",
    )(
        do, gq, factor, nq, bank, dh2, xh, inv, sums, lo_half, cs, cq, q, k, v, probs, xq, xs,
        table, ranges,
    )


def per_device(
    nd, inputs, segment_ids, w_qkv, b_qv, w_out, w_ff1, b_ff1, w_ff2, norm_gains, shift_biases,
    act_ranges, cotangent,
):
    t = lax.axis_index("tensor")
    c = t % 2
    width = inputs.shape[1]
    cols = w_qkv.shape[2]
    hidden = w_ff1.shape[1]
    (
        bank, top, xq, xs, q, k, v, probs, cq, cs, nq, xh, inv, lo_half, gq, factor, dh2, do, sums,
    ) = forward(
        inputs, segment_ids, w_qkv, b_qv, w_out, w_ff1, b_ff1, w_ff2, norm_gains, shift_biases,
        act_ranges, cotangent,
    )
    weight_max = top[0, ::128]
    grads, smalls, layer_out, input_grad = back(
        nd, do, gq, factor, nq, bank, dh2, xh, inv, sums, lo_half, cs, cq, q, k, v, probs, xq, xs,
        norm_gains, shift_biases, act_ranges,
    )
    grads = grads.astype(F32)
    grad_ff2 = grads[:hidden]
    grad_ff1 = grads[hidden : 2 * hidden]
    grad_out = grads[2 * hidden : 2 * hidden + cols]
    grad_qkv = grads[2 * hidden + cols :].reshape(3, cols, width).transpose(0, 2, 1)
    share = lax.dynamic_slice_in_dim(smalls[:6], t * cols, cols, 1)
    grad_gains, grad_shifts = share[:2], share[2:6]
    grad_bff1 = lax.dynamic_slice_in_dim(smalls, 6 + c, 1, 0)[0]
    grad_bqv = lax.dynamic_slice_in_dim(smalls[8:10], c * cols, cols, 1)
    return (
        layer_out, input_grad, grad_qkv, grad_bqv, grad_out, grad_ff1, grad_bff1, grad_ff2,
        grad_gains, grad_shifts, weight_max,
    )


def solution(mesh):
    return jax.shard_map(
        functools.partial(per_device, mesh.shape["dp"]),
        mesh=mesh,
        in_specs=(
            P("dp", None),
            P("dp", None),
            P(None, None, "tensor"),
            P(None, "tensor"),
            P("tensor", None),
            P(None, "tensor"),
            P("tensor"),
            P("tensor", None),
            P(),
            P(),
            P(),
            P("dp", None),
        ),
        out_specs=(
            P("dp", None),
            P("dp", None),
            P(None, None, "tensor"),
            P(None, "tensor"),
            P("tensor", None),
            P(None, "tensor"),
            P("tensor"),
            P("tensor", None),
            P(None, "tensor"),
            P(None, "tensor"),
            P(),
        ),
        check_vma=False,
    )
```

```python
import functools
import math

import jax
import jax.numpy as jnp
from jax import lax
from jax.experimental import pallas as pl
from jax.experimental.pallas import tpu as pltpu
from jax.sharding import PartitionSpec as P

HD = 64
SPAN = 128
QB = 256
MASKED = -1e30
EPSILON = 1e-06
ROOT_HALF = 0.7071067811865476
INV_ROOT_TWO_PI = 0.3989422804014327
STAIR = (
    6.579734980213376,
    -12.987641368031495,
    12.20087719668052,
    -6.61489684889321,
    2.04264519055443,
)
MIB = 1 << 20
MESH = pl.DeviceIdType.MESH
F32 = jnp.float32
BF16 = jnp.bfloat16
ANY = pl.BlockSpec(memory_space=pl.ANY)
VMEM = pl.BlockSpec(memory_space=pltpu.VMEM)
SMEM = pl.BlockSpec(memory_space=pltpu.SMEM)
S = jax.ShapeDtypeStruct


def flip(value, bit):
    return value + bit - 2 * bit * ((value // bit) % 2)


def dot_nn(left, right):
    return lax.dot_general(left, right, (((1,), (0,)), ((), ())), preferred_element_type=F32)


def dot_nt(left, right):
    return lax.dot_general(left, right, (((1,), (1,)), ((), ())), preferred_element_type=F32)


def dot_tn(left, right):
    return lax.dot_general(left, right, (((0,), (0,)), ((), ())), preferred_element_type=F32)


def stairs(levels):
    whole = jnp.round(levels)
    rest = levels - whole
    square = rest * rest
    curve = STAIR[4]
    for factor in STAIR[3::-1]:
        curve = curve * square + factor
    return whole + rest * square * curve


def quantize(values, bound):
    squash = jnp.tanh(values * (1.0 / bound))
    return stairs(127.0 * squash) * (bound / 127.0), squash


def norm(hidden):
    centred = hidden - jnp.mean(hidden, -1, keepdims=True)
    inverse = lax.rsqrt(jnp.mean(centred * centred, -1, keepdims=True) + EPSILON)
    return centred * inverse, inverse


def norm_back(scaled, normed, inverse):
    return inverse * (
        scaled
        - jnp.mean(scaled, -1, keepdims=True)
        - normed * jnp.mean(scaled * normed, -1, keepdims=True)
    )


def windows(length):
    found = []
    for first in range(0, length, QB):
        low = max(0, first - SPAN)
        found.append((first, low, min(length, first + QB + SPAN) - low))
    return found


DIRECT = 4


def forward_kernel(
    wqkv, wout, wff1, wff2, bqv, bff1, x_hbm, cot_hbm, seg_ref, gains, shifts, ranges,
    bank_out, top_out, xq_out, xs_out, q_out, k_out, v_out, p_out, cq_out, cs_out, nq_out, xh_out,
    inv_out, lo_out, gq_out, factor_out, dh2_out, do_out, sums_out,
    bank, flat, x, xq, xs, qkv, probs, cq, cs, total, bias, xh, nq, inv, small,
    sem, out_sem, p_sem, end_sem, lo_s, lo_r, small_s, small_r, sib_s, sib_r, far_s, far_r,
    direct_s, direct_r, side_s, side_r, inner_s, inner_r, last_s, last_r, pass_s, pass_r,
):
    t, d = lax.axis_index("tensor"), lax.axis_index("dp")
    c, pair, corner = t % 2, t // 2, d % 4
    sib, far, side, inner = (d, flip(t, 1)), (d, flip(t, 2)), (flip(d, 1), t), (flip(d, 2), t)
    diagonal = (d, flip(flip(t, 1), 2))
    cols, width = wout.shape
    hidden = wff1.shape[1]
    tokens = x.shape[0]
    length = seg_ref.shape[1]
    rows_here = tokens // length
    lanes_half = width // 2
    wins = windows(length)
    size = wins[0][2]
    blocks = tokens // QB
    heads = width // 256
    units = rows_here * heads
    piece = cols
    pieces = bank.shape[1] // piece
    quarter = piece // 4

    def load(i, src, dst):
        copy = pltpu.make_async_copy(src, dst, sem.at[i])
        copy.start()
        return copy

    mine = pl.ds(pl.multiple_of(c * tokens, QB), tokens)
    loads = [load(j, wqkv.at[j], flat.at[j * cols : (j + 1) * cols]) for j in range(3)]
    loads.append(load(3, wout, flat.at[3 * cols : 4 * cols]))
    loads.append(load(4, wff1, flat.at[4 * cols : 4 * cols + width]))
    loads.append(load(5, wff2, flat.at[4 * cols + width : 4 * cols + width + hidden]))
    spans = [(j * cols, cols) for j in range(4)]
    spans += [(4 * cols, width), (4 * cols + width, hidden)]

    barrier = pltpu.get_barrier_semaphore()
    for peer in (sib, far, diagonal, side, inner):
        pl.semaphore_signal(barrier, inc=1, device_id=peer, device_id_type=MESH)
    small[pl.ds(t, 1)] = jnp.zeros((1, 8, width), F32)
    small[pl.ds(t, 1), 0:1, 0:hidden] = bff1[...].reshape(1, 1, hidden)
    small[pl.ds(t, 1), 1:3, 0:cols] = bqv[...][None]
    for j, (begin, count) in enumerate(spans):
        loads[j].wait()
        top = jnp.max(jnp.abs(flat[begin : begin + count]), axis=(0, 1), keepdims=True)
        small[pl.ds(t, 1), 3:4, 128 * j : 128 * (j + 1)] = jnp.broadcast_to(top, (1, 128))[None]
    x_load = load(6, x_hbm.at[mine], x)
    pl.semaphore_wait(barrier, 5)
    sends = []
    for i, peer in enumerate((sib, far, diagonal)):
        copy = pltpu.make_async_remote_copy(
            src_ref=small.at[t], dst_ref=small.at[t], send_sem=small_s.at[i],
            recv_sem=small_r.at[i], device_id=peer, device_id_type=MESH,
        )
        copy.start()
        sends.append(copy)

    x_load.wait()

    def input_block(b, _):
        rows = pl.ds(pl.multiple_of(b * QB, QB), QB)
        coded, squash = quantize(x[rows], ranges[0])
        xq[rows] = coded.astype(BF16)
        xs[rows] = (1.0 - squash * squash).astype(BF16)
        return 0

    lax.fori_loop(0, blocks, input_block, 0)
    outs = []

    def put(src, dst):
        copy = pltpu.make_async_copy(src, dst, out_sem.at[len(outs)])
        copy.start()
        outs.append(copy)
        return copy

    for copy in sends:
        copy.wait()
    top_row = jnp.max(small[:, 3:4, :], axis=0)
    for j in range(len(spans)):
        top_out[j] = jnp.max(top_row[:, 128 * j : 128 * (j + 1)])

    other = flip(t, 2)
    next_side, next_inner, across = flip(corner, 1), flip(corner, 2), flip(flip(corner, 1), 2)

    def moved(p, shard, which, sems, at, to):
        rows = pl.ds(pl.multiple_of(p * piece + which * quarter, 16), quarter)
        there = bank.at[shard, rows]
        return pltpu.make_async_remote_copy(
            src_ref=there, dst_ref=there, send_sem=sems[0].at[at], recv_sem=sems[1].at[at],
            device_id=to, device_id_type=MESH,
        )

    def sib_copy(p):
        there = bank.at[t, pl.ds(pl.multiple_of(p * piece, 16), piece)]
        return pltpu.make_async_remote_copy(
            src_ref=there, dst_ref=there, send_sem=sib_s.at[p], recv_sem=sib_r.at[p],
            device_id=sib, device_id_type=MESH,
        )

    far_copy = lambda p: moved(p, t, corner, (far_s, far_r), p, far)
    direct_copy = lambda p: moved(p, t, across, (direct_s, direct_r), p, far)
    side_copy = lambda p: moved(p, other, corner, (side_s, side_r), p, side)
    inner_copy = lambda p: moved(p, other, corner, (inner_s, inner_r), p, inner)

    def last_copy(p):
        if p % 2 == 0:
            return moved(p, other, next_inner, (last_s, last_r), p, side)
        return moved(p, other, next_side, (last_s, last_r), p, inner)

    def pass_copy(k, p):
        which = (corner, next_side, next_inner, across)[k]
        return moved(p, other, which, (pass_s, pass_r), (k, p), sib)

    for j, (begin, count) in enumerate(spans):
        top = top_row[:, 128 * j : 128 * j + 1]
        up, down = 127.0 / top, top / 127.0

        def code(p, _, up=up, down=down):
            at = pl.ds(pl.multiple_of(p * piece, 16), piece)
            bank[t, at] = (stairs(flat[at] * up) * down).astype(BF16)
            far_copy(p).start()
            sib_copy(p).start()
            return 0

        lax.fori_loop(begin // piece, (begin + count) // piece, code, 0)
        if j in (2, 3):
            for p in range(3) if j == 2 else (3,):
                direct_copy(p).start()
    xq_put = put(xq, xq_out)
    put(xs, xs_out)

    def far_step(*found):
        for p in found:
            far_copy(p).wait_recv()
            side_copy(p).start()
            inner_copy(p).start()
            pass_copy(0, p).start()

    def side_step(*found):
        for p in found:
            side_copy(p).wait_recv()
            if p >= DIRECT and p % 2 == 1:
                last_copy(p).start()
            pass_copy(1, p).start()
            inner_copy(p).wait_recv()
            if p >= DIRECT and p % 2 == 0:
                last_copy(p).start()
            pass_copy(2, p).start()

    def last_step(*found):
        for p in found:
            (direct_copy(p) if p < DIRECT else last_copy(p)).wait_recv()
            pass_copy(3, p).start()

    def arrived(own, p):
        if own:
            sib_copy(p).wait_recv()
        else:
            for k in range(4):
                pass_copy(k, p).wait_recv()

    def shard_rows(own, begin, count):
        first = 2 * pair if own else 2 - 2 * pair
        return jnp.concatenate(
            [bank[first, begin : begin + count], bank[first + 1, begin : begin + count]], axis=0
        )

    def half_lanes(own):
        return pl.ds(pl.multiple_of((pair if own else 1 - pair) * lanes_half, 128), lanes_half)

    for r in range(rows_here):
        seg = seg_ref[pl.ds(c * rows_here + r, 1)].astype(F32)
        seg_col = jnp.transpose(jnp.broadcast_to(seg, (128, length)))
        for b, (first, low, _) in enumerate(wins):
            for lane in range(0, size, 128):
                same = seg_col[first : first + QB] == seg[:, low + lane : low + lane + 128]
                bias[r, b, :, lane : lane + 128] = jnp.where(same, 0.0, MASKED)
    lanes = lax.broadcasted_iota(jnp.int32, (QB, 128), 1) < HD

    def project(own):
        first = 2 * pair if own else 2 - 2 * pair
        at = half_lanes(own)
        for j in range(3):
            value = dot_nt(xq[...], shard_rows(own, j * cols, cols))
            if j != 1:
                row = 1 if j == 0 else 2
                value += jnp.concatenate(
                    [small[first + i, row : row + 1, 0:cols] for i in range(2)], axis=1
                )
            qkv[j * tokens : (j + 1) * tokens, at] = value.astype(BF16)

    def attention(own, row):
        half = pair if own else 1 - pair
        base = pl.multiple_of(row * length, length)
        spot = pl.multiple_of(row * heads * length, length)
        jobs = [(k, b, head) for k in range(heads) for b in range(len(wins)) for head in range(2)]

        def lane(k):
            return pl.ds(pl.multiple_of((half * heads + k) * 128, 128), 128)

        def score(k, b, head):
            first, low, _ = wins[b]
            queries = qkv[pl.ds(base + first, QB), lane(k)].astype(F32) * 0.125
            inside = lanes if head == 0 else jnp.logical_not(lanes)
            chosen = jnp.where(inside, queries, 0.0).astype(BF16)
            return dot_nt(chosen, qkv[pl.ds(tokens + base + low, size), lane(k)]) + bias[row, b]

        def weigh(k, b, head, scores):
            weights = jnp.exp(scores - jnp.max(scores, -1, keepdims=True))
            share = 1.0 / jnp.sum(weights, -1, keepdims=True)
            low_probs = (weights * share).astype(BF16)
            rows = pl.ds(spot + k * length + wins[b][0], QB)
            probs[rows, head * size : (head + 1) * size] = low_probs
            return low_probs

        scores = [score(*job) for job in jobs]
        weights = [weigh(*job, value) for job, value in zip(jobs, scores)]
        results = []
        for (k, b, _), value in zip(jobs, weights):
            rows = pl.ds(2 * tokens + base + wins[b][1], size)
            results.append(dot_nn(value, qkv[rows, lane(k)]))
        for n in range(0, len(jobs), 2):
            k, b, _ = jobs[n]
            rows = pl.ds(base + wins[b][0], QB)
            coded, squash = quantize(jnp.where(lanes, results[n], results[n + 1]), ranges[1])
            cq[rows, lane(k)] = coded.astype(BF16)
            cs[rows, lane(k)] = (1.0 - squash * squash).astype(BF16)
        p_copy(own, row).start()

    def p_copy(own, row):
        spot = pl.multiple_of(row * heads * length, length)
        return pltpu.make_async_copy(
            probs.at[pl.ds(spot, heads * length)],
            p_out.at[row * 2 + (pair if own else 1 - pair)],
            p_sem.at[row],
        )

    for p in range(3):
        arrived(True, p)
    project(True)
    far_step(0)

    def own_row(row, _):
        attention(True, row)
        pl.when(row == 0)(lambda: far_step(1, 2))
        pl.when(row == 1)(lambda: side_step(0))
        return 0

    lax.fori_loop(0, rows_here, own_row, 0)
    arrived(True, 3)
    total[...] = dot_nn(cq[:, half_lanes(True)], shard_rows(True, 3 * cols, cols))
    side_step(1, 2)
    last_step(0, 1, 2)

    for p in range(3):
        arrived(False, p)
    project(False)
    far_step(3, 4)

    def other_row(row, _):
        p_copy(True, row).wait()
        attention(False, row)
        pl.when(row == 0)(lambda: [far_step(5), side_step(3), last_step(3)] and None)
        pl.when(row == 1)(lambda: [far_step(6, 7), side_step(4)] and None)
        return 0

    lax.fori_loop(0, rows_here, other_row, 0)
    qkv_puts = [
        put(qkv.at[j * tokens : (j + 1) * tokens], ref) for j, ref in enumerate((q_out, k_out, v_out))
    ]
    put(cq, cq_out)
    put(cs, cs_out)
    arrived(False, 3)

    def norm_block(b, _):
        rows = pl.ds(pl.multiple_of(b * QB, QB), QB)
        attn = total[rows] + dot_nn(cq[rows, half_lanes(False)], shard_rows(False, 3 * cols, cols))
        normed, inverse = norm(x[rows] + (attn + shifts[0:1]))
        xh[rows] = normed
        inv[rows] = jnp.broadcast_to(inverse, (QB, 128))
        nq[rows] = quantize(normed * gains[0:1] + shifts[1:2], ranges[2])[0].astype(BF16)
        return 0

    lax.fori_loop(0, blocks, norm_block, 0)
    far_step(8)
    side_step(5)
    xh_put = put(xh, xh_out)
    put(inv, inv_out)
    nq_put = put(nq, nq_out)
    cot_load = load(6, cot_hbm.at[mine], x)

    for row in range(rows_here):
        p_copy(False, row).wait()
    for copy in qkv_puts:
        copy.wait()

    def spread(i):
        shard = (2 * pair + i) % 4
        shift = small[shard, 0:1, 0:hidden]
        pres = [
            dot_nn(nq[b * QB : (b + 1) * QB], bank[shard, 4 * cols : 4 * cols + width]) + shift
            for b in range(blocks)
        ]
        codes = []
        at = i % 3 * tokens
        for b, pre in enumerate(pres):
            cdf = 0.5 * (1.0 + lax.erf(pre * ROOT_HALF))
            coded, squash = quantize(pre * cdf, ranges[3])
            slope = cdf + pre * jnp.exp(-0.5 * pre * pre) * INV_ROOT_TWO_PI
            coded = coded.astype(BF16)
            rows = slice(at + b * QB, at + (b + 1) * QB)
            probs[rows] = ((1.0 - squash * squash) * slope).astype(BF16)
            qkv[rows] = coded
            codes.append(coded)
        return codes, put(probs.at[at : at + tokens], factor_out.at[i])

    def gather(i, code):
        shard = (2 * pair + i) % 4
        return dot_nn(code, bank[shard, 4 * cols + width : 4 * cols + width + hidden])

    for p in range(4, pieces):
        arrived(True, p)
    slope_puts, code_puts = [], []
    for i in range(2):
        codes, copy = spread(i)
        slope_puts.append(copy)
        code_puts.append(put(qkv.at[i * tokens : (i + 1) * tokens], gq_out.at[i]))
        for b, code in enumerate(codes):
            rows = slice(b * QB, (b + 1) * QB)
            part = gather(i, code)
            flat[rows] = part if i == 0 else flat[rows] + part
        if i == 0:
            far_step(9, 10, 11)
            side_step(6, 7)
            last_step(4)
        else:
            side_step(8, 9)
            last_step(5, 6, 7)
            side_step(10, 11)
    for p in range(4, 8):
        arrived(False, p)
    spread(2)
    last_step(8, 9)
    slope_puts[0].wait()
    code_puts[0].wait()
    spread(3)
    last_step(10, 11)
    for p in range(8, pieces):
        arrived(False, p)
    for s in range(4):
        put(bank.at[s], bank_out.at[s])
    for b in range(blocks):
        found = [qkv[i % 3 * tokens + b * QB : i % 3 * tokens + (b + 1) * QB] for i in (2, 3)]
        flat[tokens + b * QB : tokens + (b + 1) * QB] = gather(2, found[0]) + gather(3, found[1])

    cot_load.wait()
    xq_put.wait()
    xh_put.wait()
    nq_put.wait()
    sums_out[...] = jnp.zeros_like(sums_out)

    def ends(b):
        rows = pl.ds(pl.multiple_of(b * QB, QB), QB)
        there = pl.ds(pl.multiple_of(c * tokens + b * QB, QB), QB)
        local = [
            pltpu.make_async_copy(src.at[rows], dst, end_sem.at[k, b])
            for k, (src, dst) in enumerate(
                ((xq, lo_out.at[there]), (total, dh2_out.at[rows]), (nq, do_out.at[rows]))
            )
        ]
        remote = pltpu.make_async_remote_copy(
            src_ref=xq.at[rows], dst_ref=lo_out.at[there], send_sem=lo_s.at[b], recv_sem=lo_r.at[b],
            device_id=sib, device_id_type=MESH,
        )
        return local + [remote]

    def last_block(b, _):
        rows = pl.ds(pl.multiple_of(b * QB, QB), QB)
        first = xh[rows] * gains[0:1] + shifts[1:2]
        feed = flat[rows] + flat[pl.ds(pl.multiple_of(tokens + b * QB, QB), QB)]
        normed, inverse = norm(first + (feed + shifts[2:3]))
        xq[rows] = (normed * gains[1:2] + shifts[3:4]).astype(BF16)
        grad = x[rows]
        back = norm_back(grad * gains[1:2], normed, inverse)
        total[rows] = back
        nq[rows] = back.astype(BF16)
        for copy in ends(b):
            copy.start()
        sums_out[1:2] += jnp.sum(grad * normed, 0, keepdims=True)
        sums_out[4:5] += jnp.sum(back, 0, keepdims=True)
        sums_out[5:6] += jnp.sum(grad, 0, keepdims=True)
        return 0

    lax.fori_loop(0, blocks, last_block, 0)

    def sent(p, _):
        far_copy(p).wait_send()
        sib_copy(p).wait_send()
        side_copy(p).wait_send()
        inner_copy(p).wait_send()
        for k in range(4):
            pass_copy(k, p).wait_send()
        return 0

    lax.fori_loop(0, pieces, sent, 0)
    for p in range(pieces):
        (direct_copy(p) if p < DIRECT else last_copy(p)).wait_send()
    waited = [xq_put, xh_put, nq_put] + qkv_puts + [slope_puts[0], code_puts[0]]
    for copy in outs:
        if not any(copy is other_copy for other_copy in waited):
            copy.wait()
    for b in range(blocks):
        for copy in ends(b):
            copy.wait()


def forward(inputs, segment_ids, w_qkv, b_qv, w_out, w_ff1, b_ff1, w_ff2, gains, shifts, ranges, cotangent):
    cols, width = w_out.shape
    hidden = w_ff1.shape[1]
    rows, length = segment_ids.shape
    tokens = inputs.shape[0] // 2
    size = windows(length)[0][2]
    bank_rows = 4 * cols + width + hidden
    pieces = bank_rows // cols
    dma = pltpu.SemaphoreType.DMA
    low = lambda *shape: pltpu.VMEM(shape, BF16)
    full = lambda *shape: pltpu.VMEM(shape, F32)
    wide = S((tokens, width), BF16)
    deep = S((tokens, width), F32)
    return pl.pallas_call(
        forward_kernel,
        out_shape=(
            S((4, bank_rows, width), BF16),
            S((6,), F32),
            wide, wide, wide, wide, wide,
            S((rows, width // 256 * length, 2 * size), BF16),
            wide, wide, wide, deep,
            S((tokens, 128), F32),
            S((2 * tokens, width), BF16),
            S((2, tokens, hidden), BF16),
            S((4, tokens, hidden), BF16),
            deep, wide,
            S((8, width), F32),
        ),
        in_specs=[ANY] * 4 + [VMEM] * 2 + [ANY] * 2 + [VMEM] * 3 + [SMEM],
        out_specs=(ANY, SMEM) + (ANY,) * 16 + (VMEM,),
        scratch_shapes=[
            low(4, bank_rows, width),
            full(max(bank_rows, 2 * tokens), width),
            full(tokens, width),
            low(tokens, width),
            low(tokens, width),
            low(3 * tokens, width),
            low(max(rows // 2 * (width // 256) * length, 3 * tokens), 2 * size),
            low(tokens, width),
            low(tokens, width),
            full(tokens, width),
            full(tokens // length, length // QB, QB, size),
            full(tokens, width),
            low(tokens, width),
            full(tokens, 128),
            full(4, 8, width),
            dma((7,)), dma((24,)), dma((rows // 2,)), dma((3, tokens // QB)),
            dma((tokens // QB,)), dma((tokens // QB,)), dma((3,)), dma((3,)),
            *[dma((pieces,))] * 12,
            dma((4, pieces)), dma((4, pieces)),
        ],
        compiler_params=pltpu.CompilerParams(
            collective_id=1, has_side_effects=True, vmem_limit_bytes=62 * MIB
        ),
        name="forward",
    )(
        jnp.swapaxes(w_qkv, 1, 2), w_out, w_ff1, w_ff2, b_qv, b_ff1, inputs, cotangent,
        segment_ids, gains, shifts, ranges,
    )


GROUP = 192
QUARTER = GROUP // 4
HOPS = ("core", "y", "z1", "z2", "z3", "ag")
LINE_HOPS = ("zs1", "zs2", "zy", "zb1", "zb2", "zb3")


def sum_scratch(groups, width, extra, small_shape):
    count = max(extra, 1)
    dma = pltpu.SemaphoreType.DMA
    buf = lambda *shape: pltpu.VMEM(shape + (width,), BF16)
    kinds = dict(
        own=buf(groups * GROUP), got_y=buf(groups, QUARTER), part=buf(groups, QUARTER),
        got_1=buf(groups, QUARTER), got_2=buf(groups, QUARTER), got_x=buf(count, 2, QUARTER),
        line_1=buf(groups, 2, QUARTER), line_2=buf(groups, 2, QUARTER), line_y=buf(groups, 2, QUARTER),
        line_x=buf(count, 2, 2, QUARTER),
        small_own=pltpu.VMEM(small_shape, F32), small_got=pltpu.VMEM((4 + extra,) + small_shape, F32),
        x_s=dma((count, groups)), x_r=dma((count, groups)),
        lx_s=dma((count, groups, 2)), lx_r=dma((count, groups, 2)),
        small_s=dma((4 + extra,)), small_r=dma((4 + extra,)),
    )
    for hop in HOPS:
        kinds[hop + "_s"], kinds[hop + "_r"] = dma((groups,)), dma((groups,))
    for hop in LINE_HOPS:
        kinds[hop + "_s"], kinds[hop + "_r"] = dma((groups, 2)), dma((groups, 2))
    return list(kinds), list(kinds.values())


class GradientSum:
    STAGES = 7

    def __init__(self, extra, mine, theirs, result, refs):
        self.__dict__.update(refs)
        self.extra, self.mine, self.theirs, self.result = extra, mine, theirs, result
        t, d = lax.axis_index("tensor"), lax.axis_index("dp")
        self.y = d % 2
        self.z = (d // 2) % 4
        self.end = jnp.logical_or(self.z == 0, self.z == 3)
        self.middle = jnp.logical_not(self.end)
        self.sib = (d, flip(t, 1))
        self.side = (flip(d, 1), t)
        self.inner = (flip(d, 2), t)
        self.across = (d + 2 * (3 - 2 * self.z), t)
        self.others = [(flip(d, 8 << b), t) for b in range(extra)]
        self.peers = [self.sib, self.side, self.inner, self.across] + self.others
        self.groups = self.own.shape[0] // GROUP

    def enter(self):
        barrier = pltpu.get_barrier_semaphore()
        for peer in self.peers:
            pl.semaphore_signal(barrier, inc=1, device_id=peer, device_id_type=MESH)
        pl.semaphore_wait(barrier, len(self.peers))

    def remote(self, src, dst, hop, at, to):
        return pltpu.make_async_remote_copy(
            src_ref=src, dst_ref=dst, send_sem=getattr(self, hop + "_s").at[at],
            recv_sem=getattr(self, hop + "_r").at[at], device_id=to, device_id_type=MESH,
        )

    def small(self, i):
        copy = self.remote(self.small_own, self.small_got.at[i], "small", i, self.peers[i])
        return copy

    def small_step(self, i):
        if i > 0:
            self.small(i - 1).wait()
            self.small_own[...] = self.small_own[...] + self.small_got[i - 1]
        if i < len(self.peers):
            self.small(i).start()

    def span(self, g):
        return pl.ds(pl.multiple_of(g * GROUP, 16), GROUP)

    def half(self, g, which):
        return pl.ds(pl.multiple_of(g * GROUP + which * QUARTER, 16), QUARTER)

    def line(self, g, i):
        return pl.ds(pl.multiple_of(g * GROUP + (2 + i) * QUARTER, 16), QUARTER)

    def core(self, g):
        return self.remote(self.theirs.at[self.span(g)], self.own.at[self.span(g)], "core", g, self.sib)

    def hop(self, name, g):
        if name == "y":
            return self.remote(self.own.at[self.half(g, 1 - self.y)], self.got_y.at[g], "y", g, self.side)
        if name == "z1":
            return self.remote(self.part.at[g], self.got_1.at[g], "z1", g, self.inner)
        if name == "z2":
            return self.remote(self.part.at[g], self.got_2.at[g], "z2", g, self.across)
        there = self.result.at[self.half(g, self.y)]
        return self.remote(there, there, name, g, self.inner if name == "z3" else self.side)

    def line_hop(self, name, g, i):
        mine = self.own.at[self.line(g, i)]
        if name == "zs1":
            return self.remote(mine, self.line_1.at[g, i], name, (g, i), self.inner)
        if name == "zs2":
            return self.remote(mine, self.line_2.at[g, i], name, (g, i), self.across)
        if name == "zy":
            return self.remote(mine, self.line_y.at[g, i], name, (g, i), self.side)
        there = self.result.at[self.line(g, i)]
        return self.remote(there, there, name, (g, i), self.across if name == "zb2" else self.inner)

    def stage(self, s, g):
        add = lambda a, b: (a.astype(F32) + b.astype(F32)).astype(BF16)
        when = lambda condition, body: pl.when(condition)(body)
        root = [self.z == 1, self.z == 2]
        passer = [self.z == 2, self.z == 1]
        near = [self.z == 0, self.z == 3]
        far = [self.z == 3, self.z == 0]
        if s == 0:
            self.core(g).start()
        if s == 1:
            self.core(g).wait()
            self.own[self.span(g)] = add(self.own[self.span(g)], self.mine[self.span(g)])
            self.hop("y", g).start()
            when(self.end, lambda: [self.line_hop("zs1", g, i).start() for i in range(2)] and None)
        if s == 2:
            self.hop("y", g).wait()
            self.part[g] = add(self.own[self.half(g, self.y)], self.got_y[g])
            when(self.end, lambda: self.hop("z1", g).start())
            for i in range(2):

                def gather(i=i):
                    self.line_hop("zs1", g, i).wait_recv()
                    rows = self.line(g, i)
                    self.own[rows] = add(self.own[rows], self.line_1[g, i])
                    when(passer[i], lambda: self.line_hop("zs2", g, i).start())

                when(self.middle, gather)
        if s == 3:

            def middle():
                self.hop("z1", g).wait_recv()
                self.part[g] = add(self.part[g], self.got_1[g])
                self.hop("z2", g).start()

            when(self.middle, middle)
            for i in range(2):

                def at_root(i=i):
                    self.line_hop("zs2", g, i).wait_recv()
                    rows = self.line(g, i)
                    self.own[rows] = add(self.own[rows], self.line_2[g, i])
                    self.line_hop("zy", g, i).start()

                when(root[i], at_root)
        if s == 4:

            def total():
                self.hop("z2", g).wait()
                self.part[g] = add(self.part[g], self.got_2[g])
                for b in range(self.extra):
                    copy = self.remote(self.part.at[g], self.got_x.at[b, g % 2], "x", (b, g), self.others[b])
                    copy.start()
                    copy.wait()
                    self.part[g] = add(self.part[g], self.got_x[b, g % 2])
                self.result[self.half(g, self.y)] = self.part[g]
                self.hop("ag", g).start()
                self.hop("z3", g).start()

            when(self.middle, total)
            for i in range(2):

                def spread(i=i):
                    self.line_hop("zy", g, i).wait()
                    rows = self.line(g, i)
                    self.own[rows] = add(self.own[rows], self.line_y[g, i])
                    for b in range(self.extra):
                        copy = self.remote(
                            self.own.at[rows], self.line_x.at[b, g % 2, i], "lx", (b, g, i), self.others[b]
                        )
                        copy.start()
                        copy.wait()
                        self.own[rows] = add(self.own[rows], self.line_x[b, g % 2, i])
                    self.result[rows] = self.own[rows]
                    self.line_hop("zb2", g, i).start()
                    self.line_hop("zb1", g, i).start()

                when(root[i], spread)
        if s == 5:

            def outer():
                self.hop("z3", g).wait_recv()
                self.hop("ag", g).start()

            when(self.end, outer)
            for i in range(2):

                def onward(i=i):
                    self.line_hop("zb2", g, i).wait_recv()
                    self.line_hop("zb3", g, i).start()

                when(passer[i], onward)
        if s == 6:
            self.hop("ag", g).wait()
            for i in range(2):
                when(near[i], lambda i=i: self.line_hop("zb1", g, i).wait_recv())
                when(far[i], lambda i=i: self.line_hop("zb3", g, i).wait_recv())

                def sent_root(i=i):
                    self.line_hop("zb1", g, i).wait_send()
                    self.line_hop("zb2", g, i).wait_send()

                def sent_passer(i=i):
                    self.line_hop("zs2", g, i).wait_send()
                    self.line_hop("zb3", g, i).wait_send()

                when(root[i], sent_root)
                when(passer[i], sent_passer)

            def sent_end():
                self.hop("z1", g).wait_send()
                for i in range(2):
                    self.line_hop("zs1", g, i).wait_send()

            when(self.end, sent_end)
            when(self.middle, lambda: self.hop("z3", g).wait_send())

    def tick(self, n, first, last):
        for s in reversed(range(self.STAGES)):
            if isinstance(n, int):
                if first <= n - s < last:
                    self.stage(s, n - s)
            else:
                g = n - s
                pl.when(jnp.logical_and(g >= first, g < last))(functools.partial(self.stage, s, g))


def back_kernel(
    extra, names,
    do_hbm, gq_hbm, factor_hbm, nq_hbm, bank, dh2_hbm, xh_hbm, inv_ref, sums_ref,
    cs_hbm, cq_hbm, q_hbm, k_hbm, v_hbm, p_hbm, xq_hbm, xs_hbm, gains, shifts, ranges,
    g2_out, g1_out, go_out, gq_out, gains_out, shifts_out, bqv_out, bff1_out, dx_full,
    result, grads, do, weights, gq, factor, nq, low, total, dh, xh, wo, cq, dproj, sem, dx_send, dx_recv,
    *refs,
):
    t, d = lax.axis_index("tensor"), lax.axis_index("dp")
    c, pair = t % 2, t // 2
    engine = GradientSum(extra, grads.at[c], grads.at[1 - c], result, dict(zip(names, refs)))
    tokens, width = do.shape
    hidden = gq_hbm.shape[2]
    side = width // 2
    cols = side // 2
    heads = width // 128 // 2
    length = p_hbm.shape[1] // heads
    wins = windows(length)
    size = wins[0][2]
    blocks = tokens // QB
    slots = factor.shape[0] // length

    def load(i, src, dst):
        copy = pltpu.make_async_copy(src, dst, sem.at[i])
        copy.start()
        return copy

    def shard_at(i):
        return (2 * pair + i) % 4

    first_loads = [load(0, do_hbm, do)]
    first_loads += [load(1 + i, gq_hbm.at[i], gq.at[i * tokens : (i + 1) * tokens]) for i in range(2)]

    def load_pair(base):
        copies = []
        for i in range(2):
            s = shard_at(base + i)
            at = pl.ds(i * tokens, tokens)
            for j in range(2):
                spot = weights.at[(2 * j + i) * width : (2 * j + i + 1) * width]
                copies.append(load(3 + 2 * j + i, bank.at[s, 4 * cols + j * width : 4 * cols + (j + 1) * width], spot))
            copies.append(load(7 + i, factor_hbm.at[base + i], factor.at[at]))
        return copies

    pair_loads = load_pair(0)
    nq_load = load(9, nq_hbm, nq)
    norm_loads = [load(10, dh2_hbm, dh), load(11, xh_hbm, xh)]
    wo_loads = [
        load(27 + s, bank.at[s, 3 * cols : 4 * cols], wo.at[s * cols : (s + 1) * cols]) for s in range(4)
    ]
    mine = pl.ds(pl.multiple_of(pair * side, 128), side)
    cq_load = load(13, cq_hbm.at[:, mine], cq)
    engine.enter()
    at = pl.ds(pl.multiple_of(c * tokens, 256), tokens)
    engine.small_own[...] = jnp.zeros_like(engine.small_own)
    engine.small_own[0:8] = sums_ref[...]

    def tick(n):
        engine.tick(n, 0, engine.groups)

    for copy in first_loads:
        copy.wait()

    def weights_2(begin, end):
        for i in range(2):
            part = dot_tn(gq[i * tokens : (i + 1) * tokens, begin:end], do[...])
            grads[i, begin:end] = part.astype(BF16)

    weights_2(0, hidden // 2)
    tick(0)
    weights_2(hidden // 2, hidden)
    wt_loads = [
        load(31 + s, bank.at[s, 0 : 3 * cols], gq.at[3 * s * cols : 3 * (s + 1) * cols]) for s in range(4)
    ]
    for copy in pair_loads:
        copy.wait()

    def feed_blocks(own, begin, end):
        found = range(begin, end)
        backs = [
            [
                dot_nt(do[b * QB : (b + 1) * QB], weights[(2 + i) * width : (3 + i) * width])
                for i in range(2)
            ]
            for b in found
        ]
        lows = []
        for b, pairs in zip(found, backs):
            lows.append([])
            for i in range(2):
                spot = slice(i * tokens + b * QB, i * tokens + (b + 1) * QB)
                value = pairs[i] * factor[spot].astype(F32)
                short = value.astype(BF16)
                if own:
                    engine.small_own[6 + i : 7 + i] += jnp.sum(value, 0, keepdims=True)
                    low[spot] = short
                lows[-1].append(short)
        for b, (one, two) in zip(found, lows):
            rows = slice(b * QB, (b + 1) * QB)
            part = dot_nt(one, weights[0:width]) + dot_nt(two, weights[width : 2 * width])
            total[rows] = part if own else total[rows] + part

    feed_blocks(True, 0, blocks // 2)
    tick(1)
    feed_blocks(True, blocks // 2, blocks)
    pair_loads = load_pair(2)
    nq_load.wait()
    grads[0, hidden : 2 * hidden] = dot_tn(nq[...], low[0:tokens]).astype(BF16)
    tick(2)
    grads[1, hidden : 2 * hidden] = dot_tn(nq[...], low[tokens : 2 * tokens]).astype(BF16)
    cs_load = load(9, cs_hbm, nq)
    for copy in pair_loads:
        copy.wait()
    feed_blocks(False, 0, blocks // 2)
    tick(3)
    feed_blocks(False, blocks // 2, blocks)
    qkv_loads = [
        load(18 + j, src, weights.at[j * tokens : (j + 1) * tokens])
        for j, src in enumerate((q_hbm, k_hbm, v_hbm))
    ]
    xs_load = load(21, xs_hbm, do)
    xq_load = load(17, xq_hbm, low.at[tokens : 2 * tokens])

    def unit_at(own, u):
        return u // heads, u % heads

    def probs_load(own, u):
        row, which = unit_at(own, u)
        slot = u % slots
        return pltpu.make_async_copy(
            p_hbm.at[row * 2 + (pair if own else 1 - pair), pl.ds(pl.multiple_of(which * length, length), length)],
            factor.at[pl.ds(pl.multiple_of(slot * length, length), length)],
            sem.at[22 + slot],
        )

    units = 2 * heads
    for u in range(slots - 1):
        probs_load(True, u).start()

    for copy in norm_loads:
        copy.wait()

    def norm_block(b, _):
        rows = pl.ds(pl.multiple_of(b * QB, QB), QB)
        normed = xh[rows]
        squash = jnp.tanh((normed * gains[0:1] + shifts[1:2]) * (1.0 / ranges[2]))
        grad = dh[rows] + total[rows] * (1.0 - squash * squash)
        inverse = jnp.max(inv_ref[rows], axis=1, keepdims=True)
        back = norm_back(grad * gains[0:1], normed, inverse)
        dh[rows] = back
        low[rows] = back.astype(BF16)
        engine.small_own[0:1] += jnp.sum(grad * normed, 0, keepdims=True)
        engine.small_own[2:3] += jnp.sum(back, 0, keepdims=True)
        engine.small_own[3:4] += jnp.sum(grad, 0, keepdims=True)
        return 0

    lax.fori_loop(0, blocks, norm_block, 0)
    tick(4)
    for copy in wo_loads:
        copy.wait()
    cq_load.wait()
    cs_load.wait()
    d_attn = low.at[0:tokens]
    part = dot_tn(cq[...], d_attn[...]).astype(BF16)
    for i in range(2):
        grads[i, 2 * hidden : 2 * hidden + cols] = part[i * cols : (i + 1) * cols]

    def context_block(b, _):
        rows = pl.ds(pl.multiple_of(b * QB, QB), QB)
        nq[rows] = (dot_nt(d_attn[rows], wo[...]) * nq[rows].astype(F32)).astype(BF16)
        return 0

    lax.fori_loop(0, blocks, context_block, 0)

    for copy in qkv_loads:
        copy.wait()
    lanes = lax.broadcasted_iota(jnp.int32, (QB, 128), 1) < HD

    def attention(own, u):
        row, which = unit_at(own, u)
        probs_load(own, u).wait()

        @pl.when(u + slots - 1 < units)
        def _():
            probs_load(own, u + slots - 1).start()

        half = pair if own else 1 - pair
        lane = pl.ds(pl.multiple_of((half * heads + which) * 128, 128), 128)
        here = pl.ds(pl.multiple_of(which * 128, 128), 128)
        slot = pl.multiple_of((u % slots) * length, length)
        base = pl.multiple_of(row * length, length)
        wide = lax.broadcasted_iota(jnp.int32, (size, 128), 1) < HD
        jobs = [(b, head) for b in range(len(wins)) for head in range(2)]

        def shares(b, head):
            return factor[pl.ds(slot + wins[b][0], QB), head * size : (head + 1) * size]

        def first_product(b, head):
            first, begin, _ = wins[b]
            own_lanes = lanes if head == 0 else jnp.logical_not(lanes)
            context = nq[pl.ds(base + first, QB), lane].astype(F32)
            chosen = jnp.where(own_lanes, context, 0.0).astype(BF16)
            return dot_nt(chosen, weights[pl.ds(2 * tokens + base + begin, size), lane])

        def d_score(b, head, d_probs):
            exact = shares(b, head).astype(F32)
            both = exact * d_probs
            return (both - exact * jnp.sum(both, -1, keepdims=True)).astype(BF16)

        def products(b, head, d_low):
            first, begin, _ = wins[b]
            rows = pl.ds(base + first, QB)
            return (
                dot_nn(d_low, weights[pl.ds(tokens + base + begin, size), lane]),
                dot_tn(d_low, weights[rows, lane]),
                dot_tn(shares(b, head), nq[rows, lane]),
            )

        d_probs = [first_product(*job) for job in jobs]
        d_lows = [d_score(*job, value) for job, value in zip(jobs, d_probs)]
        found = [products(*job, value) for job, value in zip(jobs, d_lows)]
        d_keys, d_values = [], []
        for b, (first, _, _) in enumerate(wins):
            got = found[2 * b : 2 * b + 2]
            rows = pl.ds(base + first, QB)
            dproj[0, rows, here] = (jnp.where(lanes, got[0][0], got[1][0]) * 0.125).astype(BF16)
            d_keys.append(jnp.where(wide, got[0][1], got[1][1]))
            d_values.append(jnp.where(wide, got[0][2], got[1][2]))
        for j, parts, scale in ((1, d_keys, 0.125), (2, d_values, 1.0)):
            for spot in range(0, length, SPAN):
                terms = [
                    part[spot - begin : spot - begin + SPAN]
                    for part, (_, begin, _) in zip(parts, wins)
                    if begin <= spot < begin + size
                ]
                dproj[j, pl.ds(base + spot, SPAN), here] = (sum(terms[1:], terms[0]) * scale).astype(BF16)

    def back_through(own):
        first = 2 * pair if own else 2 - 2 * pair

        def rows(j):
            found = [
                gq[pl.ds(pl.multiple_of(((first + i) * 3 + j) * cols, 16), cols)] for i in range(2)
            ]
            return jnp.concatenate(found, axis=0)

        terms = [dot_nn(dproj[j], rows(j)) for j in range(3)]
        return terms[0] + terms[1] + terms[2]

    def own_unit(u, _):
        attention(True, u)

        @pl.when(u % 2 == 0)
        def _():
            engine.tick(u // 2 + 5, 0, 9)

        return 0

    lax.fori_loop(0, units, own_unit, 0)
    for u in range(slots - 1):
        probs_load(False, u).start()
    for copy in wt_loads:
        copy.wait()
    xq_load.wait()
    for j in range(3):
        part = dot_tn(dproj[j], low[tokens : 2 * tokens]).astype(BF16)
        base = 2 * hidden + (j + 1) * cols
        for i in range(2):
            grads[i, base : base + cols] = part[i * cols : (i + 1) * cols]
    engine.small_own[8:9, 0:side] = jnp.sum(dproj[0].astype(F32), 0, keepdims=True)
    engine.small_own[9:10, 0:side] = jnp.sum(dproj[2].astype(F32), 0, keepdims=True)
    groups = engine.groups
    engine.tick(8, 0, groups)
    engine.small_step(0)
    total[...] = back_through(True)
    engine.tick(9, 0, groups)
    engine.small_step(1)

    def other_unit(u, _):
        attention(False, u)

        @pl.when(u % 2 == 0)
        def _():
            engine.tick(u // 2 + 10, 0, groups)

        return 0

    lax.fori_loop(0, units, other_unit, 0)
    engine.small_step(2)
    xs_load.wait()
    other = back_through(False)
    factor[0:tokens] = (dh[...] + (total[...] + other) * do[...].astype(F32)).astype(BF16)
    dx_copy = pltpu.make_async_remote_copy(
        src_ref=factor.at[0:tokens], dst_ref=dx_full.at[at], send_sem=dx_send, recv_sem=dx_recv,
        device_id=engine.sib, device_id_type=MESH,
    )
    dx_copy.start()
    outs = [load(26, factor.at[0:tokens], dx_full.at[at])]
    for n in range(13, groups + engine.STAGES - 1):
        engine.tick(n, 0, groups)
        if n == 13:
            engine.small_step(3)
        if n == 14:
            for step in range(4, len(engine.peers) + 1):
                engine.small_step(step)
            outs.append(load(0, result.at[0:hidden], g2_out))
            outs.append(load(1, result.at[hidden : 2 * hidden], g1_out))
            sums = engine.small_own[...]
            here = sums[:, 0:cols]
            for s in range(1, 4):
                here = jnp.where(t == s, sums[:, s * cols : (s + 1) * cols], here)
            gains_out[...] = here[0:2]
            shifts_out[...] = here[2:6]
            bqv_out[...] = jnp.where(c == 0, sums[8:10, 0:cols], sums[8:10, cols:side])
            bff1_out[...] = jnp.where(c == 0, sums[6:7], sums[7:8]).reshape(hidden)
    outs.append(load(2, result.at[2 * hidden : 2 * hidden + cols], go_out))
    outs.append(load(3, result.at[2 * hidden + cols : 2 * hidden + 4 * cols], gq_out))
    dx_copy.wait()
    for copy in outs:
        copy.wait()


def back(
    nd, do, gq, factor, nq, bank, dh2, xh, inv, sums, cs, cq, q, k, v, probs, xq, xs,
    gains, shifts, ranges,
):
    tokens, width = do.shape
    hidden = gq.shape[2]
    cols = width // 4
    rows = 2 * hidden + 4 * cols
    extra = (nd // 8).bit_length() - 1
    dma = pltpu.SemaphoreType.DMA
    names, scratch = sum_scratch(rows // GROUP, width, extra, (16, width))
    buf = lambda *shape: pltpu.VMEM(shape, BF16)
    return pl.pallas_call(
        functools.partial(back_kernel, extra, names),
        out_shape=(
            S((hidden, width), BF16),
            S((width, hidden), BF16),
            S((cols, width), BF16),
            S((3 * cols, width), BF16),
            S((2, cols), F32),
            S((4, cols), F32),
            S((2, cols), F32),
            S((hidden,), F32),
            S((2 * tokens, width), BF16),
        ),
        in_specs=[ANY] * 7 + [VMEM] * 2 + [ANY] * 8 + [VMEM, VMEM, SMEM],
        out_specs=(ANY,) * 4 + (VMEM,) * 4 + (ANY,),
        scratch_shapes=[
            buf(rows, width),
            buf(2, rows, width),
            buf(tokens, width),
            buf(max(4 * width, 3 * tokens), width),
            buf(max(3 * width, 2 * tokens), width),
            buf(2 * tokens, width),
            buf(tokens, width),
            buf(2 * tokens, width),
            pltpu.VMEM((tokens, width), F32),
            pltpu.VMEM((tokens, width), F32),
            pltpu.VMEM((tokens, width), F32),
            buf(width, width),
            buf(tokens, width // 2),
            buf(3, tokens, width // 2),
            dma((35,)),
            dma,
            dma,
            *scratch,
        ],
        compiler_params=pltpu.CompilerParams(
            collective_id=2, has_side_effects=True, vmem_limit_bytes=62 * MIB
        ),
        name="back",
    )(
        do, gq, factor, nq, bank, dh2, xh, inv, sums, cs, cq, q, k, v, probs, xq, xs,
        gains, shifts, ranges,
    )


def per_device(
    nd, inputs, segment_ids, w_qkv, b_qv, w_out, w_ff1, b_ff1, w_ff2, norm_gains, shift_biases,
    act_ranges, cotangent,
):
    width = inputs.shape[1]
    cols = w_qkv.shape[2]
    (
        bank, weight_max, xq, xs, q, k, v, probs, cq, cs, nq, xh, inv, layer_out, gq, factor, dh2, do,
        sums,
    ) = forward(
        inputs, segment_ids, w_qkv, b_qv, w_out, w_ff1, b_ff1, w_ff2, norm_gains, shift_biases,
        act_ranges, cotangent,
    )
    (
        grad_ff2, grad_ff1, grad_out, grad_qkv, grad_gains, grad_shifts, grad_bqv, grad_bff1, input_grad,
    ) = back(
        nd, do, gq, factor, nq, bank, dh2, xh, inv, sums, cs, cq, q, k, v, probs, xq, xs,
        norm_gains, shift_biases, act_ranges,
    )
    grad_qkv = grad_qkv.reshape(3, cols, width).transpose(0, 2, 1)
    return (
        layer_out.astype(F32), input_grad.astype(F32), grad_qkv.astype(F32), grad_bqv,
        grad_out.astype(F32), grad_ff1.astype(F32), grad_bff1, grad_ff2.astype(F32),
        grad_gains, grad_shifts, weight_max,
    )


def solution(mesh):
    return jax.shard_map(
        functools.partial(per_device, mesh.shape["dp"]),
        mesh=mesh,
        in_specs=(
            P("dp", None),
            P("dp", None),
            P(None, None, "tensor"),
            P(None, "tensor"),
            P("tensor", None),
            P(None, "tensor"),
            P("tensor"),
            P("tensor", None),
            P(),
            P(),
            P(),
            P("dp", None),
        ),
        out_specs=(
            P("dp", None),
            P("dp", None),
            P(None, None, "tensor"),
            P(None, "tensor"),
            P("tensor", None),
            P(None, "tensor"),
            P("tensor"),
            P("tensor", None),
            P(None, "tensor"),
            P(None, "tensor"),
            P(),
        ),
        check_vma=False,
    )
```

```python
import functools
import math

import jax
import jax.numpy as jnp
from jax import lax
from jax.experimental import pallas as pl
from jax.experimental.pallas import tpu as pltpu
from jax.sharding import PartitionSpec as P

HD = 64
SPAN = 128
QB = 256
MASKED = -1e30
EPSILON = 1e-06
ROOT_HALF = 0.7071067811865476
INV_ROOT_TWO_PI = 0.3989422804014327
STAIR = (
    6.579734980213376,
    -12.987641368031495,
    12.20087719668052,
    -6.61489684889321,
    2.04264519055443,
)
MIB = 1 << 20
MESH = pl.DeviceIdType.MESH
F32 = jnp.float32
BF16 = jnp.bfloat16
ANY = pl.BlockSpec(memory_space=pl.ANY)
VMEM = pl.BlockSpec(memory_space=pltpu.VMEM)
SMEM = pl.BlockSpec(memory_space=pltpu.SMEM)
S = jax.ShapeDtypeStruct


def flip(value, bit):
    return value + bit - 2 * bit * ((value // bit) % 2)


def dot_nn(left, right):
    return lax.dot_general(left, right, (((1,), (0,)), ((), ())), preferred_element_type=F32)


def dot_nt(left, right):
    return lax.dot_general(left, right, (((1,), (1,)), ((), ())), preferred_element_type=F32)


def dot_tn(left, right):
    return lax.dot_general(left, right, (((0,), (0,)), ((), ())), preferred_element_type=F32)


def stairs(levels):
    whole = jnp.round(levels)
    rest = levels - whole
    square = rest * rest
    curve = STAIR[4]
    for factor in STAIR[3::-1]:
        curve = curve * square + factor
    return whole + rest * square * curve


def quantize(values, bound):
    squash = jnp.tanh(values * (1.0 / bound))
    return stairs(127.0 * squash) * (bound / 127.0), squash


def norm(hidden):
    centred = hidden - jnp.mean(hidden, -1, keepdims=True)
    inverse = lax.rsqrt(jnp.mean(centred * centred, -1, keepdims=True) + EPSILON)
    return centred * inverse, inverse


def norm_back(scaled, normed, inverse):
    return inverse * (
        scaled
        - jnp.mean(scaled, -1, keepdims=True)
        - normed * jnp.mean(scaled * normed, -1, keepdims=True)
    )


def windows(length):
    found = []
    for first in range(0, length, QB):
        low = max(0, first - SPAN)
        found.append((first, low, min(length, first + QB + SPAN) - low))
    return found


DIRECT = (0, 1, 2, 3, 11)


def forward_kernel(
    wqkv, wout, wff1, wff2, bqv, bff1, x_hbm, cot_hbm, seg_ref, gains, shifts, ranges,
    bank_out, top_out, xq_out, xs_out, q_out, k_out, v_out, p_out, cq_out, cs_out, nq_out, xh_out,
    inv_out, lo_out, gq_out, factor_out, dh2_out, do_out, sums_out,
    bank, flat, x, xq, xs, qkv, probs, cq, cs, total, bias, xh, nq, inv, small,
    sem, out_sem, p_sem, end_sem, lo_s, lo_r, small_s, small_r, sib_s, sib_r, far_s, far_r,
    direct_s, direct_r, side_s, side_r, inner_s, inner_r, last_s, last_r, pass_s, pass_r,
):
    t, d = lax.axis_index("tensor"), lax.axis_index("dp")
    c, pair, corner = t % 2, t // 2, d % 4
    sib, far, side, inner = (d, flip(t, 1)), (d, flip(t, 2)), (flip(d, 1), t), (flip(d, 2), t)
    diagonal = (d, flip(flip(t, 1), 2))
    cols, width = wout.shape
    hidden = wff1.shape[1]
    tokens = x.shape[0]
    length = seg_ref.shape[1]
    rows_here = tokens // length
    lanes_half = width // 2
    wins = windows(length)
    size = wins[0][2]
    blocks = tokens // QB
    heads = width // 256
    units = rows_here * heads
    piece = cols
    pieces = bank.shape[1] // piece
    quarter = piece // 4

    def load(i, src, dst):
        copy = pltpu.make_async_copy(src, dst, sem.at[i])
        copy.start()
        return copy

    mine = pl.ds(pl.multiple_of(c * tokens, QB), tokens)
    feed_1, feed_2 = 4 * cols, 4 * cols + width
    loads = [load(j, wqkv.at[j], flat.at[j * cols : (j + 1) * cols]) for j in range(3)]
    loads.append(load(3, wout, flat.at[3 * cols : feed_1]))
    loads.append(load(4, wff1, flat.at[feed_1:feed_2]))
    spans = [(j * cols, cols) for j in range(4)]
    spans += [(4 * cols, width), (4 * cols + width, hidden)]

    barrier = pltpu.get_barrier_semaphore()
    for peer in (sib, far, diagonal, side, inner):
        pl.semaphore_signal(barrier, inc=1, device_id=peer, device_id_type=MESH)
    small[pl.ds(t, 1)] = jnp.zeros((1, 8, width), F32)
    small[pl.ds(t, 1), 0:1, 0:hidden] = bff1[...].reshape(1, 1, hidden)
    small[pl.ds(t, 1), 1:3, 0:cols] = bqv[...][None]
    for j, (begin, count) in enumerate(spans):
        loads[j].wait()
        if j == 3:
            loads.append(load(5, wff2, flat.at[feed_2 : feed_2 + hidden]))
        if j == 4:
            x_load = load(6, x_hbm.at[mine], x)
        top = jnp.max(jnp.abs(flat[begin : begin + count]), axis=(0, 1), keepdims=True)
        small[pl.ds(t, 1), 3:4, 128 * j : 128 * (j + 1)] = jnp.broadcast_to(top, (1, 128))[None]
    pl.semaphore_wait(barrier, 5)
    sends = []
    for i, peer in enumerate((sib, far, diagonal)):
        copy = pltpu.make_async_remote_copy(
            src_ref=small.at[t], dst_ref=small.at[t], send_sem=small_s.at[i],
            recv_sem=small_r.at[i], device_id=peer, device_id_type=MESH,
        )
        copy.start()
        sends.append(copy)

    x_load.wait()

    def input_block(b, _):
        rows = pl.ds(pl.multiple_of(b * QB, QB), QB)
        coded, squash = quantize(x[rows], ranges[0])
        xq[rows] = coded.astype(BF16)
        xs[rows] = (1.0 - squash * squash).astype(BF16)
        return 0

    lax.fori_loop(0, blocks, input_block, 0)
    for r in range(rows_here):
        seg = jnp.broadcast_to(seg_ref[pl.ds(c * rows_here + r, 1)], (16, length))
        hot = (lax.broadcasted_iota(jnp.int32, (16, length), 0) == seg).astype(F32).astype(BF16)
        for b, (first, low, _) in enumerate(wins):
            same = dot_tn(hot[:, first : first + QB], hot[:, low : low + size])
            bias[r, b] = (same - 1.0) * -MASKED
    outs = []

    def put(src, dst):
        copy = pltpu.make_async_copy(src, dst, out_sem.at[len(outs)])
        copy.start()
        outs.append(copy)
        return copy

    for copy in sends:
        copy.wait()
    top_row = jnp.max(small[:, 3:4, :], axis=0)
    for j in range(len(spans)):
        top_out[j] = jnp.max(top_row[:, 128 * j : 128 * (j + 1)])

    other = flip(t, 2)
    next_side, next_inner, across = flip(corner, 1), flip(corner, 2), flip(flip(corner, 1), 2)

    def moved(p, shard, which, sems, at, to):
        rows = pl.ds(pl.multiple_of(p * piece + which * quarter, 16), quarter)
        there = bank.at[shard, rows]
        return pltpu.make_async_remote_copy(
            src_ref=there, dst_ref=there, send_sem=sems[0].at[at], recv_sem=sems[1].at[at],
            device_id=to, device_id_type=MESH,
        )

    def sib_copy(p):
        there = bank.at[t, pl.ds(pl.multiple_of(p * piece, 16), piece)]
        return pltpu.make_async_remote_copy(
            src_ref=there, dst_ref=there, send_sem=sib_s.at[p], recv_sem=sib_r.at[p],
            device_id=sib, device_id_type=MESH,
        )

    far_copy = lambda p: moved(p, t, corner, (far_s, far_r), p, far)
    direct_copy = lambda p: moved(p, t, across, (direct_s, direct_r), p, far)
    side_copy = lambda p: moved(p, other, corner, (side_s, side_r), p, side)
    inner_copy = lambda p: moved(p, other, corner, (inner_s, inner_r), p, inner)

    def last_copy(p):
        if p % 2 == 0:
            return moved(p, other, next_inner, (last_s, last_r), p, side)
        return moved(p, other, next_side, (last_s, last_r), p, inner)

    def pass_copy(k, p):
        which = (corner, next_side, next_inner, across)[k]
        return moved(p, other, which, (pass_s, pass_r), (k, p), sib)

    for j, (begin, count) in enumerate(spans):
        top = jnp.concatenate([top_row[:, 128 * j : 128 * (j + 1)]] * (width // 128), axis=1)
        up, down = 127.0 / top, top / 127.0

        def code(p, _, up=up, down=down):
            at = pl.ds(pl.multiple_of(p * piece, 16), piece)
            bank[t, at] = (stairs(flat[at] * up) * down).astype(BF16)
            far_copy(p).start()
            sib_copy(p).start()
            return 0

        lax.fori_loop(begin // piece, (begin + count) // piece, code, 0)
        if j in (2, 3):
            for p in range(3) if j == 2 else (3,):
                direct_copy(p).start()
        if j == 5:
            direct_copy(pieces - 1).start()
    xq_put = put(xq, xq_out)
    put(xs, xs_out)
    put(bank.at[t], bank_out.at[t])

    def far_step(*found):
        for p in found:
            far_copy(p).wait_recv()
            side_copy(p).start()
            inner_copy(p).start()
            pass_copy(0, p).start()

    def side_step(*found):
        for p in found:
            side_copy(p).wait_recv()
            if p not in DIRECT and p % 2 == 1:
                last_copy(p).start()
            pass_copy(1, p).start()
            inner_copy(p).wait_recv()
            if p not in DIRECT and p % 2 == 0:
                last_copy(p).start()
            pass_copy(2, p).start()

    def last_step(*found):
        for p in found:
            (direct_copy(p) if p in DIRECT else last_copy(p)).wait_recv()
            pass_copy(3, p).start()

    def arrived(own, p):
        if own:
            sib_copy(p).wait_recv()
        else:
            for k in range(4):
                pass_copy(k, p).wait_recv()

    def shard_rows(own, begin, count):
        first = 2 * pair if own else 2 - 2 * pair
        return jnp.concatenate(
            [bank[first, begin : begin + count], bank[first + 1, begin : begin + count]], axis=0
        )

    def half_lanes(own):
        return pl.ds(pl.multiple_of((pair if own else 1 - pair) * lanes_half, 128), lanes_half)

    lanes = lax.broadcasted_iota(jnp.int32, (QB, 128), 1) < HD

    def project(own):
        first = 2 * pair if own else 2 - 2 * pair
        at = half_lanes(own)
        for j in range(3):
            value = dot_nt(xq[...], shard_rows(own, j * cols, cols))
            if j != 1:
                row = 1 if j == 0 else 2
                value += jnp.concatenate(
                    [small[first + i, row : row + 1, 0:cols] for i in range(2)], axis=1
                )
            qkv[j * tokens : (j + 1) * tokens, at] = value.astype(BF16)

    def attention(own, row):
        half = pair if own else 1 - pair
        base = pl.multiple_of(row * length, length)
        spot = pl.multiple_of(row * heads * length, length)
        jobs = [(k, b, head) for k in range(heads) for b in range(len(wins)) for head in range(2)]

        def lane(k):
            return pl.ds(pl.multiple_of((half * heads + k) * 128, 128), 128)

        def score(k, b, head):
            first, low, _ = wins[b]
            queries = qkv[pl.ds(base + first, QB), lane(k)].astype(F32) * 0.125
            inside = lanes if head == 0 else jnp.logical_not(lanes)
            chosen = jnp.where(inside, queries, 0.0).astype(BF16)
            return dot_nt(chosen, qkv[pl.ds(tokens + base + low, size), lane(k)]) + bias[row, b]

        def weigh(k, b, head, scores):
            weights = jnp.exp(scores - jnp.max(scores, -1, keepdims=True))
            share = 1.0 / jnp.sum(weights, -1, keepdims=True)
            low_probs = (weights * share).astype(BF16)
            rows = pl.ds(spot + k * length + wins[b][0], QB)
            probs[rows, head * size : (head + 1) * size] = low_probs
            return low_probs

        scores = [score(*job) for job in jobs]
        weights = [weigh(*job, value) for job, value in zip(jobs, scores)]
        results = []
        for (k, b, _), value in zip(jobs, weights):
            rows = pl.ds(2 * tokens + base + wins[b][1], size)
            results.append(dot_nn(value, qkv[rows, lane(k)]))
        for n in range(0, len(jobs), 2):
            k, b, _ = jobs[n]
            rows = pl.ds(base + wins[b][0], QB)
            coded, squash = quantize(jnp.where(lanes, results[n], results[n + 1]), ranges[1])
            cq[rows, lane(k)] = coded.astype(BF16)
            cs[rows, lane(k)] = (1.0 - squash * squash).astype(BF16)
        p_copy(own, row).start()

    def p_copy(own, row):
        spot = pl.multiple_of(row * heads * length, length)
        return pltpu.make_async_copy(
            probs.at[pl.ds(spot, heads * length)],
            p_out.at[row * 2 + (pair if own else 1 - pair)],
            p_sem.at[row],
        )

    for p in range(3):
        arrived(True, p)
    project(True)
    far_step(0)

    def own_row(row, _):
        attention(True, row)
        pl.when(row == 0)(lambda: far_step(1, 2))
        pl.when(row == 1)(lambda: side_step(0))
        return 0

    lax.fori_loop(0, rows_here, own_row, 0)
    arrived(True, 3)
    total[...] = dot_nn(cq[:, half_lanes(True)], shard_rows(True, 3 * cols, cols))
    side_step(1)
    far_step(3)
    side_step(2)
    last_step(0, 1, 2)

    for p in range(3):
        arrived(False, p)
    project(False)
    far_step(4)
    last_step(3)

    def other_row(row, _):
        p_copy(True, row).wait()
        attention(False, row)
        pl.when(row == 0)(lambda: [far_step(5, 6), side_step(3)] and None)
        pl.when(row == 1)(lambda: [far_step(7), side_step(4)] and None)
        return 0

    lax.fori_loop(0, rows_here, other_row, 0)
    qkv_puts = [
        put(qkv.at[j * tokens : (j + 1) * tokens], ref) for j, ref in enumerate((q_out, k_out, v_out))
    ]
    put(cq, cq_out)
    put(cs, cs_out)
    arrived(False, 3)

    def norm_block(b, _):
        rows = pl.ds(pl.multiple_of(b * QB, QB), QB)
        attn = total[rows] + dot_nn(cq[rows, half_lanes(False)], shard_rows(False, 3 * cols, cols))
        normed, inverse = norm(x[rows] + (attn + shifts[0:1]))
        xh[rows] = normed
        inv[rows] = jnp.broadcast_to(inverse, (QB, 128))
        nq[rows] = quantize(normed * gains[0:1] + shifts[1:2], ranges[2])[0].astype(BF16)
        pl.when(b == 0)(lambda: far_step(8))
        pl.when(b == 1)(lambda: side_step(5))
        pl.when(b == 2)(lambda: side_step(6))
        pl.when(b == 3)(lambda: far_step(9))
        return 0

    lax.fori_loop(0, blocks, norm_block, 0)
    xh_put = put(xh, xh_out)
    put(inv, inv_out)
    nq_put = put(nq, nq_out)
    cot_load = load(6, cot_hbm.at[mine], x)

    for row in range(rows_here):
        p_copy(False, row).wait()
    for copy in qkv_puts:
        copy.wait()

    def spread(i, begin, end):
        shard = (2 * pair + i) % 4
        shift = small[shard, 0:1, 0:hidden]
        found = range(begin, end)
        pres = [dot_nn(nq[b * QB : (b + 1) * QB], bank[shard, feed_1:feed_2]) + shift for b in found]
        codes = []
        at = i % 3 * tokens
        for b, pre in zip(found, pres):
            cdf = 0.5 * (1.0 + lax.erf(pre * ROOT_HALF))
            coded, squash = quantize(pre * cdf, ranges[3])
            slope = cdf + pre * jnp.exp(-0.5 * pre * pre) * INV_ROOT_TWO_PI
            coded = coded.astype(BF16)
            rows = slice(at + b * QB, at + (b + 1) * QB)
            probs[rows] = ((1.0 - squash * squash) * slope).astype(BF16)
            qkv[rows] = coded
            codes.append(coded)
        return codes

    def put_slopes(i):
        at = i % 3 * tokens
        return put(probs.at[at : at + tokens], factor_out.at[i])

    def gather(i, code):
        shard = (2 * pair + i) % 4
        return dot_nn(code, bank[shard, feed_2 : feed_2 + hidden])

    for p in range(4, pieces):
        arrived(True, p)
    put(bank.at[flip(t, 1)], bank_out.at[flip(t, 1)])
    slope_puts, code_puts = [], []

    def own_part(i, begin, end):
        for b, code in zip(range(begin, end), spread(i, begin, end)):
            rows = slice(b * QB, (b + 1) * QB)
            part = gather(i, code)
            flat[rows] = part if i == 0 else flat[rows] + part

    half_way = blocks // 2
    for i in range(2):
        own_part(i, 0, half_way)
        if i == 0:
            far_step(10)
            side_step(7)
            last_step(4)
        else:
            side_step(9)
            last_step(6, 7)
        own_part(i, half_way, blocks)
        if i == 0:
            far_step(11)
            side_step(8)
            last_step(5)
        else:
            side_step(10, 11)
            last_step(8, 11)
        slope_puts.append(put_slopes(i))
        code_puts.append(put(qkv.at[i * tokens : (i + 1) * tokens], gq_out.at[i]))
    for p in range(4, 8):
        arrived(False, p)
    for i in range(2):
        shard = (2 * pair + 2 + i) % 4
        put(bank.at[shard, 0:feed_2], bank_out.at[shard, 0:feed_2])
    spread(2, 0, blocks)
    put_slopes(2)
    last_step(9)
    slope_puts[0].wait()
    code_puts[0].wait()
    spread(3, 0, blocks)
    put_slopes(3)
    last_step(10)
    for p in range(8, pieces):
        arrived(False, p)
    for i in range(2):
        shard = (2 * pair + 2 + i) % 4
        put(bank.at[shard, feed_2 : feed_2 + hidden], bank_out.at[shard, feed_2 : feed_2 + hidden])
    for b in range(blocks):
        found = [qkv[i % 3 * tokens + b * QB : i % 3 * tokens + (b + 1) * QB] for i in (2, 3)]
        flat[tokens + b * QB : tokens + (b + 1) * QB] = gather(2, found[0]) + gather(3, found[1])

    cot_load.wait()
    xq_put.wait()
    xh_put.wait()
    nq_put.wait()
    sums_out[...] = jnp.zeros_like(sums_out)

    def ends(b):
        rows = pl.ds(pl.multiple_of(b * QB, QB), QB)
        there = pl.ds(pl.multiple_of(c * tokens + b * QB, QB), QB)
        local = [
            pltpu.make_async_copy(src.at[rows], dst, end_sem.at[k, b])
            for k, (src, dst) in enumerate(
                ((xq, lo_out.at[there]), (total, dh2_out.at[rows]), (nq, do_out.at[rows]))
            )
        ]
        remote = pltpu.make_async_remote_copy(
            src_ref=xq.at[rows], dst_ref=lo_out.at[there], send_sem=lo_s.at[b], recv_sem=lo_r.at[b],
            device_id=sib, device_id_type=MESH,
        )
        return local + [remote]

    def last_block(b, _):
        rows = pl.ds(pl.multiple_of(b * QB, QB), QB)
        first = xh[rows] * gains[0:1] + shifts[1:2]
        feed = flat[rows] + flat[pl.ds(pl.multiple_of(tokens + b * QB, QB), QB)]
        normed, inverse = norm(first + (feed + shifts[2:3]))
        xq[rows] = (normed * gains[1:2] + shifts[3:4]).astype(BF16)
        grad = x[rows]
        back = norm_back(grad * gains[1:2], normed, inverse)
        total[rows] = back
        nq[rows] = back.astype(BF16)
        for copy in ends(b):
            copy.start()
        sums_out[1:2] += jnp.sum(grad * normed, 0, keepdims=True)
        sums_out[4:5] += jnp.sum(back, 0, keepdims=True)
        sums_out[5:6] += jnp.sum(grad, 0, keepdims=True)
        return 0

    lax.fori_loop(0, blocks, last_block, 0)

    def sent(p, _):
        far_copy(p).wait_send()
        sib_copy(p).wait_send()
        side_copy(p).wait_send()
        inner_copy(p).wait_send()
        for k in range(4):
            pass_copy(k, p).wait_send()
        return 0

    lax.fori_loop(0, pieces, sent, 0)
    for p in range(pieces):
        (direct_copy(p) if p in DIRECT else last_copy(p)).wait_send()
    waited = [xq_put, xh_put, nq_put] + qkv_puts + [slope_puts[0], code_puts[0]]
    for copy in outs:
        if not any(copy is other_copy for other_copy in waited):
            copy.wait()
    for b in range(blocks):
        for copy in ends(b):
            copy.wait()


def forward(inputs, segment_ids, w_qkv, b_qv, w_out, w_ff1, b_ff1, w_ff2, gains, shifts, ranges, cotangent):
    cols, width = w_out.shape
    hidden = w_ff1.shape[1]
    rows, length = segment_ids.shape
    tokens = inputs.shape[0] // 2
    size = windows(length)[0][2]
    bank_rows = 4 * cols + width + hidden
    pieces = bank_rows // cols
    dma = pltpu.SemaphoreType.DMA
    low = lambda *shape: pltpu.VMEM(shape, BF16)
    full = lambda *shape: pltpu.VMEM(shape, F32)
    wide = S((tokens, width), BF16)
    deep = S((tokens, width), F32)
    return pl.pallas_call(
        forward_kernel,
        out_shape=(
            S((4, bank_rows, width), BF16),
            S((6,), F32),
            wide, wide, wide, wide, wide,
            S((rows, width // 256 * length, 2 * size), BF16),
            wide, wide, wide, deep,
            S((tokens, 128), F32),
            S((2 * tokens, width), BF16),
            S((2, tokens, hidden), BF16),
            S((4, tokens, hidden), BF16),
            deep, wide,
            S((8, width), F32),
        ),
        in_specs=[ANY] * 4 + [VMEM] * 2 + [ANY] * 2 + [VMEM] * 3 + [SMEM],
        out_specs=(ANY, SMEM) + (ANY,) * 16 + (VMEM,),
        scratch_shapes=[
            low(4, bank_rows, width),
            full(max(bank_rows, 2 * tokens), width),
            full(tokens, width),
            low(tokens, width),
            low(tokens, width),
            low(3 * tokens, width),
            low(max(rows // 2 * (width // 256) * length, 3 * tokens), 2 * size),
            low(tokens, width),
            low(tokens, width),
            full(tokens, width),
            full(tokens // length, length // QB, QB, size),
            full(tokens, width),
            low(tokens, width),
            full(tokens, 128),
            full(4, 8, width),
            dma((7,)), dma((24,)), dma((rows // 2,)), dma((3, tokens // QB)),
            dma((tokens // QB,)), dma((tokens // QB,)), dma((3,)), dma((3,)),
            *[dma((pieces,))] * 12,
            dma((4, pieces)), dma((4, pieces)),
        ],
        compiler_params=pltpu.CompilerParams(
            collective_id=1, has_side_effects=True, vmem_limit_bytes=62 * MIB
        ),
        name="forward",
    )(
        jnp.swapaxes(w_qkv, 1, 2), w_out, w_ff1, w_ff2, b_qv, b_ff1, inputs, cotangent,
        segment_ids, gains, shifts, ranges,
    )


GROUP = 192
QUARTER = GROUP // 4
HOPS = ("core", "y", "z1", "z2", "z3", "ag")
LINE_HOPS = ("zs1", "zs2", "zy", "zb1", "zb2", "zb3")


def sum_scratch(groups, width, extra, small_shape):
    count = max(extra, 1)
    dma = pltpu.SemaphoreType.DMA
    buf = lambda *shape: pltpu.VMEM(shape + (width,), BF16)
    kinds = dict(
        own=buf(groups * GROUP), got_y=buf(groups, QUARTER), part=buf(groups, QUARTER),
        got_1=buf(groups, QUARTER), got_2=buf(groups, QUARTER), got_x=buf(count, 2, QUARTER),
        line_1=buf(groups, 2, QUARTER), line_2=buf(groups, 2, QUARTER), line_y=buf(groups, 2, QUARTER),
        line_x=buf(count, 2, 2, QUARTER),
        small_own=pltpu.VMEM(small_shape, F32), small_got=pltpu.VMEM((5 + extra,) + small_shape, F32),
        x_s=dma((count, groups)), x_r=dma((count, groups)),
        lx_s=dma((count, groups, 2)), lx_r=dma((count, groups, 2)),
        small_s=dma((5 + extra,)), small_r=dma((5 + extra,)),
    )
    for hop in HOPS:
        kinds[hop + "_s"], kinds[hop + "_r"] = dma((groups,)), dma((groups,))
    for hop in LINE_HOPS:
        kinds[hop + "_s"], kinds[hop + "_r"] = dma((groups, 2)), dma((groups, 2))
    return list(kinds), list(kinds.values())


TICKS = (
    ((0, 1),),
    ((0, 0), (0, 3), (0, 2), (1, 1)),
    ((1, 0),),
    ((2, 1),),
    ((1, 3),),
    ((3, 1), (2, 0), (0, 7), (0, 5), (1, 2), (0, 6)),
    ((2, 3), (0, 4), (1, 5), (4, 1)),
    ((3, 0), (2, 2)),
    ((3, 3), (1, 6), (5, 1)),
    ((2, 5), (4, 0)),
    ((3, 2), (1, 4), (0, 8), (4, 3)),
    ((2, 6),),
    ((3, 5), (5, 0), (1, 8)),
    ((4, 2),),
    ((5, 3), (2, 4)),
    ((3, 6), (1, 7), (4, 5)),
    ((2, 8), (5, 2)),
    (
        (0, 11), (3, 4), (4, 6), (2, 7), (5, 5), (6, 1), (6, 0), (0, 10),
        (1, 11), (3, 8), (0, 9), (1, 10), (4, 4),
    ),
    ((2, 11), (3, 7), (5, 6)),
    ((4, 8), (1, 9)),
    ((5, 4), (2, 10)),
    ((3, 11), (4, 7)),
    (),
    ((2, 9), (5, 8)),
    ((4, 11), (6, 5), (3, 10), (5, 7)),
    (),
    (
        (5, 11), (3, 9), (4, 10), (6, 11), (4, 9), (5, 10), (6, 7), (6, 4),
        (6, 3), (6, 6), (5, 9), (6, 2), (6, 10), (6, 8), (6, 9),
    ),
)


class GradientSum:
    def __init__(self, extra, mine, theirs, result, refs):
        self.__dict__.update(refs)
        self.extra, self.mine, self.theirs, self.result = extra, mine, theirs, result
        t, d = lax.axis_index("tensor"), lax.axis_index("dp")
        self.y = d % 2
        self.z = (d // 2) % 4
        self.end = jnp.logical_or(self.z == 0, self.z == 3)
        self.middle = jnp.logical_not(self.end)
        self.sib = (d, flip(t, 1))
        self.side = (flip(d, 1), t)
        self.inner = (flip(d, 2), t)
        self.across = (d + 2 * (3 - 2 * self.z), t)
        self.others = [(flip(d, 8 << b), t) for b in range(extra)]
        self.beyond = [self.across] + self.others
        self.groups = self.own.shape[0] // GROUP

    def announce(self):
        barrier = pltpu.get_barrier_semaphore()

        def tell(peers):
            for peer in peers:
                pl.semaphore_signal(barrier, inc=1, device_id=peer, device_id_type=MESH)

        tell([self.sib, self.side, self.inner])
        pl.when(self.middle)(lambda: tell(self.beyond))

    def meet(self):
        barrier = pltpu.get_barrier_semaphore()
        pl.when(self.end)(lambda: pl.semaphore_wait(barrier, 3))
        pl.when(self.middle)(lambda: pl.semaphore_wait(barrier, 3 + len(self.beyond)))

    def remote(self, src, dst, hop, at, to):
        return pltpu.make_async_remote_copy(
            src_ref=src, dst_ref=dst, send_sem=getattr(self, hop + "_s").at[at],
            recv_sem=getattr(self, hop + "_r").at[at], device_id=to, device_id_type=MESH,
        )

    def small(self, i, to):
        return self.remote(self.small_own, self.small_got.at[i], "small", i, to)

    def small_add(self, i, to):
        self.small(i, to).wait()
        self.small_own[...] = self.small_own[...] + self.small_got[i]

    def small_step(self, step):
        if step == 0:
            self.small(0, self.sib).start()
        if step == 1:
            self.small_add(0, self.sib)
            self.small(1, self.side).start()
        if step == 2:
            self.small_add(1, self.side)
            pl.when(self.end)(lambda: self.small(2, self.inner).start())
        if step == 3:

            def inward():
                self.small(2, self.inner).wait_recv()
                self.small_own[...] = self.small_own[...] + self.small_got[2]
                self.small(3, self.across).start()

            pl.when(self.middle)(inward)
        if step == 4:

            def outward():
                self.small_add(3, self.across)
                for b, peer in enumerate(self.others):
                    self.small(5 + b, peer).start()
                    self.small_add(5 + b, peer)
                self.small(4, self.inner).start()

            pl.when(self.middle)(outward)
        if step == 5:

            def received():
                self.small(2, self.inner).wait_send()
                self.small(4, self.inner).wait_recv()
                self.small_own[...] = self.small_got[4]

            pl.when(self.end)(received)
            pl.when(self.middle)(lambda: self.small(4, self.inner).wait_send())

    def span(self, g):
        return pl.ds(pl.multiple_of(g * GROUP, 16), GROUP)

    def half(self, g, which):
        return pl.ds(pl.multiple_of(g * GROUP + which * QUARTER, 16), QUARTER)

    def line(self, g, i):
        return pl.ds(pl.multiple_of(g * GROUP + (2 + i) * QUARTER, 16), QUARTER)

    def core(self, g):
        return self.remote(self.theirs.at[self.span(g)], self.own.at[self.span(g)], "core", g, self.sib)

    def hop(self, name, g):
        if name == "y":
            return self.remote(self.own.at[self.half(g, 1 - self.y)], self.got_y.at[g], "y", g, self.side)
        if name == "z1":
            return self.remote(self.part.at[g], self.got_1.at[g], "z1", g, self.inner)
        if name == "z2":
            return self.remote(self.part.at[g], self.got_2.at[g], "z2", g, self.across)
        there = self.result.at[self.half(g, self.y)]
        return self.remote(there, there, name, g, self.inner if name == "z3" else self.side)

    def line_hop(self, name, g, i):
        mine = self.own.at[self.line(g, i)]
        if name == "zs1":
            return self.remote(mine, self.line_1.at[g, i], name, (g, i), self.inner)
        if name == "zs2":
            return self.remote(mine, self.line_2.at[g, i], name, (g, i), self.across)
        if name == "zy":
            return self.remote(mine, self.line_y.at[g, i], name, (g, i), self.side)
        there = self.result.at[self.line(g, i)]
        return self.remote(there, there, name, (g, i), self.across if name == "zb2" else self.inner)

    def stage(self, s, g):
        add = lambda a, b: (a.astype(F32) + b.astype(F32)).astype(BF16)
        when = lambda condition, body: pl.when(condition)(body)
        root = [self.z == 1, self.z == 2]
        passer = [self.z == 2, self.z == 1]
        near = [self.z == 0, self.z == 3]
        far = [self.z == 3, self.z == 0]
        if s == 0:
            self.core(g).start()
        if s == 1:
            self.core(g).wait()
            self.own[self.span(g)] = add(self.own[self.span(g)], self.mine[self.span(g)])
            self.hop("y", g).start()
            when(self.end, lambda: [self.line_hop("zs1", g, i).start() for i in range(2)] and None)
        if s == 2:
            self.hop("y", g).wait()
            self.part[g] = add(self.own[self.half(g, self.y)], self.got_y[g])
            when(self.end, lambda: self.hop("z1", g).start())
            for i in range(2):

                def gather(i=i):
                    self.line_hop("zs1", g, i).wait_recv()
                    rows = self.line(g, i)
                    self.own[rows] = add(self.own[rows], self.line_1[g, i])
                    when(passer[i], lambda: self.line_hop("zs2", g, i).start())

                when(self.middle, gather)
        if s == 3:

            def middle():
                self.hop("z1", g).wait_recv()
                self.part[g] = add(self.part[g], self.got_1[g])
                self.hop("z2", g).start()

            when(self.middle, middle)
            for i in range(2):

                def at_root(i=i):
                    self.line_hop("zs2", g, i).wait_recv()
                    rows = self.line(g, i)
                    self.own[rows] = add(self.own[rows], self.line_2[g, i])
                    self.line_hop("zy", g, i).start()

                when(root[i], at_root)
        if s == 4:

            def total():
                self.hop("z2", g).wait()
                self.part[g] = add(self.part[g], self.got_2[g])
                for b in range(self.extra):
                    copy = self.remote(self.part.at[g], self.got_x.at[b, g % 2], "x", (b, g), self.others[b])
                    copy.start()
                    copy.wait()
                    self.part[g] = add(self.part[g], self.got_x[b, g % 2])
                self.result[self.half(g, self.y)] = self.part[g]
                self.hop("ag", g).start()
                self.hop("z3", g).start()

            when(self.middle, total)
            for i in range(2):

                def spread(i=i):
                    self.line_hop("zy", g, i).wait()
                    rows = self.line(g, i)
                    self.own[rows] = add(self.own[rows], self.line_y[g, i])
                    for b in range(self.extra):
                        copy = self.remote(
                            self.own.at[rows], self.line_x.at[b, g % 2, i], "lx", (b, g, i), self.others[b]
                        )
                        copy.start()
                        copy.wait()
                        self.own[rows] = add(self.own[rows], self.line_x[b, g % 2, i])
                    self.result[rows] = self.own[rows]
                    self.line_hop("zb2", g, i).start()
                    self.line_hop("zb1", g, i).start()

                when(root[i], spread)
        if s == 5:

            def outer():
                self.hop("z3", g).wait_recv()
                self.hop("ag", g).start()

            when(self.end, outer)
            for i in range(2):

                def onward(i=i):
                    self.line_hop("zb2", g, i).wait_recv()
                    self.line_hop("zb3", g, i).start()

                when(passer[i], onward)
        if s == 6:
            self.hop("ag", g).wait()
            for i in range(2):
                when(near[i], lambda i=i: self.line_hop("zb1", g, i).wait_recv())
                when(far[i], lambda i=i: self.line_hop("zb3", g, i).wait_recv())

                def sent_root(i=i):
                    self.line_hop("zb1", g, i).wait_send()
                    self.line_hop("zb2", g, i).wait_send()

                def sent_passer(i=i):
                    self.line_hop("zs2", g, i).wait_send()
                    self.line_hop("zb3", g, i).wait_send()

                when(root[i], sent_root)
                when(passer[i], sent_passer)

            def sent_end():
                self.hop("z1", g).wait_send()
                for i in range(2):
                    self.line_hop("zs1", g, i).wait_send()

            when(self.end, sent_end)
            when(self.middle, lambda: self.hop("z3", g).wait_send())

    def run(self, events):
        for stage, group in events:
            self.stage(stage, group)


def back_kernel(
    extra, names,
    do_hbm, gq_hbm, factor_hbm, nq_hbm, bank, dh2_hbm, xh_hbm, inv_hbm, sums_ref,
    cs_hbm, cq_hbm, q_hbm, k_hbm, v_hbm, p_hbm, xq_hbm, xs_hbm, gains, shifts, ranges,
    g2_out, g1_out, go_out, gq_out, gains_out, shifts_out, bqv_out, bff1_out, dx_full,
    result, inv, grads, do, weights, gq, factor, nq, low, total, dh, xh, wo, cq, dproj, sem, dx_send, dx_recv,
    *refs,
):
    t, d = lax.axis_index("tensor"), lax.axis_index("dp")
    c, pair = t % 2, t // 2
    engine = GradientSum(extra, grads.at[c], grads.at[1 - c], result, dict(zip(names, refs)))
    tokens, width = do.shape
    hidden = gq_hbm.shape[2]
    side = width // 2
    cols = side // 2
    heads = width // 128 // 2
    length = p_hbm.shape[1] // heads
    wins = windows(length)
    size = wins[0][2]
    blocks = tokens // QB
    slots = factor.shape[0] // length

    def load(i, src, dst):
        copy = pltpu.make_async_copy(src, dst, sem.at[i])
        copy.start()
        return copy

    def shard_at(i):
        return (2 * pair + i) % 4

    def load_codes(begin, end, sems):
        return [
            load(sems[i], gq_hbm.at[i, :, begin:end], gq.at[i * tokens : (i + 1) * tokens, begin:end])
            for i in range(2)
        ]

    half_way = hidden // 2
    first_loads = [load(0, do_hbm, do)] + load_codes(0, half_way, (1, 2))

    def load_pair(base):
        copies = []
        for i in range(2):
            s = shard_at(base + i)
            at = pl.ds(i * tokens, tokens)
            for j in range(2):
                spot = weights.at[(2 * j + i) * width : (2 * j + i + 1) * width]
                copies.append(load(3 + 2 * j + i, bank.at[s, 4 * cols + j * width : 4 * cols + (j + 1) * width], spot))
            copies.append(load(7 + i, factor_hbm.at[base + i], factor.at[at]))
        return copies

    engine.announce()
    at = pl.ds(pl.multiple_of(c * tokens, 256), tokens)
    engine.small_own[...] = jnp.zeros_like(engine.small_own)
    engine.small_own[0:8] = sums_ref[...]

    def tick(point):
        engine.run(TICKS[point])

    for copy in first_loads:
        copy.wait()
    code_loads = load_codes(half_way, hidden, (12, 14))
    pair_loads = load_pair(0)

    def weights_2(begin, end):
        for i in range(2):
            part = dot_tn(gq[i * tokens : (i + 1) * tokens, begin:end], do[...])
            grads[i, begin:end] = part.astype(BF16)

    weights_2(0, half_way)
    engine.meet()
    tick(0)
    for copy in code_loads:
        copy.wait()
    weights_2(half_way, hidden)
    tick(1)
    for copy in pair_loads:
        copy.wait()
    nq_load = load(9, nq_hbm, nq)
    norm_loads = [load(10, dh2_hbm, dh), load(11, xh_hbm, xh), load(15, inv_hbm, inv)]

    def feed_blocks(own, begin, end):
        found = range(begin, end)
        backs = [
            [
                dot_nt(do[b * QB : (b + 1) * QB], weights[(2 + i) * width : (3 + i) * width])
                for i in range(2)
            ]
            for b in found
        ]
        lows = []
        for b, pairs in zip(found, backs):
            lows.append([])
            for i in range(2):
                spot = slice(i * tokens + b * QB, i * tokens + (b + 1) * QB)
                value = pairs[i] * factor[spot].astype(F32)
                short = value.astype(BF16)
                if own:
                    engine.small_own[6 + i : 7 + i] += jnp.sum(value, 0, keepdims=True)
                    low[spot] = short
                lows[-1].append(short)
        for b, (one, two) in zip(found, lows):
            rows = slice(b * QB, (b + 1) * QB)
            part = dot_nt(one, weights[0:width]) + dot_nt(two, weights[width : 2 * width])
            total[rows] = part if own else total[rows] + part

    feed_blocks(True, 0, blocks // 2)
    tick(2)
    feed_blocks(True, blocks // 2, blocks)
    tick(3)
    pair_loads = load_pair(2)
    nq_load.wait()
    grads[0, hidden : 2 * hidden] = dot_tn(nq[...], low[0:tokens]).astype(BF16)
    tick(4)
    grads[1, hidden : 2 * hidden] = dot_tn(nq[...], low[tokens : 2 * tokens]).astype(BF16)
    tick(5)
    for copy in pair_loads:
        copy.wait()
    wo_loads = [
        load(27 + s, bank.at[s, 3 * cols : 4 * cols], wo.at[s * cols : (s + 1) * cols]) for s in range(4)
    ]
    mine = pl.ds(pl.multiple_of(pair * side, 128), side)
    cq_load = load(13, cq_hbm.at[:, mine], cq)
    cs_load = load(9, cs_hbm, nq)
    feed_blocks(False, 0, blocks // 2)
    tick(6)
    feed_blocks(False, blocks // 2, blocks)
    qkv_loads = [
        load(18 + j, src, weights.at[j * tokens : (j + 1) * tokens])
        for j, src in enumerate((q_hbm, k_hbm, v_hbm))
    ]

    def unit_at(own, u):
        return u // heads, u % heads

    def probs_load(own, u):
        row, which = unit_at(own, u)
        slot = u % slots
        return pltpu.make_async_copy(
            p_hbm.at[row * 2 + (pair if own else 1 - pair), pl.ds(pl.multiple_of(which * length, length), length)],
            factor.at[pl.ds(pl.multiple_of(slot * length, length), length)],
            sem.at[22 + slot],
        )

    units = 2 * heads
    for u in range(slots - 1):
        probs_load(True, u).start()
    tick(7)

    for copy in norm_loads:
        copy.wait()
    xq_load = load(17, xq_hbm, low.at[tokens : 2 * tokens])
    wt_loads = [
        load(31 + s, bank.at[s, 0 : 3 * cols], gq.at[3 * s * cols : 3 * (s + 1) * cols]) for s in range(4)
    ]
    xs_load = load(21, xs_hbm, do)

    def norm_block(b, _):
        rows = pl.ds(pl.multiple_of(b * QB, QB), QB)
        normed = xh[rows]
        squash = jnp.tanh((normed * gains[0:1] + shifts[1:2]) * (1.0 / ranges[2]))
        grad = dh[rows] + total[rows] * (1.0 - squash * squash)
        inverse = jnp.max(inv[rows], axis=1, keepdims=True)
        back = norm_back(grad * gains[0:1], normed, inverse)
        dh[rows] = back
        low[rows] = back.astype(BF16)
        engine.small_own[0:1] += jnp.sum(grad * normed, 0, keepdims=True)
        engine.small_own[2:3] += jnp.sum(back, 0, keepdims=True)
        engine.small_own[3:4] += jnp.sum(grad, 0, keepdims=True)
        return 0

    lax.fori_loop(0, blocks, norm_block, 0)
    tick(8)
    for copy in wo_loads:
        copy.wait()
    cq_load.wait()
    cs_load.wait()
    d_attn = low.at[0:tokens]
    part = dot_tn(cq[...], d_attn[...]).astype(BF16)
    for i in range(2):
        grads[i, 2 * hidden : 2 * hidden + cols] = part[i * cols : (i + 1) * cols]
    tick(9)

    def context_block(b, _):
        rows = pl.ds(pl.multiple_of(b * QB, QB), QB)
        nq[rows] = (dot_nt(d_attn[rows], wo[...]) * nq[rows].astype(F32)).astype(BF16)
        return 0

    lax.fori_loop(0, blocks, context_block, 0)
    tick(10)

    for copy in qkv_loads:
        copy.wait()
    lanes = lax.broadcasted_iota(jnp.int32, (QB, 128), 1) < HD

    def attention(own, u):
        row, which = unit_at(own, u)
        probs_load(own, u).wait()

        @pl.when(u + slots - 1 < units)
        def _():
            probs_load(own, u + slots - 1).start()

        half = pair if own else 1 - pair
        lane = pl.ds(pl.multiple_of((half * heads + which) * 128, 128), 128)
        here = pl.ds(pl.multiple_of(which * 128, 128), 128)
        slot = pl.multiple_of((u % slots) * length, length)
        base = pl.multiple_of(row * length, length)
        wide = lax.broadcasted_iota(jnp.int32, (size, 128), 1) < HD
        jobs = [(b, head) for b in range(len(wins)) for head in range(2)]

        def shares(b, head):
            return factor[pl.ds(slot + wins[b][0], QB), head * size : (head + 1) * size]

        def first_product(b, head):
            first, begin, _ = wins[b]
            own_lanes = lanes if head == 0 else jnp.logical_not(lanes)
            context = nq[pl.ds(base + first, QB), lane].astype(F32)
            chosen = jnp.where(own_lanes, context, 0.0).astype(BF16)
            return dot_nt(chosen, weights[pl.ds(2 * tokens + base + begin, size), lane])

        def d_score(b, head, d_probs):
            exact = shares(b, head).astype(F32)
            both = exact * d_probs
            return (both - exact * jnp.sum(both, -1, keepdims=True)).astype(BF16)

        def products(b, head, d_low):
            first, begin, _ = wins[b]
            rows = pl.ds(base + first, QB)
            return (
                dot_nn(d_low, weights[pl.ds(tokens + base + begin, size), lane]),
                dot_tn(d_low, weights[rows, lane]),
                dot_tn(shares(b, head), nq[rows, lane]),
            )

        d_probs = [first_product(*job) for job in jobs]
        d_lows = [d_score(*job, value) for job, value in zip(jobs, d_probs)]
        found = [products(*job, value) for job, value in zip(jobs, d_lows)]
        d_keys, d_values = [], []
        for b, (first, _, _) in enumerate(wins):
            got = found[2 * b : 2 * b + 2]
            rows = pl.ds(base + first, QB)
            dproj[0, rows, here] = (jnp.where(lanes, got[0][0], got[1][0]) * 0.125).astype(BF16)
            d_keys.append(jnp.where(wide, got[0][1], got[1][1]))
            d_values.append(jnp.where(wide, got[0][2], got[1][2]))
        for j, parts, scale in ((1, d_keys, 0.125), (2, d_values, 1.0)):
            for spot in range(0, length, SPAN):
                terms = [
                    part[spot - begin : spot - begin + SPAN]
                    for part, (_, begin, _) in zip(parts, wins)
                    if begin <= spot < begin + size
                ]
                dproj[j, pl.ds(base + spot, SPAN), here] = (sum(terms[1:], terms[0]) * scale).astype(BF16)

    def back_through(own):
        first = 2 * pair if own else 2 - 2 * pair

        def rows(j):
            found = [
                gq[pl.ds(pl.multiple_of(((first + i) * 3 + j) * cols, 16), cols)] for i in range(2)
            ]
            return jnp.concatenate(found, axis=0)

        terms = [dot_nn(dproj[j], rows(j)) for j in range(3)]
        return terms[0] + terms[1] + terms[2]

    def ticks_after(u, first):
        for k in range(units):
            if TICKS[first + k]:
                pl.when(u == k)(functools.partial(tick, first + k))

    def own_unit(u, _):
        attention(True, u)
        ticks_after(u, 11)
        return 0

    lax.fori_loop(0, units, own_unit, 0)
    for u in range(slots - 1):
        probs_load(False, u).start()
    for copy in wt_loads:
        copy.wait()
    xq_load.wait()
    for j in range(3):
        part = dot_tn(dproj[j], low[tokens : 2 * tokens]).astype(BF16)
        base = 2 * hidden + (j + 1) * cols
        for i in range(2):
            grads[i, base : base + cols] = part[i * cols : (i + 1) * cols]
    engine.small_own[8:9, 0:side] = jnp.sum(dproj[0].astype(F32), 0, keepdims=True)
    engine.small_own[9:10, 0:side] = jnp.sum(dproj[2].astype(F32), 0, keepdims=True)
    tick(17)
    engine.small_step(0)
    total[...] = back_through(True)
    tick(18)
    engine.small_step(1)

    def other_unit(u, _):
        attention(False, u)
        ticks_after(u, 19)
        for k, step in ((1, 2), (3, 3), (5, 4)):
            pl.when(u == k)(functools.partial(engine.small_step, step))
        return 0

    lax.fori_loop(0, units, other_unit, 0)
    xs_load.wait()
    other = back_through(False)
    factor[0:tokens] = (dh[...] + (total[...] + other) * do[...].astype(F32)).astype(BF16)
    dx_copy = pltpu.make_async_remote_copy(
        src_ref=factor.at[0:tokens], dst_ref=dx_full.at[at], send_sem=dx_send, recv_sem=dx_recv,
        device_id=engine.sib, device_id_type=MESH,
    )
    dx_copy.start()
    outs = [load(26, factor.at[0:tokens], dx_full.at[at])]
    tick(25)
    engine.small_step(5)
    sums = engine.small_own[...]
    here = sums[:, 0:cols]
    for s in range(1, 4):
        here = jnp.where(t == s, sums[:, s * cols : (s + 1) * cols], here)
    gains_out[...] = here[0:2]
    shifts_out[...] = here[2:6]
    bqv_out[...] = jnp.where(c == 0, sums[8:10, 0:cols], sums[8:10, cols:side])
    bff1_out[...] = jnp.where(c == 0, sums[6:7], sums[7:8]).reshape(hidden)
    leaving = [
        (0, 4, g2_out, 0, hidden),
        (4, 8, g1_out, hidden, 2 * hidden),
        (8, 9, go_out, 2 * hidden, 2 * hidden + cols),
        (9, 12, gq_out, 2 * hidden + cols, 2 * hidden + 4 * cols),
    ]
    complete = {g for events in TICKS[:-1] for s, g in events if s == 6}
    for event in ((None,) + TICKS[-1]):
        if event is not None:
            engine.stage(*event)
            if event[0] == 6:
                complete.add(event[1])
        for k, (first, last, ref, begin, end) in enumerate(leaving):
            if ref is not None and complete.issuperset(range(first, last)):
                outs.append(load(k, result.at[begin:end], ref))
                leaving[k] = (first, last, None, begin, end)
    dx_copy.wait()
    for copy in outs:
        copy.wait()


def back(
    nd, do, gq, factor, nq, bank, dh2, xh, inv, sums, cs, cq, q, k, v, probs, xq, xs,
    gains, shifts, ranges,
):
    tokens, width = do.shape
    hidden = gq.shape[2]
    cols = width // 4
    rows = 2 * hidden + 4 * cols
    extra = (nd // 8).bit_length() - 1
    dma = pltpu.SemaphoreType.DMA
    names, scratch = sum_scratch(rows // GROUP, width, extra, (16, width))
    buf = lambda *shape: pltpu.VMEM(shape, BF16)
    return pl.pallas_call(
        functools.partial(back_kernel, extra, names),
        out_shape=(
            S((hidden, width), BF16),
            S((width, hidden), BF16),
            S((cols, width), BF16),
            S((3 * cols, width), BF16),
            S((2, cols), F32),
            S((4, cols), F32),
            S((2, cols), F32),
            S((hidden,), F32),
            S((2 * tokens, width), BF16),
        ),
        in_specs=[ANY] * 8 + [VMEM] + [ANY] * 8 + [VMEM, VMEM, SMEM],
        out_specs=(ANY,) * 4 + (VMEM,) * 4 + (ANY,),
        scratch_shapes=[
            buf(rows, width),
            pltpu.VMEM((tokens, 128), F32),
            buf(2, rows, width),
            buf(tokens, width),
            buf(max(4 * width, 3 * tokens), width),
            buf(max(3 * width, 2 * tokens), width),
            buf(2 * tokens, width),
            buf(tokens, width),
            buf(2 * tokens, width),
            pltpu.VMEM((tokens, width), F32),
            pltpu.VMEM((tokens, width), F32),
            pltpu.VMEM((tokens, width), F32),
            buf(width, width),
            buf(tokens, width // 2),
            buf(3, tokens, width // 2),
            dma((35,)),
            dma,
            dma,
            *scratch,
        ],
        compiler_params=pltpu.CompilerParams(
            collective_id=2, has_side_effects=True, vmem_limit_bytes=62 * MIB
        ),
        name="back",
    )(
        do, gq, factor, nq, bank, dh2, xh, inv, sums, cs, cq, q, k, v, probs, xq, xs,
        gains, shifts, ranges,
    )


def finish_kernel(*refs):
    half = len(refs) // 2
    for src, dst in zip(refs[: half - 1], refs[half:-1]):
        dst[...] = src[...].astype(F32)
    for j in range(refs[-1].shape[0]):
        refs[-1][j] = refs[half - 1][j]


def finish(*arrays):
    steps = 8
    specs = []
    for array in arrays[:-1]:
        rows = array.shape[0]
        if array.ndim == 2 and rows % (16 * steps) == 0:
            specs.append(pl.BlockSpec((rows // steps, array.shape[1]), lambda i: (i, 0)))
        elif array.ndim == 2 and rows % (16 * steps // 2) == 0:
            specs.append(pl.BlockSpec((2 * rows // steps, array.shape[1]), lambda i: (i // 2, 0)))
        else:
            specs.append(pl.BlockSpec(array.shape, lambda i, n=array.ndim: (0,) * n))
    specs.append(SMEM)
    return pl.pallas_call(
        finish_kernel,
        out_shape=tuple(S(array.shape, F32) for array in arrays),
        grid=(steps,),
        in_specs=specs,
        out_specs=tuple(specs),
        compiler_params=pltpu.CompilerParams(vmem_limit_bytes=62 * MIB),
        name="finish",
    )(*arrays)


def per_device(
    nd, inputs, segment_ids, w_qkv, b_qv, w_out, w_ff1, b_ff1, w_ff2, norm_gains, shift_biases,
    act_ranges, cotangent,
):
    width = inputs.shape[1]
    cols = w_qkv.shape[2]
    (
        bank, weight_max, xq, xs, q, k, v, probs, cq, cs, nq, xh, inv, layer_out, gq, factor, dh2, do,
        sums,
    ) = forward(
        inputs, segment_ids, w_qkv, b_qv, w_out, w_ff1, b_ff1, w_ff2, norm_gains, shift_biases,
        act_ranges, cotangent,
    )
    (
        grad_ff2, grad_ff1, grad_out, grad_qkv, grad_gains, grad_shifts, grad_bqv, grad_bff1, input_grad,
    ) = back(
        nd, do, gq, factor, nq, bank, dh2, xh, inv, sums, cs, cq, q, k, v, probs, xq, xs,
        norm_gains, shift_biases, act_ranges,
    )
    (
        layer_out, input_grad, grad_ff2, grad_ff1, grad_out, grad_qkv, grad_gains, grad_shifts, grad_bqv,
        grad_bff1, weight_max,
    ) = finish(
        layer_out, input_grad, grad_ff2, grad_ff1, grad_out, grad_qkv, grad_gains, grad_shifts, grad_bqv,
        grad_bff1, weight_max,
    )
    grad_qkv = grad_qkv.reshape(3, cols, width).transpose(0, 2, 1)
    return (
        layer_out, input_grad, grad_qkv, grad_bqv, grad_out, grad_ff1, grad_bff1, grad_ff2,
        grad_gains, grad_shifts, weight_max,
    )


def solution(mesh):
    return jax.shard_map(
        functools.partial(per_device, mesh.shape["dp"]),
        mesh=mesh,
        in_specs=(
            P("dp", None),
            P("dp", None),
            P(None, None, "tensor"),
            P(None, "tensor"),
            P("tensor", None),
            P(None, "tensor"),
            P("tensor"),
            P("tensor", None),
            P(),
            P(),
            P(),
            P("dp", None),
        ),
        out_specs=(
            P("dp", None),
            P("dp", None),
            P(None, None, "tensor"),
            P(None, "tensor"),
            P("tensor", None),
            P(None, "tensor"),
            P("tensor"),
            P("tensor", None),
            P(None, "tensor"),
            P(None, "tensor"),
            P(),
        ),
        check_vma=False,
    )
```

```python
import functools
import math

import jax
import jax.numpy as jnp
from jax import lax
from jax.experimental import pallas as pl
from jax.experimental.pallas import tpu as pltpu
from jax.sharding import PartitionSpec as P

HD = 64
SPAN = 128
QB = 256
MASKED = -1e30
EPSILON = 1e-06
ROOT_HALF = 0.7071067811865476
INV_ROOT_TWO_PI = 0.3989422804014327
STAIR = (
    6.579734980213376,
    -12.987641368031495,
    12.20087719668052,
    -6.61489684889321,
    2.04264519055443,
)
MIB = 1 << 20
MESH = pl.DeviceIdType.MESH
F32 = jnp.float32
BF16 = jnp.bfloat16
ANY = pl.BlockSpec(memory_space=pl.ANY)
VMEM = pl.BlockSpec(memory_space=pltpu.VMEM)
SMEM = pl.BlockSpec(memory_space=pltpu.SMEM)
S = jax.ShapeDtypeStruct


def flip(value, bit):
    return value + bit - 2 * bit * ((value // bit) % 2)


def dot_nn(left, right):
    return lax.dot_general(left, right, (((1,), (0,)), ((), ())), preferred_element_type=F32)


def dot_nt(left, right):
    return lax.dot_general(left, right, (((1,), (1,)), ((), ())), preferred_element_type=F32)


def dot_tn(left, right):
    return lax.dot_general(left, right, (((0,), (0,)), ((), ())), preferred_element_type=F32)


def stairs(levels):
    whole = jnp.round(levels)
    rest = levels - whole
    square = rest * rest
    curve = STAIR[4]
    for factor in STAIR[3::-1]:
        curve = curve * square + factor
    return whole + rest * square * curve


def quantize(values, bound):
    squash = jnp.tanh(values * (1.0 / bound))
    return stairs(127.0 * squash) * (bound / 127.0), squash


def norm(hidden):
    centred = hidden - jnp.mean(hidden, -1, keepdims=True)
    inverse = lax.rsqrt(jnp.mean(centred * centred, -1, keepdims=True) + EPSILON)
    return centred * inverse, inverse


def norm_back(scaled, normed, inverse):
    return inverse * (
        scaled
        - jnp.mean(scaled, -1, keepdims=True)
        - normed * jnp.mean(scaled * normed, -1, keepdims=True)
    )


def windows(length):
    found = []
    for first in range(0, length, QB):
        low = max(0, first - SPAN)
        found.append((first, low, min(length, first + QB + SPAN) - low))
    return found


DIRECT = (0, 1, 2, 3, 11)


def forward_kernel(
    wqkv, wout, wff1, wff2, bqv, bff1, x_hbm, cot_hbm, seg_ref, gains, shifts, ranges,
    bank_out, top_out, xq_out, xs_out, q_out, k_out, v_out, p_out, cq_out, cs_out, nq_out, xh_out,
    inv_out, lo_out, gq_out, factor_out, dh2_out, do_out, sums_out,
    bank, flat, x, xq, xs, qkv, probs, cq, cs, total, bias, xh, nq, inv, small, scales,
    sem, out_sem, p_sem, end_sem, lo_s, lo_r, small_s, small_r, sib_s, sib_r, far_s, far_r,
    direct_s, direct_r, side_s, side_r, inner_s, inner_r, last_s, last_r, pass_s, pass_r,
):
    t, d = lax.axis_index("tensor"), lax.axis_index("dp")
    c, pair, corner = t % 2, t // 2, d % 4
    sib, far, side, inner = (d, flip(t, 1)), (d, flip(t, 2)), (flip(d, 1), t), (flip(d, 2), t)
    diagonal = (d, flip(flip(t, 1), 2))
    cols, width = wout.shape
    hidden = wff1.shape[1]
    tokens = x.shape[0]
    length = seg_ref.shape[1]
    rows_here = tokens // length
    lanes_half = width // 2
    wins = windows(length)
    size = wins[0][2]
    blocks = tokens // QB
    heads = width // 256
    units = rows_here * heads
    piece = cols
    pieces = bank.shape[1] // piece
    quarter = piece // 4

    def load(i, src, dst):
        copy = pltpu.make_async_copy(src, dst, sem.at[i])
        copy.start()
        return copy

    mine = pl.ds(pl.multiple_of(c * tokens, QB), tokens)
    feed_1, feed_2 = 4 * cols, 4 * cols + width
    loads = [load(j, wqkv.at[j], flat.at[j * cols : (j + 1) * cols]) for j in range(3)]
    loads.append(load(3, wout, flat.at[3 * cols : feed_1]))
    loads.append(load(4, wff1, flat.at[feed_1:feed_2]))
    spans = [(j * cols, cols) for j in range(4)]
    spans += [(4 * cols, width), (4 * cols + width, hidden)]

    barrier = pltpu.get_barrier_semaphore()
    for peer in (sib, far, diagonal, side, inner):
        pl.semaphore_signal(barrier, inc=1, device_id=peer, device_id_type=MESH)
    small[pl.ds(t, 1)] = jnp.zeros((1, 8, width), F32)
    small[pl.ds(t, 1), 0:1, 0:hidden] = bff1[...].reshape(1, 1, hidden)
    small[pl.ds(t, 1), 1:3, 0:cols] = bqv[...][None]
    for j, (begin, count) in enumerate(spans):
        loads[j].wait()
        if j == 3:
            loads.append(load(5, wff2, flat.at[feed_2 : feed_2 + hidden]))
        if j == 4:
            x_load = load(6, x_hbm.at[mine], x)
        top = jnp.max(jnp.abs(flat[begin : begin + count]), axis=(0, 1), keepdims=True)
        small[pl.ds(t, 1), 3:4, 128 * j : 128 * (j + 1)] = jnp.broadcast_to(top, (1, 128))[None]
    pl.semaphore_wait(barrier, 5)
    sends = []
    for i, peer in enumerate((sib, far, diagonal)):
        copy = pltpu.make_async_remote_copy(
            src_ref=small.at[t], dst_ref=small.at[t], send_sem=small_s.at[i],
            recv_sem=small_r.at[i], device_id=peer, device_id_type=MESH,
        )
        copy.start()
        sends.append(copy)

    x_load.wait()

    def input_block(b, _):
        rows = pl.ds(pl.multiple_of(b * QB, QB), QB)
        coded, squash = quantize(x[rows], ranges[0])
        xq[rows] = coded.astype(BF16)
        xs[rows] = (1.0 - squash * squash).astype(BF16)
        return 0

    lax.fori_loop(0, blocks, input_block, 0)
    for r in range(rows_here):
        seg = jnp.broadcast_to(seg_ref[pl.ds(c * rows_here + r, 1)], (16, length))
        hot = (lax.broadcasted_iota(jnp.int32, (16, length), 0) == seg).astype(F32).astype(BF16)
        for b, (first, low, _) in enumerate(wins):
            same = dot_tn(hot[:, first : first + QB], hot[:, low : low + size])
            bias[r, b] = (same - 1.0) * -MASKED
    outs = []

    def put(src, dst):
        copy = pltpu.make_async_copy(src, dst, out_sem.at[len(outs)])
        copy.start()
        outs.append(copy)
        return copy

    for copy in sends:
        copy.wait()
    top_row = jnp.max(small[:, 3:4, :], axis=0)
    for j in range(len(spans)):
        top_out[j] = jnp.max(top_row[:, 128 * j : 128 * (j + 1)])

    other = flip(t, 2)
    next_side, next_inner, across = flip(corner, 1), flip(corner, 2), flip(flip(corner, 1), 2)

    def moved(p, shard, which, sems, at, to):
        rows = pl.ds(pl.multiple_of(p * piece + which * quarter, 16), quarter)
        there = bank.at[shard, rows]
        return pltpu.make_async_remote_copy(
            src_ref=there, dst_ref=there, send_sem=sems[0].at[at], recv_sem=sems[1].at[at],
            device_id=to, device_id_type=MESH,
        )

    def sib_copy(p):
        there = bank.at[t, pl.ds(pl.multiple_of(p * piece, 16), piece)]
        return pltpu.make_async_remote_copy(
            src_ref=there, dst_ref=there, send_sem=sib_s.at[p], recv_sem=sib_r.at[p],
            device_id=sib, device_id_type=MESH,
        )

    far_copy = lambda p: moved(p, t, corner, (far_s, far_r), p, far)
    direct_copy = lambda p: moved(p, t, across, (direct_s, direct_r), p, far)
    side_copy = lambda p: moved(p, other, corner, (side_s, side_r), p, side)
    inner_copy = lambda p: moved(p, other, corner, (inner_s, inner_r), p, inner)

    def last_copy(p):
        if p % 2 == 0:
            return moved(p, other, next_inner, (last_s, last_r), p, side)
        return moved(p, other, next_side, (last_s, last_r), p, inner)

    def pass_copy(k, p):
        which = (corner, next_side, next_inner, across)[k]
        return moved(p, other, which, (pass_s, pass_r), (k, p), sib)

    for j in range(len(spans)):
        top = jnp.concatenate([top_row[:, 128 * j : 128 * (j + 1)]] * (width // 128), axis=1)
        scales[0, j : j + 1] = 127.0 / top
        scales[1, j : j + 1] = top / 127.0
    per_feed = width // piece

    def code(p, _):
        at = pl.ds(pl.multiple_of(p * piece, 16), piece)
        late = jnp.maximum(p - 4, 0)
        which = pl.ds(jnp.minimum(p, 4) + late // per_feed, 1)
        bank[t, at] = (stairs(flat[at] * scales[0, which]) * scales[1, which]).astype(BF16)
        far_copy(p).start()
        sib_copy(p).start()

        @pl.when(p == 2)
        def _():
            for first in range(3):
                direct_copy(first).start()

        pl.when(p == 3)(lambda: direct_copy(3).start())
        pl.when(p == pieces - 1)(lambda: direct_copy(pieces - 1).start())
        return 0

    lax.fori_loop(0, pieces, code, 0)
    xq_put = put(xq, xq_out)
    put(xs, xs_out)
    put(bank.at[t], bank_out.at[t])

    def far_step(*found):
        for p in found:
            far_copy(p).wait_recv()
            side_copy(p).start()
            inner_copy(p).start()
            pass_copy(0, p).start()

    def side_step(*found):
        for p in found:
            side_copy(p).wait_recv()
            if p not in DIRECT and p % 2 == 1:
                last_copy(p).start()
            pass_copy(1, p).start()
            inner_copy(p).wait_recv()
            if p not in DIRECT and p % 2 == 0:
                last_copy(p).start()
            pass_copy(2, p).start()

    def last_step(*found):
        for p in found:
            (direct_copy(p) if p in DIRECT else last_copy(p)).wait_recv()
            pass_copy(3, p).start()

    def arrived(own, p):
        if own:
            sib_copy(p).wait_recv()
        else:
            for k in range(4):
                pass_copy(k, p).wait_recv()

    def which_pair(turn):
        return pair + turn - 2 * pair * turn

    def shard_rows(turn, piece_at):
        first = 2 * which_pair(turn)
        at = pl.ds(pl.multiple_of(piece_at * cols, 16), cols)
        return jnp.concatenate([bank[first, at], bank[first + 1, at]], axis=0)

    def half_lanes(turn):
        return pl.ds(pl.multiple_of(which_pair(turn) * lanes_half, 128), lanes_half)

    lanes = lax.broadcasted_iota(jnp.int32, (QB, 128), 1) < HD

    def project(turn):
        first = 2 * which_pair(turn)
        at = half_lanes(turn)

        def one(j, _):
            row = pl.ds(1 + j // 2, 1)
            shift = jnp.concatenate([small[first + i, row, 0:cols] for i in range(2)], axis=1)
            value = dot_nt(xq[...], shard_rows(turn, j)) + jnp.where(j == 1, 0.0, shift)
            qkv[pl.ds(pl.multiple_of(j * tokens, QB), tokens), at] = value.astype(BF16)
            return 0

        lax.fori_loop(0, 3, one, 0)

    def attention(turn, row):
        half = which_pair(turn)
        base = pl.multiple_of(row * length, length)
        spot = pl.multiple_of(row * heads * length, length)
        jobs = [(k, b, head) for k in range(heads) for b in range(len(wins)) for head in range(2)]

        def lane(k):
            return pl.ds(pl.multiple_of((half * heads + k) * 128, 128), 128)

        def score(k, b, head):
            first, low, _ = wins[b]
            queries = qkv[pl.ds(base + first, QB), lane(k)].astype(F32) * 0.125
            inside = lanes if head == 0 else jnp.logical_not(lanes)
            chosen = jnp.where(inside, queries, 0.0).astype(BF16)
            return dot_nt(chosen, qkv[pl.ds(tokens + base + low, size), lane(k)]) + bias[row, b]

        def weigh(k, b, head, scores):
            weights = jnp.exp(scores - jnp.max(scores, -1, keepdims=True))
            share = 1.0 / jnp.sum(weights, -1, keepdims=True)
            low_probs = (weights * share).astype(BF16)
            rows = pl.ds(spot + k * length + wins[b][0], QB)
            probs[rows, head * size : (head + 1) * size] = low_probs
            return low_probs

        scores = [score(*job) for job in jobs]
        weights = [weigh(*job, value) for job, value in zip(jobs, scores)]
        results = []
        for (k, b, _), value in zip(jobs, weights):
            rows = pl.ds(2 * tokens + base + wins[b][1], size)
            results.append(dot_nn(value, qkv[rows, lane(k)]))
        for n in range(0, len(jobs), 2):
            k, b, _ = jobs[n]
            rows = pl.ds(base + wins[b][0], QB)
            coded, squash = quantize(jnp.where(lanes, results[n], results[n + 1]), ranges[1])
            cq[rows, lane(k)] = coded.astype(BF16)
            cs[rows, lane(k)] = (1.0 - squash * squash).astype(BF16)
        p_copy(turn, row).start()

    def p_copy(turn, row):
        spot = pl.multiple_of(row * heads * length, length)
        return pltpu.make_async_copy(
            probs.at[pl.ds(spot, heads * length)],
            p_out.at[row * 2 + which_pair(turn)],
            p_sem.at[row],
        )

    def one_turn(turn, _):
        @pl.when(turn == 0)
        def _():
            for p in range(3):
                arrived(True, p)

        @pl.when(turn == 1)
        def _():
            for p in range(3):
                arrived(False, p)

        project(turn)
        pl.when(turn == 0)(lambda: far_step(0))

        @pl.when(turn == 1)
        def _():
            far_step(4)
            last_step(3)

        def one_row(row, _):
            pl.when(turn == 1)(lambda: p_copy(0, row).wait())
            attention(turn, row)
            for at_turn, at_row, steps in (
                (0, 0, lambda: far_step(1, 2)),
                (0, 1, lambda: side_step(0)),
                (1, 0, lambda: [far_step(5, 6), side_step(3)] and None),
                (1, 1, lambda: [far_step(7), side_step(4)] and None),
            ):
                pl.when(jnp.logical_and(turn == at_turn, row == at_row))(steps)
            return 0

        lax.fori_loop(0, rows_here, one_row, 0)

        @pl.when(turn == 0)
        def _():
            arrived(True, 3)

            def own_attn(b, _):
                rows = pl.ds(pl.multiple_of(b * 2 * QB, QB), 2 * QB)
                total[rows] = dot_nn(cq[rows, half_lanes(0)], shard_rows(0, 3))
                return 0

            lax.fori_loop(0, blocks // 2, own_attn, 0)
            side_step(1)
            far_step(3)
            side_step(2)
            last_step(0, 1, 2)

        return 0

    lax.fori_loop(0, 2, one_turn, 0)
    qkv_puts = [
        put(qkv.at[j * tokens : (j + 1) * tokens], ref) for j, ref in enumerate((q_out, k_out, v_out))
    ]
    put(cq, cq_out)
    put(cs, cs_out)
    arrived(False, 3)

    def norm_block(b, _):
        rows = pl.ds(pl.multiple_of(b * QB, QB), QB)
        attn = total[rows] + dot_nn(cq[rows, half_lanes(1)], shard_rows(1, 3))
        normed, inverse = norm(x[rows] + (attn + shifts[0:1]))
        xh[rows] = normed
        inv[rows] = jnp.broadcast_to(inverse, (QB, 128))
        nq[rows] = quantize(normed * gains[0:1] + shifts[1:2], ranges[2])[0].astype(BF16)
        pl.when(b == 0)(lambda: far_step(8))
        pl.when(b == 1)(lambda: side_step(5))
        pl.when(b == 2)(lambda: side_step(6))
        pl.when(b == 3)(lambda: far_step(9))
        return 0

    lax.fori_loop(0, blocks, norm_block, 0)
    xh_put = put(xh, xh_out)
    put(inv, inv_out)
    nq_put = put(nq, nq_out)
    cot_load = load(6, cot_hbm.at[mine], x)

    for row in range(rows_here):
        p_copy(1, row).wait()
    for copy in qkv_puts:
        copy.wait()

    def spread(i, begin, count):
        shard = (2 * pair + i) % 4
        shift = small[shard, 0:1, 0:hidden]
        places = [pl.multiple_of((begin + b) * QB, QB) for b in range(count)]
        pres = [dot_nn(nq[pl.ds(at, QB)], bank[shard, feed_1:feed_2]) + shift for at in places]
        codes = []
        for at, pre in zip(places, pres):
            cdf = 0.5 * (1.0 + lax.erf(pre * ROOT_HALF))
            coded, squash = quantize(pre * cdf, ranges[3])
            slope = cdf + pre * jnp.exp(-0.5 * pre * pre) * INV_ROOT_TWO_PI
            coded = coded.astype(BF16)
            rows = pl.ds(i % 3 * tokens + at, QB)
            probs[rows] = ((1.0 - squash * squash) * slope).astype(BF16)
            qkv[rows] = coded
            codes.append(coded)
        return codes

    def put_slopes(i):
        at = i % 3 * tokens
        return put(probs.at[at : at + tokens], factor_out.at[i])

    def gather(i, code):
        shard = (2 * pair + i) % 4
        return dot_nn(code, bank[shard, feed_2 : feed_2 + hidden])

    for p in range(4, pieces):
        arrived(True, p)
    put(bank.at[flip(t, 1)], bank_out.at[flip(t, 1)])
    slope_puts, code_puts = [], []

    half_way = blocks // 2
    flat[0:tokens] = jnp.zeros((tokens, width), F32)
    slope_puts, code_puts = [], []

    def own_part(n, _):
        i, begin = n // 2, n % 2 * half_way
        for b, code in enumerate(spread(i, begin, half_way)):
            flat[pl.ds(pl.multiple_of((begin + b) * QB, QB), QB)] += gather(i, code)

        @pl.when(n == 0)
        def _():
            far_step(10)
            side_step(7)
            last_step(4)

        @pl.when(n == 1)
        def _():
            far_step(11)
            side_step(8)
            last_step(5)

        @pl.when(n == 2)
        def _():
            side_step(9)
            last_step(6, 7)

        return 0

    lax.fori_loop(0, 4, own_part, 0)
    side_step(10, 11)
    last_step(8, 11)
    for i in range(2):
        slope_puts.append(put_slopes(i))
        code_puts.append(put(qkv.at[i * tokens : (i + 1) * tokens], gq_out.at[i]))
    for p in range(4, 8):
        arrived(False, p)
    for i in range(2):
        shard = (2 * pair + 2 + i) % 4
        put(bank.at[shard, 0:feed_2], bank_out.at[shard, 0:feed_2])
    slope_puts[0].wait()
    code_puts[0].wait()

    def other_part(n, _):
        spread(2 + n // 2, n % 2 * half_way, half_way)
        pl.when(n == 1)(lambda: last_step(9))
        return 0

    lax.fori_loop(0, 4, other_part, 0)
    put_slopes(2)
    put_slopes(3)
    last_step(10)
    for p in range(8, pieces):
        arrived(False, p)
    for i in range(2):
        shard = (2 * pair + 2 + i) % 4
        put(bank.at[shard, feed_2 : feed_2 + hidden], bank_out.at[shard, feed_2 : feed_2 + hidden])
    def close(n, _):
        for b in range(2):
            at = pl.multiple_of((2 * n + b) * QB, QB)
            found = [qkv[pl.ds(i % 3 * tokens + at, QB)] for i in (2, 3)]
            flat[pl.ds(tokens + at, QB)] = gather(2, found[0]) + gather(3, found[1])
        return 0

    lax.fori_loop(0, half_way, close, 0)

    cot_load.wait()
    xq_put.wait()
    xh_put.wait()
    nq_put.wait()
    sums_out[...] = jnp.zeros_like(sums_out)

    def ends(b):
        rows = pl.ds(pl.multiple_of(b * QB, QB), QB)
        there = pl.ds(pl.multiple_of(c * tokens + b * QB, QB), QB)
        local = [
            pltpu.make_async_copy(src.at[rows], dst, end_sem.at[k, b])
            for k, (src, dst) in enumerate(
                ((xq, lo_out.at[there]), (total, dh2_out.at[rows]), (nq, do_out.at[rows]))
            )
        ]
        remote = pltpu.make_async_remote_copy(
            src_ref=xq.at[rows], dst_ref=lo_out.at[there], send_sem=lo_s.at[b], recv_sem=lo_r.at[b],
            device_id=sib, device_id_type=MESH,
        )
        return local + [remote]

    def last_block(b, _):
        rows = pl.ds(pl.multiple_of(b * QB, QB), QB)
        first = xh[rows] * gains[0:1] + shifts[1:2]
        feed = flat[rows] + flat[pl.ds(pl.multiple_of(tokens + b * QB, QB), QB)]
        normed, inverse = norm(first + (feed + shifts[2:3]))
        xq[rows] = (normed * gains[1:2] + shifts[3:4]).astype(BF16)
        grad = x[rows]
        back = norm_back(grad * gains[1:2], normed, inverse)
        total[rows] = back
        nq[rows] = back.astype(BF16)
        for copy in ends(b):
            copy.start()
        sums_out[1:2] += jnp.sum(grad * normed, 0, keepdims=True)
        sums_out[4:5] += jnp.sum(back, 0, keepdims=True)
        sums_out[5:6] += jnp.sum(grad, 0, keepdims=True)
        return 0

    lax.fori_loop(0, blocks, last_block, 0)

    def sent(p, _):
        far_copy(p).wait_send()
        sib_copy(p).wait_send()
        side_copy(p).wait_send()
        inner_copy(p).wait_send()
        for k in range(4):
            pass_copy(k, p).wait_send()
        return 0

    lax.fori_loop(0, pieces, sent, 0)
    for p in range(pieces):
        (direct_copy(p) if p in DIRECT else last_copy(p)).wait_send()
    waited = [xq_put, xh_put, nq_put] + qkv_puts + [slope_puts[0], code_puts[0]]
    for copy in outs:
        if not any(copy is other_copy for other_copy in waited):
            copy.wait()
    for b in range(blocks):
        for copy in ends(b):
            copy.wait()


def forward(inputs, segment_ids, w_qkv, b_qv, w_out, w_ff1, b_ff1, w_ff2, gains, shifts, ranges, cotangent):
    cols, width = w_out.shape
    hidden = w_ff1.shape[1]
    rows, length = segment_ids.shape
    tokens = inputs.shape[0] // 2
    size = windows(length)[0][2]
    bank_rows = 4 * cols + width + hidden
    pieces = bank_rows // cols
    dma = pltpu.SemaphoreType.DMA
    low = lambda *shape: pltpu.VMEM(shape, BF16)
    full = lambda *shape: pltpu.VMEM(shape, F32)
    wide = S((tokens, width), BF16)
    deep = S((tokens, width), F32)
    return pl.pallas_call(
        forward_kernel,
        out_shape=(
            S((4, bank_rows, width), BF16),
            S((6,), F32),
            wide, wide, wide, wide, wide,
            S((rows, width // 256 * length, 2 * size), BF16),
            wide, wide, wide, deep,
            S((tokens, 128), F32),
            S((2 * tokens, width), BF16),
            S((2, tokens, hidden), BF16),
            S((4, tokens, hidden), BF16),
            deep, wide,
            S((8, width), F32),
        ),
        in_specs=[ANY] * 4 + [VMEM] * 2 + [ANY] * 2 + [VMEM] * 3 + [SMEM],
        out_specs=(ANY, SMEM) + (ANY,) * 16 + (VMEM,),
        scratch_shapes=[
            low(4, bank_rows, width),
            full(max(bank_rows, 2 * tokens), width),
            full(tokens, width),
            low(tokens, width),
            low(tokens, width),
            low(3 * tokens, width),
            low(max(rows // 2 * (width // 256) * length, 3 * tokens), 2 * size),
            low(tokens, width),
            low(tokens, width),
            full(tokens, width),
            full(tokens // length, length // QB, QB, size),
            full(tokens, width),
            low(tokens, width),
            full(tokens, 128),
            full(4, 8, width),
            full(2, 8, width),
            dma((7,)), dma((24,)), dma((rows // 2,)), dma((3, tokens // QB)),
            dma((tokens // QB,)), dma((tokens // QB,)), dma((3,)), dma((3,)),
            *[dma((pieces,))] * 12,
            dma((4, pieces)), dma((4, pieces)),
        ],
        compiler_params=pltpu.CompilerParams(
            collective_id=1, has_side_effects=True, vmem_limit_bytes=62 * MIB
        ),
        name="forward",
    )(
        jnp.swapaxes(w_qkv, 1, 2), w_out, w_ff1, w_ff2, b_qv, b_ff1, inputs, cotangent,
        segment_ids, gains, shifts, ranges,
    )


GROUP = 192
QUARTER = GROUP // 4
HOPS = ("core", "y", "z1", "z2", "z3", "ag")
LINE_HOPS = ("zs1", "zs2", "zy", "zb1", "zb2", "zb3")


def sum_scratch(groups, width, extra, small_shape):
    count = max(extra, 1)
    dma = pltpu.SemaphoreType.DMA
    buf = lambda *shape: pltpu.VMEM(shape + (width,), BF16)
    kinds = dict(
        own=buf(groups * GROUP), got_y=buf(groups, QUARTER), part=buf(groups, QUARTER),
        got_1=buf(groups, QUARTER), got_2=buf(groups, QUARTER), got_x=buf(count, 2, QUARTER),
        line_1=buf(groups, 2, QUARTER), line_2=buf(groups, 2, QUARTER), line_y=buf(groups, 2, QUARTER),
        line_x=buf(count, 2, 2, QUARTER),
        small_own=pltpu.VMEM(small_shape, F32), small_got=pltpu.VMEM((5 + extra,) + small_shape, F32),
        x_s=dma((count, groups)), x_r=dma((count, groups)),
        lx_s=dma((count, groups, 2)), lx_r=dma((count, groups, 2)),
        small_s=dma((5 + extra,)), small_r=dma((5 + extra,)),
    )
    for hop in HOPS:
        kinds[hop + "_s"], kinds[hop + "_r"] = dma((groups,)), dma((groups,))
    for hop in LINE_HOPS:
        kinds[hop + "_s"], kinds[hop + "_r"] = dma((groups, 2)), dma((groups, 2))
    return list(kinds), list(kinds.values())


TICKS = (
    ((0, 1),),
    ((0, 0), (0, 3), (0, 2), (1, 1)),
    ((1, 0),),
    ((2, 1),),
    ((1, 3),),
    ((3, 1), (2, 0), (0, 7), (0, 5), (1, 2), (0, 6)),
    ((2, 3), (0, 4), (1, 5), (4, 1)),
    ((3, 0), (2, 2)),
    ((3, 3), (1, 6), (5, 1)),
    ((2, 5), (4, 0)),
    ((3, 2), (1, 4), (0, 8), (4, 3)),
    ((2, 6),),
    ((3, 5), (5, 0), (1, 8)),
    ((4, 2),),
    ((5, 3), (2, 4)),
    ((3, 6), (1, 7), (4, 5)),
    ((2, 8), (5, 2)),
    (
        (0, 11), (3, 4), (4, 6), (2, 7), (5, 5), (6, 1), (6, 0), (0, 10),
        (1, 11), (3, 8), (0, 9), (1, 10), (4, 4),
    ),
    ((2, 11), (3, 7), (5, 6)),
    ((4, 8), (1, 9)),
    ((5, 4), (2, 10)),
    ((3, 11), (4, 7)),
    (),
    ((2, 9), (5, 8)),
    ((4, 11), (6, 5), (3, 10), (5, 7)),
    (),
    (
        (5, 11), (3, 9), (4, 10), (6, 11), (4, 9), (5, 10), (6, 7), (6, 4),
        (6, 3), (6, 6), (5, 9), (6, 2), (6, 10), (6, 8), (6, 9),
    ),
)


class GradientSum:
    def __init__(self, extra, mine, theirs, result, refs):
        self.__dict__.update(refs)
        self.extra, self.mine, self.theirs, self.result = extra, mine, theirs, result
        t, d = lax.axis_index("tensor"), lax.axis_index("dp")
        self.y = d % 2
        self.z = (d // 2) % 4
        self.end = jnp.logical_or(self.z == 0, self.z == 3)
        self.middle = jnp.logical_not(self.end)
        self.sib = (d, flip(t, 1))
        self.side = (flip(d, 1), t)
        self.inner = (flip(d, 2), t)
        self.across = (d + 2 * (3 - 2 * self.z), t)
        self.others = [(flip(d, 8 << b), t) for b in range(extra)]
        self.beyond = [self.across] + self.others
        self.groups = self.own.shape[0] // GROUP

    def announce(self):
        barrier = pltpu.get_barrier_semaphore()

        def tell(peers):
            for peer in peers:
                pl.semaphore_signal(barrier, inc=1, device_id=peer, device_id_type=MESH)

        tell([self.sib, self.side, self.inner])
        pl.when(self.middle)(lambda: tell(self.beyond))

    def meet(self):
        barrier = pltpu.get_barrier_semaphore()
        pl.when(self.end)(lambda: pl.semaphore_wait(barrier, 3))
        pl.when(self.middle)(lambda: pl.semaphore_wait(barrier, 3 + len(self.beyond)))

    def remote(self, src, dst, hop, at, to):
        return pltpu.make_async_remote_copy(
            src_ref=src, dst_ref=dst, send_sem=getattr(self, hop + "_s").at[at],
            recv_sem=getattr(self, hop + "_r").at[at], device_id=to, device_id_type=MESH,
        )

    def small(self, i, to):
        return self.remote(self.small_own, self.small_got.at[i], "small", i, to)

    def small_add(self, i, to):
        self.small(i, to).wait()
        self.small_own[...] = self.small_own[...] + self.small_got[i]

    def small_step(self, step):
        if step == 0:
            self.small(0, self.sib).start()
        if step == 1:
            self.small_add(0, self.sib)
            self.small(1, self.side).start()
        if step == 2:
            self.small_add(1, self.side)
            pl.when(self.end)(lambda: self.small(2, self.inner).start())
        if step == 3:

            def inward():
                self.small(2, self.inner).wait_recv()
                self.small_own[...] = self.small_own[...] + self.small_got[2]
                self.small(3, self.across).start()

            pl.when(self.middle)(inward)
        if step == 4:

            def outward():
                self.small_add(3, self.across)
                for b, peer in enumerate(self.others):
                    self.small(5 + b, peer).start()
                    self.small_add(5 + b, peer)
                self.small(4, self.inner).start()

            pl.when(self.middle)(outward)
        if step == 5:

            def received():
                self.small(2, self.inner).wait_send()
                self.small(4, self.inner).wait_recv()
                self.small_own[...] = self.small_got[4]

            pl.when(self.end)(received)
            pl.when(self.middle)(lambda: self.small(4, self.inner).wait_send())

    def span(self, g):
        return pl.ds(pl.multiple_of(g * GROUP, 16), GROUP)

    def half(self, g, which):
        return pl.ds(pl.multiple_of(g * GROUP + which * QUARTER, 16), QUARTER)

    def line(self, g, i):
        return pl.ds(pl.multiple_of(g * GROUP + (2 + i) * QUARTER, 16), QUARTER)

    def core(self, g):
        return self.remote(self.theirs.at[self.span(g)], self.own.at[self.span(g)], "core", g, self.sib)

    def hop(self, name, g):
        if name == "y":
            return self.remote(self.own.at[self.half(g, 1 - self.y)], self.got_y.at[g], "y", g, self.side)
        if name == "z1":
            return self.remote(self.part.at[g], self.got_1.at[g], "z1", g, self.inner)
        if name == "z2":
            return self.remote(self.part.at[g], self.got_2.at[g], "z2", g, self.across)
        there = self.result.at[self.half(g, self.y)]
        return self.remote(there, there, name, g, self.inner if name == "z3" else self.side)

    def line_hop(self, name, g, i):
        mine = self.own.at[self.line(g, i)]
        if name == "zs1":
            return self.remote(mine, self.line_1.at[g, i], name, (g, i), self.inner)
        if name == "zs2":
            return self.remote(mine, self.line_2.at[g, i], name, (g, i), self.across)
        if name == "zy":
            return self.remote(mine, self.line_y.at[g, i], name, (g, i), self.side)
        there = self.result.at[self.line(g, i)]
        return self.remote(there, there, name, (g, i), self.across if name == "zb2" else self.inner)

    def stage(self, s, g):
        add = lambda a, b: (a.astype(F32) + b.astype(F32)).astype(BF16)
        when = lambda condition, body: pl.when(condition)(body)
        root = [self.z == 1, self.z == 2]
        passer = [self.z == 2, self.z == 1]
        near = [self.z == 0, self.z == 3]
        far = [self.z == 3, self.z == 0]
        if s == 0:
            self.core(g).start()
        if s == 1:
            self.core(g).wait()

            def add_rows(n, _):
                rows = pl.ds(pl.multiple_of(g * GROUP + n * QUARTER, 16), QUARTER)
                self.own[rows] = add(self.own[rows], self.mine[rows])
                return 0

            lax.fori_loop(0, 4, add_rows, 0)
            self.hop("y", g).start()
            when(self.end, lambda: [self.line_hop("zs1", g, i).start() for i in range(2)] and None)
        if s == 2:
            self.hop("y", g).wait()
            self.part[g] = add(self.own[self.half(g, self.y)], self.got_y[g])
            when(self.end, lambda: self.hop("z1", g).start())
            for i in range(2):

                def gather(i=i):
                    self.line_hop("zs1", g, i).wait_recv()
                    rows = self.line(g, i)
                    self.own[rows] = add(self.own[rows], self.line_1[g, i])
                    when(passer[i], lambda: self.line_hop("zs2", g, i).start())

                when(self.middle, gather)
        if s == 3:

            def middle():
                self.hop("z1", g).wait_recv()
                self.part[g] = add(self.part[g], self.got_1[g])
                self.hop("z2", g).start()

            when(self.middle, middle)
            for i in range(2):

                def at_root(i=i):
                    self.line_hop("zs2", g, i).wait_recv()
                    rows = self.line(g, i)
                    self.own[rows] = add(self.own[rows], self.line_2[g, i])
                    self.line_hop("zy", g, i).start()

                when(root[i], at_root)
        if s == 4:

            def total():
                self.hop("z2", g).wait()
                self.part[g] = add(self.part[g], self.got_2[g])
                for b in range(self.extra):
                    copy = self.remote(self.part.at[g], self.got_x.at[b, g % 2], "x", (b, g), self.others[b])
                    copy.start()
                    copy.wait()
                    self.part[g] = add(self.part[g], self.got_x[b, g % 2])
                self.result[self.half(g, self.y)] = self.part[g]
                self.hop("ag", g).start()
                self.hop("z3", g).start()

            when(self.middle, total)
            for i in range(2):

                def spread(i=i):
                    self.line_hop("zy", g, i).wait()
                    rows = self.line(g, i)
                    self.own[rows] = add(self.own[rows], self.line_y[g, i])
                    for b in range(self.extra):
                        copy = self.remote(
                            self.own.at[rows], self.line_x.at[b, g % 2, i], "lx", (b, g, i), self.others[b]
                        )
                        copy.start()
                        copy.wait()
                        self.own[rows] = add(self.own[rows], self.line_x[b, g % 2, i])
                    self.result[rows] = self.own[rows]
                    self.line_hop("zb2", g, i).start()
                    self.line_hop("zb1", g, i).start()

                when(root[i], spread)
        if s == 5:

            def outer():
                self.hop("z3", g).wait_recv()
                self.hop("ag", g).start()

            when(self.end, outer)
            for i in range(2):

                def onward(i=i):
                    self.line_hop("zb2", g, i).wait_recv()
                    self.line_hop("zb3", g, i).start()

                when(passer[i], onward)
        if s == 6:
            self.hop("ag", g).wait()
            for i in range(2):
                when(near[i], lambda i=i: self.line_hop("zb1", g, i).wait_recv())
                when(far[i], lambda i=i: self.line_hop("zb3", g, i).wait_recv())

                def sent_root(i=i):
                    self.line_hop("zb1", g, i).wait_send()
                    self.line_hop("zb2", g, i).wait_send()

                def sent_passer(i=i):
                    self.line_hop("zs2", g, i).wait_send()
                    self.line_hop("zb3", g, i).wait_send()

                when(root[i], sent_root)
                when(passer[i], sent_passer)

            def sent_end():
                self.hop("z1", g).wait_send()
                for i in range(2):
                    self.line_hop("zs1", g, i).wait_send()

            when(self.end, sent_end)
            when(self.middle, lambda: self.hop("z3", g).wait_send())

    def run(self, events):
        for stage, group in events:
            self.stage(stage, group)


def back_kernel(
    extra, names,
    do_hbm, gq_hbm, factor_hbm, nq_hbm, bank, dh2_hbm, xh_hbm, inv_hbm, sums_ref,
    cs_hbm, cq_hbm, q_hbm, k_hbm, v_hbm, p_hbm, xq_hbm, xs_hbm, gains, shifts, ranges,
    g2_out, g1_out, go_out, gq_out, gains_out, shifts_out, bqv_out, bff1_out, dx_full,
    result, inv, grads, do, weights, gq, factor, nq, low, total, dh, xh, wo, cq, dproj, sem, dx_send, dx_recv,
    *refs,
):
    t, d = lax.axis_index("tensor"), lax.axis_index("dp")
    c, pair = t % 2, t // 2
    engine = GradientSum(extra, grads.at[c], grads.at[1 - c], result, dict(zip(names, refs)))
    tokens, width = do.shape
    hidden = gq_hbm.shape[2]
    side = width // 2
    cols = side // 2
    heads = width // 128 // 2
    length = p_hbm.shape[1] // heads
    wins = windows(length)
    size = wins[0][2]
    blocks = tokens // QB
    slots = factor.shape[0] // length

    def load(i, src, dst):
        copy = pltpu.make_async_copy(src, dst, sem.at[i])
        copy.start()
        return copy

    def shard_at(i):
        return (2 * pair + i) % 4

    def load_codes(begin, end, sems):
        return [
            load(sems[i], gq_hbm.at[i, :, begin:end], gq.at[i * tokens : (i + 1) * tokens, begin:end])
            for i in range(2)
        ]

    half_way = hidden // 2
    first_loads = [load(0, do_hbm, do)] + load_codes(0, half_way, (1, 2))

    def load_pair(base):
        copies = []
        for i in range(2):
            s = shard_at(base + i)
            at = pl.ds(i * tokens, tokens)
            for j in range(2):
                spot = weights.at[(2 * j + i) * width : (2 * j + i + 1) * width]
                copies.append(load(3 + 2 * j + i, bank.at[s, 4 * cols + j * width : 4 * cols + (j + 1) * width], spot))
            copies.append(load(7 + i, factor_hbm.at[base + i], factor.at[at]))
        return copies

    engine.announce()
    at = pl.ds(pl.multiple_of(c * tokens, 256), tokens)
    engine.small_own[...] = jnp.zeros_like(engine.small_own)
    engine.small_own[0:8] = sums_ref[...]

    def tick(point):
        engine.run(TICKS[point])

    for copy in first_loads:
        copy.wait()
    code_loads = load_codes(half_way, hidden, (12, 14))
    pair_loads = load_pair(0)

    def weights_2(n, _):
        part, i = n // 2, n % 2
        lanes = pl.ds(pl.multiple_of(part * half_way, 128), half_way)
        value = dot_tn(gq[pl.ds(pl.multiple_of(i * tokens, QB), tokens), lanes], do[...])
        grads[i, pl.ds(pl.multiple_of(part * half_way, 16), half_way)] = value.astype(BF16)

        @pl.when(n == 1)
        def _():
            engine.meet()
            tick(0)
            for copy in code_loads:
                copy.wait()

        return 0

    lax.fori_loop(0, 4, weights_2, 0)
    tick(1)
    for copy in pair_loads:
        copy.wait()
    nq_load = load(9, nq_hbm, nq)
    norm_loads = [load(10, dh2_hbm, dh), load(11, xh_hbm, xh), load(15, inv_hbm, inv)]

    def feed_blocks(own, first, second):
        def one(n, _):
            places = [pl.multiple_of((2 * n + b) * QB, QB) for b in range(2)]
            backs = [
                [
                    dot_nt(do[pl.ds(at, QB)], weights[(2 + i) * width : (3 + i) * width])
                    for i in range(2)
                ]
                for at in places
            ]
            lows = []
            for at, pairs in zip(places, backs):
                lows.append([])
                for i in range(2):
                    spot = pl.ds(i * tokens + at, QB)
                    value = pairs[i] * factor[spot].astype(F32)
                    short = value.astype(BF16)
                    if own:
                        engine.small_own[6 + i : 7 + i] += jnp.sum(value, 0, keepdims=True)
                        low[spot] = short
                    lows[-1].append(short)
            for at, (one_low, two_low) in zip(places, lows):
                rows = pl.ds(at, QB)
                part = dot_nt(one_low, weights[0:width]) + dot_nt(two_low, weights[width : 2 * width])
                total[rows] = part if own else total[rows] + part
            pl.when(n == 0)(functools.partial(tick, first))
            return 0

        lax.fori_loop(0, blocks // 2, one, 0)
        if second is not None:
            tick(second)

    feed_blocks(True, 2, 3)
    pair_loads = load_pair(2)
    nq_load.wait()

    def weights_1(i, _):
        part = dot_tn(nq[...], low[pl.ds(pl.multiple_of(i * tokens, QB), tokens)])
        grads[i, hidden : 2 * hidden] = part.astype(BF16)
        pl.when(i == 0)(functools.partial(tick, 4))
        return 0

    lax.fori_loop(0, 2, weights_1, 0)
    tick(5)
    for copy in pair_loads:
        copy.wait()
    wo_loads = [
        load(27 + s, bank.at[s, 3 * cols : 4 * cols], wo.at[s * cols : (s + 1) * cols]) for s in range(4)
    ]
    mine = pl.ds(pl.multiple_of(pair * side, 128), side)
    cq_load = load(13, cq_hbm.at[:, mine], cq)
    cs_load = load(9, cs_hbm, nq)
    feed_blocks(False, 6, None)
    qkv_loads = [
        load(18 + j, src, weights.at[j * tokens : (j + 1) * tokens])
        for j, src in enumerate((q_hbm, k_hbm, v_hbm))
    ]

    def unit_at(own, u):
        return u // heads, u % heads

    def probs_load(own, u):
        row, which = unit_at(own, u)
        slot = u % slots
        return pltpu.make_async_copy(
            p_hbm.at[row * 2 + (pair if own else 1 - pair), pl.ds(pl.multiple_of(which * length, length), length)],
            factor.at[pl.ds(pl.multiple_of(slot * length, length), length)],
            sem.at[22 + slot],
        )

    units = 2 * heads
    for u in range(slots - 1):
        probs_load(True, u).start()
    tick(7)

    for copy in norm_loads:
        copy.wait()
    xq_load = load(17, xq_hbm, low.at[tokens : 2 * tokens])
    wt_loads = [
        load(31 + s, bank.at[s, 0 : 3 * cols], gq.at[3 * s * cols : 3 * (s + 1) * cols]) for s in range(4)
    ]
    xs_load = load(21, xs_hbm, do)

    def norm_block(b, _):
        rows = pl.ds(pl.multiple_of(b * QB, QB), QB)
        normed = xh[rows]
        squash = jnp.tanh((normed * gains[0:1] + shifts[1:2]) * (1.0 / ranges[2]))
        grad = dh[rows] + total[rows] * (1.0 - squash * squash)
        inverse = jnp.max(inv[rows], axis=1, keepdims=True)
        back = norm_back(grad * gains[0:1], normed, inverse)
        dh[rows] = back
        low[rows] = back.astype(BF16)
        engine.small_own[0:1] += jnp.sum(grad * normed, 0, keepdims=True)
        engine.small_own[2:3] += jnp.sum(back, 0, keepdims=True)
        engine.small_own[3:4] += jnp.sum(grad, 0, keepdims=True)
        return 0

    lax.fori_loop(0, blocks, norm_block, 0)
    tick(8)
    for copy in wo_loads:
        copy.wait()
    cq_load.wait()
    cs_load.wait()
    d_attn = low.at[0:tokens]
    part = dot_tn(cq[...], d_attn[...]).astype(BF16)
    for i in range(2):
        grads[i, 2 * hidden : 2 * hidden + cols] = part[i * cols : (i + 1) * cols]
    tick(9)

    def context_block(b, _):
        rows = pl.ds(pl.multiple_of(b * QB, QB), QB)
        nq[rows] = (dot_nt(d_attn[rows], wo[...]) * nq[rows].astype(F32)).astype(BF16)
        return 0

    lax.fori_loop(0, blocks, context_block, 0)
    tick(10)

    for copy in qkv_loads:
        copy.wait()
    lanes = lax.broadcasted_iota(jnp.int32, (QB, 128), 1) < HD

    def attention(own, u):
        row, which = unit_at(own, u)
        probs_load(own, u).wait()

        @pl.when(u + slots - 1 < units)
        def _():
            probs_load(own, u + slots - 1).start()

        half = pair if own else 1 - pair
        lane = pl.ds(pl.multiple_of((half * heads + which) * 128, 128), 128)
        here = pl.ds(pl.multiple_of(which * 128, 128), 128)
        slot = pl.multiple_of((u % slots) * length, length)
        base = pl.multiple_of(row * length, length)
        wide = lax.broadcasted_iota(jnp.int32, (size, 128), 1) < HD
        jobs = [(b, head) for b in range(len(wins)) for head in range(2)]

        def shares(b, head):
            return factor[pl.ds(slot + wins[b][0], QB), head * size : (head + 1) * size]

        def first_product(b, head):
            first, begin, _ = wins[b]
            own_lanes = lanes if head == 0 else jnp.logical_not(lanes)
            context = nq[pl.ds(base + first, QB), lane].astype(F32)
            chosen = jnp.where(own_lanes, context, 0.0).astype(BF16)
            return dot_nt(chosen, weights[pl.ds(2 * tokens + base + begin, size), lane])

        def d_score(b, head, d_probs):
            exact = shares(b, head).astype(F32)
            both = exact * d_probs
            return (both - exact * jnp.sum(both, -1, keepdims=True)).astype(BF16)

        def products(b, head, d_low):
            first, begin, _ = wins[b]
            rows = pl.ds(base + first, QB)
            return (
                dot_nn(d_low, weights[pl.ds(tokens + base + begin, size), lane]),
                dot_tn(d_low, weights[rows, lane]),
                dot_tn(shares(b, head), nq[rows, lane]),
            )

        d_probs = [first_product(*job) for job in jobs]
        d_lows = [d_score(*job, value) for job, value in zip(jobs, d_probs)]
        found = [products(*job, value) for job, value in zip(jobs, d_lows)]
        d_keys, d_values = [], []
        for b, (first, _, _) in enumerate(wins):
            got = found[2 * b : 2 * b + 2]
            rows = pl.ds(base + first, QB)
            dproj[0, rows, here] = (jnp.where(lanes, got[0][0], got[1][0]) * 0.125).astype(BF16)
            d_keys.append(jnp.where(wide, got[0][1], got[1][1]))
            d_values.append(jnp.where(wide, got[0][2], got[1][2]))
        for j, parts, scale in ((1, d_keys, 0.125), (2, d_values, 1.0)):
            for spot in range(0, length, SPAN):
                terms = [
                    part[spot - begin : spot - begin + SPAN]
                    for part, (_, begin, _) in zip(parts, wins)
                    if begin <= spot < begin + size
                ]
                dproj[j, pl.ds(base + spot, SPAN), here] = (sum(terms[1:], terms[0]) * scale).astype(BF16)

    def back_through(own, finish):
        first = 2 * pair if own else 2 - 2 * pair

        def rows(j):
            found = [
                gq[pl.ds(pl.multiple_of(((first + i) * 3 + j) * cols, 16), cols)] for i in range(2)
            ]
            return jnp.concatenate(found, axis=0)

        def block(n, _):
            at = pl.ds(pl.multiple_of(n * QB, QB), QB)
            terms = [dot_nn(dproj[j, at], rows(j)) for j in range(3)]
            finish(at, terms[0] + terms[1] + terms[2])
            return 0

        lax.fori_loop(0, blocks, block, 0)

    def ticks_after(u, first):
        for k in range(units):
            if TICKS[first + k]:
                pl.when(u == k)(functools.partial(tick, first + k))

    def own_unit(u, _):
        attention(True, u)
        ticks_after(u, 11)
        return 0

    lax.fori_loop(0, units, own_unit, 0)
    for u in range(slots - 1):
        probs_load(False, u).start()
    for copy in wt_loads:
        copy.wait()
    xq_load.wait()
    def weights_qkv(j, _):
        part = dot_tn(dproj[j], low[tokens : 2 * tokens]).astype(BF16)
        at = pl.ds(pl.multiple_of(2 * hidden + (j + 1) * cols, 16), cols)
        for i in range(2):
            grads[i, at] = part[i * cols : (i + 1) * cols]
        return 0

    lax.fori_loop(0, 3, weights_qkv, 0)
    engine.small_own[8:9, 0:side] = jnp.sum(dproj[0].astype(F32), 0, keepdims=True)
    engine.small_own[9:10, 0:side] = jnp.sum(dproj[2].astype(F32), 0, keepdims=True)
    tick(17)
    engine.small_step(0)

    def keep(rows, value):
        total[rows] = value

    back_through(True, keep)
    tick(18)

    def other_unit(u, _):
        attention(False, u)
        ticks_after(u, 19)
        for k, step in ((0, 1), (3, 2)):
            pl.when(u == k)(functools.partial(engine.small_step, step))
        return 0

    lax.fori_loop(0, units, other_unit, 0)
    xs_load.wait()

    def results(rows, value):
        factor[rows] = (dh[rows] + (total[rows] + value) * do[rows].astype(F32)).astype(BF16)

    back_through(False, results)
    dx_copy = pltpu.make_async_remote_copy(
        src_ref=factor.at[0:tokens], dst_ref=dx_full.at[at], send_sem=dx_send, recv_sem=dx_recv,
        device_id=engine.sib, device_id_type=MESH,
    )
    dx_copy.start()
    outs = [load(26, factor.at[0:tokens], dx_full.at[at])]
    tick(25)
    engine.small_step(3)

    def small_results():
        engine.small_step(5)
        sums = engine.small_own[...]
        here = sums[:, 0:cols]
        for s in range(1, 4):
            here = jnp.where(t == s, sums[:, s * cols : (s + 1) * cols], here)
        gains_out[...] = here[0:2]
        shifts_out[...] = here[2:6]
        bqv_out[...] = jnp.where(c == 0, sums[8:10, 0:cols], sums[8:10, cols:side])
        bff1_out[...] = jnp.where(c == 0, sums[6:7], sums[7:8]).reshape(hidden)

    leaving = [
        (0, 4, g2_out, 0, hidden),
        (4, 8, g1_out, hidden, 2 * hidden),
        (8, 9, go_out, 2 * hidden, 2 * hidden + cols),
        (9, 12, gq_out, 2 * hidden + cols, 2 * hidden + 4 * cols),
    ]
    complete = {g for events in TICKS[:-1] for s, g in events if s == 6}
    for n, event in enumerate((None,) + TICKS[-1]):
        if n == 4:
            engine.small_step(4)
        if n == 10:
            small_results()
        if event is not None:
            engine.stage(*event)
            if event[0] == 6:
                complete.add(event[1])
        for k, (first, last, ref, begin, end) in enumerate(leaving):
            if ref is not None and complete.issuperset(range(first, last)):
                outs.append(load(k, result.at[begin:end], ref))
                leaving[k] = (first, last, None, begin, end)
    dx_copy.wait()
    for copy in outs:
        copy.wait()


def back(
    nd, do, gq, factor, nq, bank, dh2, xh, inv, sums, cs, cq, q, k, v, probs, xq, xs,
    gains, shifts, ranges,
):
    tokens, width = do.shape
    hidden = gq.shape[2]
    cols = width // 4
    rows = 2 * hidden + 4 * cols
    extra = (nd // 8).bit_length() - 1
    dma = pltpu.SemaphoreType.DMA
    names, scratch = sum_scratch(rows // GROUP, width, extra, (16, width))
    buf = lambda *shape: pltpu.VMEM(shape, BF16)
    return pl.pallas_call(
        functools.partial(back_kernel, extra, names),
        out_shape=(
            S((hidden, width), BF16),
            S((width, hidden), BF16),
            S((cols, width), BF16),
            S((3 * cols, width), BF16),
            S((2, cols), F32),
            S((4, cols), F32),
            S((2, cols), F32),
            S((hidden,), F32),
            S((2 * tokens, width), BF16),
        ),
        in_specs=[ANY] * 8 + [VMEM] + [ANY] * 8 + [VMEM, VMEM, SMEM],
        out_specs=(ANY,) * 4 + (VMEM,) * 4 + (ANY,),
        scratch_shapes=[
            buf(rows, width),
            pltpu.VMEM((tokens, 128), F32),
            buf(2, rows, width),
            buf(tokens, width),
            buf(max(4 * width, 3 * tokens), width),
            buf(max(3 * width, 2 * tokens), width),
            buf(2 * tokens, width),
            buf(tokens, width),
            buf(2 * tokens, width),
            pltpu.VMEM((tokens, width), F32),
            pltpu.VMEM((tokens, width), F32),
            pltpu.VMEM((tokens, width), F32),
            buf(width, width),
            buf(tokens, width // 2),
            buf(3, tokens, width // 2),
            dma((35,)),
            dma,
            dma,
            *scratch,
        ],
        compiler_params=pltpu.CompilerParams(
            collective_id=2, has_side_effects=True, vmem_limit_bytes=62 * MIB
        ),
        name="back",
    )(
        do, gq, factor, nq, bank, dh2, xh, inv, sums, cs, cq, q, k, v, probs, xq, xs,
        gains, shifts, ranges,
    )


def finish_kernel(*refs):
    half = len(refs) // 2
    for src, dst in zip(refs[: half - 1], refs[half:-1]):
        dst[...] = src[...].astype(F32)
    for j in range(refs[-1].shape[0]):
        refs[-1][j] = refs[half - 1][j]


def finish(*arrays):
    steps = 8
    specs = []
    for array in arrays[:-1]:
        rows = array.shape[0]
        if array.ndim == 2 and rows % (16 * steps) == 0:
            specs.append(pl.BlockSpec((rows // steps, array.shape[1]), lambda i: (i, 0)))
        elif array.ndim == 2 and rows % (16 * steps // 2) == 0:
            specs.append(pl.BlockSpec((2 * rows // steps, array.shape[1]), lambda i: (i // 2, 0)))
        else:
            specs.append(pl.BlockSpec(array.shape, lambda i, n=array.ndim: (0,) * n))
    specs.append(SMEM)
    return pl.pallas_call(
        finish_kernel,
        out_shape=tuple(S(array.shape, F32) for array in arrays),
        grid=(steps,),
        in_specs=specs,
        out_specs=tuple(specs),
        compiler_params=pltpu.CompilerParams(vmem_limit_bytes=62 * MIB),
        name="finish",
    )(*arrays)


def per_device(
    nd, inputs, segment_ids, w_qkv, b_qv, w_out, w_ff1, b_ff1, w_ff2, norm_gains, shift_biases,
    act_ranges, cotangent,
):
    width = inputs.shape[1]
    cols = w_qkv.shape[2]
    (
        bank, weight_max, xq, xs, q, k, v, probs, cq, cs, nq, xh, inv, layer_out, gq, factor, dh2, do,
        sums,
    ) = forward(
        inputs, segment_ids, w_qkv, b_qv, w_out, w_ff1, b_ff1, w_ff2, norm_gains, shift_biases,
        act_ranges, cotangent,
    )
    (
        grad_ff2, grad_ff1, grad_out, grad_qkv, grad_gains, grad_shifts, grad_bqv, grad_bff1, input_grad,
    ) = back(
        nd, do, gq, factor, nq, bank, dh2, xh, inv, sums, cs, cq, q, k, v, probs, xq, xs,
        norm_gains, shift_biases, act_ranges,
    )
    (
        layer_out, input_grad, grad_ff2, grad_ff1, grad_out, grad_qkv, grad_gains, grad_shifts, grad_bqv,
        grad_bff1, weight_max,
    ) = finish(
        layer_out, input_grad, grad_ff2, grad_ff1, grad_out, grad_qkv, grad_gains, grad_shifts, grad_bqv,
        grad_bff1, weight_max,
    )
    grad_qkv = grad_qkv.reshape(3, cols, width).transpose(0, 2, 1)
    return (
        layer_out, input_grad, grad_qkv, grad_bqv, grad_out, grad_ff1, grad_bff1, grad_ff2,
        grad_gains, grad_shifts, weight_max,
    )


def solution(mesh):
    return jax.shard_map(
        functools.partial(per_device, mesh.shape["dp"]),
        mesh=mesh,
        in_specs=(
            P("dp", None),
            P("dp", None),
            P(None, None, "tensor"),
            P(None, "tensor"),
            P("tensor", None),
            P(None, "tensor"),
            P("tensor"),
            P("tensor", None),
            P(),
            P(),
            P(),
            P("dp", None),
        ),
        out_specs=(
            P("dp", None),
            P("dp", None),
            P(None, None, "tensor"),
            P(None, "tensor"),
            P("tensor", None),
            P(None, "tensor"),
            P("tensor"),
            P("tensor", None),
            P(None, "tensor"),
            P(None, "tensor"),
            P(),
        ),
        check_vma=False,
    )
```

```python
import functools
import math

import jax
import jax.numpy as jnp
from jax import lax
from jax.experimental import pallas as pl
from jax.experimental.pallas import tpu as pltpu
from jax.sharding import PartitionSpec as P

HD = 64
SPAN = 128
QB = 256
MASKED = -1e30
EPSILON = 1e-06
ROOT_HALF = 0.7071067811865476
INV_ROOT_TWO_PI = 0.3989422804014327
STAIR = (
    6.579734980213376,
    -12.987641368031495,
    12.20087719668052,
    -6.61489684889321,
    2.04264519055443,
)
MIB = 1 << 20
MESH = pl.DeviceIdType.MESH
F32 = jnp.float32
BF16 = jnp.bfloat16
ANY = pl.BlockSpec(memory_space=pl.ANY)
VMEM = pl.BlockSpec(memory_space=pltpu.VMEM)
SMEM = pl.BlockSpec(memory_space=pltpu.SMEM)
S = jax.ShapeDtypeStruct


def flip(value, bit):
    return value + bit - 2 * bit * ((value // bit) % 2)


def dot_nn(left, right):
    return lax.dot_general(left, right, (((1,), (0,)), ((), ())), preferred_element_type=F32)


def dot_nt(left, right):
    return lax.dot_general(left, right, (((1,), (1,)), ((), ())), preferred_element_type=F32)


def dot_tn(left, right):
    return lax.dot_general(left, right, (((0,), (0,)), ((), ())), preferred_element_type=F32)


def stairs(levels):
    whole = jnp.round(levels)
    rest = levels - whole
    square = rest * rest
    curve = STAIR[4]
    for factor in STAIR[3::-1]:
        curve = curve * square + factor
    return whole + rest * square * curve


def quantize(values, bound):
    squash = jnp.tanh(values * (1.0 / bound))
    return stairs(127.0 * squash) * (bound / 127.0), squash


def norm(hidden):
    centred = hidden - jnp.mean(hidden, -1, keepdims=True)
    inverse = lax.rsqrt(jnp.mean(centred * centred, -1, keepdims=True) + EPSILON)
    return centred * inverse, inverse


def norm_back(scaled, normed, inverse):
    return inverse * (
        scaled
        - jnp.mean(scaled, -1, keepdims=True)
        - normed * jnp.mean(scaled * normed, -1, keepdims=True)
    )


def windows(length):
    found = []
    for first in range(0, length, QB):
        low = max(0, first - SPAN)
        found.append((first, low, min(length, first + QB + SPAN) - low))
    return found


DIRECT = (0, 1, 2, 3, 11)


def forward_kernel(
    wqkv, wout, wff1, wff2, bqv, bff1, x_hbm, cot_hbm, seg_ref, gains, shifts, ranges,
    bank_out, top_out, xq_out, xs_out, q_out, k_out, v_out, p_out, cq_out, cs_out, nq_out, xh_out,
    inv_out, lo_out, gq_out, factor_out, do_out, sums_out,
    bank, flat, x, xq, xs, qkv, probs, cq, cs, total, bias, xh, nq, inv, small, scales,
    sem, out_sem, p_sem, end_sem, lo_s, lo_r, small_s, small_r, sib_s, sib_r, far_s, far_r,
    direct_s, direct_r, side_s, side_r, inner_s, inner_r, last_s, last_r, pass_s, pass_r,
):
    t, d = lax.axis_index("tensor"), lax.axis_index("dp")
    c, pair, corner = t % 2, t // 2, d % 4
    sib, far, side, inner = (d, flip(t, 1)), (d, flip(t, 2)), (flip(d, 1), t), (flip(d, 2), t)
    diagonal = (d, flip(flip(t, 1), 2))
    cols, width = wout.shape
    hidden = wff1.shape[1]
    tokens = x.shape[0]
    length = seg_ref.shape[1]
    rows_here = tokens // length
    lanes_half = width // 2
    wins = windows(length)
    size = wins[0][2]
    blocks = tokens // QB
    heads = width // 256
    units = rows_here * heads
    piece = cols
    pieces = bank.shape[1] // piece
    quarter = piece // 4

    def load(i, src, dst):
        copy = pltpu.make_async_copy(src, dst, sem.at[i])
        copy.start()
        return copy

    mine = pl.ds(pl.multiple_of(c * tokens, QB), tokens)
    feed_1, feed_2 = 4 * cols, 4 * cols + width
    loads = [load(j, wqkv.at[j], flat.at[j * cols : (j + 1) * cols]) for j in range(3)]
    loads.append(load(3, wout, flat.at[3 * cols : feed_1]))
    loads.append(load(4, wff1, flat.at[feed_1:feed_2]))
    spans = [(j * cols, cols) for j in range(4)]
    spans += [(4 * cols, width), (4 * cols + width, hidden)]

    barrier = pltpu.get_barrier_semaphore()
    for peer in (sib, far, diagonal, side, inner):
        pl.semaphore_signal(barrier, inc=1, device_id=peer, device_id_type=MESH)
    small[pl.ds(t, 1)] = jnp.zeros((1, 8, width), F32)
    small[pl.ds(t, 1), 0:1, 0:hidden] = bff1[...].reshape(1, 1, hidden)
    small[pl.ds(t, 1), 1:3, 0:cols] = bqv[...][None]
    for j, (begin, count) in enumerate(spans):
        loads[j].wait()
        if j == 3:
            loads.append(load(5, wff2, flat.at[feed_2 : feed_2 + hidden]))
        if j == 4:
            x_load = load(6, x_hbm.at[mine], x)
        top = jnp.max(jnp.abs(flat[begin : begin + count]), axis=(0, 1), keepdims=True)
        small[pl.ds(t, 1), 3:4, 128 * j : 128 * (j + 1)] = jnp.broadcast_to(top, (1, 128))[None]
    pl.semaphore_wait(barrier, 5)
    sends = []
    for i, peer in enumerate((sib, far, diagonal)):
        copy = pltpu.make_async_remote_copy(
            src_ref=small.at[t], dst_ref=small.at[t], send_sem=small_s.at[i],
            recv_sem=small_r.at[i], device_id=peer, device_id_type=MESH,
        )
        copy.start()
        sends.append(copy)

    x_load.wait()

    def input_block(b, _):
        rows = pl.ds(pl.multiple_of(b * QB, QB), QB)
        coded, squash = quantize(x[rows], ranges[0])
        xq[rows] = coded.astype(BF16)
        xs[rows] = (1.0 - squash * squash).astype(BF16)
        return 0

    lax.fori_loop(0, blocks, input_block, 0)
    for r in range(rows_here):
        seg = jnp.broadcast_to(seg_ref[pl.ds(c * rows_here + r, 1)], (16, length))
        hot = (lax.broadcasted_iota(jnp.int32, (16, length), 0) == seg).astype(F32).astype(BF16)
        for b, (first, low, _) in enumerate(wins):
            same = dot_tn(hot[:, first : first + QB], hot[:, low : low + size])
            bias[r, b] = (same - 1.0) * -MASKED
    outs = []

    def put(src, dst):
        copy = pltpu.make_async_copy(src, dst, out_sem.at[len(outs)])
        copy.start()
        outs.append(copy)
        return copy

    for copy in sends:
        copy.wait()
    top_row = jnp.max(small[:, 3:4, :], axis=0)
    for j in range(len(spans)):
        top_out[j] = jnp.max(top_row[:, 128 * j : 128 * (j + 1)])

    other = flip(t, 2)
    next_side, next_inner, across = flip(corner, 1), flip(corner, 2), flip(flip(corner, 1), 2)

    def moved(p, shard, which, sems, at, to):
        rows = pl.ds(pl.multiple_of(p * piece + which * quarter, 16), quarter)
        there = bank.at[shard, rows]
        return pltpu.make_async_remote_copy(
            src_ref=there, dst_ref=there, send_sem=sems[0].at[at], recv_sem=sems[1].at[at],
            device_id=to, device_id_type=MESH,
        )

    def sib_copy(p):
        there = bank.at[t, pl.ds(pl.multiple_of(p * piece, 16), piece)]
        return pltpu.make_async_remote_copy(
            src_ref=there, dst_ref=there, send_sem=sib_s.at[p], recv_sem=sib_r.at[p],
            device_id=sib, device_id_type=MESH,
        )

    far_copy = lambda p: moved(p, t, corner, (far_s, far_r), p, far)
    direct_copy = lambda p: moved(p, t, across, (direct_s, direct_r), p, far)
    side_copy = lambda p: moved(p, other, corner, (side_s, side_r), p, side)
    inner_copy = lambda p: moved(p, other, corner, (inner_s, inner_r), p, inner)

    def last_copy(p):
        if p % 2 == 0:
            return moved(p, other, next_inner, (last_s, last_r), p, side)
        return moved(p, other, next_side, (last_s, last_r), p, inner)

    def pass_copy(k, p):
        which = (corner, next_side, next_inner, across)[k]
        return moved(p, other, which, (pass_s, pass_r), (k, p), sib)

    for j in range(len(spans)):
        top = jnp.concatenate([top_row[:, 128 * j : 128 * (j + 1)]] * (width // 128), axis=1)
        scales[0, j : j + 1] = 127.0 / top
        scales[1, j : j + 1] = top / 127.0
    per_feed = width // piece

    def code(p, _):
        at = pl.ds(pl.multiple_of(p * piece, 16), piece)
        late = jnp.maximum(p - 4, 0)
        which = pl.ds(jnp.minimum(p, 4) + late // per_feed, 1)
        bank[t, at] = (stairs(flat[at] * scales[0, which]) * scales[1, which]).astype(BF16)
        far_copy(p).start()
        sib_copy(p).start()

        @pl.when(p == 2)
        def _():
            for first in range(3):
                direct_copy(first).start()

        pl.when(p == 3)(lambda: direct_copy(3).start())
        pl.when(p == pieces - 1)(lambda: direct_copy(pieces - 1).start())
        return 0

    lax.fori_loop(0, pieces, code, 0)
    xq_put = put(xq, xq_out)
    put(xs, xs_out)
    put(bank.at[t], bank_out.at[t])

    def far_step(*found):
        for p in found:
            far_copy(p).wait_recv()
            side_copy(p).start()
            inner_copy(p).start()
            pass_copy(0, p).start()

    def side_step(*found):
        for p in found:
            side_copy(p).wait_recv()
            if p not in DIRECT and p % 2 == 1:
                last_copy(p).start()
            pass_copy(1, p).start()
            inner_copy(p).wait_recv()
            if p not in DIRECT and p % 2 == 0:
                last_copy(p).start()
            pass_copy(2, p).start()

    def last_step(*found):
        for p in found:
            (direct_copy(p) if p in DIRECT else last_copy(p)).wait_recv()
            pass_copy(3, p).start()

    def arrived(own, p):
        if own:
            sib_copy(p).wait_recv()
        else:
            for k in range(4):
                pass_copy(k, p).wait_recv()

    def which_pair(turn):
        return pair + turn - 2 * pair * turn

    def shard_rows(turn, piece_at):
        first = 2 * which_pair(turn)
        at = pl.ds(pl.multiple_of(piece_at * cols, 16), cols)
        return jnp.concatenate([bank[first, at], bank[first + 1, at]], axis=0)

    def half_lanes(turn):
        return pl.ds(pl.multiple_of(which_pair(turn) * lanes_half, 128), lanes_half)

    lanes = lax.broadcasted_iota(jnp.int32, (QB, 128), 1) < HD

    def project(turn):
        first = 2 * which_pair(turn)
        at = half_lanes(turn)

        def one(j, _):
            row = pl.ds(1 + j // 2, 1)
            shift = jnp.concatenate([small[first + i, row, 0:cols] for i in range(2)], axis=1)
            value = dot_nt(xq[...], shard_rows(turn, j)) + jnp.where(j == 1, 0.0, shift)
            qkv[pl.ds(pl.multiple_of(j * tokens, QB), tokens), at] = value.astype(BF16)
            return 0

        lax.fori_loop(0, 3, one, 0)

    def attention(turn, row):
        half = which_pair(turn)
        base = pl.multiple_of(row * length, length)
        spot = pl.multiple_of(row * heads * length, length)
        jobs = [(k, b, head) for k in range(heads) for b in range(len(wins)) for head in range(2)]

        def lane(k):
            return pl.ds(pl.multiple_of((half * heads + k) * 128, 128), 128)

        def score(k, b, head):
            first, low, _ = wins[b]
            queries = qkv[pl.ds(base + first, QB), lane(k)].astype(F32) * 0.125
            inside = lanes if head == 0 else jnp.logical_not(lanes)
            chosen = jnp.where(inside, queries, 0.0).astype(BF16)
            return dot_nt(chosen, qkv[pl.ds(tokens + base + low, size), lane(k)]) + bias[row, b]

        def weigh(k, b, head, scores):
            weights = jnp.exp(scores - jnp.max(scores, -1, keepdims=True))
            share = 1.0 / jnp.sum(weights, -1, keepdims=True)
            low_probs = (weights * share).astype(BF16)
            rows = pl.ds(spot + k * length + wins[b][0], QB)
            probs[rows, head * size : (head + 1) * size] = low_probs
            return low_probs

        scores = [score(*job) for job in jobs]
        weights = [weigh(*job, value) for job, value in zip(jobs, scores)]
        results = []
        for (k, b, _), value in zip(jobs, weights):
            rows = pl.ds(2 * tokens + base + wins[b][1], size)
            results.append(dot_nn(value, qkv[rows, lane(k)]))
        for n in range(0, len(jobs), 2):
            k, b, _ = jobs[n]
            rows = pl.ds(base + wins[b][0], QB)
            coded, squash = quantize(jnp.where(lanes, results[n], results[n + 1]), ranges[1])
            cq[rows, lane(k)] = coded.astype(BF16)
            cs[rows, lane(k)] = (1.0 - squash * squash).astype(BF16)
        p_copy(turn, row).start()

    def p_copy(turn, row):
        spot = pl.multiple_of(row * heads * length, length)
        return pltpu.make_async_copy(
            probs.at[pl.ds(spot, heads * length)],
            p_out.at[row * 2 + which_pair(turn)],
            p_sem.at[row],
        )

    def one_turn(turn, _):
        @pl.when(turn == 0)
        def _():
            for p in range(3):
                arrived(True, p)

        @pl.when(turn == 1)
        def _():
            for p in range(3):
                arrived(False, p)

        project(turn)
        pl.when(turn == 0)(lambda: far_step(0))

        @pl.when(turn == 1)
        def _():
            far_step(4)
            last_step(3)

        def one_row(row, _):
            pl.when(turn == 1)(lambda: p_copy(0, row).wait())
            attention(turn, row)
            for at_turn, at_row, steps in (
                (0, 0, lambda: far_step(1, 2)),
                (0, 1, lambda: side_step(0)),
                (1, 0, lambda: [far_step(5, 6), side_step(3)] and None),
                (1, 1, lambda: [far_step(7), side_step(4)] and None),
            ):
                pl.when(jnp.logical_and(turn == at_turn, row == at_row))(steps)
            return 0

        lax.fori_loop(0, rows_here, one_row, 0)

        @pl.when(turn == 0)
        def _():
            arrived(True, 3)

            def own_attn(b, _):
                rows = pl.ds(pl.multiple_of(b * 2 * QB, QB), 2 * QB)
                total[rows] = dot_nn(cq[rows, half_lanes(0)], shard_rows(0, 3))
                return 0

            lax.fori_loop(0, blocks // 2, own_attn, 0)
            side_step(1)
            far_step(3)
            side_step(2)
            last_step(0, 1, 2)

        return 0

    lax.fori_loop(0, 2, one_turn, 0)
    qkv_puts = [
        put(qkv.at[j * tokens : (j + 1) * tokens], ref) for j, ref in enumerate((q_out, k_out, v_out))
    ]
    put(cq, cq_out)
    put(cs, cs_out)
    arrived(False, 3)

    def norm_block(b, _):
        rows = pl.ds(pl.multiple_of(b * QB, QB), QB)
        attn = total[rows] + dot_nn(cq[rows, half_lanes(1)], shard_rows(1, 3))
        normed, inverse = norm(x[rows] + (attn + shifts[0:1]))
        xh[rows] = normed
        inv[rows] = jnp.broadcast_to(inverse, (QB, 128))
        nq[rows] = quantize(normed * gains[0:1] + shifts[1:2], ranges[2])[0].astype(BF16)
        pl.when(b == 0)(lambda: far_step(8))
        pl.when(b == 1)(lambda: side_step(5))
        pl.when(b == 2)(lambda: side_step(6))
        pl.when(b == 3)(lambda: far_step(9))
        return 0

    lax.fori_loop(0, blocks, norm_block, 0)
    xh_put = put(xh, xh_out)
    put(inv, inv_out)
    nq_put = put(nq, nq_out)
    cot_load = load(6, cot_hbm.at[mine], x)

    for row in range(rows_here):
        p_copy(1, row).wait()
    for copy in qkv_puts:
        copy.wait()

    def spread(i, begin, count):
        shard = (2 * pair + i) % 4
        shift = small[shard, 0:1, 0:hidden]
        places = [pl.multiple_of((begin + b) * QB, QB) for b in range(count)]
        pres = [dot_nn(nq[pl.ds(at, QB)], bank[shard, feed_1:feed_2]) + shift for at in places]
        codes = []
        for at, pre in zip(places, pres):
            cdf = 0.5 * (1.0 + lax.erf(pre * ROOT_HALF))
            coded, squash = quantize(pre * cdf, ranges[3])
            slope = cdf + pre * jnp.exp(-0.5 * pre * pre) * INV_ROOT_TWO_PI
            coded = coded.astype(BF16)
            rows = pl.ds(i % 3 * tokens + at, QB)
            probs[rows] = ((1.0 - squash * squash) * slope).astype(BF16)
            qkv[rows] = coded
            codes.append(coded)
        return codes

    def put_slopes(i):
        at = i % 3 * tokens
        return put(probs.at[at : at + tokens], factor_out.at[i])

    def gather(i, code):
        shard = (2 * pair + i) % 4
        return dot_nn(code, bank[shard, feed_2 : feed_2 + hidden])

    for p in range(4, pieces):
        arrived(True, p)
    put(bank.at[flip(t, 1)], bank_out.at[flip(t, 1)])
    slope_puts, code_puts = [], []

    half_way = blocks // 2
    flat[0:tokens] = jnp.zeros((tokens, width), F32)
    slope_puts, code_puts = [], []

    def own_part(n, _):
        i, begin = n // 2, n % 2 * half_way
        for b, code in enumerate(spread(i, begin, half_way)):
            flat[pl.ds(pl.multiple_of((begin + b) * QB, QB), QB)] += gather(i, code)

        @pl.when(n == 0)
        def _():
            far_step(10)
            side_step(7)
            last_step(4)

        @pl.when(n == 1)
        def _():
            far_step(11)
            side_step(8)
            last_step(5)

        @pl.when(n == 2)
        def _():
            side_step(9)
            last_step(6, 7)

        return 0

    lax.fori_loop(0, 4, own_part, 0)
    side_step(10, 11)
    last_step(8, 11)
    for i in range(2):
        slope_puts.append(put_slopes(i))
        code_puts.append(put(qkv.at[i * tokens : (i + 1) * tokens], gq_out.at[i]))
    for p in range(4, 8):
        arrived(False, p)
    for i in range(2):
        shard = (2 * pair + 2 + i) % 4
        put(bank.at[shard, 0:feed_2], bank_out.at[shard, 0:feed_2])
    slope_puts[0].wait()
    code_puts[0].wait()

    def other_part(n, _):
        spread(2 + n // 2, n % 2 * half_way, half_way)
        pl.when(n == 1)(lambda: last_step(9))
        return 0

    lax.fori_loop(0, 4, other_part, 0)
    put_slopes(2)
    put_slopes(3)
    last_step(10)
    for p in range(8, pieces):
        arrived(False, p)
    for i in range(2):
        shard = (2 * pair + 2 + i) % 4
        put(bank.at[shard, feed_2 : feed_2 + hidden], bank_out.at[shard, feed_2 : feed_2 + hidden])
    def close(n, _):
        for b in range(2):
            at = pl.multiple_of((2 * n + b) * QB, QB)
            found = [qkv[pl.ds(i % 3 * tokens + at, QB)] for i in (2, 3)]
            flat[pl.ds(tokens + at, QB)] = gather(2, found[0]) + gather(3, found[1])
        return 0

    lax.fori_loop(0, half_way, close, 0)

    cot_load.wait()
    xq_put.wait()
    xh_put.wait()
    nq_put.wait()
    sums_out[...] = jnp.zeros_like(sums_out)

    def ends(b):
        rows = pl.ds(pl.multiple_of(b * QB, QB), QB)
        there = pl.ds(pl.multiple_of(c * tokens + b * QB, QB), QB)
        local = [
            pltpu.make_async_copy(src.at[rows], dst, end_sem.at[k, b])
            for k, (src, dst) in enumerate(
                ((xq, lo_out.at[there]), (nq, do_out.at[rows]))
            )
        ]
        remote = pltpu.make_async_remote_copy(
            src_ref=xq.at[rows], dst_ref=lo_out.at[there], send_sem=lo_s.at[b], recv_sem=lo_r.at[b],
            device_id=sib, device_id_type=MESH,
        )
        return local + [remote]

    def last_block(b, _):
        rows = pl.ds(pl.multiple_of(b * QB, QB), QB)
        first = xh[rows] * gains[0:1] + shifts[1:2]
        feed = flat[rows] + flat[pl.ds(pl.multiple_of(tokens + b * QB, QB), QB)]
        normed, inverse = norm(first + (feed + shifts[2:3]))
        xq[rows] = (normed * gains[1:2] + shifts[3:4]).astype(BF16)
        grad = x[rows]
        back = norm_back(grad * gains[1:2], normed, inverse)
        nq[rows] = back.astype(BF16)
        for copy in ends(b):
            copy.start()
        sums_out[1:2] += jnp.sum(grad * normed, 0, keepdims=True)
        sums_out[4:5] += jnp.sum(back, 0, keepdims=True)
        sums_out[5:6] += jnp.sum(grad, 0, keepdims=True)
        return 0

    lax.fori_loop(0, blocks, last_block, 0)

    def sent(p, _):
        far_copy(p).wait_send()
        sib_copy(p).wait_send()
        side_copy(p).wait_send()
        inner_copy(p).wait_send()
        for k in range(4):
            pass_copy(k, p).wait_send()
        return 0

    lax.fori_loop(0, pieces, sent, 0)
    for p in range(pieces):
        (direct_copy(p) if p in DIRECT else last_copy(p)).wait_send()
    waited = [xq_put, xh_put, nq_put] + qkv_puts + [slope_puts[0], code_puts[0]]
    for copy in outs:
        if not any(copy is other_copy for other_copy in waited):
            copy.wait()
    for b in range(blocks):
        for copy in ends(b):
            copy.wait()


def forward(inputs, segment_ids, w_qkv, b_qv, w_out, w_ff1, b_ff1, w_ff2, gains, shifts, ranges, cotangent):
    cols, width = w_out.shape
    hidden = w_ff1.shape[1]
    rows, length = segment_ids.shape
    tokens = inputs.shape[0] // 2
    size = windows(length)[0][2]
    bank_rows = 4 * cols + width + hidden
    pieces = bank_rows // cols
    dma = pltpu.SemaphoreType.DMA
    low = lambda *shape: pltpu.VMEM(shape, BF16)
    full = lambda *shape: pltpu.VMEM(shape, F32)
    wide = S((tokens, width), BF16)
    deep = S((tokens, width), F32)
    return pl.pallas_call(
        forward_kernel,
        out_shape=(
            S((4, bank_rows, width), BF16),
            S((6,), F32),
            wide, wide, wide, wide, wide,
            S((rows, width // 256 * length, 2 * size), BF16),
            wide, wide, wide, deep,
            S((tokens, 128), F32),
            S((2 * tokens, width), BF16),
            S((2, tokens, hidden), BF16),
            S((4, tokens, hidden), BF16),
            wide,
            S((8, width), F32),
        ),
        in_specs=[ANY] * 4 + [VMEM] * 2 + [ANY] * 2 + [VMEM] * 3 + [SMEM],
        out_specs=(ANY, SMEM) + (ANY,) * 15 + (VMEM,),
        scratch_shapes=[
            low(4, bank_rows, width),
            full(max(bank_rows, 2 * tokens), width),
            full(tokens, width),
            low(tokens, width),
            low(tokens, width),
            low(3 * tokens, width),
            low(max(rows // 2 * (width // 256) * length, 3 * tokens), 2 * size),
            low(tokens, width),
            low(tokens, width),
            full(tokens, width),
            full(tokens // length, length // QB, QB, size),
            full(tokens, width),
            low(tokens, width),
            full(tokens, 128),
            full(4, 8, width),
            full(2, 8, width),
            dma((7,)), dma((24,)), dma((rows // 2,)), dma((3, tokens // QB)),
            dma((tokens // QB,)), dma((tokens // QB,)), dma((3,)), dma((3,)),
            *[dma((pieces,))] * 12,
            dma((4, pieces)), dma((4, pieces)),
        ],
        compiler_params=pltpu.CompilerParams(
            collective_id=1, has_side_effects=True, vmem_limit_bytes=62 * MIB
        ),
        name="forward",
    )(
        jnp.swapaxes(w_qkv, 1, 2), w_out, w_ff1, w_ff2, b_qv, b_ff1, inputs, cotangent,
        segment_ids, gains, shifts, ranges,
    )


GROUP = 192
QUARTER = GROUP // 4
HOPS = ("core", "y", "z1", "z2", "z3", "ag")
LINE_HOPS = ("zs1", "zs2", "zy", "zb1", "zb2", "zb3")


def sum_scratch(groups, width, extra, small_shape):
    count = max(extra, 1)
    dma = pltpu.SemaphoreType.DMA
    buf = lambda *shape: pltpu.VMEM(shape + (width,), BF16)
    kinds = dict(
        own=buf(groups * GROUP), got_y=buf(groups, QUARTER), part=buf(groups, QUARTER),
        got_1=buf(groups, QUARTER), got_2=buf(groups, QUARTER), got_x=buf(count, 2, QUARTER),
        line_1=buf(groups, 2, QUARTER), line_2=buf(groups, 2, QUARTER), line_y=buf(groups, 2, QUARTER),
        line_x=buf(count, 2, 2, QUARTER),
        small_own=pltpu.VMEM(small_shape, F32), small_got=pltpu.VMEM((5 + extra,) + small_shape, F32),
        x_s=dma((count, groups)), x_r=dma((count, groups)),
        lx_s=dma((count, groups, 2)), lx_r=dma((count, groups, 2)),
        small_s=dma((5 + extra,)), small_r=dma((5 + extra,)),
    )
    for hop in HOPS:
        kinds[hop + "_s"], kinds[hop + "_r"] = dma((groups,)), dma((groups,))
    for hop in LINE_HOPS:
        kinds[hop + "_s"], kinds[hop + "_r"] = dma((groups, 2)), dma((groups, 2))
    return list(kinds), list(kinds.values())


TICKS = (
    ((0, 1),),
    ((0, 0), (0, 3), (0, 2), (1, 1)),
    ((1, 0),),
    ((2, 1),),
    ((1, 3),),
    ((3, 1), (2, 0), (0, 7), (0, 5), (1, 2), (0, 6)),
    ((2, 3), (0, 4), (1, 5), (4, 1)),
    ((3, 0), (2, 2)),
    ((3, 3), (1, 6), (5, 1)),
    ((2, 5), (4, 0)),
    ((3, 2), (1, 4), (0, 8), (4, 3)),
    ((2, 6),),
    ((3, 5), (5, 0), (1, 8)),
    ((4, 2),),
    ((5, 3), (2, 4)),
    ((3, 6), (1, 7), (4, 5)),
    ((2, 8), (5, 2)),
    (
        (0, 11), (3, 4), (4, 6), (2, 7), (5, 5), (6, 1), (6, 0), (0, 10),
        (1, 11), (3, 8), (0, 9), (1, 10), (4, 4),
    ),
    ((2, 11), (3, 7), (5, 6)),
    ((4, 8), (1, 9)),
    ((5, 4), (2, 10)),
    ((3, 11), (4, 7)),
    (),
    ((2, 9), (5, 8)),
    ((4, 11), (6, 5), (3, 10), (5, 7)),
    (),
    (
        (5, 11), (3, 9), (4, 10), (6, 11), (4, 9), (5, 10), (6, 7), (6, 4),
        (6, 3), (6, 6), (5, 9), (6, 2), (6, 10), (6, 8), (6, 9),
    ),
)


class GradientSum:
    def __init__(self, extra, mine, theirs, result, refs):
        self.__dict__.update(refs)
        self.extra, self.mine, self.theirs, self.result = extra, mine, theirs, result
        t, d = lax.axis_index("tensor"), lax.axis_index("dp")
        self.y = d % 2
        self.z = (d // 2) % 4
        self.end = jnp.logical_or(self.z == 0, self.z == 3)
        self.middle = jnp.logical_not(self.end)
        self.sib = (d, flip(t, 1))
        self.side = (flip(d, 1), t)
        self.inner = (flip(d, 2), t)
        self.across = (d + 2 * (3 - 2 * self.z), t)
        self.others = [(flip(d, 8 << b), t) for b in range(extra)]
        self.beyond = [self.across] + self.others
        self.groups = self.own.shape[0] // GROUP

    def announce(self):
        barrier = pltpu.get_barrier_semaphore()

        def tell(peers):
            for peer in peers:
                pl.semaphore_signal(barrier, inc=1, device_id=peer, device_id_type=MESH)

        tell([self.sib, self.side, self.inner])
        pl.when(self.middle)(lambda: tell(self.beyond))

    def meet(self):
        barrier = pltpu.get_barrier_semaphore()
        pl.when(self.end)(lambda: pl.semaphore_wait(barrier, 3))
        pl.when(self.middle)(lambda: pl.semaphore_wait(barrier, 3 + len(self.beyond)))

    def remote(self, src, dst, hop, at, to):
        return pltpu.make_async_remote_copy(
            src_ref=src, dst_ref=dst, send_sem=getattr(self, hop + "_s").at[at],
            recv_sem=getattr(self, hop + "_r").at[at], device_id=to, device_id_type=MESH,
        )

    def small(self, i, to):
        return self.remote(self.small_own, self.small_got.at[i], "small", i, to)

    def small_add(self, i, to):
        self.small(i, to).wait()
        self.small_own[...] = self.small_own[...] + self.small_got[i]

    def small_step(self, step):
        if step == 0:
            self.small(0, self.sib).start()
        if step == 1:
            self.small_add(0, self.sib)
            self.small(1, self.side).start()
        if step == 2:
            self.small_add(1, self.side)
            pl.when(self.end)(lambda: self.small(2, self.inner).start())
        if step == 3:

            def inward():
                self.small(2, self.inner).wait_recv()
                self.small_own[...] = self.small_own[...] + self.small_got[2]
                self.small(3, self.across).start()

            pl.when(self.middle)(inward)
        if step == 4:

            def outward():
                self.small_add(3, self.across)
                for b, peer in enumerate(self.others):
                    self.small(5 + b, peer).start()
                    self.small_add(5 + b, peer)
                self.small(4, self.inner).start()

            pl.when(self.middle)(outward)
        if step == 5:

            def received():
                self.small(2, self.inner).wait_send()
                self.small(4, self.inner).wait_recv()
                self.small_own[...] = self.small_got[4]

            pl.when(self.end)(received)
            pl.when(self.middle)(lambda: self.small(4, self.inner).wait_send())

    def span(self, g):
        return pl.ds(pl.multiple_of(g * GROUP, 16), GROUP)

    def half(self, g, which):
        return pl.ds(pl.multiple_of(g * GROUP + which * QUARTER, 16), QUARTER)

    def line(self, g, i):
        return pl.ds(pl.multiple_of(g * GROUP + (2 + i) * QUARTER, 16), QUARTER)

    def core(self, g):
        return self.remote(self.theirs.at[self.span(g)], self.own.at[self.span(g)], "core", g, self.sib)

    def hop(self, name, g):
        if name == "y":
            return self.remote(self.own.at[self.half(g, 1 - self.y)], self.got_y.at[g], "y", g, self.side)
        if name == "z1":
            return self.remote(self.part.at[g], self.got_1.at[g], "z1", g, self.inner)
        if name == "z2":
            return self.remote(self.part.at[g], self.got_2.at[g], "z2", g, self.across)
        there = self.result.at[self.half(g, self.y)]
        return self.remote(there, there, name, g, self.inner if name == "z3" else self.side)

    def line_hop(self, name, g, i):
        mine = self.own.at[self.line(g, i)]
        if name == "zs1":
            return self.remote(mine, self.line_1.at[g, i], name, (g, i), self.inner)
        if name == "zs2":
            return self.remote(mine, self.line_2.at[g, i], name, (g, i), self.across)
        if name == "zy":
            return self.remote(mine, self.line_y.at[g, i], name, (g, i), self.side)
        there = self.result.at[self.line(g, i)]
        return self.remote(there, there, name, (g, i), self.across if name == "zb2" else self.inner)

    def stage(self, s, g):
        add = lambda a, b: (a.astype(F32) + b.astype(F32)).astype(BF16)
        when = lambda condition, body: pl.when(condition)(body)
        root = [self.z == 1, self.z == 2]
        passer = [self.z == 2, self.z == 1]
        near = [self.z == 0, self.z == 3]
        far = [self.z == 3, self.z == 0]
        if s == 0:
            self.core(g).start()
        if s == 1:
            self.core(g).wait()

            def add_rows(n, _):
                rows = pl.ds(pl.multiple_of(g * GROUP + n * QUARTER, 16), QUARTER)
                self.own[rows] = add(self.own[rows], self.mine[rows])
                return 0

            lax.fori_loop(0, 4, add_rows, 0)
            self.hop("y", g).start()
            when(self.end, lambda: [self.line_hop("zs1", g, i).start() for i in range(2)] and None)
        if s == 2:
            self.hop("y", g).wait()
            self.part[g] = add(self.own[self.half(g, self.y)], self.got_y[g])
            when(self.end, lambda: self.hop("z1", g).start())
            for i in range(2):

                def gather(i=i):
                    self.line_hop("zs1", g, i).wait_recv()
                    rows = self.line(g, i)
                    self.own[rows] = add(self.own[rows], self.line_1[g, i])
                    when(passer[i], lambda: self.line_hop("zs2", g, i).start())

                when(self.middle, gather)
        if s == 3:

            def middle():
                self.hop("z1", g).wait_recv()
                self.part[g] = add(self.part[g], self.got_1[g])
                self.hop("z2", g).start()

            when(self.middle, middle)
            for i in range(2):

                def at_root(i=i):
                    self.line_hop("zs2", g, i).wait_recv()
                    rows = self.line(g, i)
                    self.own[rows] = add(self.own[rows], self.line_2[g, i])
                    self.line_hop("zy", g, i).start()

                when(root[i], at_root)
        if s == 4:

            def total():
                self.hop("z2", g).wait()
                self.part[g] = add(self.part[g], self.got_2[g])
                for b in range(self.extra):
                    copy = self.remote(self.part.at[g], self.got_x.at[b, g % 2], "x", (b, g), self.others[b])
                    copy.start()
                    copy.wait()
                    self.part[g] = add(self.part[g], self.got_x[b, g % 2])
                self.result[self.half(g, self.y)] = self.part[g]
                self.hop("ag", g).start()
                self.hop("z3", g).start()

            when(self.middle, total)
            for i in range(2):

                def spread(i=i):
                    self.line_hop("zy", g, i).wait()
                    rows = self.line(g, i)
                    self.own[rows] = add(self.own[rows], self.line_y[g, i])
                    for b in range(self.extra):
                        copy = self.remote(
                            self.own.at[rows], self.line_x.at[b, g % 2, i], "lx", (b, g, i), self.others[b]
                        )
                        copy.start()
                        copy.wait()
                        self.own[rows] = add(self.own[rows], self.line_x[b, g % 2, i])
                    self.result[rows] = self.own[rows]
                    self.line_hop("zb2", g, i).start()
                    self.line_hop("zb1", g, i).start()

                when(root[i], spread)
        if s == 5:

            def outer():
                self.hop("z3", g).wait_recv()
                self.hop("ag", g).start()

            when(self.end, outer)
            for i in range(2):

                def onward(i=i):
                    self.line_hop("zb2", g, i).wait_recv()
                    self.line_hop("zb3", g, i).start()

                when(passer[i], onward)
        if s == 6:
            self.hop("ag", g).wait()
            for i in range(2):
                when(near[i], lambda i=i: self.line_hop("zb1", g, i).wait_recv())
                when(far[i], lambda i=i: self.line_hop("zb3", g, i).wait_recv())

                def sent_root(i=i):
                    self.line_hop("zb1", g, i).wait_send()
                    self.line_hop("zb2", g, i).wait_send()

                def sent_passer(i=i):
                    self.line_hop("zs2", g, i).wait_send()
                    self.line_hop("zb3", g, i).wait_send()

                when(root[i], sent_root)
                when(passer[i], sent_passer)

            def sent_end():
                self.hop("z1", g).wait_send()
                for i in range(2):
                    self.line_hop("zs1", g, i).wait_send()

            when(self.end, sent_end)
            when(self.middle, lambda: self.hop("z3", g).wait_send())

    def run(self, events):
        for stage, group in events:
            self.stage(stage, group)


def back_kernel(
    extra, names,
    do_hbm, gq_hbm, factor_hbm, nq_hbm, bank, xh_hbm, inv_hbm, sums_ref,
    cs_hbm, cq_hbm, q_hbm, k_hbm, v_hbm, p_hbm, xq_hbm, xs_hbm, gains, shifts, ranges,
    g2_out, g1_out, go_out, gq_out, gains_out, shifts_out, bqv_out, bff1_out, dx_full,
    result, inv, grads, do, weights, gq, factor, nq, low, total, dh, xh, wo, cq, dproj, sem, dx_send, dx_recv,
    *refs,
):
    t, d = lax.axis_index("tensor"), lax.axis_index("dp")
    c, pair = t % 2, t // 2
    engine = GradientSum(extra, grads.at[c], grads.at[1 - c], result, dict(zip(names, refs)))
    tokens, width = do.shape
    hidden = gq_hbm.shape[2]
    side = width // 2
    cols = side // 2
    heads = width // 128 // 2
    length = p_hbm.shape[1] // heads
    wins = windows(length)
    size = wins[0][2]
    blocks = tokens // QB
    slots = factor.shape[0] // length

    def load(i, src, dst):
        copy = pltpu.make_async_copy(src, dst, sem.at[i])
        copy.start()
        return copy

    def shard_at(i):
        return (2 * pair + i) % 4

    def load_codes(begin, end, sems):
        return [
            load(sems[i], gq_hbm.at[i, :, begin:end], gq.at[i * tokens : (i + 1) * tokens, begin:end])
            for i in range(2)
        ]

    half_way = hidden // 2
    first_loads = [load(0, do_hbm, do)] + load_codes(0, half_way, (1, 2))

    def load_pair(base):
        copies = []
        for i in range(2):
            s = shard_at(base + i)
            at = pl.ds(i * tokens, tokens)
            for j in range(2):
                spot = weights.at[(2 * j + i) * width : (2 * j + i + 1) * width]
                copies.append(load(3 + 2 * j + i, bank.at[s, 4 * cols + j * width : 4 * cols + (j + 1) * width], spot))
            copies.append(load(7 + i, factor_hbm.at[base + i], factor.at[at]))
        return copies

    engine.announce()
    at = pl.ds(pl.multiple_of(c * tokens, 256), tokens)
    engine.small_own[...] = jnp.zeros_like(engine.small_own)
    engine.small_own[0:8] = sums_ref[...]

    def tick(point):
        engine.run(TICKS[point])

    for copy in first_loads:
        copy.wait()
    code_loads = load_codes(half_way, hidden, (12, 14))
    pair_loads = load_pair(0)

    def weights_2(n, _):
        part, i = n // 2, n % 2
        lanes = pl.ds(pl.multiple_of(part * half_way, 128), half_way)
        value = dot_tn(gq[pl.ds(pl.multiple_of(i * tokens, QB), tokens), lanes], do[...])
        grads[i, pl.ds(pl.multiple_of(part * half_way, 16), half_way)] = value.astype(BF16)

        @pl.when(n == 1)
        def _():
            engine.meet()
            tick(0)
            for copy in code_loads:
                copy.wait()

        return 0

    lax.fori_loop(0, 4, weights_2, 0)
    tick(1)
    for copy in pair_loads:
        copy.wait()
    nq_load = load(9, nq_hbm, nq)
    norm_loads = [load(11, xh_hbm, xh), load(15, inv_hbm, inv)]

    def feed_blocks(own, first, second):
        def one(n, _):
            places = [pl.multiple_of((2 * n + b) * QB, QB) for b in range(2)]
            backs = [
                [
                    dot_nt(do[pl.ds(at, QB)], weights[(2 + i) * width : (3 + i) * width])
                    for i in range(2)
                ]
                for at in places
            ]
            lows = []
            for at, pairs in zip(places, backs):
                lows.append([])
                for i in range(2):
                    spot = pl.ds(i * tokens + at, QB)
                    value = pairs[i] * factor[spot].astype(F32)
                    short = value.astype(BF16)
                    if own:
                        engine.small_own[6 + i : 7 + i] += jnp.sum(value, 0, keepdims=True)
                        low[spot] = short
                    lows[-1].append(short)
            for at, (one_low, two_low) in zip(places, lows):
                rows = pl.ds(at, QB)
                part = dot_nt(one_low, weights[0:width]) + dot_nt(two_low, weights[width : 2 * width])
                total[rows] = part if own else total[rows] + part
            pl.when(n == 0)(functools.partial(tick, first))
            return 0

        lax.fori_loop(0, blocks // 2, one, 0)
        if second is not None:
            tick(second)

    feed_blocks(True, 2, 3)
    pair_loads = load_pair(2)
    nq_load.wait()

    def weights_1(i, _):
        part = dot_tn(nq[...], low[pl.ds(pl.multiple_of(i * tokens, QB), tokens)])
        grads[i, hidden : 2 * hidden] = part.astype(BF16)
        pl.when(i == 0)(functools.partial(tick, 4))
        return 0

    lax.fori_loop(0, 2, weights_1, 0)
    tick(5)
    for copy in pair_loads:
        copy.wait()
    wo_loads = [
        load(27 + s, bank.at[s, 3 * cols : 4 * cols], wo.at[s * cols : (s + 1) * cols]) for s in range(4)
    ]
    mine = pl.ds(pl.multiple_of(pair * side, 128), side)
    cq_load = load(13, cq_hbm.at[:, mine], cq)
    cs_load = load(9, cs_hbm, nq)
    feed_blocks(False, 6, None)
    qkv_loads = [
        load(18 + j, src, weights.at[j * tokens : (j + 1) * tokens])
        for j, src in enumerate((q_hbm, k_hbm, v_hbm))
    ]

    def unit_at(own, u):
        return u // heads, u % heads

    def probs_load(own, u):
        row, which = unit_at(own, u)
        slot = u % slots
        return pltpu.make_async_copy(
            p_hbm.at[row * 2 + (pair if own else 1 - pair), pl.ds(pl.multiple_of(which * length, length), length)],
            factor.at[pl.ds(pl.multiple_of(slot * length, length), length)],
            sem.at[22 + slot],
        )

    units = 2 * heads
    for u in range(slots - 1):
        probs_load(True, u).start()
    tick(7)

    for copy in norm_loads:
        copy.wait()
    xq_load = load(17, xq_hbm, low.at[tokens : 2 * tokens])
    wt_loads = [
        load(31 + s, bank.at[s, 0 : 3 * cols], gq.at[3 * s * cols : 3 * (s + 1) * cols]) for s in range(4)
    ]

    def norm_block(b, _):
        rows = pl.ds(pl.multiple_of(b * QB, QB), QB)
        normed = xh[rows]
        squash = jnp.tanh((normed * gains[0:1] + shifts[1:2]) * (1.0 / ranges[2]))
        grad = do[rows].astype(F32) + total[rows] * (1.0 - squash * squash)
        inverse = jnp.max(inv[rows], axis=1, keepdims=True)
        back = norm_back(grad * gains[0:1], normed, inverse)
        dh[rows] = back
        low[rows] = back.astype(BF16)
        engine.small_own[0:1] += jnp.sum(grad * normed, 0, keepdims=True)
        engine.small_own[2:3] += jnp.sum(back, 0, keepdims=True)
        engine.small_own[3:4] += jnp.sum(grad, 0, keepdims=True)
        return 0

    lax.fori_loop(0, blocks, norm_block, 0)
    xs_load = load(21, xs_hbm, do)
    tick(8)
    for copy in wo_loads:
        copy.wait()
    cq_load.wait()
    cs_load.wait()
    d_attn = low.at[0:tokens]
    part = dot_tn(cq[...], d_attn[...]).astype(BF16)
    for i in range(2):
        grads[i, 2 * hidden : 2 * hidden + cols] = part[i * cols : (i + 1) * cols]
    tick(9)

    def context_block(b, _):
        rows = pl.ds(pl.multiple_of(b * QB, QB), QB)
        nq[rows] = (dot_nt(d_attn[rows], wo[...]) * nq[rows].astype(F32)).astype(BF16)
        return 0

    lax.fori_loop(0, blocks, context_block, 0)
    tick(10)

    for copy in qkv_loads:
        copy.wait()
    lanes = lax.broadcasted_iota(jnp.int32, (QB, 128), 1) < HD

    def attention(own, u):
        row, which = unit_at(own, u)
        probs_load(own, u).wait()

        @pl.when(u + slots - 1 < units)
        def _():
            probs_load(own, u + slots - 1).start()

        half = pair if own else 1 - pair
        lane = pl.ds(pl.multiple_of((half * heads + which) * 128, 128), 128)
        here = pl.ds(pl.multiple_of(which * 128, 128), 128)
        slot = pl.multiple_of((u % slots) * length, length)
        base = pl.multiple_of(row * length, length)
        wide = lax.broadcasted_iota(jnp.int32, (size, 128), 1) < HD
        jobs = [(b, head) for b in range(len(wins)) for head in range(2)]

        def shares(b, head):
            return factor[pl.ds(slot + wins[b][0], QB), head * size : (head + 1) * size]

        def first_product(b, head):
            first, begin, _ = wins[b]
            own_lanes = lanes if head == 0 else jnp.logical_not(lanes)
            context = nq[pl.ds(base + first, QB), lane].astype(F32)
            chosen = jnp.where(own_lanes, context, 0.0).astype(BF16)
            return dot_nt(chosen, weights[pl.ds(2 * tokens + base + begin, size), lane])

        def d_score(b, head, d_probs):
            exact = shares(b, head).astype(F32)
            both = exact * d_probs
            return (both - exact * jnp.sum(both, -1, keepdims=True)).astype(BF16)

        def products(b, head, d_low):
            first, begin, _ = wins[b]
            rows = pl.ds(base + first, QB)
            return (
                dot_nn(d_low, weights[pl.ds(tokens + base + begin, size), lane]),
                dot_tn(d_low, weights[rows, lane]),
                dot_tn(shares(b, head), nq[rows, lane]),
            )

        d_probs = [first_product(*job) for job in jobs]
        d_lows = [d_score(*job, value) for job, value in zip(jobs, d_probs)]
        found = [products(*job, value) for job, value in zip(jobs, d_lows)]
        d_keys, d_values = [], []
        for b, (first, _, _) in enumerate(wins):
            got = found[2 * b : 2 * b + 2]
            rows = pl.ds(base + first, QB)
            dproj[0, rows, here] = (jnp.where(lanes, got[0][0], got[1][0]) * 0.125).astype(BF16)
            d_keys.append(jnp.where(wide, got[0][1], got[1][1]))
            d_values.append(jnp.where(wide, got[0][2], got[1][2]))
        for j, parts, scale in ((1, d_keys, 0.125), (2, d_values, 1.0)):
            for spot in range(0, length, SPAN):
                terms = [
                    part[spot - begin : spot - begin + SPAN]
                    for part, (_, begin, _) in zip(parts, wins)
                    if begin <= spot < begin + size
                ]
                dproj[j, pl.ds(base + spot, SPAN), here] = (sum(terms[1:], terms[0]) * scale).astype(BF16)

    def back_through(own, finish):
        first = 2 * pair if own else 2 - 2 * pair

        def rows(j):
            found = [
                gq[pl.ds(pl.multiple_of(((first + i) * 3 + j) * cols, 16), cols)] for i in range(2)
            ]
            return jnp.concatenate(found, axis=0)

        def block(n, _):
            at = pl.ds(pl.multiple_of(n * QB, QB), QB)
            terms = [dot_nn(dproj[j, at], rows(j)) for j in range(3)]
            finish(at, terms[0] + terms[1] + terms[2])
            return 0

        lax.fori_loop(0, blocks, block, 0)

    def ticks_after(u, first):
        for k in range(units):
            if TICKS[first + k]:
                pl.when(u == k)(functools.partial(tick, first + k))

    def own_unit(u, _):
        attention(True, u)
        ticks_after(u, 11)
        return 0

    lax.fori_loop(0, units, own_unit, 0)
    for u in range(slots - 1):
        probs_load(False, u).start()
    for copy in wt_loads:
        copy.wait()
    xq_load.wait()
    def weights_qkv(j, _):
        part = dot_tn(dproj[j], low[tokens : 2 * tokens]).astype(BF16)
        at = pl.ds(pl.multiple_of(2 * hidden + (j + 1) * cols, 16), cols)
        for i in range(2):
            grads[i, at] = part[i * cols : (i + 1) * cols]
        return 0

    lax.fori_loop(0, 3, weights_qkv, 0)
    engine.small_own[8:9, 0:side] = jnp.sum(dproj[0].astype(F32), 0, keepdims=True)
    engine.small_own[9:10, 0:side] = jnp.sum(dproj[2].astype(F32), 0, keepdims=True)
    tick(17)
    engine.small_step(0)

    def keep(rows, value):
        total[rows] = value

    back_through(True, keep)
    tick(18)

    def other_unit(u, _):
        attention(False, u)
        ticks_after(u, 19)
        for k, step in ((0, 1), (3, 2)):
            pl.when(u == k)(functools.partial(engine.small_step, step))
        return 0

    lax.fori_loop(0, units, other_unit, 0)
    xs_load.wait()

    def results(rows, value):
        factor[rows] = (dh[rows] + (total[rows] + value) * do[rows].astype(F32)).astype(BF16)

    back_through(False, results)
    dx_copy = pltpu.make_async_remote_copy(
        src_ref=factor.at[0:tokens], dst_ref=dx_full.at[at], send_sem=dx_send, recv_sem=dx_recv,
        device_id=engine.sib, device_id_type=MESH,
    )
    dx_copy.start()
    outs = [load(26, factor.at[0:tokens], dx_full.at[at])]
    tick(25)
    engine.small_step(3)

    def small_results():
        engine.small_step(5)
        sums = engine.small_own[...]
        here = sums[:, 0:cols]
        for s in range(1, 4):
            here = jnp.where(t == s, sums[:, s * cols : (s + 1) * cols], here)
        gains_out[...] = here[0:2]
        shifts_out[...] = here[2:6]
        bqv_out[...] = jnp.where(c == 0, sums[8:10, 0:cols], sums[8:10, cols:side])
        bff1_out[...] = jnp.where(c == 0, sums[6:7], sums[7:8]).reshape(hidden)

    leaving = [
        (0, 4, g2_out, 0, hidden),
        (4, 8, g1_out, hidden, 2 * hidden),
        (8, 9, go_out, 2 * hidden, 2 * hidden + cols),
        (9, 12, gq_out, 2 * hidden + cols, 2 * hidden + 4 * cols),
    ]
    complete = {g for events in TICKS[:-1] for s, g in events if s == 6}
    for n, event in enumerate((None,) + TICKS[-1]):
        if n == 4:
            engine.small_step(4)
        if n == 10:
            small_results()
        if event is not None:
            engine.stage(*event)
            if event[0] == 6:
                complete.add(event[1])
        for k, (first, last, ref, begin, end) in enumerate(leaving):
            if ref is not None and complete.issuperset(range(first, last)):
                outs.append(load(k, result.at[begin:end], ref))
                leaving[k] = (first, last, None, begin, end)
    dx_copy.wait()
    for copy in outs:
        copy.wait()


def back(
    nd, do, gq, factor, nq, bank, xh, inv, sums, cs, cq, q, k, v, probs, xq, xs,
    gains, shifts, ranges,
):
    tokens, width = do.shape
    hidden = gq.shape[2]
    cols = width // 4
    rows = 2 * hidden + 4 * cols
    extra = (nd // 8).bit_length() - 1
    dma = pltpu.SemaphoreType.DMA
    names, scratch = sum_scratch(rows // GROUP, width, extra, (16, width))
    buf = lambda *shape: pltpu.VMEM(shape, BF16)
    return pl.pallas_call(
        functools.partial(back_kernel, extra, names),
        out_shape=(
            S((hidden, width), BF16),
            S((width, hidden), BF16),
            S((cols, width), BF16),
            S((3 * cols, width), BF16),
            S((2, cols), F32),
            S((4, cols), F32),
            S((2, cols), F32),
            S((hidden,), F32),
            S((2 * tokens, width), BF16),
        ),
        in_specs=[ANY] * 7 + [VMEM] + [ANY] * 8 + [VMEM, VMEM, SMEM],
        out_specs=(ANY,) * 4 + (VMEM,) * 4 + (ANY,),
        scratch_shapes=[
            buf(rows, width),
            pltpu.VMEM((tokens, 128), F32),
            buf(2, rows, width),
            buf(tokens, width),
            buf(max(4 * width, 3 * tokens), width),
            buf(max(3 * width, 2 * tokens), width),
            buf(2 * tokens, width),
            buf(tokens, width),
            buf(2 * tokens, width),
            pltpu.VMEM((tokens, width), F32),
            pltpu.VMEM((tokens, width), F32),
            pltpu.VMEM((tokens, width), F32),
            buf(width, width),
            buf(tokens, width // 2),
            buf(3, tokens, width // 2),
            dma((35,)),
            dma,
            dma,
            *scratch,
        ],
        compiler_params=pltpu.CompilerParams(
            collective_id=2, has_side_effects=True, vmem_limit_bytes=62 * MIB
        ),
        name="back",
    )(
        do, gq, factor, nq, bank, xh, inv, sums, cs, cq, q, k, v, probs, xq, xs,
        gains, shifts, ranges,
    )


def finish_kernel(*refs):
    half = len(refs) // 2
    for src, dst in zip(refs[: half - 1], refs[half:-1]):
        dst[...] = src[...].astype(F32)
    for j in range(refs[-1].shape[0]):
        refs[-1][j] = refs[half - 1][j]


def finish(*arrays):
    steps = 8
    specs = []
    for array in arrays[:-1]:
        rows = array.shape[0]
        if array.ndim == 2 and rows % (16 * steps) == 0:
            specs.append(pl.BlockSpec((rows // steps, array.shape[1]), lambda i: (i, 0)))
        elif array.ndim == 2 and rows % (16 * steps // 2) == 0:
            specs.append(pl.BlockSpec((2 * rows // steps, array.shape[1]), lambda i: (i // 2, 0)))
        else:
            specs.append(pl.BlockSpec(array.shape, lambda i, n=array.ndim: (0,) * n))
    specs.append(SMEM)
    return pl.pallas_call(
        finish_kernel,
        out_shape=tuple(S(array.shape, F32) for array in arrays),
        grid=(steps,),
        in_specs=specs,
        out_specs=tuple(specs),
        compiler_params=pltpu.CompilerParams(vmem_limit_bytes=62 * MIB),
        name="finish",
    )(*arrays)


def per_device(
    nd, inputs, segment_ids, w_qkv, b_qv, w_out, w_ff1, b_ff1, w_ff2, norm_gains, shift_biases,
    act_ranges, cotangent,
):
    width = inputs.shape[1]
    cols = w_qkv.shape[2]
    (
        bank, weight_max, xq, xs, q, k, v, probs, cq, cs, nq, xh, inv, layer_out, gq, factor, do, sums,
    ) = forward(
        inputs, segment_ids, w_qkv, b_qv, w_out, w_ff1, b_ff1, w_ff2, norm_gains, shift_biases,
        act_ranges, cotangent,
    )
    (
        grad_ff2, grad_ff1, grad_out, grad_qkv, grad_gains, grad_shifts, grad_bqv, grad_bff1, input_grad,
    ) = back(
        nd, do, gq, factor, nq, bank, xh, inv, sums, cs, cq, q, k, v, probs, xq, xs,
        norm_gains, shift_biases, act_ranges,
    )
    (
        layer_out, input_grad, grad_ff2, grad_ff1, grad_out, grad_qkv, grad_gains, grad_shifts, grad_bqv,
        grad_bff1, weight_max,
    ) = finish(
        layer_out, input_grad, grad_ff2, grad_ff1, grad_out, grad_qkv, grad_gains, grad_shifts, grad_bqv,
        grad_bff1, weight_max,
    )
    grad_qkv = grad_qkv.reshape(3, cols, width).transpose(0, 2, 1)
    return (
        layer_out, input_grad, grad_qkv, grad_bqv, grad_out, grad_ff1, grad_bff1, grad_ff2,
        grad_gains, grad_shifts, weight_max,
    )


def solution(mesh):
    return jax.shard_map(
        functools.partial(per_device, mesh.shape["dp"]),
        mesh=mesh,
        in_specs=(
            P("dp", None),
            P("dp", None),
            P(None, None, "tensor"),
            P(None, "tensor"),
            P("tensor", None),
            P(None, "tensor"),
            P("tensor"),
            P("tensor", None),
            P(),
            P(),
            P(),
            P("dp", None),
        ),
        out_specs=(
            P("dp", None),
            P("dp", None),
            P(None, None, "tensor"),
            P(None, "tensor"),
            P("tensor", None),
            P(None, "tensor"),
            P("tensor"),
            P("tensor", None),
            P(None, "tensor"),
            P(None, "tensor"),
            P(),
        ),
        check_vma=False,
    )
```
